32 devices in a mesh: dp: 16 (over z, y, x), seq: 2 (over core).
Axes of the slice: x: 2, y: 2, z: 4, core: 2. Of those that a mesh axis runs over, the one named last changes fastest.
Arguments:
- inputs: bfloat16 [64, 512, 1024], P('dp', 'seq'), may hold values from -6 to 6
- memory: bfloat16 [64, 512, 1024], P('dp', 'seq'), may hold values from -6 to 6
- compressed: bfloat16 [64, 512, 1024], P('dp', 'seq'), may hold values from -6 to 6
- offsets: int32 [64], P('dp'), may hold values from 0 to 1024, as said below
- resets: int32 [64], P('dp'), may hold values from 0 to 1, as said below
- w_query: bfloat16 [1024, 1024], replicated, may hold values from -0.1875 to 0.1875
- w_key: bfloat16 [1024, 1024], replicated, may hold values from -0.1875 to 0.1875
- w_value: bfloat16 [1024, 1024], replicated, may hold values from -0.1875 to 0.1875
- w_output: bfloat16 [1024, 1024], replicated, may hold values from -3 to 3
- w_hidden: bfloat16 [1024, 4096], P(None, 'seq'), may hold values from -0.1875 to 0.1875
- w_return: bfloat16 [4096, 1024], P('seq'), may hold values from -0.09375 to 0.09375
- w_compress: bfloat16 [3072, 1024], replicated, may hold values from -0.109375 to 0.109375
- gain_attn: bfloat16 [1024], replicated, may hold values from 0.099609375 to 1.8984375
- gain_ffn: bfloat16 [1024], replicated, may hold values from 0.099609375 to 1.8984375
- out_grad: bfloat16 [64, 512, 1024], P('dp', 'seq'), may hold values from -6 to 6
- comp_grad: bfloat16 [64, 170, 1024], P('dp'), may hold values from -6 to 6
Outputs:
- outputs: bfloat16 [64, 512, 1024], P('dp', 'seq')
- new_compressed: bfloat16 [64, 170, 1024], P('dp')
- input_grad: bfloat16 [64, 512, 1024], P('dp', 'seq')
- grad_query: float32 [1024, 1024], P('dp', 'seq')
- grad_key: float32 [1024, 1024], P('dp', 'seq')
- grad_value: float32 [1024, 1024], P('dp', 'seq')
- grad_output: float32 [1024, 1024], P('dp', 'seq')
- grad_hidden: float32 [1024, 4096], P('dp', 'seq')
- grad_return: float32 [4096, 1024], P('seq', 'dp')
- grad_compress: float32 [3072, 1024], P('dp', 'seq')
- grad_gain_attn: float32 [1024], P('dp')
- grad_gain_ffn: float32 [1024], P('dp')
The draws below stay inside these ranges and needn't reach their ends.
Inputs may be any that keep to these rules, and one draw needn't show every extreme that they name: `offsets`: memory slots count oldest first, the 512 compressed slots before the 512 memory slots; slots below a stream's offset are masked. In each block of 4 consecutive streams one stream, at a place drawn from the seed, has offset 0 and reset 0, and the next stream of the block (cyclically) has offset 2 * 512. `resets`: A 1 clears the stream's memories: all its memory slots are masked and its memory enters the compression as zeros. In each block of 4 consecutive streams the stream two places after the one with offset 0 (cyclically) has reset 1.
All inputs are finite; a program needn't handle non-finite values.
Results may differ from the reference program's by a relative error of at most 0.018.
Values may be sent and summed in bfloat16 or wider, within the bound.
A program may use at most 384 MiB of HBM per device.

```python
import jax
import jax.numpy as jnp
from jax import lax

D = 1024
HEADS = 8
HEAD_DIM = 128
FF = 4096
SEG = 512
RATE = 3
STREAM_DEV = 4
STREAMS = 64
CNEW = 170


def stream_roles(key):
    blocks = STREAMS // STREAM_DEV
    chosen = jax.random.randint(jax.random.fold_in(key, 5), (blocks,), 0, STREAM_DEV)
    within_block = jnp.arange(STREAMS, dtype=jnp.int32) % STREAM_DEV
    return (within_block - jnp.repeat(chosen, STREAM_DEV)) % STREAM_DEV


def draw_offsets(key, part):
    stream_role = stream_roles(key)
    key = jax.random.fold_in(key, 3)
    drawn = jax.random.randint(key, (STREAMS,), 0, 2 * SEG + 1)
    return jnp.where(stream_role == 0, 0, jnp.where(stream_role == 1, 2 * SEG, drawn)).astype(jnp.int32)


def draw_resets(key, part):
    stream_role = stream_roles(key)
    key = jax.random.fold_in(key, 4)
    drawn = (jax.random.randint(key, (STREAMS,), 0, 6) == 0).astype(jnp.int32)
    return jnp.where(stream_role == 0, 0, jnp.where(stream_role == 2, 1, drawn)).astype(jnp.int32)


def block_levels(stream_key, shape, cuts, low, largest):
    def one(position, blocks):
        draws = jax.random.uniform(jax.random.fold_in(jax.random.fold_in(stream_key, 6), position), (blocks,), jnp.float32, low / len(cuts), largest / len(cuts))
        return jnp.repeat(jnp.exp(draws), shape[position] // blocks).reshape((-1,) + (1,) * (len(shape) - position - 1))

    factor_of = one(*cuts[0])
    for cut in cuts[1:]:
        factor_of = factor_of * one(*cut)
    return factor_of


def scatter_about(own_key, dims, deviation, reach, cuts=(), held_as=jnp.bfloat16):
    values = deviation * jax.random.normal(own_key, dims, jnp.float32)
    if cuts:
        values = values * block_levels(own_key, dims, cuts, -0.22, 0.18)
    return jnp.clip(values, -reach, reach).astype(held_as)


def setup_inputs(seed: int = 0) -> dict:
    keys = jax.random.split(jax.random.key(seed), 17)
    return {
        "inputs": scatter_about(keys[0], (STREAMS, SEG, D), 1.0, 6.0, ((0, 16), (1, 2))),
        "memory": scatter_about(keys[1], (STREAMS, SEG, D), 1.0, 6.0, ((0, 16), (1, 2))),
        "compressed": scatter_about(keys[2], (STREAMS, SEG, D), 1.0, 6.0, ((0, 16), (1, 2))),
        "offsets": draw_offsets(jax.random.fold_in(keys[16], 71), 0),
        "resets": draw_resets(jax.random.fold_in(keys[16], 71), 0),
        "w_query": scatter_about(keys[5], (D, D), D ** -0.5, 0.1875),
        "w_key": scatter_about(keys[6], (D, D), D ** -0.5, 0.1875),
        "w_value": scatter_about(keys[7], (D, D), D ** -0.5, 0.1875),
        "w_output": scatter_about(keys[8], (D, D), (max(D // 256, 2)) ** -0.5, 3.0),
        "w_hidden": scatter_about(keys[9], (D, FF), D ** -0.5, 0.1875, ((1, 2),)),
        "w_return": scatter_about(keys[10], (FF, D), FF ** -0.5, 0.09375, ((0, 2),)),
        "w_compress": scatter_about(keys[11], (RATE * D, D), (RATE * D) ** -0.5, 0.109375),
        "gain_attn": jnp.clip(1.0 + 0.18 * jax.random.normal(keys[12], (D,), jnp.float32), 0.099609375, 1.8984375).astype(jnp.bfloat16),
        "gain_ffn": jnp.clip(1.0 + 0.18 * jax.random.normal(keys[13], (D,), jnp.float32), 0.099609375, 1.8984375).astype(jnp.bfloat16),
        "out_grad": scatter_about(keys[14], (STREAMS, SEG, D), 1.0, 6.0, ((0, 16), (1, 2))),
        "comp_grad": scatter_about(keys[15], (STREAMS, CNEW, D), 1.0, 6.0, ((0, 16),)),
    }


epsilon = 1e-05
masked_score = -1e+30
highest = lax.Precision.HIGHEST

@jax.custom_vjp
def low(v):
    return lax.optimization_barrier(v.astype(jnp.bfloat16)).astype(jnp.float32)

@jax.custom_vjp
def low_back(v):
    return v

def low_keep(v):
    return (low(v), None)

def low_pass(kept, grad):
    return (grad,)

def back_keep(v):
    return (v, None)

def back_low(kept, grad):
    return (low(grad),)
low.defvjp(low_keep, low_pass)
low_back.defvjp(back_keep, back_low)

def layer_norm(values, gain):
    centred = values - lax.optimization_barrier(jnp.mean(values, axis=-1, keepdims=True))
    spread = lax.optimization_barrier(jnp.mean(centred * centred, axis=-1, keepdims=True))
    return centred * lax.rsqrt(spread + epsilon) * gain

def matmul(left, right):
    return jnp.einsum('...d,de->...e', left, right, precision=highest)

def forward(weights, inputs, memory, compressed, offsets, resets):
    w_query, w_key, w_value, w_output, w_hidden, w_return, w_compress, gain_attn, gain_ffn = weights
    group_size = inputs.shape[0]
    keep_flag = (resets == 0).astype(jnp.float32)
    all_rows = jnp.concatenate([compressed, memory, inputs], axis=1)
    normed = low(layer_norm(all_rows, gain_attn))
    query_heads = low(low_back(matmul(normed[:, 2 * SEG:], w_query))).reshape(group_size, SEG, HEADS, HEAD_DIM)
    key_heads = low(low_back(matmul(normed, w_key))).reshape(group_size, 3 * SEG, HEADS, HEAD_DIM)
    value_heads = low(low_back(matmul(normed, w_value))).reshape(group_size, 3 * SEG, HEADS, HEAD_DIM)
    scores = low_back(jnp.einsum('gthe,gkhe->ghtk', query_heads, key_heads, precision=highest) * HEAD_DIM ** (-0.5))
    key_slot = jnp.arange(3 * SEG, dtype=jnp.int32)
    query_place = jnp.arange(SEG, dtype=jnp.int32)
    memory_ok = (key_slot[None, :] >= offsets[:, None]) & (resets[:, None] == 0)
    causal = key_slot[None, :] - 2 * SEG <= query_place[:, None]
    allowed = jnp.where(key_slot[None, None, :] < 2 * SEG, memory_ok[:, None, :], causal[None, :, :])
    scores = jnp.where(allowed[:, None], scores, masked_score)
    row_top = lax.optimization_barrier(jnp.max(scores, axis=-1, keepdims=True))
    exp_scores = jnp.exp(scores - row_top)
    attn_prob = exp_scores / lax.optimization_barrier(jnp.sum(exp_scores, axis=-1, keepdims=True))
    mixed = jnp.einsum('ghtk,gkhe->gthe', low(attn_prob), value_heads, precision=highest).reshape(group_size, SEG, D)
    mixed = low(low_back(mixed))
    hidden = inputs + low_back(matmul(mixed, w_output))
    ffn_in = low(layer_norm(hidden, gain_ffn))
    pre_act = low_back(matmul(ffn_in, w_hidden))
    activated = low(jax.nn.gelu(pre_act))
    layer_out = hidden + low_back(matmul(activated, w_return))
    grouped = (memory * keep_flag[:, None, None])[:, :RATE * CNEW].reshape(group_size, CNEW, RATE * D)
    return (layer_out, matmul(grouped, w_compress))

def reference(inputs, memory, compressed, offsets, resets, w_query, w_key, w_value, w_output, w_hidden, w_return, w_compress, gain_attn, gain_ffn, out_grad, comp_grad):
    weights = tuple((weight_arg.astype(jnp.float32) for weight_arg in (w_query, w_key, w_value, w_output, w_hidden, w_return, w_compress, gain_attn, gain_ffn)))
    scan_steps = STREAMS // STREAM_DEV

    def by_group(array):
        return array.reshape((scan_steps, STREAM_DEV) + array.shape[1:])

    def group_step(totals, pieces):
        part_in, part_mem, part_comp, part_off, part_reset, part_out, part_cgrad = pieces

        def local_layer(weight_set, layer_in):
            return forward(weight_set, layer_in, part_mem, part_comp, part_off, part_reset)
        (layer_out, packed), pullback = jax.vjp(local_layer, weights, part_in)
        weight_grads, in_grad = pullback((part_out, part_cgrad))
        totals = jax.tree.map(lambda left, right: left + right, totals, weight_grads)
        return (totals, (layer_out.astype(jnp.bfloat16), packed.astype(jnp.bfloat16), in_grad.astype(jnp.bfloat16)))
    zero_grads = tuple((jnp.zeros_like(weight_arg) for weight_arg in weights))
    totals, results = lax.scan(group_step, zero_grads, (by_group(inputs.astype(jnp.float32)), by_group(memory.astype(jnp.float32)), by_group(compressed.astype(jnp.float32)), by_group(offsets), by_group(resets), by_group(out_grad.astype(jnp.float32)), by_group(comp_grad.astype(jnp.float32))))
    outputs = results[0].reshape(STREAMS, SEG, D)
    new_compressed = results[1].reshape(STREAMS, CNEW, D)
    input_grad = results[2].reshape(STREAMS, SEG, D)
    return (outputs, new_compressed, input_grad, totals[0], totals[1], totals[2], totals[3], totals[4], totals[5], totals[6], totals[7], totals[8])
```

```python
import functools
import math

import jax
import jax.numpy as jnp
from jax import lax
from jax.experimental import pallas as pl
from jax.experimental.pallas import tpu as pltpu
from jax.sharding import PartitionSpec as P

HEADS = 8
HEAD_DIM = 128
RATE = 3


epsilon = 1e-05
masked_score = -1e30


def shifted(block, axis, distance):
    devices = range(lax.axis_size(axis))
    route = [(i - distance, i) for i in devices if i - distance in devices]
    return lax.ppermute(block, axis, route)


def layer_norm(values, gain):
    centred = values - jnp.mean(values, axis=-1, keepdims=True)
    spread = jnp.mean(centred * centred, axis=-1, keepdims=True)
    return centred * lax.rsqrt(spread + epsilon) * gain


def project(left, right):
    return jnp.einsum("srd,de->sre", left, right, preferred_element_type=jnp.float32)


def project_back(left, right):
    return jnp.einsum("sre,de->srd", left, right, preferred_element_type=jnp.float32)


def weight_term(left, right):
    return jnp.einsum("srd,sre->de", left, right, preferred_element_type=jnp.float32)


def key_layout(key_index, local_rows, seg_len):
    key_owner = key_index // (3 * local_rows)
    inside = key_index % (3 * local_rows)
    key_kind = inside // local_rows
    key_place = key_owner * local_rows + inside % local_rows
    mem_slot = jnp.where(key_kind == 0, key_place, seg_len + key_place)
    return (key_kind, mem_slot, key_place)


def allowed_mask(key_kind, mem_slot, key_place, query_place, offsets, keep_flag):
    memory_ok = (mem_slot[None, :] >= offsets[:, None]) & keep_flag[:, None]
    causal = key_place[None, :] <= query_place[:, None]
    return jnp.where(key_kind[None, None, :] < 2, memory_ok[:, None, :], causal[None, :, :])


def score_block(query_heads, key_heads, allowed, score_scale):
    scores = (
        jnp.einsum("sthe,skhe->shtk", query_heads, key_heads, preferred_element_type=jnp.float32)
        * score_scale
    )
    return jnp.where(allowed[:, None], scores, masked_score)


def tile_matrix(matrix, dp_count, seq_count):
    rows_total, cols_total = matrix.shape
    blocks = matrix.reshape(dp_count, rows_total // dp_count, seq_count, cols_total // seq_count)
    return blocks.transpose(0, 2, 1, 3).reshape(
        dp_count * seq_count, rows_total // dp_count, cols_total // seq_count
    )


def tile_vector(vector, dp_count, seq_count):
    piece_len = vector.shape[0] // dp_count
    pieces = vector.reshape(dp_count, 1, piece_len)
    return jnp.broadcast_to(pieces, (dp_count, seq_count, piece_len)).reshape(
        dp_count * seq_count, piece_len
    )


def on_device(
    inputs,
    memory,
    compressed,
    offsets,
    resets,
    w_query,
    w_key,
    w_value,
    w_output,
    w_hidden,
    w_return,
    w_compress,
    gain_attn,
    gain_ffn,
    out_grad,
    comp_grad,
):
    seq_count = lax.axis_size("seq")
    dp_count = lax.axis_size("dp")
    seq_rank = lax.axis_index("seq")
    streams, local_rows, feat_width = inputs.shape
    seg_len = local_rows * seq_count
    score_scale = HEAD_DIM ** (-0.5)
    keep_flag = resets == 0
    all_rows = jnp.concatenate([compressed, memory, inputs], axis=1).astype(jnp.float32)
    normed, attn_norm_back = jax.vjp(layer_norm, all_rows, gain_attn.astype(jnp.float32))
    normed_low = normed.astype(jnp.bfloat16)
    query_in = normed_low[:, 2 * local_rows :]
    query_low = project(query_in, w_query).astype(jnp.bfloat16)
    key_low = project(normed_low, w_key).astype(jnp.bfloat16)
    value_low = project(normed_low, w_value).astype(jnp.bfloat16)
    key_all, value_all = (
        lax.all_gather(key_low, "seq", axis=1, tiled=True),
        lax.all_gather(value_low, "seq", axis=1, tiled=True),
    )
    total_keys = key_all.shape[1]
    key_kind, mem_slot, key_place = key_layout(
        jnp.arange(total_keys, dtype=jnp.int32), local_rows, seg_len
    )
    query_place = seq_rank * local_rows + jnp.arange(local_rows, dtype=jnp.int32)
    allowed = allowed_mask(key_kind, mem_slot, key_place, query_place, offsets, keep_flag)
    query_heads = query_low.reshape(streams, local_rows, HEADS, HEAD_DIM)
    key_heads = key_all.reshape(streams, total_keys, HEADS, HEAD_DIM)
    value_heads = value_all.reshape(streams, total_keys, HEADS, HEAD_DIM)
    scores = score_block(query_heads, key_heads, allowed, score_scale)
    row_top = jnp.max(scores, axis=-1, keepdims=True)
    exp_scores = jnp.exp(scores - row_top)
    row_total = jnp.sum(exp_scores, axis=-1, keepdims=True)
    attn_prob = exp_scores / row_total
    log_total = row_top + jnp.log(row_total)
    mixed_low = (
        jnp.einsum(
            "shtk,skhe->sthe",
            attn_prob.astype(jnp.bfloat16),
            value_heads,
            preferred_element_type=jnp.float32,
        )
        .reshape(streams, local_rows, feat_width)
        .astype(jnp.bfloat16)
    )
    hidden = inputs.astype(jnp.float32) + project(mixed_low, w_output)
    ffn_in, ffn_norm_back = jax.vjp(layer_norm, hidden, gain_ffn.astype(jnp.float32))
    ffn_low = ffn_in.astype(jnp.bfloat16)
    ffn_all = lax.all_gather(ffn_low, "seq", axis=1, tiled=True)
    pre_act = jnp.einsum("std,df->stf", ffn_all, w_hidden, preferred_element_type=jnp.float32)
    act_float, gelu_back = jax.vjp(jax.nn.gelu, pre_act)
    act_low = act_float.astype(jnp.bfloat16)
    partial_out = jnp.einsum("stf,fd->std", act_low, w_return, preferred_element_type=jnp.float32)
    ffn_out = lax.psum_scatter(
        partial_out.astype(jnp.bfloat16), "seq", scatter_dimension=1, tiled=True
    ).astype(jnp.float32)
    cot_all = lax.all_gather(out_grad, "seq", axis=1, tiled=True)
    act_grad = jnp.einsum("std,fd->stf", cot_all, w_return, preferred_element_type=jnp.float32)
    return_part = jnp.einsum("stf,std->fd", act_low, cot_all, preferred_element_type=jnp.float32)
    pre_grad = gelu_back(act_grad)[0].astype(jnp.bfloat16)
    hidden_part = jnp.einsum("std,stf->df", ffn_all, pre_grad, preferred_element_type=jnp.float32)
    in_part = jnp.einsum("stf,df->std", pre_grad, w_hidden, preferred_element_type=jnp.float32)
    ffn_in_grad = lax.psum_scatter(in_part, "seq", scatter_dimension=1, tiled=True)
    hidden_sum, return_sum = (
        lax.psum_scatter(
            hidden_part.astype(jnp.bfloat16), "dp", scatter_dimension=0, tiled=True
        ).astype(jnp.float32),
        lax.psum_scatter(
            return_part.T.astype(jnp.bfloat16), "dp", scatter_dimension=0, tiled=True
        ).astype(jnp.float32),
    )
    grad_return = return_sum.T
    outputs = (hidden + ffn_out).astype(jnp.bfloat16)
    hidden_grad, gain_ffn_grad = ffn_norm_back(ffn_in_grad)
    hidden_grad = hidden_grad + out_grad.astype(jnp.float32)
    attn_grad_low = hidden_grad.astype(jnp.bfloat16)
    output_part = weight_term(mixed_low, attn_grad_low)
    mixed_grad = project_back(attn_grad_low, w_output).astype(jnp.bfloat16)
    mixed_heads = mixed_grad.reshape(streams, local_rows, HEADS, HEAD_DIM)
    prob_again = jnp.exp(score_block(query_heads, key_heads, allowed, score_scale) - log_total)
    prob_grad = jnp.einsum(
        "sthe,skhe->shtk", mixed_heads, value_heads, preferred_element_type=jnp.float32
    )
    prob_delta = jnp.sum(prob_again * prob_grad, axis=-1)
    score_grad = (prob_again * (prob_grad - prob_delta[..., None])).astype(jnp.bfloat16)
    query_grad = (
        (
            jnp.einsum("shtk,skhe->sthe", score_grad, key_heads, preferred_element_type=jnp.float32)
            * score_scale
        )
        .reshape(streams, local_rows, feat_width)
        .astype(jnp.bfloat16)
    )
    key_part = (
        jnp.einsum("shtk,sthe->skhe", score_grad, query_heads, preferred_element_type=jnp.float32)
        * score_scale
    ).reshape(streams, total_keys, feat_width)
    value_part = jnp.einsum(
        "shtk,sthe->skhe",
        prob_again.astype(jnp.bfloat16),
        mixed_heads,
        preferred_element_type=jnp.float32,
    ).reshape(streams, total_keys, feat_width)
    key_sum, value_sum = (
        lax.psum_scatter(
            key_part.astype(jnp.bfloat16), "seq", scatter_dimension=1, tiled=True
        ).astype(jnp.float32),
        lax.psum_scatter(
            value_part.astype(jnp.bfloat16), "seq", scatter_dimension=1, tiled=True
        ).astype(jnp.float32),
    )
    key_grad = key_sum.astype(jnp.bfloat16)
    value_grad = value_sum.astype(jnp.bfloat16)
    query_part = weight_term(query_in, query_grad)
    key_wpart = weight_term(normed_low, key_grad)
    value_wpart = weight_term(normed_low, value_grad)
    query_back = project_back(query_grad, w_query)
    normed_grad = project_back(key_grad, w_key) + project_back(value_grad, w_value)
    normed_grad = normed_grad + jnp.concatenate(
        [jnp.zeros((streams, 2 * local_rows, feat_width), jnp.float32), query_back], axis=1
    )
    rows_grad, gain_attn_grad = attn_norm_back(normed_grad)
    input_grad = (rows_grad[:, 2 * local_rows :] + hidden_grad).astype(jnp.bfloat16)
    kept_memory = memory * keep_flag[:, None, None].astype(jnp.bfloat16)
    edge_rows = shifted(kept_memory[:, : 2 * (RATE - 1)], "seq", -1)
    extended = jnp.concatenate([kept_memory, edge_rows], axis=1)
    group_count = (local_rows + RATE - 1) // RATE
    first_group = (seq_rank * local_rows + RATE - 1) // RATE
    slice_start = RATE * first_group - seq_rank * local_rows
    grouped = lax.dynamic_slice_in_dim(extended, slice_start, RATE * group_count, 1).reshape(
        streams, group_count, RATE * feat_width
    )
    piece_rows = jnp.einsum(
        "sgc,cd->sgd", grouped, w_compress, preferred_element_type=jnp.float32
    ).astype(jnp.bfloat16)
    comp_all = lax.all_gather(piece_rows, "seq", axis=1, tiled=True)
    comp_count = comp_grad.shape[1]
    out_index = jnp.arange(comp_count, dtype=jnp.int32)
    holder = RATE * out_index // local_rows
    lookup = holder * group_count + out_index - (holder * local_rows + RATE - 1) // RATE
    new_compressed = jnp.take(comp_all, lookup, axis=1)
    slot_index = first_group + jnp.arange(group_count, dtype=jnp.int32)
    slot_valid = (RATE * slot_index < (seq_rank + 1) * local_rows) & (slot_index < comp_count)
    picked = jnp.take(comp_grad, jnp.minimum(slot_index, comp_count - 1), axis=1) * slot_valid[
        None, :, None
    ].astype(jnp.bfloat16)
    compress_part = jnp.einsum("sgc,sgd->cd", grouped, picked, preferred_element_type=jnp.float32)
    reduced = (
        lax.psum_scatter(
            tile_matrix(query_part, dp_count, seq_count),
            ("dp", "seq"),
            scatter_dimension=0,
            tiled=True,
        ),
        lax.psum_scatter(
            tile_matrix(key_wpart, dp_count, seq_count),
            ("dp", "seq"),
            scatter_dimension=0,
            tiled=True,
        ),
        lax.psum_scatter(
            tile_matrix(value_wpart, dp_count, seq_count),
            ("dp", "seq"),
            scatter_dimension=0,
            tiled=True,
        ),
        lax.psum_scatter(
            tile_matrix(output_part, dp_count, seq_count),
            ("dp", "seq"),
            scatter_dimension=0,
            tiled=True,
        ),
        lax.psum_scatter(
            tile_matrix(compress_part, dp_count, seq_count),
            ("dp", "seq"),
            scatter_dimension=0,
            tiled=True,
        ),
        lax.psum_scatter(
            tile_vector(gain_attn_grad, dp_count, seq_count),
            ("dp", "seq"),
            scatter_dimension=0,
            tiled=True,
        ),
        lax.psum_scatter(
            tile_vector(gain_ffn_grad, dp_count, seq_count),
            ("dp", "seq"),
            scatter_dimension=0,
            tiled=True,
        ),
    )
    return (
        outputs,
        new_compressed,
        input_grad,
        reduced[0][0],
        reduced[1][0],
        reduced[2][0],
        reduced[3][0],
        hidden_sum,
        grad_return,
        reduced[4][0],
        reduced[5][0],
        reduced[6][0],
    )


F32 = jnp.float32
BF16 = jnp.bfloat16
NN = (((1,), (0,)), ((), ()))
NT = (((1,), (1,)), ((), ()))
TN = (((0,), (0,)), ((), ()))
VMEM_LIMIT = 60 * 1024 * 1024
SCALE = HEAD_DIM ** (-0.5)
EXP2_SCALE = SCALE * math.log2(math.e)


def dot(left, right, dims=NN):
    return lax.dot_general(left, right, dims, preferred_element_type=F32)


def params(steps=1):
    return pltpu.CompilerParams(
        vmem_limit_bytes=VMEM_LIMIT, dimension_semantics=("arbitrary",) * steps
    )


def cost(flops, bytes_accessed=0, transcendentals=0):
    return pl.CostEstimate(
        flops=int(flops), bytes_accessed=int(bytes_accessed), transcendentals=int(transcendentals)
    )


def held(shape):
    zeros = (0,) * len(shape)
    return pl.BlockSpec(shape, lambda *_: zeros, pipeline_mode=pl.Buffered(1))


def norm_parts(rows):
    centred = rows - jnp.mean(rows, axis=-1, keepdims=True)
    inverse = lax.rsqrt(jnp.mean(centred * centred, axis=-1, keepdims=True) + epsilon)
    return centred * inverse, inverse


def norm_back(grad, unit, inverse):
    return inverse * (
        grad
        - jnp.mean(grad, axis=-1, keepdims=True)
        - unit * jnp.mean(grad * unit, axis=-1, keepdims=True)
    )


def attn_fwd_kernel(
    off_ref, q_ref, k_ref, v_ref, in_ref, wo_ref, gain_ref,
    mixed_ref, hidden_ref, ffn_ref, lse_ref,
):
    step = pl.program_id(0)
    half = q_ref.shape[0]
    seg = 2 * half

    def run(pieces):
        def one_head(h, stats):
            cols = pl.ds(pl.multiple_of(h * HEAD_DIM, HEAD_DIM), HEAD_DIM)
            q = q_ref[:, cols]
            scores = []
            for start, size, kind in pieces:
                s = dot(q, k_ref[start : start + size, cols], NT) * EXP2_SCALE
                if kind == "mem":
                    slot = lax.broadcasted_iota(jnp.int32, s.shape, 1)
                    s = jnp.where(slot >= off_ref[0], s, masked_score)
                if kind == "diag":
                    key = lax.broadcasted_iota(jnp.int32, s.shape, 1)
                    row = lax.broadcasted_iota(jnp.int32, s.shape, 0)
                    s = jnp.where(key <= row, s, masked_score)
                scores.append(s)
            top = functools.reduce(
                jnp.maximum, [jnp.max(s, axis=-1, keepdims=True) for s in scores]
            )
            total = jnp.zeros_like(top)
            mix = jnp.zeros((half, HEAD_DIM), F32)
            for s, (start, size, _) in zip(scores, pieces):
                p = jnp.exp2(s - top)
                total = total + jnp.sum(p, axis=-1, keepdims=True)
                mix = mix + dot(p.astype(BF16), v_ref[start : start + size, cols])
            mixed_ref[:, cols] = (mix / total).astype(BF16)
            lane = lax.broadcasted_iota(jnp.int32, stats.shape, 1)
            return jnp.where(lane == h, top + jnp.log2(total), stats)

        stats = lax.fori_loop(0, HEADS, one_head, jnp.zeros((half, 128), F32))
        lse_ref[...] = stats.T[:HEADS]

    cases = (
        ((0, 2 * seg, "mem"), (2 * seg, half, "diag")),
        ((0, 2 * seg, "mem"), (2 * seg, half, "full"), (2 * seg + half, half, "diag")),
        ((3 * seg, half, "diag"),),
        ((3 * seg, half, "full"), (3 * seg + half, half, "diag")),
    )
    for i, pieces in enumerate(cases):
        pl.when(step == i)(functools.partial(run, pieces))
    hidden = in_ref[...].astype(F32) + dot(mixed_ref[...], wo_ref[...])
    hidden_ref[...] = hidden
    unit, _ = norm_parts(hidden)
    ffn_ref[...] = (unit * gain_ref[...]).astype(BF16)


def attn_fwd(first_slot, q, k, v, inputs, wo, gain):
    rows, width = q.shape
    half = rows // 4
    by_block = pl.BlockSpec((half, width), lambda i: (i, 0))
    return pl.pallas_call(
        attn_fwd_kernel,
        grid=(4,),
        out_shape=(
            jax.ShapeDtypeStruct((rows, width), BF16),
            jax.ShapeDtypeStruct((rows, width), F32),
            jax.ShapeDtypeStruct((rows, width), BF16),
            jax.ShapeDtypeStruct((HEADS, rows), F32),
        ),
        in_specs=[
            pl.BlockSpec(memory_space=pltpu.SMEM),
            by_block, held(k.shape), held(v.shape), by_block, held(wo.shape), held(gain.shape),
        ],
        out_specs=(by_block, by_block, by_block, pl.BlockSpec((HEADS, half), lambda i: (0, i))),
        compiler_params=params(),
        cost_estimate=cost(20e9, 20e6),
        name="attn_fwd",
    )(first_slot, q, k, v, inputs, wo, gain)


def attn_bwd_kernel(
    off_ref, q_ref, k_ref, v_ref, do_ref, mixed_ref, lse_ref,
    dq_ref, dk_ref, dv_ref,
):
    h = pl.program_id(0)
    seg = q_ref.shape[0] // 2
    half = seg // 2
    for stream in range(2):
        base = stream * seg
        lse_row = lse_ref[pl.ds(h, 1), base : base + seg]
        weight = do_ref[base : base + seg].astype(F32) * mixed_ref[base : base + seg].astype(F32)
        delta_row = jnp.sum(weight.T, axis=0, keepdims=True)
        key_base = 2 * seg + stream * seg
        pieces = []
        if stream == 0:
            pieces += [(start, half, 0, "mem") for start in range(0, 2 * seg, half)]
        pieces += [(key_base, half, 0, "diag"), (key_base + half, half, half, "diag")]
        dq_low = jnp.zeros((half, HEAD_DIM), F32)
        dq_high = jnp.zeros((half, HEAD_DIM), F32)
        for start, size, first, kind in pieces:
            q = q_ref[base + first : base + seg]
            do = do_ref[base + first : base + seg]
            k = k_ref[start : start + size]
            s = dot(k, q, NT) * EXP2_SCALE - lse_row[:, first:]
            if kind == "mem":
                slot = start + lax.broadcasted_iota(jnp.int32, s.shape, 0)
                s = jnp.where(slot >= off_ref[0], s, masked_score)
            else:
                key = lax.broadcasted_iota(jnp.int32, s.shape, 0)
                row = lax.broadcasted_iota(jnp.int32, s.shape, 1)
                s = jnp.where(key <= row, s, masked_score)
            p = jnp.exp2(s)
            dp = dot(v_ref[start : start + size], do, NT)
            ds = (p * (dp - delta_row[:, first:])).astype(BF16)
            dv_ref[start : start + size] = dot(p.astype(BF16), do).astype(BF16)
            dk_ref[start : start + size] = (dot(ds, q) * SCALE).astype(BF16)
            dq = dot(ds, k, TN)
            if first == 0:
                dq_low = dq_low + dq[:half]
                dq_high = dq_high + dq[half:]
            else:
                dq_high = dq_high + dq
        dq_ref[base : base + half] = (dq_low * SCALE).astype(BF16)
        dq_ref[base + half : base + seg] = (dq_high * SCALE).astype(BF16)


def attn_bwd(first_slot, q, k, v, do, mixed, lse):
    rows, width = q.shape
    keys = k.shape[0]
    q_spec = pl.BlockSpec((rows, HEAD_DIM), lambda h: (0, h))
    k_spec = pl.BlockSpec((keys, HEAD_DIM), lambda h: (0, h))
    return pl.pallas_call(
        attn_bwd_kernel,
        grid=(HEADS,),
        out_shape=(
            jax.ShapeDtypeStruct((rows, width), BF16),
            jax.ShapeDtypeStruct((keys, width), BF16),
            jax.ShapeDtypeStruct((keys, width), BF16),
        ),
        in_specs=[
            pl.BlockSpec(memory_space=pltpu.SMEM),
            q_spec, k_spec, k_spec, q_spec, q_spec, held(lse.shape),
        ],
        out_specs=(q_spec, k_spec, k_spec),
        compiler_params=params(),
        cost_estimate=cost(25e9, 24e6),
        name="attn_bwd",
    )(first_slot, q, k, v, do, mixed, lse)


GELU_C = math.sqrt(2.0 / math.pi)
GELU_A = 0.044715
CHUNK = 512


def add_low(left, right):
    return (left.astype(F32) + right.astype(F32)).astype(BF16)


def mesh_place():
    rank, core = lax.axis_index("dp"), lax.axis_index("seq")

    def bit(b):
        return lax.rem(lax.div(rank, 1 << b), 2)

    def across(b):
        return rank + (1 << b) * (1 - 2 * bit(b))

    return core, bit, across


def greet(devices):
    barrier = pltpu.get_barrier_semaphore()
    for device in devices:
        pl.semaphore_signal(
            barrier, inc=1, device_id=device, device_id_type=pl.DeviceIdType.MESH
        )
    pl.semaphore_wait(barrier, len(devices))


def remote(src, dst, sems, device):
    return pltpu.make_async_remote_copy(
        src_ref=src,
        dst_ref=dst,
        send_sem=sems[0],
        recv_sem=sems[1],
        device_id=device,
        device_id_type=pl.DeviceIdType.MESH,
    )


def gelu_pair(pre, act_grad):
    square = pre * pre
    t = jnp.tanh(pre * (GELU_C + (GELU_C * GELU_A) * square))
    cdf = 0.5 + 0.5 * t
    slope = cdf + (0.5 * pre) * (1.0 - t * t) * (GELU_C + (3.0 * GELU_C * GELU_A) * square)
    return (pre * cdf).astype(BF16), (act_grad * slope).astype(BF16)


def ffn_kernel(
    x_ref, og_ref, hidden_ref, gain_ref, wo_ref, wh0_ref, wh1_ref, wr0_ref, wr1_ref,
    out_ref, attn_grad_ref, do_ref, gain_grad_ref,
    sent_h_ref, kept_h_ref, sent_r_ref, kept_r_ref,
    out_acc, in_acc, act_ref, pre_ref, core_out, core_in, own_ref, chip_in,
    core_sems, chip_sems,
):
    step = pl.program_id(0)
    last = pl.num_programs(0) - 1
    rows, width = x_ref.shape
    tile = wh0_ref.shape[1]
    chunks = rows // CHUNK
    core, bit, across = mesh_place()
    partner = {"seq": 1 - core}
    beside = ({"dp": across(0)}, {"dp": across(1)})
    slot = lax.rem(step, 2)

    def part(m):
        return pl.ds(pl.multiple_of(m * CHUNK, CHUNK), CHUNK)

    @pl.when(step == 0)
    def _():
        greet((partner,) + beside)
        out_acc[...] = jnp.zeros_like(out_acc)
        in_acc[...] = jnp.zeros_like(in_acc)

    def core_copy(which, index):
        return remote(
            core_out.at[which],
            core_in.at[which, lax.rem(index, 2)],
            (core_sems.at[0, which, index], core_sems.at[1, which, index]),
            partner,
        )

    def chip_copy(which, index):
        own = own_ref.at[which, lax.rem(index, 2)]
        away = 1 - bit(which)
        src = own.at[:, :, away] if which == 0 else own.at[:, away]
        return remote(
            src,
            chip_in.at[which, index],
            (chip_sems.at[0, which, index], chip_sems.at[1, which, index]),
            beside[which],
        )

    def tile_grads(wh_ref, wr_ref):
        for m in range(chunks):
            at = slice(m * CHUNK, (m + 1) * CHUNK)
            pre = dot(x_ref[at], wh_ref[...])
            act_grad = dot(og_ref[at], wr_ref[...], NT)
            act, pre_grad = gelu_pair(pre, act_grad)
            act_ref[at] = act
            pre_ref[at] = pre_grad
            out_acc[at] += dot(act, wr_ref[...])
            in_acc[at] += dot(pre_grad, wh_ref[...], NT)
        return (
            lambda: dot(x_ref[...], pre_ref[...], TN),
            lambda: dot(og_ref[...], act_ref[...], TN),
        )

    def settle(index):
        cols = pl.ds(pl.multiple_of(index * tile, tile), tile)
        at = lax.rem(index, 2)
        for which, sent_ref, kept_ref in ((0, sent_h_ref, kept_h_ref), (1, sent_r_ref, kept_r_ref)):
            chip_copy(which, index).wait()
            own = own_ref.at[which, at]
            near = bit(which)
            mine = own.at[:, :, near] if which == 0 else own.at[:, near]
            here = bit(1 - which)
            got = chip_in.at[which, index]
            kept_ref[:, :, cols] = add_low(mine[:, here], got[:, here])
            sent_ref[:, :, cols] = add_low(mine[:, 1 - here], got[:, 1 - here])

    grads = tile_grads(wh0_ref, wr0_ref)
    for which in range(2):

        @pl.when(step > 0)
        def _():
            core_copy(which, step - 1).wait_send()

        core_out[which] = grads[which]().astype(BF16)
        core_copy(which, step).start()

    grads = tile_grads(wh1_ref, wr1_ref)

    @pl.when(step > 0)
    def _():
        settle(step - 1)

    for which in range(2):
        total = grads[which]()
        core_copy(which, step).wait_recv()
        total = (total + core_in[which, slot].astype(F32)).astype(BF16)
        own_ref[which, slot] = total.reshape(own_ref.shape[2:])
        chip_copy(which, step).start()

    @pl.when(step == last)
    def _():
        def finish(m, gain_sum):
            at = pl.ds(pl.multiple_of(m * 256, 256), 256)
            hidden = hidden_ref[at, :]
            out_ref[at, :] = (hidden + out_acc[at, :]).astype(BF16)
            unit, inverse = norm_parts(hidden)
            grad = in_acc[at, :]
            hidden_grad = og_ref[at, :].astype(F32) + norm_back(
                grad * gain_ref[...], unit, inverse
            )
            low = hidden_grad.astype(BF16)
            attn_grad_ref[at, :] = low
            do_ref[at, :] = dot(low, wo_ref[...], NT).astype(BF16)
            return gain_sum + jnp.sum(grad * unit, axis=0, keepdims=True)

        gain_grad_ref[...] = lax.fori_loop(
            0, rows // 256, finish, jnp.zeros(gain_grad_ref.shape, F32)
        )
        settle(last)
        for which in range(2):
            core_copy(which, step).wait_send()


def ffn(x, og, hidden, gain, wo, wh0, wh1, wr0, wr1):
    rows, width = x.shape
    units = wh0.shape[1]
    tile = 512
    steps = units // tile
    count = lax.axis_size("dp")
    block = width // count
    col = pl.BlockSpec((width, tile), lambda i: (0, i))
    row = pl.BlockSpec((tile, width), lambda i: (i, 0))
    whole = held((rows, width))
    quarter = (count // 4, block, units)
    low_rows = jax.ShapeDtypeStruct((rows, width), BF16)
    low_quarter = jax.ShapeDtypeStruct(quarter, BF16)
    return pl.pallas_call(
        ffn_kernel,
        grid=(steps,),
        out_shape=(
            low_rows, low_rows, low_rows, jax.ShapeDtypeStruct((1, width), F32),
            low_quarter, low_quarter, low_quarter, low_quarter,
        ),
        in_specs=[whole, whole, whole, held(gain.shape), held(wo.shape), col, col, row, row],
        out_specs=(whole, whole, whole, held((1, width))) + (held(quarter),) * 4,
        scratch_shapes=[
            pltpu.VMEM((rows, width), F32),
            pltpu.VMEM((rows, width), F32),
            pltpu.VMEM((rows, tile), BF16),
            pltpu.VMEM((rows, tile), BF16),
            pltpu.VMEM((2, width, tile), BF16),
            pltpu.VMEM((2, 2, width, tile), BF16),
            pltpu.VMEM((2, 2, count // 4, 2, 2, block, tile), BF16),
            pltpu.VMEM((2, steps, count // 4, 2, block, tile), BF16),
            pltpu.SemaphoreType.DMA((2, 2, steps)),
            pltpu.SemaphoreType.DMA((2, 2, steps)),
        ],
        compiler_params=pltpu.CompilerParams(
            vmem_limit_bytes=VMEM_LIMIT, dimension_semantics=("arbitrary",),
            collective_id=1, has_side_effects=True,
        ),
        cost_estimate=cost(75e9, 50e6),
        name="ffn",
    )(x, og, hidden, gain, wo, wh0, wh1, wr0, wr1)


def swap_dp(block, bit):
    count = lax.axis_size("dp")
    return lax.ppermute(block, "dp", [(i, i ^ (1 << bit)) for i in range(count)])


def swap_core(block):
    return lax.ppermute(block, "seq", [(0, 1), (1, 0)])


def reduce_chips(own, other, order, left=(3, 2, 1, 0)):
    rank = lax.axis_index("dp")
    bits = len(left)
    shape = own.shape[1:]
    left = list(left)
    own = own.reshape((2,) * bits + shape)
    other = other.reshape((2,) * bits + shape)
    for bit in order:
        axis = left.index(bit)
        left.remove(bit)
        mine = (rank >> bit) & 1

        def half(which):
            pick = functools.partial(lax.dynamic_index_in_dim, axis=axis, keepdims=False)
            return add_low(pick(own, which), pick(other, which))

        sent = half(1 - mine)
        own = half(mine)
        other = swap_dp(sent, bit)
    return own.astype(F32) + other.astype(F32)


def reduce_gains(parts):
    rank = lax.axis_index("dp")
    parts = parts + swap_core(parts)
    for bit in range(lax.axis_size("dp").bit_length() - 1):
        parts = parts + swap_dp(parts, bit)
    return lax.dynamic_index_in_dim(parts, rank, 0, False)


def on_device_pair(
    inputs, memory, compressed, offsets, resets, w_query, w_key, w_value, w_output, w_hidden,
    w_return, w_compress, gain_attn, gain_ffn, out_grad, comp_grad,
):
    core = lax.axis_index("seq")
    dp_count = lax.axis_size("dp")
    streams, half, width = inputs.shape
    seg = 2 * half
    low_core = core == 0

    unused = (resets != 0) | (offsets >= 2 * seg)

    def pair(which):
        first_unused = lax.dynamic_index_in_dim(unused, which, 0, False)
        return jnp.where(first_unused, which + 2, which), jnp.where(first_unused, which, which + 2)

    mine, theirs = pair(core), pair(1 - core)

    def take(array, index):
        return lax.dynamic_index_in_dim(array, index, 0, False)

    def rows_of(which):
        a, b = which
        return jnp.stack(
            [take(compressed, a), take(memory, a), take(inputs, a), take(inputs, b),
             take(memory, b), take(out_grad, a), take(out_grad, b)]
        )

    sent = rows_of(theirs)
    got = swap_core(sent)
    kept = rows_of(mine)
    whole = jnp.concatenate(
        [jnp.where(low_core, kept, got), jnp.where(low_core, got, kept)], axis=1
    )
    wh_other, wr_other = swap_core(w_hidden), swap_core(w_return)

    all_rows = whole[:4].reshape(4 * seg, width)
    in_rows = whole[2:4].reshape(2 * seg, width)
    og = whole[5:7].reshape(2 * seg, width)
    reset_a, reset_b = take(resets, mine[0]), take(resets, mine[1])
    first_slot = jnp.where(reset_a != 0, 2 * seg, take(offsets, mine[0])).reshape(1)

    gain_a = gain_attn.astype(F32).reshape(1, width)
    gain_f = gain_ffn.astype(F32).reshape(1, width)
    normed_unit, normed_inverse = norm_parts(all_rows.astype(F32))
    normed = (normed_unit * gain_a).astype(BF16)
    q = dot(normed[2 * seg :], w_query).astype(BF16)
    k = dot(normed, w_key).astype(BF16)
    v = dot(normed, w_value).astype(BF16)

    groups = comp_grad.shape[1]
    keep_pair = jnp.stack([reset_a == 0, reset_b == 0]).astype(BF16)
    mem_pair = jnp.stack([whole[1], whole[4]]) * keep_pair[:, None, None]
    grouped = mem_pair[:, : RATE * groups].reshape(2 * groups, RATE * width)
    comp_rows = dot(grouped, w_compress).astype(BF16).reshape(2, groups, width)
    comp_cot = jnp.stack([take(comp_grad, mine[0]), take(comp_grad, mine[1])]).reshape(
        2 * groups, width
    )

    def split_cores(grad):
        cols = grad.reshape(grad.shape[0], 2, grad.shape[1] // 2)
        return (
            lax.dynamic_index_in_dim(cols, core, 1, False),
            lax.dynamic_index_in_dim(cols, 1 - core, 1, False),
        )

    def by_chip(grad):
        return grad.reshape(dp_count, grad.shape[0] // dp_count, grad.shape[1])

    orders = ((0, 1, 2, 3), (1, 0, 2, 3))

    def reduce_columns(own, other):
        own, other = by_chip(own), by_chip(other)
        cols = own.shape[2] // 2
        return jnp.concatenate(
            [
                reduce_chips(own[:, :, part], other[:, :, part], order)
                for part, order in zip((slice(0, cols), slice(cols, None)), orders)
            ],
            axis=1,
        )

    compress_part = dot(grouped, comp_cot, TN).astype(BF16)
    compress_own, compress_sent = split_cores(compress_part)
    grad_compress = reduce_columns(compress_own, swap_core(compress_sent))

    mixed, hidden, ffn_in, lse = attn_fwd(first_slot, q, k, v, in_rows, w_output, gain_f)
    outputs, attn_grad, mixed_grad, gain_ffn_grad, sent_h, kept_h, sent_r, kept_r = ffn(
        ffn_in, og, hidden, gain_f, w_output, wh_other, w_hidden, wr_other, w_return
    )
    got_h, got_r = swap_dp(sent_h, 1), swap_dp(sent_r, 0)
    dq, dk, dv = attn_bwd(first_slot, q, k, v, mixed_grad, mixed, lse)
    grad_hidden = reduce_chips(kept_h, got_h, (2, 3), (3, 2))
    grad_return = reduce_chips(kept_r, got_r, (2, 3), (3, 2)).T
    output_part = dot(mixed, attn_grad, TN).astype(BF16)
    query_part = dot(normed[2 * seg :], dq, TN).astype(BF16)
    key_part = dot(normed, dk, TN).astype(BF16)
    value_part = dot(normed, dv, TN).astype(BF16)
    parts = [split_cores(part) for part in (query_part, key_part, value_part, output_part)]
    own = jnp.concatenate([part[0] for part in parts], axis=1)
    got_parts = swap_core(jnp.concatenate([part[1] for part in parts], axis=1))
    grads = reduce_columns(own, got_parts)
    cols = width // 2
    grad_query, grad_key, grad_value, grad_output = (
        grads[:, i * cols : (i + 1) * cols] for i in range(4)
    )

    normed_grad = dot(dk, w_key, NT) + dot(dv, w_value, NT)
    query_back = dot(dq, w_query, NT)
    normed_grad = normed_grad.at[2 * seg :].add(query_back)
    gain_attn_grad = jnp.sum(normed_grad * normed_unit, axis=0)
    input_unit, input_inverse = norm_parts(in_rows.astype(F32))
    rows_grad = norm_back(normed_grad[2 * seg :] * gain_a, input_unit, input_inverse)
    input_grad = (rows_grad + attn_grad.astype(F32)).astype(BF16)

    gains = jnp.stack([gain_attn_grad, gain_ffn_grad.reshape(width)])
    gains = gains.reshape(2, dp_count, width // dp_count).transpose(1, 0, 2)
    gains = reduce_gains(gains)

    def to_streams(a, b, which):
        swapped = lax.dynamic_index_in_dim(unused, which, 0, False)
        return jnp.where(swapped, b, a), jnp.where(swapped, a, b)

    def spread(own_pair, other_pair):
        own = to_streams(own_pair[0], own_pair[1], core)
        other = to_streams(other_pair[0], other_pair[1], 1 - core)
        return jnp.stack(
            [
                jnp.where(low_core, own[0], other[0]),
                jnp.where(low_core, other[0], own[0]),
                jnp.where(low_core, own[1], other[1]),
                jnp.where(low_core, other[1], own[1]),
            ]
        )

    def place_rows(rows):
        halves = rows.reshape(2, 2, half, width)
        return spread(
            lax.dynamic_index_in_dim(halves, core, 1, False),
            swap_core(lax.dynamic_index_in_dim(halves, 1 - core, 1, False)),
        )

    return (
        place_rows(outputs),
        spread(comp_rows, swap_core(comp_rows)),
        place_rows(input_grad),
        grad_query,
        grad_key,
        grad_value,
        grad_output,
        grad_hidden,
        grad_return,
        grad_compress,
        gains[0],
        gains[1],
    )


def solution(mesh):
    placed = (
        P("dp", "seq", None),
        P("dp", "seq", None),
        P("dp", "seq", None),
        P("dp"),
        P("dp"),
        P(),
        P(),
        P(),
        P(),
        P(None, "seq"),
        P("seq", None),
        P(),
        P(),
        P(),
        P("dp", "seq", None),
        P("dp", None, None),
    )
    fast = mesh.shape["seq"] == 2 and mesh.shape["dp"] == 16
    return jax.shard_map(
        on_device_pair if fast else on_device,
        mesh=mesh,
        in_specs=placed,
        out_specs=(
            P("dp", "seq", None),
            P("dp", None, None),
            P("dp", "seq", None),
            P("dp", "seq"),
            P("dp", "seq"),
            P("dp", "seq"),
            P("dp", "seq"),
            P("dp", "seq"),
            P("seq", "dp"),
            P("dp", "seq"),
            P("dp"),
            P("dp"),
        ),
        check_vma=False,
    )
```

```python
import functools
import math

import jax
import jax.numpy as jnp
from jax import lax
from jax.experimental import pallas as pl
from jax.experimental.pallas import tpu as pltpu
from jax.sharding import PartitionSpec as P

HEADS = 8
HEAD_DIM = 128
RATE = 3


epsilon = 1e-05
masked_score = -1e30


def shifted(block, axis, distance):
    devices = range(lax.axis_size(axis))
    route = [(i - distance, i) for i in devices if i - distance in devices]
    return lax.ppermute(block, axis, route)


def layer_norm(values, gain):
    centred = values - jnp.mean(values, axis=-1, keepdims=True)
    spread = jnp.mean(centred * centred, axis=-1, keepdims=True)
    return centred * lax.rsqrt(spread + epsilon) * gain


def project(left, right):
    return jnp.einsum("srd,de->sre", left, right, preferred_element_type=jnp.float32)


def project_back(left, right):
    return jnp.einsum("sre,de->srd", left, right, preferred_element_type=jnp.float32)


def weight_term(left, right):
    return jnp.einsum("srd,sre->de", left, right, preferred_element_type=jnp.float32)


def key_layout(key_index, local_rows, seg_len):
    key_owner = key_index // (3 * local_rows)
    inside = key_index % (3 * local_rows)
    key_kind = inside // local_rows
    key_place = key_owner * local_rows + inside % local_rows
    mem_slot = jnp.where(key_kind == 0, key_place, seg_len + key_place)
    return (key_kind, mem_slot, key_place)


def allowed_mask(key_kind, mem_slot, key_place, query_place, offsets, keep_flag):
    memory_ok = (mem_slot[None, :] >= offsets[:, None]) & keep_flag[:, None]
    causal = key_place[None, :] <= query_place[:, None]
    return jnp.where(key_kind[None, None, :] < 2, memory_ok[:, None, :], causal[None, :, :])


def score_block(query_heads, key_heads, allowed, score_scale):
    scores = (
        jnp.einsum("sthe,skhe->shtk", query_heads, key_heads, preferred_element_type=jnp.float32)
        * score_scale
    )
    return jnp.where(allowed[:, None], scores, masked_score)


def tile_matrix(matrix, dp_count, seq_count):
    rows_total, cols_total = matrix.shape
    blocks = matrix.reshape(dp_count, rows_total // dp_count, seq_count, cols_total // seq_count)
    return blocks.transpose(0, 2, 1, 3).reshape(
        dp_count * seq_count, rows_total // dp_count, cols_total // seq_count
    )


def tile_vector(vector, dp_count, seq_count):
    piece_len = vector.shape[0] // dp_count
    pieces = vector.reshape(dp_count, 1, piece_len)
    return jnp.broadcast_to(pieces, (dp_count, seq_count, piece_len)).reshape(
        dp_count * seq_count, piece_len
    )


def on_device(
    inputs,
    memory,
    compressed,
    offsets,
    resets,
    w_query,
    w_key,
    w_value,
    w_output,
    w_hidden,
    w_return,
    w_compress,
    gain_attn,
    gain_ffn,
    out_grad,
    comp_grad,
):
    seq_count = lax.axis_size("seq")
    dp_count = lax.axis_size("dp")
    seq_rank = lax.axis_index("seq")
    streams, local_rows, feat_width = inputs.shape
    seg_len = local_rows * seq_count
    score_scale = HEAD_DIM ** (-0.5)
    keep_flag = resets == 0
    all_rows = jnp.concatenate([compressed, memory, inputs], axis=1).astype(jnp.float32)
    normed, attn_norm_back = jax.vjp(layer_norm, all_rows, gain_attn.astype(jnp.float32))
    normed_low = normed.astype(jnp.bfloat16)
    query_in = normed_low[:, 2 * local_rows :]
    query_low = project(query_in, w_query).astype(jnp.bfloat16)
    key_low = project(normed_low, w_key).astype(jnp.bfloat16)
    value_low = project(normed_low, w_value).astype(jnp.bfloat16)
    key_all, value_all = (
        lax.all_gather(key_low, "seq", axis=1, tiled=True),
        lax.all_gather(value_low, "seq", axis=1, tiled=True),
    )
    total_keys = key_all.shape[1]
    key_kind, mem_slot, key_place = key_layout(
        jnp.arange(total_keys, dtype=jnp.int32), local_rows, seg_len
    )
    query_place = seq_rank * local_rows + jnp.arange(local_rows, dtype=jnp.int32)
    allowed = allowed_mask(key_kind, mem_slot, key_place, query_place, offsets, keep_flag)
    query_heads = query_low.reshape(streams, local_rows, HEADS, HEAD_DIM)
    key_heads = key_all.reshape(streams, total_keys, HEADS, HEAD_DIM)
    value_heads = value_all.reshape(streams, total_keys, HEADS, HEAD_DIM)
    scores = score_block(query_heads, key_heads, allowed, score_scale)
    row_top = jnp.max(scores, axis=-1, keepdims=True)
    exp_scores = jnp.exp(scores - row_top)
    row_total = jnp.sum(exp_scores, axis=-1, keepdims=True)
    attn_prob = exp_scores / row_total
    log_total = row_top + jnp.log(row_total)
    mixed_low = (
        jnp.einsum(
            "shtk,skhe->sthe",
            attn_prob.astype(jnp.bfloat16),
            value_heads,
            preferred_element_type=jnp.float32,
        )
        .reshape(streams, local_rows, feat_width)
        .astype(jnp.bfloat16)
    )
    hidden = inputs.astype(jnp.float32) + project(mixed_low, w_output)
    ffn_in, ffn_norm_back = jax.vjp(layer_norm, hidden, gain_ffn.astype(jnp.float32))
    ffn_low = ffn_in.astype(jnp.bfloat16)
    ffn_all = lax.all_gather(ffn_low, "seq", axis=1, tiled=True)
    pre_act = jnp.einsum("std,df->stf", ffn_all, w_hidden, preferred_element_type=jnp.float32)
    act_float, gelu_back = jax.vjp(jax.nn.gelu, pre_act)
    act_low = act_float.astype(jnp.bfloat16)
    partial_out = jnp.einsum("stf,fd->std", act_low, w_return, preferred_element_type=jnp.float32)
    ffn_out = lax.psum_scatter(
        partial_out.astype(jnp.bfloat16), "seq", scatter_dimension=1, tiled=True
    ).astype(jnp.float32)
    cot_all = lax.all_gather(out_grad, "seq", axis=1, tiled=True)
    act_grad = jnp.einsum("std,fd->stf", cot_all, w_return, preferred_element_type=jnp.float32)
    return_part = jnp.einsum("stf,std->fd", act_low, cot_all, preferred_element_type=jnp.float32)
    pre_grad = gelu_back(act_grad)[0].astype(jnp.bfloat16)
    hidden_part = jnp.einsum("std,stf->df", ffn_all, pre_grad, preferred_element_type=jnp.float32)
    in_part = jnp.einsum("stf,df->std", pre_grad, w_hidden, preferred_element_type=jnp.float32)
    ffn_in_grad = lax.psum_scatter(in_part, "seq", scatter_dimension=1, tiled=True)
    hidden_sum, return_sum = (
        lax.psum_scatter(
            hidden_part.astype(jnp.bfloat16), "dp", scatter_dimension=0, tiled=True
        ).astype(jnp.float32),
        lax.psum_scatter(
            return_part.T.astype(jnp.bfloat16), "dp", scatter_dimension=0, tiled=True
        ).astype(jnp.float32),
    )
    grad_return = return_sum.T
    outputs = (hidden + ffn_out).astype(jnp.bfloat16)
    hidden_grad, gain_ffn_grad = ffn_norm_back(ffn_in_grad)
    hidden_grad = hidden_grad + out_grad.astype(jnp.float32)
    attn_grad_low = hidden_grad.astype(jnp.bfloat16)
    output_part = weight_term(mixed_low, attn_grad_low)
    mixed_grad = project_back(attn_grad_low, w_output).astype(jnp.bfloat16)
    mixed_heads = mixed_grad.reshape(streams, local_rows, HEADS, HEAD_DIM)
    prob_again = jnp.exp(score_block(query_heads, key_heads, allowed, score_scale) - log_total)
    prob_grad = jnp.einsum(
        "sthe,skhe->shtk", mixed_heads, value_heads, preferred_element_type=jnp.float32
    )
    prob_delta = jnp.sum(prob_again * prob_grad, axis=-1)
    score_grad = (prob_again * (prob_grad - prob_delta[..., None])).astype(jnp.bfloat16)
    query_grad = (
        (
            jnp.einsum("shtk,skhe->sthe", score_grad, key_heads, preferred_element_type=jnp.float32)
            * score_scale
        )
        .reshape(streams, local_rows, feat_width)
        .astype(jnp.bfloat16)
    )
    key_part = (
        jnp.einsum("shtk,sthe->skhe", score_grad, query_heads, preferred_element_type=jnp.float32)
        * score_scale
    ).reshape(streams, total_keys, feat_width)
    value_part = jnp.einsum(
        "shtk,sthe->skhe",
        prob_again.astype(jnp.bfloat16),
        mixed_heads,
        preferred_element_type=jnp.float32,
    ).reshape(streams, total_keys, feat_width)
    key_sum, value_sum = (
        lax.psum_scatter(
            key_part.astype(jnp.bfloat16), "seq", scatter_dimension=1, tiled=True
        ).astype(jnp.float32),
        lax.psum_scatter(
            value_part.astype(jnp.bfloat16), "seq", scatter_dimension=1, tiled=True
        ).astype(jnp.float32),
    )
    key_grad = key_sum.astype(jnp.bfloat16)
    value_grad = value_sum.astype(jnp.bfloat16)
    query_part = weight_term(query_in, query_grad)
    key_wpart = weight_term(normed_low, key_grad)
    value_wpart = weight_term(normed_low, value_grad)
    query_back = project_back(query_grad, w_query)
    normed_grad = project_back(key_grad, w_key) + project_back(value_grad, w_value)
    normed_grad = normed_grad + jnp.concatenate(
        [jnp.zeros((streams, 2 * local_rows, feat_width), jnp.float32), query_back], axis=1
    )
    rows_grad, gain_attn_grad = attn_norm_back(normed_grad)
    input_grad = (rows_grad[:, 2 * local_rows :] + hidden_grad).astype(jnp.bfloat16)
    kept_memory = memory * keep_flag[:, None, None].astype(jnp.bfloat16)
    edge_rows = shifted(kept_memory[:, : 2 * (RATE - 1)], "seq", -1)
    extended = jnp.concatenate([kept_memory, edge_rows], axis=1)
    group_count = (local_rows + RATE - 1) // RATE
    first_group = (seq_rank * local_rows + RATE - 1) // RATE
    slice_start = RATE * first_group - seq_rank * local_rows
    grouped = lax.dynamic_slice_in_dim(extended, slice_start, RATE * group_count, 1).reshape(
        streams, group_count, RATE * feat_width
    )
    piece_rows = jnp.einsum(
        "sgc,cd->sgd", grouped, w_compress, preferred_element_type=jnp.float32
    ).astype(jnp.bfloat16)
    comp_all = lax.all_gather(piece_rows, "seq", axis=1, tiled=True)
    comp_count = comp_grad.shape[1]
    out_index = jnp.arange(comp_count, dtype=jnp.int32)
    holder = RATE * out_index // local_rows
    lookup = holder * group_count + out_index - (holder * local_rows + RATE - 1) // RATE
    new_compressed = jnp.take(comp_all, lookup, axis=1)
    slot_index = first_group + jnp.arange(group_count, dtype=jnp.int32)
    slot_valid = (RATE * slot_index < (seq_rank + 1) * local_rows) & (slot_index < comp_count)
    picked = jnp.take(comp_grad, jnp.minimum(slot_index, comp_count - 1), axis=1) * slot_valid[
        None, :, None
    ].astype(jnp.bfloat16)
    compress_part = jnp.einsum("sgc,sgd->cd", grouped, picked, preferred_element_type=jnp.float32)
    reduced = (
        lax.psum_scatter(
            tile_matrix(query_part, dp_count, seq_count),
            ("dp", "seq"),
            scatter_dimension=0,
            tiled=True,
        ),
        lax.psum_scatter(
            tile_matrix(key_wpart, dp_count, seq_count),
            ("dp", "seq"),
            scatter_dimension=0,
            tiled=True,
        ),
        lax.psum_scatter(
            tile_matrix(value_wpart, dp_count, seq_count),
            ("dp", "seq"),
            scatter_dimension=0,
            tiled=True,
        ),
        lax.psum_scatter(
            tile_matrix(output_part, dp_count, seq_count),
            ("dp", "seq"),
            scatter_dimension=0,
            tiled=True,
        ),
        lax.psum_scatter(
            tile_matrix(compress_part, dp_count, seq_count),
            ("dp", "seq"),
            scatter_dimension=0,
            tiled=True,
        ),
        lax.psum_scatter(
            tile_vector(gain_attn_grad, dp_count, seq_count),
            ("dp", "seq"),
            scatter_dimension=0,
            tiled=True,
        ),
        lax.psum_scatter(
            tile_vector(gain_ffn_grad, dp_count, seq_count),
            ("dp", "seq"),
            scatter_dimension=0,
            tiled=True,
        ),
    )
    return (
        outputs,
        new_compressed,
        input_grad,
        reduced[0][0],
        reduced[1][0],
        reduced[2][0],
        reduced[3][0],
        hidden_sum,
        grad_return,
        reduced[4][0],
        reduced[5][0],
        reduced[6][0],
    )


F32 = jnp.float32
BF16 = jnp.bfloat16
NN = (((1,), (0,)), ((), ()))
NT = (((1,), (1,)), ((), ()))
TN = (((0,), (0,)), ((), ()))
VMEM_LIMIT = 60 * 1024 * 1024
SCALE = HEAD_DIM ** (-0.5)
EXP2_SCALE = SCALE * math.log2(math.e)


def dot(left, right, dims=NN):
    return lax.dot_general(left, right, dims, preferred_element_type=F32)


def params(steps=1):
    return pltpu.CompilerParams(
        vmem_limit_bytes=VMEM_LIMIT, dimension_semantics=("arbitrary",) * steps
    )


def cost(flops, bytes_accessed=0, transcendentals=0):
    return pl.CostEstimate(
        flops=int(flops), bytes_accessed=int(bytes_accessed), transcendentals=int(transcendentals)
    )


def held(shape):
    zeros = (0,) * len(shape)
    return pl.BlockSpec(shape, lambda *_: zeros, pipeline_mode=pl.Buffered(1))


def norm_parts(rows):
    centred = rows - jnp.mean(rows, axis=-1, keepdims=True)
    inverse = lax.rsqrt(jnp.mean(centred * centred, axis=-1, keepdims=True) + epsilon)
    return centred * inverse, inverse


def norm_back(grad, unit, inverse):
    return inverse * (
        grad
        - jnp.mean(grad, axis=-1, keepdims=True)
        - unit * jnp.mean(grad * unit, axis=-1, keepdims=True)
    )


def attn_fwd_kernel(
    off_ref, q_ref, k_ref, v_ref, in_ref, wo_ref, gain_ref,
    mixed_ref, hidden_ref, ffn_ref, lse_ref,
):
    step = pl.program_id(0)
    half = q_ref.shape[0]
    seg = 2 * half

    def run(pieces):
        def one_head(h, stats):
            cols = pl.ds(pl.multiple_of(h * HEAD_DIM, HEAD_DIM), HEAD_DIM)
            q = q_ref[:, cols]
            scores = []
            for start, size, kind in pieces:
                s = dot(q, k_ref[start : start + size, cols], NT) * EXP2_SCALE
                if kind == "mem":
                    slot = lax.broadcasted_iota(jnp.int32, s.shape, 1)
                    s = jnp.where(slot >= off_ref[0], s, masked_score)
                if kind == "diag":
                    key = lax.broadcasted_iota(jnp.int32, s.shape, 1)
                    row = lax.broadcasted_iota(jnp.int32, s.shape, 0)
                    s = jnp.where(key <= row, s, masked_score)
                scores.append(s)
            top = functools.reduce(
                jnp.maximum, [jnp.max(s, axis=-1, keepdims=True) for s in scores]
            )
            total = jnp.zeros_like(top)
            mix = jnp.zeros((half, HEAD_DIM), F32)
            for s, (start, size, _) in zip(scores, pieces):
                p = jnp.exp2(s - top)
                total = total + jnp.sum(p, axis=-1, keepdims=True)
                mix = mix + dot(p.astype(BF16), v_ref[start : start + size, cols])
            mixed_ref[:, cols] = (mix / total).astype(BF16)
            lane = lax.broadcasted_iota(jnp.int32, stats.shape, 1)
            return jnp.where(lane == h, top + jnp.log2(total), stats)

        stats = lax.fori_loop(0, HEADS, one_head, jnp.zeros((half, 128), F32))
        lse_ref[...] = stats.T[:HEADS]

    cases = (
        ((0, 2 * seg, "mem"), (2 * seg, half, "diag")),
        ((0, 2 * seg, "mem"), (2 * seg, half, "full"), (2 * seg + half, half, "diag")),
        ((3 * seg, half, "diag"),),
        ((3 * seg, half, "full"), (3 * seg + half, half, "diag")),
    )
    for i, pieces in enumerate(cases):
        pl.when(step == i)(functools.partial(run, pieces))
    hidden = in_ref[...].astype(F32) + dot(mixed_ref[...], wo_ref[...])
    hidden_ref[...] = hidden
    unit, _ = norm_parts(hidden)
    ffn_ref[...] = (unit * gain_ref[...]).astype(BF16)


def attn_fwd(first_slot, q, k, v, inputs, wo, gain):
    rows, width = q.shape
    half = rows // 4
    by_block = pl.BlockSpec((half, width), lambda i: (i, 0))
    return pl.pallas_call(
        attn_fwd_kernel,
        grid=(4,),
        out_shape=(
            jax.ShapeDtypeStruct((rows, width), BF16),
            jax.ShapeDtypeStruct((rows, width), F32),
            jax.ShapeDtypeStruct((rows, width), BF16),
            jax.ShapeDtypeStruct((HEADS, rows), F32),
        ),
        in_specs=[
            pl.BlockSpec(memory_space=pltpu.SMEM),
            by_block, held(k.shape), held(v.shape), by_block, held(wo.shape), held(gain.shape),
        ],
        out_specs=(by_block, by_block, by_block, pl.BlockSpec((HEADS, half), lambda i: (0, i))),
        compiler_params=params(),
        cost_estimate=cost(20e9, 20e6),
        name="attn_fwd",
    )(first_slot, q, k, v, inputs, wo, gain)


GELU_C = math.sqrt(2.0 / math.pi)
GELU_A = 0.044715
CHUNK = 512


def add_low(left, right):
    return (left.astype(F32) + right.astype(F32)).astype(BF16)


def mesh_place():
    rank, core = lax.axis_index("dp"), lax.axis_index("seq")

    def bit(b):
        return lax.rem(lax.div(rank, 1 << b), 2)

    def across(b):
        return rank + (1 << b) * (1 - 2 * bit(b))

    return core, bit, across


def greet(devices):
    barrier = pltpu.get_barrier_semaphore()
    for device in devices:
        pl.semaphore_signal(
            barrier, inc=1, device_id=device, device_id_type=pl.DeviceIdType.MESH
        )
    pl.semaphore_wait(barrier, len(devices))


def remote(src, dst, sems, device):
    return pltpu.make_async_remote_copy(
        src_ref=src,
        dst_ref=dst,
        send_sem=sems[0],
        recv_sem=sems[1],
        device_id=device,
        device_id_type=pl.DeviceIdType.MESH,
    )


def gelu_pair(pre, act_grad):
    square = pre * pre
    t = jnp.tanh(pre * (GELU_C + (GELU_C * GELU_A) * square))
    cdf = 0.5 + 0.5 * t
    slope = cdf + (0.5 * pre) * (1.0 - t * t) * (GELU_C + (3.0 * GELU_C * GELU_A) * square)
    return (pre * cdf).astype(BF16), (act_grad * slope).astype(BF16)


def ffn_kernel(
    x_ref, og_ref, hidden_ref, gain_ref, wo_ref, wh0_ref, wh1_ref, wr0_ref, wr1_ref,
    out_ref, attn_grad_ref, do_ref, gain_grad_ref,
    sent_h_ref, kept_h_ref, sent_r_ref, kept_r_ref,
    out_acc, in_acc, act_ref, pre_ref, core_out, core_in, own_ref, chip_in,
    core_sems, chip_sems,
):
    step = pl.program_id(0)
    last = pl.num_programs(0) - 1
    rows, width = x_ref.shape
    tile = wh0_ref.shape[1]
    chunks = rows // CHUNK
    core, bit, across = mesh_place()
    partner = {"seq": 1 - core}
    beside = ({"dp": across(0)}, {"dp": across(1)})
    slot = lax.rem(step, 2)

    def part(m):
        return pl.ds(pl.multiple_of(m * CHUNK, CHUNK), CHUNK)

    @pl.when(step == 0)
    def _():
        greet((partner,) + beside)
        out_acc[...] = jnp.zeros_like(out_acc)
        in_acc[...] = jnp.zeros_like(in_acc)

    def core_copy(which, index):
        return remote(
            core_out.at[which],
            core_in.at[which, lax.rem(index, 2)],
            (core_sems.at[0, which, index], core_sems.at[1, which, index]),
            partner,
        )

    def chip_copy(which, index):
        own = own_ref.at[which, lax.rem(index, 2)]
        away = 1 - bit(which)
        src = own.at[:, :, away] if which == 0 else own.at[:, away]
        return remote(
            src,
            chip_in.at[which, index],
            (chip_sems.at[0, which, index], chip_sems.at[1, which, index]),
            beside[which],
        )

    def tile_grads(wh_ref, wr_ref):
        for m in range(chunks):
            at = slice(m * CHUNK, (m + 1) * CHUNK)
            pre = dot(x_ref[at], wh_ref[...])
            act_grad = dot(og_ref[at], wr_ref[...], NT)
            act, pre_grad = gelu_pair(pre, act_grad)
            act_ref[at] = act
            pre_ref[at] = pre_grad
            out_acc[at] += dot(act, wr_ref[...])
            in_acc[at] += dot(pre_grad, wh_ref[...], NT)
        return (
            lambda: dot(x_ref[...], pre_ref[...], TN),
            lambda: dot(og_ref[...], act_ref[...], TN),
        )

    def settle(index):
        cols = pl.ds(pl.multiple_of(index * tile, tile), tile)
        at = lax.rem(index, 2)
        for which, sent_ref, kept_ref in ((0, sent_h_ref, kept_h_ref), (1, sent_r_ref, kept_r_ref)):
            chip_copy(which, index).wait()
            own = own_ref.at[which, at]
            near = bit(which)
            mine = own.at[:, :, near] if which == 0 else own.at[:, near]
            here = bit(1 - which)
            got = chip_in.at[which, index]
            kept_ref[:, :, cols] = add_low(mine[:, here], got[:, here])
            sent_ref[:, :, cols] = add_low(mine[:, 1 - here], got[:, 1 - here])

    grads = tile_grads(wh0_ref, wr0_ref)
    for which in range(2):

        @pl.when(step > 0)
        def _():
            core_copy(which, step - 1).wait_send()

        core_out[which] = grads[which]().astype(BF16)
        core_copy(which, step).start()

    grads = tile_grads(wh1_ref, wr1_ref)

    @pl.when(step > 0)
    def _():
        settle(step - 1)

    for which in range(2):
        total = grads[which]()
        core_copy(which, step).wait_recv()
        total = (total + core_in[which, slot].astype(F32)).astype(BF16)
        own_ref[which, slot] = total.reshape(own_ref.shape[2:])
        chip_copy(which, step).start()

    @pl.when(step == last)
    def _():
        def finish(m, gain_sum):
            at = pl.ds(pl.multiple_of(m * 256, 256), 256)
            hidden = hidden_ref[at, :]
            out_ref[at, :] = (hidden + out_acc[at, :]).astype(BF16)
            unit, inverse = norm_parts(hidden)
            grad = in_acc[at, :]
            hidden_grad = og_ref[at, :].astype(F32) + norm_back(
                grad * gain_ref[...], unit, inverse
            )
            low = hidden_grad.astype(BF16)
            attn_grad_ref[at, :] = low
            do_ref[at, :] = dot(low, wo_ref[...], NT).astype(BF16)
            return gain_sum + jnp.sum(grad * unit, axis=0, keepdims=True)

        gain_grad_ref[...] = lax.fori_loop(
            0, rows // 256, finish, jnp.zeros(gain_grad_ref.shape, F32)
        )
        settle(last)
        for which in range(2):
            core_copy(which, step).wait_send()


def ffn(x, og, hidden, gain, wo, wh0, wh1, wr0, wr1):
    rows, width = x.shape
    units = wh0.shape[1]
    tile = 512
    steps = units // tile
    count = lax.axis_size("dp")
    block = width // count
    col = pl.BlockSpec((width, tile), lambda i: (0, i))
    row = pl.BlockSpec((tile, width), lambda i: (i, 0))
    whole = held((rows, width))
    quarter = (count // 4, block, units)
    low_rows = jax.ShapeDtypeStruct((rows, width), BF16)
    low_quarter = jax.ShapeDtypeStruct(quarter, BF16)
    return pl.pallas_call(
        ffn_kernel,
        grid=(steps,),
        out_shape=(
            low_rows, low_rows, low_rows, jax.ShapeDtypeStruct((1, width), F32),
            low_quarter, low_quarter, low_quarter, low_quarter,
        ),
        in_specs=[whole, whole, whole, held(gain.shape), held(wo.shape), col, col, row, row],
        out_specs=(whole, whole, whole, held((1, width))) + (held(quarter),) * 4,
        scratch_shapes=[
            pltpu.VMEM((rows, width), F32),
            pltpu.VMEM((rows, width), F32),
            pltpu.VMEM((rows, tile), BF16),
            pltpu.VMEM((rows, tile), BF16),
            pltpu.VMEM((2, width, tile), BF16),
            pltpu.VMEM((2, 2, width, tile), BF16),
            pltpu.VMEM((2, 2, count // 4, 2, 2, block, tile), BF16),
            pltpu.VMEM((2, steps, count // 4, 2, block, tile), BF16),
            pltpu.SemaphoreType.DMA((2, 2, steps)),
            pltpu.SemaphoreType.DMA((2, 2, steps)),
        ],
        compiler_params=pltpu.CompilerParams(
            vmem_limit_bytes=VMEM_LIMIT, dimension_semantics=("arbitrary",),
            collective_id=1, has_side_effects=True,
        ),
        cost_estimate=cost(75e9, 50e6),
        name="ffn",
    )(x, og, hidden, gain, wo, wh0, wh1, wr0, wr1)


def attn_bwd_head(first_slot, q_ref, k_ref, v_ref, do_ref, mixed_ref, lse, dq_ref, dk_ref, dv_ref, cols):
    seg = q_ref.shape[0] // 2
    half = seg // 2
    for stream in range(2):
        base = stream * seg
        rows = slice(base, base + seg)
        lse_row = lse[:, rows]
        weight = do_ref[rows, cols].astype(F32) * mixed_ref[rows, cols].astype(F32)
        delta_row = jnp.sum(weight.T, axis=0, keepdims=True)
        key_base = 2 * seg + stream * seg
        pieces = []
        if stream == 0:
            pieces += [(start, half, 0, "mem") for start in range(0, 2 * seg, half)]
        pieces += [(key_base, half, 0, "diag"), (key_base + half, half, half, "diag")]
        dq_low = jnp.zeros((half, HEAD_DIM), F32)
        dq_high = jnp.zeros((half, HEAD_DIM), F32)
        for start, size, first, kind in pieces:
            q = q_ref[base + first : base + seg, cols]
            do = do_ref[base + first : base + seg, cols]
            k = k_ref[start : start + size, cols]
            s = dot(k, q, NT) * EXP2_SCALE - lse_row[:, first:]
            if kind == "mem":
                slot = start + lax.broadcasted_iota(jnp.int32, s.shape, 0)
                s = jnp.where(slot >= first_slot, s, masked_score)
            else:
                key = lax.broadcasted_iota(jnp.int32, s.shape, 0)
                row = lax.broadcasted_iota(jnp.int32, s.shape, 1)
                s = jnp.where(key <= row, s, masked_score)
            p = jnp.exp2(s)
            dp = dot(v_ref[start : start + size, cols], do, NT)
            ds = (p * (dp - delta_row[:, first:])).astype(BF16)
            dv_ref[start : start + size, cols] = dot(p.astype(BF16), do).astype(BF16)
            dk_ref[start : start + size, cols] = (dot(ds, q) * SCALE).astype(BF16)
            dq = dot(ds, k, TN)
            if first == 0:
                dq_low = dq_low + dq[:half]
                dq_high = dq_high + dq[half:]
            else:
                dq_high = dq_high + dq
        dq_ref[base : base + half, cols] = (dq_low * SCALE).astype(BF16)
        dq_ref[base + half : base + seg, cols] = (dq_high * SCALE).astype(BF16)


class Chunk:
    def __init__(self, data, left, order, landing, sems, place):
        self.data, self.left, self.order = data, left, order
        self.landing, self.sems = landing, sems
        _, self.bit, self.across = place

    def at(self, swap, away):
        index = []
        for b in self.left:
            if b in self.order[:swap]:
                index.append(self.bit(b))
            elif swap < len(self.order) and b == self.order[swap]:
                index.append(1 - self.bit(b) if away else self.bit(b))
            else:
                index.append(slice(None))
        return tuple(index)

    def copy(self, swap):
        return remote(
            self.data.at[self.at(swap, True)],
            self.landing[swap],
            (self.sems.at[0, swap], self.sems.at[1, swap]),
            {"dp": self.across(self.order[swap])},
        )

    def start(self, swap):
        self.copy(swap).start()

    def settle(self, swap):
        self.copy(swap).wait()
        here = self.at(swap, False)
        self.data[here] = add_low(self.data[here], self.landing[swap][...])

    def last(self, swap):
        self.copy(swap).wait()
        return self.data[self.at(swap, False)].astype(F32) + self.landing[swap][...].astype(F32)


def landings(left, order, block):
    shapes, count = [], len(left)
    for _ in order:
        count -= 1
        shapes.append(pltpu.VMEM((2,) * count + block, BF16))
    return shapes


BITS = (3, 2, 1, 0)
ORDERS = ((0, 1, 2, 3), (1, 0, 2, 3))


def attn_back_kernel(
    off_ref, q_ref, k_ref, v_ref, do_ref, mix_ref, lse_ref, normed_ref, mixed_ref, ag_ref,
    dq_ref, dk_ref, dv_ref, early_ref, late_ref,
    core_out, core_in, own_ref, land_p, land_q, core_sems, chip_sems,
):
    step = pl.program_id(0)
    last = pl.num_programs(0) - 1
    place = mesh_place()
    core = place[0]
    partner = {"seq": 1 - core}
    beside = ({"dp": place[2](0)}, {"dp": place[2](1)})
    index = lax.div(step, 2)
    rows = q_ref.shape[0]
    keys = k_ref.shape[0]
    pair = q_ref.shape[1]

    @pl.when(step == 0)
    def _():
        greet((partner,) + beside)

    def core_copy(which, index):
        return remote(
            core_out.at[which, index],
            core_in.at[which, index],
            (core_sems.at[0, which, index], core_sems.at[1, which, index]),
            partner,
        )

    chunks = [
        Chunk(own_ref.at[which], BITS, ORDERS[which][:1], [land], chip_sems.at[which], place)
        for which, land in ((0, land_p), (1, land_q))
    ]

    head = 4 * jnp.where(lax.rem(step, 2) == 0, 1 - core, core) + 2 * index
    for h in range(2):
        attn_bwd_head(
            off_ref[0], q_ref, k_ref, v_ref, do_ref, mix_ref, lse_ref[pl.ds(head + h, 1), :],
            dq_ref, dk_ref, dv_ref, slice(h * HEAD_DIM, (h + 1) * HEAD_DIM),
        )
    grads = (
        (
            lambda: dot(normed_ref[keys - rows :], dq_ref[...], TN),
            lambda: dot(normed_ref[...], dk_ref[...], TN),
        ),
        (
            lambda: dot(normed_ref[...], dv_ref[...], TN),
            lambda: dot(mixed_ref[...], ag_ref[...], TN),
        ),
    )

    @pl.when(lax.rem(step, 2) == 0)
    def _():
        for which in range(2):
            for side in range(2):
                core_out[which, index, :, side * pair : (side + 1) * pair] = grads[which][side]().astype(BF16)
            core_copy(which, index).start()

    def own_grads(which, index, out_ref):
        parts = [grads[which][side]() for side in range(2)]
        core_copy(which, index).wait()
        for side in range(2):
            cols = slice(side * pair, (side + 1) * pair)
            total = parts[side] + core_in[which, index, :, cols].astype(F32)
            out_ref[:, :, :, :, :, cols] = total.astype(BF16).reshape(out_ref.shape[:5] + (pair,))

    @pl.when(step == 1)
    def _():
        for which in range(2):
            own_grads(which, 0, own_ref.at[which])
            chunks[which].start(0)

    @pl.when(step == last)
    def _():
        for which in range(2):
            own_grads(which, 1, late_ref.at[which])
        for which in range(2):
            chunks[which].settle(0)
            early_ref[which] = own_ref[(which,) + chunks[which].at(1, False)]


def attn_back(first_slot, q, k, v, do, mixed, lse, normed, attn_grad):
    rows, width = q.shape
    keys = k.shape[0]
    pair = 2 * HEAD_DIM
    block = (width // 16, 2 * pair)

    def by_pair(count):
        def index(i):
            core = lax.axis_index("seq")
            half = jnp.where(lax.rem(i, 2) == 0, 1 - core, core)
            return 0, 2 * half + lax.div(i, 2)

        return pl.BlockSpec((count, pair), index)

    early, late = (2, 2, 2, 2) + block, (2, 2, 2, 2, 2) + block
    return pl.pallas_call(
        attn_back_kernel,
        grid=(4,),
        out_shape=(
            jax.ShapeDtypeStruct((rows, width), BF16),
            jax.ShapeDtypeStruct((keys, width), BF16),
            jax.ShapeDtypeStruct((keys, width), BF16),
            jax.ShapeDtypeStruct(early, BF16),
            jax.ShapeDtypeStruct(late, BF16),
        ),
        in_specs=[
            pl.BlockSpec(memory_space=pltpu.SMEM),
            by_pair(rows), by_pair(keys), by_pair(keys), by_pair(rows), by_pair(rows),
            held(lse.shape), held(normed.shape), held(mixed.shape), by_pair(rows),
        ],
        out_specs=(by_pair(rows), by_pair(keys), by_pair(keys), held(early), held(late)),
        scratch_shapes=[
            pltpu.VMEM((2, 2, width, 2 * pair), BF16),
            pltpu.VMEM((2, 2, width, 2 * pair), BF16),
            pltpu.VMEM(late, BF16),
            pltpu.VMEM(early[1:], BF16),
            pltpu.VMEM(early[1:], BF16),
            pltpu.SemaphoreType.DMA((2, 2, 2)),
            pltpu.SemaphoreType.DMA((2, 2, 1)),
        ],
        compiler_params=pltpu.CompilerParams(
            vmem_limit_bytes=VMEM_LIMIT, dimension_semantics=("arbitrary",),
            collective_id=2, has_side_effects=True,
        ),
        cost_estimate=cost(45e9, 24e6),
        name="attn_back",
    )(first_slot, q, k, v, do, mixed, lse, normed, mixed, attn_grad)


def rows_back_kernel(
    dq_ref, dk_ref, dv_ref, raw_ref, ag_ref, gain_ref, gain_ffn_ref, wq_ref, wk_ref, wv_ref,
    early_ref, late_ref, kept_h_ref, got_h_ref, kept_r_ref, got_r_ref,
    mine_ref, theirs_ref, gains_ref, early_out_ref, late_out_ref, grad_h_ref, grad_r_ref,
    rows_out, gain_acc, gain_in, ffn_ref, *scratch,
):
    step = pl.program_id(0)
    last = pl.num_programs(0) - 1
    place = mesh_place()
    core, _, across = place
    partner = {"seq": 1 - core}
    lands, (row_sems, local_sems, gain_sems, chip_sems) = list(scratch[:-4]), scratch[-4:]

    chunks = []

    def chunk(data, left, order):
        number = len(chunks)
        mine = [lands.pop(0) for _ in order]
        chunks.append(Chunk(data, left, order, mine, chip_sems.at[number], place))
        return chunks[-1]

    early, late, ffns = [], [], []
    for which in range(2):
        left = tuple(b for b in BITS if b != ORDERS[which][0])
        early.append(chunk(early_ref.at[which], left, ORDERS[which][1:]))
        late.append(chunk(late_ref.at[which], BITS, ORDERS[which]))
        ffns.append(chunk(ffn_ref.at[which], (3, 2), (2, 3)))

    def gain_copy(n):
        device = partner if n == 0 else {"dp": across(n - 1)}
        return remote(gain_acc.at[n], gain_in.at[n], (gain_sems.at[0, n], gain_sems.at[1, n]), device)

    def row_copy(block):
        stream = block // 2
        return remote(
            rows_out.at[block], theirs_ref.at[stream], (row_sems.at[0, stream], row_sems.at[1, stream]), partner
        )

    def row_keep(block):
        stream = block // 2
        return pltpu.make_async_copy(rows_out.at[block], mine_ref.at[stream], local_sems.at[stream])

    @pl.when(step == 0)
    def _():
        greet((partner,) + tuple({"dp": across(b)} for b in range(4)))
        for part in late + early:
            part.start(0)
        for which, (kept, got) in enumerate(((kept_h_ref, got_h_ref), (kept_r_ref, got_r_ref))):
            ffn_ref[which] = add_low(kept[...], got[...]).reshape(ffn_ref.shape[1:])
            ffns[which].start(0)
        gain_acc[...] = jnp.zeros_like(gain_acc)

    def normed_grad():
        return dot(dk_ref[...], wk_ref[...], NT) + dot(dv_ref[...], wv_ref[...], NT)

    unit, inverse = norm_parts(raw_ref[...].astype(F32))

    @pl.when(step < 4)
    def _():
        gain_acc[0, 0:1] += jnp.sum(normed_grad() * unit, axis=0, keepdims=True)

    @pl.when(step >= 4)
    def _():
        grad = normed_grad() + dot(dq_ref[...], wq_ref[...], NT)
        gain_acc[0, 0:1] += jnp.sum(grad * unit, axis=0, keepdims=True)
        rows_grad = norm_back(grad * gain_ref[...], unit, inverse)
        rows_out[step - 4] = (rows_grad + ag_ref[...].astype(F32)).astype(BF16)

    for block in range(4):
        stays = core == block % 2
        pl.when((step == block + 4) & stays)(row_keep(block).start)
        pl.when((step == block + 4) & jnp.logical_not(stays))(row_copy(block).start)

    @pl.when(step == 3)
    def _():
        for part in early:
            part.settle(0)
            part.start(1)

    @pl.when(step == 6)
    def _():
        for part in late:
            part.settle(0)
            part.start(1)

    @pl.when(step == last)
    def _():
        def gain_step(n):
            gain_copy(n).wait()
            total = gain_acc[n] + gain_in[n]
            if n < 4:
                gain_acc[n + 1] = total
                gain_copy(n + 1).start()
            else:
                gains_ref[...] = total

        gain_acc[0, 1:2] = gain_ffn_ref[...]
        gain_copy(0).start()
        for part in early:
            part.settle(1)
            part.start(2)
        gain_step(0)
        for part in ffns:
            part.settle(0)
            part.start(1)
        gain_step(1)
        for part in late:
            part.settle(1)
            part.start(2)
        gain_step(2)
        for which in range(2):
            early_out_ref[which] = early[which].last(2)
        gain_step(3)
        for part in late:
            part.settle(2)
            part.start(3)
        gain_step(4)
        for which, out in enumerate((grad_h_ref, grad_r_ref)):
            out[...] = ffns[which].last(1)
        for which in range(2):
            late_out_ref[which] = late[which].last(3)
        for block in range(4):
            stays = core == block % 2
            pl.when(stays)(row_keep(block).wait)
            pl.when(jnp.logical_not(stays))(row_copy(block).wait_send)
        for stream in range(2):
            row_copy(2 * stream).wait_recv()


def rows_back(
    dq, dk, dv, raw, attn_grad, gain, gain_ffn, wq, wk, wv, early, late, kept_h, got_h, kept_r, got_r
):
    keys, width = dk.shape
    rows = dq.shape[0]
    size = keys // 8
    key_block = pl.BlockSpec((size, width), lambda i: (i, 0))
    row_block = pl.BlockSpec((size, width), lambda i: (jnp.maximum(i - 4, 0), 0))
    anywhere = pl.BlockSpec(memory_space=pl.ANY)
    rows_shape = jax.ShapeDtypeStruct((2, size, width), BF16)
    block = early.shape[-2:]
    ffn_block = kept_h.shape[1:]
    lands = []
    for which in range(2):
        lands += landings(BITS[1:], ORDERS[which][1:], block)
        lands += landings(BITS, ORDERS[which], block)
        lands += landings((3, 2), (2, 3), ffn_block)
    out = (2,) + block
    vector = (8, width)
    return pl.pallas_call(
        rows_back_kernel,
        grid=(8,),
        out_shape=(
            rows_shape, rows_shape,
            jax.ShapeDtypeStruct(vector, F32),
            jax.ShapeDtypeStruct(out, F32),
            jax.ShapeDtypeStruct(out, F32),
            jax.ShapeDtypeStruct(ffn_block, F32),
            jax.ShapeDtypeStruct(ffn_block, F32),
        ),
        in_specs=[
            row_block, key_block, key_block, key_block, row_block,
            held(gain.shape), held(gain_ffn.shape), held(wq.shape), held(wk.shape), held(wv.shape),
            held(early.shape), held(late.shape),
            held(kept_h.shape), held(got_h.shape), held(kept_r.shape), held(got_r.shape),
        ],
        out_specs=(
            anywhere, anywhere, held(vector), held(out), held(out), held(ffn_block), held(ffn_block),
        ),
        scratch_shapes=[
            pltpu.VMEM((4, size, width), BF16),
            pltpu.VMEM((5,) + vector, F32),
            pltpu.VMEM((5,) + vector, F32),
            pltpu.VMEM((2, 2, 2) + ffn_block, BF16),
        ] + lands + [
            pltpu.SemaphoreType.DMA((2, 2)),
            pltpu.SemaphoreType.DMA((2,)),
            pltpu.SemaphoreType.DMA((2, 5)),
            pltpu.SemaphoreType.DMA((6, 2, 4)),
        ],
        compiler_params=pltpu.CompilerParams(
            vmem_limit_bytes=VMEM_LIMIT, dimension_semantics=("arbitrary",),
            collective_id=3, has_side_effects=True,
        ),
        cost_estimate=cost(20e9, 24e6),
        name="rows_back",
    )(
        dq, dk, dv, raw, attn_grad, gain, gain_ffn, wq, wk, wv,
        early, late, kept_h, got_h, kept_r, got_r,
    )


def swap_dp(block, bit):
    count = lax.axis_size("dp")
    return lax.ppermute(block, "dp", [(i, i ^ (1 << bit)) for i in range(count)])


def swap_core(block):
    return lax.ppermute(block, "seq", [(0, 1), (1, 0)])


def reduce_chips(own, other, order, left=(3, 2, 1, 0)):
    rank = lax.axis_index("dp")
    bits = len(left)
    shape = own.shape[1:]
    left = list(left)
    own = own.reshape((2,) * bits + shape)
    other = other.reshape((2,) * bits + shape)
    for bit in order:
        axis = left.index(bit)
        left.remove(bit)
        mine = (rank >> bit) & 1

        def half(which):
            pick = functools.partial(lax.dynamic_index_in_dim, axis=axis, keepdims=False)
            return add_low(pick(own, which), pick(other, which))

        sent = half(1 - mine)
        own = half(mine)
        other = swap_dp(sent, bit)
    return own.astype(F32) + other.astype(F32)


def on_device_pair(
    inputs, memory, compressed, offsets, resets, w_query, w_key, w_value, w_output, w_hidden,
    w_return, w_compress, gain_attn, gain_ffn, out_grad, comp_grad,
):
    core = lax.axis_index("seq")
    dp_count = lax.axis_size("dp")
    streams, half, width = inputs.shape
    seg = 2 * half
    low_core = core == 0

    unused = (resets != 0) | (offsets >= 2 * seg)

    def pair(which):
        first_unused = lax.dynamic_index_in_dim(unused, which, 0, False)
        return jnp.where(first_unused, which + 2, which), jnp.where(first_unused, which, which + 2)

    mine, theirs = pair(core), pair(1 - core)

    def take(array, index):
        return lax.dynamic_index_in_dim(array, index, 0, False)

    def rows_of(which):
        a, b = which
        return jnp.stack(
            [take(compressed, a), take(memory, a), take(inputs, a), take(inputs, b),
             take(memory, b), take(out_grad, a), take(out_grad, b)]
        )

    sent = rows_of(theirs)
    got = swap_core(sent)
    kept = rows_of(mine)
    whole = jnp.concatenate(
        [jnp.where(low_core, kept, got), jnp.where(low_core, got, kept)], axis=1
    )
    wh_other, wr_other = swap_core(w_hidden), swap_core(w_return)

    all_rows = whole[:4].reshape(4 * seg, width)
    in_rows = whole[2:4].reshape(2 * seg, width)
    og = whole[5:7].reshape(2 * seg, width)
    reset_a, reset_b = take(resets, mine[0]), take(resets, mine[1])
    first_slot = jnp.where(reset_a != 0, 2 * seg, take(offsets, mine[0])).reshape(1)

    gain_a = gain_attn.astype(F32).reshape(1, width)
    gain_f = gain_ffn.astype(F32).reshape(1, width)
    normed_unit, normed_inverse = norm_parts(all_rows.astype(F32))
    normed = (normed_unit * gain_a).astype(BF16)
    q = dot(normed[2 * seg :], w_query).astype(BF16)
    k = dot(normed, w_key).astype(BF16)
    v = dot(normed, w_value).astype(BF16)

    groups = comp_grad.shape[1]
    keep_pair = jnp.stack([reset_a == 0, reset_b == 0]).astype(BF16)
    mem_pair = jnp.stack([whole[1], whole[4]]) * keep_pair[:, None, None]
    grouped = mem_pair[:, : RATE * groups].reshape(2 * groups, RATE * width)
    comp_rows = dot(grouped, w_compress).astype(BF16).reshape(2, groups, width)
    comp_cot = jnp.stack([take(comp_grad, mine[0]), take(comp_grad, mine[1])]).reshape(
        2 * groups, width
    )

    def split_cores(grad):
        cols = grad.reshape(grad.shape[0], 2, grad.shape[1] // 2)
        return (
            lax.dynamic_index_in_dim(cols, core, 1, False),
            lax.dynamic_index_in_dim(cols, 1 - core, 1, False),
        )

    def by_chip(grad):
        return grad.reshape(dp_count, grad.shape[0] // dp_count, grad.shape[1])

    orders = ((0, 1, 2, 3), (1, 0, 2, 3))

    def reduce_columns(own, other):
        own, other = by_chip(own), by_chip(other)
        cols = own.shape[2] // 2
        return jnp.concatenate(
            [
                reduce_chips(own[:, :, part], other[:, :, part], order)
                for part, order in zip((slice(0, cols), slice(cols, None)), orders)
            ],
            axis=1,
        )

    compress_part = dot(grouped, comp_cot, TN).astype(BF16)
    compress_own, compress_sent = split_cores(compress_part)
    grad_compress = reduce_columns(compress_own, swap_core(compress_sent))

    mixed, hidden, ffn_in, lse = attn_fwd(first_slot, q, k, v, in_rows, w_output, gain_f)
    outputs, attn_grad, mixed_grad, gain_ffn_grad, sent_h, kept_h, sent_r, kept_r = ffn(
        ffn_in, og, hidden, gain_f, w_output, wh_other, w_hidden, wr_other, w_return
    )
    got_h, got_r = swap_dp(sent_h, 1), swap_dp(sent_r, 0)
    dq, dk, dv, early, late = attn_back(
        first_slot, q, k, v, mixed_grad, mixed, lse, normed, attn_grad
    )
    mine_rows, their_rows, gains, early_out, late_out, grad_hidden, grad_return = rows_back(
        dq, dk, dv, all_rows, attn_grad, gain_a, gain_ffn_grad, w_query, w_key, w_value,
        early, late, kept_h, got_h, kept_r, got_r,
    )
    grad_return = grad_return.T
    pair = 2 * HEAD_DIM

    def weight_grad(which, side):
        cols = slice(side * pair, (side + 1) * pair)
        return jnp.concatenate([early_out[which, :, cols], late_out[which, :, cols]], axis=1)

    grad_query, grad_key = weight_grad(0, 0), weight_grad(0, 1)
    grad_value, grad_output = weight_grad(1, 0), weight_grad(1, 1)
    rank = lax.axis_index("dp")
    gains = lax.dynamic_slice_in_dim(gains[:2], rank * (width // dp_count), width // dp_count, 1)

    def to_streams(a, b, which):
        swapped = lax.dynamic_index_in_dim(unused, which, 0, False)
        return jnp.where(swapped, b, a), jnp.where(swapped, a, b)

    def spread(own_pair, other_pair):
        own = to_streams(own_pair[0], own_pair[1], core)
        other = to_streams(other_pair[0], other_pair[1], 1 - core)
        return jnp.stack(
            [
                jnp.where(low_core, own[0], other[0]),
                jnp.where(low_core, other[0], own[0]),
                jnp.where(low_core, own[1], other[1]),
                jnp.where(low_core, other[1], own[1]),
            ]
        )

    def place_rows(rows):
        halves = rows.reshape(2, 2, half, width)
        return spread(
            lax.dynamic_index_in_dim(halves, core, 1, False),
            swap_core(lax.dynamic_index_in_dim(halves, 1 - core, 1, False)),
        )

    return (
        place_rows(outputs),
        spread(comp_rows, swap_core(comp_rows)),
        spread(mine_rows, their_rows),
        grad_query,
        grad_key,
        grad_value,
        grad_output,
        grad_hidden,
        grad_return,
        grad_compress,
        gains[0],
        gains[1],
    )


def solution(mesh):
    placed = (
        P("dp", "seq", None),
        P("dp", "seq", None),
        P("dp", "seq", None),
        P("dp"),
        P("dp"),
        P(),
        P(),
        P(),
        P(),
        P(None, "seq"),
        P("seq", None),
        P(),
        P(),
        P(),
        P("dp", "seq", None),
        P("dp", None, None),
    )
    fast = mesh.shape["seq"] == 2 and mesh.shape["dp"] == 16
    return jax.shard_map(
        on_device_pair if fast else on_device,
        mesh=mesh,
        in_specs=placed,
        out_specs=(
            P("dp", "seq", None),
            P("dp", None, None),
            P("dp", "seq", None),
            P("dp", "seq"),
            P("dp", "seq"),
            P("dp", "seq"),
            P("dp", "seq"),
            P("dp", "seq"),
            P("seq", "dp"),
            P("dp", "seq"),
            P("dp"),
            P("dp"),
        ),
        check_vma=False,
    )
```

```python
import functools
import math

import jax
import jax.numpy as jnp
from jax import lax
from jax.experimental import pallas as pl
from jax.experimental.pallas import tpu as pltpu
from jax.sharding import PartitionSpec as P

HEADS = 8
HEAD_DIM = 128
RATE = 3


epsilon = 1e-05
masked_score = -1e30


def shifted(block, axis, distance):
    devices = range(lax.axis_size(axis))
    route = [(i - distance, i) for i in devices if i - distance in devices]
    return lax.ppermute(block, axis, route)


def layer_norm(values, gain):
    centred = values - jnp.mean(values, axis=-1, keepdims=True)
    spread = jnp.mean(centred * centred, axis=-1, keepdims=True)
    return centred * lax.rsqrt(spread + epsilon) * gain


def project(left, right):
    return jnp.einsum("srd,de->sre", left, right, preferred_element_type=jnp.float32)


def project_back(left, right):
    return jnp.einsum("sre,de->srd", left, right, preferred_element_type=jnp.float32)


def weight_term(left, right):
    return jnp.einsum("srd,sre->de", left, right, preferred_element_type=jnp.float32)


def key_layout(key_index, local_rows, seg_len):
    key_owner = key_index // (3 * local_rows)
    inside = key_index % (3 * local_rows)
    key_kind = inside // local_rows
    key_place = key_owner * local_rows + inside % local_rows
    mem_slot = jnp.where(key_kind == 0, key_place, seg_len + key_place)
    return (key_kind, mem_slot, key_place)


def allowed_mask(key_kind, mem_slot, key_place, query_place, offsets, keep_flag):
    memory_ok = (mem_slot[None, :] >= offsets[:, None]) & keep_flag[:, None]
    causal = key_place[None, :] <= query_place[:, None]
    return jnp.where(key_kind[None, None, :] < 2, memory_ok[:, None, :], causal[None, :, :])


def score_block(query_heads, key_heads, allowed, score_scale):
    scores = (
        jnp.einsum("sthe,skhe->shtk", query_heads, key_heads, preferred_element_type=jnp.float32)
        * score_scale
    )
    return jnp.where(allowed[:, None], scores, masked_score)


def tile_matrix(matrix, dp_count, seq_count):
    rows_total, cols_total = matrix.shape
    blocks = matrix.reshape(dp_count, rows_total // dp_count, seq_count, cols_total // seq_count)
    return blocks.transpose(0, 2, 1, 3).reshape(
        dp_count * seq_count, rows_total // dp_count, cols_total // seq_count
    )


def tile_vector(vector, dp_count, seq_count):
    piece_len = vector.shape[0] // dp_count
    pieces = vector.reshape(dp_count, 1, piece_len)
    return jnp.broadcast_to(pieces, (dp_count, seq_count, piece_len)).reshape(
        dp_count * seq_count, piece_len
    )


def on_device(
    inputs,
    memory,
    compressed,
    offsets,
    resets,
    w_query,
    w_key,
    w_value,
    w_output,
    w_hidden,
    w_return,
    w_compress,
    gain_attn,
    gain_ffn,
    out_grad,
    comp_grad,
):
    seq_count = lax.axis_size("seq")
    dp_count = lax.axis_size("dp")
    seq_rank = lax.axis_index("seq")
    streams, local_rows, feat_width = inputs.shape
    seg_len = local_rows * seq_count
    score_scale = HEAD_DIM ** (-0.5)
    keep_flag = resets == 0
    all_rows = jnp.concatenate([compressed, memory, inputs], axis=1).astype(jnp.float32)
    normed, attn_norm_back = jax.vjp(layer_norm, all_rows, gain_attn.astype(jnp.float32))
    normed_low = normed.astype(jnp.bfloat16)
    query_in = normed_low[:, 2 * local_rows :]
    query_low = project(query_in, w_query).astype(jnp.bfloat16)
    key_low = project(normed_low, w_key).astype(jnp.bfloat16)
    value_low = project(normed_low, w_value).astype(jnp.bfloat16)
    key_all, value_all = (
        lax.all_gather(key_low, "seq", axis=1, tiled=True),
        lax.all_gather(value_low, "seq", axis=1, tiled=True),
    )
    total_keys = key_all.shape[1]
    key_kind, mem_slot, key_place = key_layout(
        jnp.arange(total_keys, dtype=jnp.int32), local_rows, seg_len
    )
    query_place = seq_rank * local_rows + jnp.arange(local_rows, dtype=jnp.int32)
    allowed = allowed_mask(key_kind, mem_slot, key_place, query_place, offsets, keep_flag)
    query_heads = query_low.reshape(streams, local_rows, HEADS, HEAD_DIM)
    key_heads = key_all.reshape(streams, total_keys, HEADS, HEAD_DIM)
    value_heads = value_all.reshape(streams, total_keys, HEADS, HEAD_DIM)
    scores = score_block(query_heads, key_heads, allowed, score_scale)
    row_top = jnp.max(scores, axis=-1, keepdims=True)
    exp_scores = jnp.exp(scores - row_top)
    row_total = jnp.sum(exp_scores, axis=-1, keepdims=True)
    attn_prob = exp_scores / row_total
    log_total = row_top + jnp.log(row_total)
    mixed_low = (
        jnp.einsum(
            "shtk,skhe->sthe",
            attn_prob.astype(jnp.bfloat16),
            value_heads,
            preferred_element_type=jnp.float32,
        )
        .reshape(streams, local_rows, feat_width)
        .astype(jnp.bfloat16)
    )
    hidden = inputs.astype(jnp.float32) + project(mixed_low, w_output)
    ffn_in, ffn_norm_back = jax.vjp(layer_norm, hidden, gain_ffn.astype(jnp.float32))
    ffn_low = ffn_in.astype(jnp.bfloat16)
    ffn_all = lax.all_gather(ffn_low, "seq", axis=1, tiled=True)
    pre_act = jnp.einsum("std,df->stf", ffn_all, w_hidden, preferred_element_type=jnp.float32)
    act_float, gelu_back = jax.vjp(jax.nn.gelu, pre_act)
    act_low = act_float.astype(jnp.bfloat16)
    partial_out = jnp.einsum("stf,fd->std", act_low, w_return, preferred_element_type=jnp.float32)
    ffn_out = lax.psum_scatter(
        partial_out.astype(jnp.bfloat16), "seq", scatter_dimension=1, tiled=True
    ).astype(jnp.float32)
    cot_all = lax.all_gather(out_grad, "seq", axis=1, tiled=True)
    act_grad = jnp.einsum("std,fd->stf", cot_all, w_return, preferred_element_type=jnp.float32)
    return_part = jnp.einsum("stf,std->fd", act_low, cot_all, preferred_element_type=jnp.float32)
    pre_grad = gelu_back(act_grad)[0].astype(jnp.bfloat16)
    hidden_part = jnp.einsum("std,stf->df", ffn_all, pre_grad, preferred_element_type=jnp.float32)
    in_part = jnp.einsum("stf,df->std", pre_grad, w_hidden, preferred_element_type=jnp.float32)
    ffn_in_grad = lax.psum_scatter(in_part, "seq", scatter_dimension=1, tiled=True)
    hidden_sum, return_sum = (
        lax.psum_scatter(
            hidden_part.astype(jnp.bfloat16), "dp", scatter_dimension=0, tiled=True
        ).astype(jnp.float32),
        lax.psum_scatter(
            return_part.T.astype(jnp.bfloat16), "dp", scatter_dimension=0, tiled=True
        ).astype(jnp.float32),
    )
    grad_return = return_sum.T
    outputs = (hidden + ffn_out).astype(jnp.bfloat16)
    hidden_grad, gain_ffn_grad = ffn_norm_back(ffn_in_grad)
    hidden_grad = hidden_grad + out_grad.astype(jnp.float32)
    attn_grad_low = hidden_grad.astype(jnp.bfloat16)
    output_part = weight_term(mixed_low, attn_grad_low)
    mixed_grad = project_back(attn_grad_low, w_output).astype(jnp.bfloat16)
    mixed_heads = mixed_grad.reshape(streams, local_rows, HEADS, HEAD_DIM)
    prob_again = jnp.exp(score_block(query_heads, key_heads, allowed, score_scale) - log_total)
    prob_grad = jnp.einsum(
        "sthe,skhe->shtk", mixed_heads, value_heads, preferred_element_type=jnp.float32
    )
    prob_delta = jnp.sum(prob_again * prob_grad, axis=-1)
    score_grad = (prob_again * (prob_grad - prob_delta[..., None])).astype(jnp.bfloat16)
    query_grad = (
        (
            jnp.einsum("shtk,skhe->sthe", score_grad, key_heads, preferred_element_type=jnp.float32)
            * score_scale
        )
        .reshape(streams, local_rows, feat_width)
        .astype(jnp.bfloat16)
    )
    key_part = (
        jnp.einsum("shtk,sthe->skhe", score_grad, query_heads, preferred_element_type=jnp.float32)
        * score_scale
    ).reshape(streams, total_keys, feat_width)
    value_part = jnp.einsum(
        "shtk,sthe->skhe",
        prob_again.astype(jnp.bfloat16),
        mixed_heads,
        preferred_element_type=jnp.float32,
    ).reshape(streams, total_keys, feat_width)
    key_sum, value_sum = (
        lax.psum_scatter(
            key_part.astype(jnp.bfloat16), "seq", scatter_dimension=1, tiled=True
        ).astype(jnp.float32),
        lax.psum_scatter(
            value_part.astype(jnp.bfloat16), "seq", scatter_dimension=1, tiled=True
        ).astype(jnp.float32),
    )
    key_grad = key_sum.astype(jnp.bfloat16)
    value_grad = value_sum.astype(jnp.bfloat16)
    query_part = weight_term(query_in, query_grad)
    key_wpart = weight_term(normed_low, key_grad)
    value_wpart = weight_term(normed_low, value_grad)
    query_back = project_back(query_grad, w_query)
    normed_grad = project_back(key_grad, w_key) + project_back(value_grad, w_value)
    normed_grad = normed_grad + jnp.concatenate(
        [jnp.zeros((streams, 2 * local_rows, feat_width), jnp.float32), query_back], axis=1
    )
    rows_grad, gain_attn_grad = attn_norm_back(normed_grad)
    input_grad = (rows_grad[:, 2 * local_rows :] + hidden_grad).astype(jnp.bfloat16)
    kept_memory = memory * keep_flag[:, None, None].astype(jnp.bfloat16)
    edge_rows = shifted(kept_memory[:, : 2 * (RATE - 1)], "seq", -1)
    extended = jnp.concatenate([kept_memory, edge_rows], axis=1)
    group_count = (local_rows + RATE - 1) // RATE
    first_group = (seq_rank * local_rows + RATE - 1) // RATE
    slice_start = RATE * first_group - seq_rank * local_rows
    grouped = lax.dynamic_slice_in_dim(extended, slice_start, RATE * group_count, 1).reshape(
        streams, group_count, RATE * feat_width
    )
    piece_rows = jnp.einsum(
        "sgc,cd->sgd", grouped, w_compress, preferred_element_type=jnp.float32
    ).astype(jnp.bfloat16)
    comp_all = lax.all_gather(piece_rows, "seq", axis=1, tiled=True)
    comp_count = comp_grad.shape[1]
    out_index = jnp.arange(comp_count, dtype=jnp.int32)
    holder = RATE * out_index // local_rows
    lookup = holder * group_count + out_index - (holder * local_rows + RATE - 1) // RATE
    new_compressed = jnp.take(comp_all, lookup, axis=1)
    slot_index = first_group + jnp.arange(group_count, dtype=jnp.int32)
    slot_valid = (RATE * slot_index < (seq_rank + 1) * local_rows) & (slot_index < comp_count)
    picked = jnp.take(comp_grad, jnp.minimum(slot_index, comp_count - 1), axis=1) * slot_valid[
        None, :, None
    ].astype(jnp.bfloat16)
    compress_part = jnp.einsum("sgc,sgd->cd", grouped, picked, preferred_element_type=jnp.float32)
    reduced = (
        lax.psum_scatter(
            tile_matrix(query_part, dp_count, seq_count),
            ("dp", "seq"),
            scatter_dimension=0,
            tiled=True,
        ),
        lax.psum_scatter(
            tile_matrix(key_wpart, dp_count, seq_count),
            ("dp", "seq"),
            scatter_dimension=0,
            tiled=True,
        ),
        lax.psum_scatter(
            tile_matrix(value_wpart, dp_count, seq_count),
            ("dp", "seq"),
            scatter_dimension=0,
            tiled=True,
        ),
        lax.psum_scatter(
            tile_matrix(output_part, dp_count, seq_count),
            ("dp", "seq"),
            scatter_dimension=0,
            tiled=True,
        ),
        lax.psum_scatter(
            tile_matrix(compress_part, dp_count, seq_count),
            ("dp", "seq"),
            scatter_dimension=0,
            tiled=True,
        ),
        lax.psum_scatter(
            tile_vector(gain_attn_grad, dp_count, seq_count),
            ("dp", "seq"),
            scatter_dimension=0,
            tiled=True,
        ),
        lax.psum_scatter(
            tile_vector(gain_ffn_grad, dp_count, seq_count),
            ("dp", "seq"),
            scatter_dimension=0,
            tiled=True,
        ),
    )
    return (
        outputs,
        new_compressed,
        input_grad,
        reduced[0][0],
        reduced[1][0],
        reduced[2][0],
        reduced[3][0],
        hidden_sum,
        grad_return,
        reduced[4][0],
        reduced[5][0],
        reduced[6][0],
    )


F32 = jnp.float32
BF16 = jnp.bfloat16
NN = (((1,), (0,)), ((), ()))
NT = (((1,), (1,)), ((), ()))
TN = (((0,), (0,)), ((), ()))
VMEM_LIMIT = 60 * 1024 * 1024
SCALE = HEAD_DIM ** (-0.5)
EXP2_SCALE = SCALE * math.log2(math.e)


def dot(left, right, dims=NN):
    return lax.dot_general(left, right, dims, preferred_element_type=F32)


def params(steps=1):
    return pltpu.CompilerParams(
        vmem_limit_bytes=VMEM_LIMIT, dimension_semantics=("arbitrary",) * steps
    )


def cost(flops, bytes_accessed=0, transcendentals=0):
    return pl.CostEstimate(
        flops=int(flops), bytes_accessed=int(bytes_accessed), transcendentals=int(transcendentals)
    )


def held(shape):
    zeros = (0,) * len(shape)
    return pl.BlockSpec(shape, lambda *_: zeros, pipeline_mode=pl.Buffered(1))


def norm_parts(rows):
    centred = rows - jnp.mean(rows, axis=-1, keepdims=True)
    inverse = lax.rsqrt(jnp.mean(centred * centred, axis=-1, keepdims=True) + epsilon)
    return centred * inverse, inverse


def norm_back(grad, unit, inverse):
    return inverse * (
        grad
        - jnp.mean(grad, axis=-1, keepdims=True)
        - unit * jnp.mean(grad * unit, axis=-1, keepdims=True)
    )


def add_low(left, right):
    return (left.astype(F32) + right.astype(F32)).astype(BF16)


def mesh_place():
    rank, core = lax.axis_index("dp"), lax.axis_index("seq")

    def bit(b):
        return lax.rem(lax.div(rank, 1 << b), 2)

    def across(b):
        return rank + (1 << b) * (1 - 2 * bit(b))

    return core, bit, across


def greet(devices):
    barrier = pltpu.get_barrier_semaphore()
    for device in devices:
        pl.semaphore_signal(
            barrier, inc=1, device_id=device, device_id_type=pl.DeviceIdType.MESH
        )
    pl.semaphore_wait(barrier, len(devices))


def remote(src, dst, sems, device):
    return pltpu.make_async_remote_copy(
        src_ref=src,
        dst_ref=dst,
        send_sem=sems[0],
        recv_sem=sems[1],
        device_id=device,
        device_id_type=pl.DeviceIdType.MESH,
    )


class Chunk:
    def __init__(self, data, left, order, landing, sems, place):
        self.data, self.left, self.order = data, left, order
        self.landing, self.sems = landing, sems
        _, self.bit, self.across = place

    def at(self, swap, away):
        index = []
        for b in self.left:
            if b in self.order[:swap]:
                index.append(self.bit(b))
            elif swap < len(self.order) and b == self.order[swap]:
                index.append(1 - self.bit(b) if away else self.bit(b))
            else:
                index.append(slice(None))
        return tuple(index)

    def rest(self, swap):
        done = self.order[:swap]
        return tuple(self.bit(b) if b in done else slice(None) for b in self.left)

    def copy(self, swap):
        return remote(
            self.data.at[self.at(swap, True)],
            self.landing[swap],
            (self.sems.at[0, swap], self.sems.at[1, swap]),
            {"dp": self.across(self.order[swap])},
        )

    def start(self, swap):
        self.copy(swap).start()

    def settle(self, swap):
        self.copy(swap).wait()
        here = self.at(swap, False)
        self.data[here] = add_low(self.data[here], self.landing[swap][...])

    def last(self, swap):
        self.copy(swap).wait()
        return self.data[self.at(swap, False)].astype(F32) + self.landing[swap][...].astype(F32)


def landings(left, order, block):
    shapes, count = [], len(left)
    for _ in order:
        count -= 1
        shapes.append(pltpu.VMEM((2,) * count + block, BF16))
    return shapes


BITS = (3, 2, 1, 0)
ORDERS = ((0, 1, 2, 3), (1, 0, 2, 3))


def front_kernel(
    resets_ref, in_ref, mem_ref, old_ref, og_ref, wc_ref, cg_ref,
    x_in_ref, x_mem_ref, x_old_ref, x_og_ref, new_ref, kept_p_ref, sent_p_ref, kept_q_ref, sent_q_ref,
    mem, x_in, x_old, x_og, wc, new, core_out, core_in, row_sems, wc_sem, new_sems, core_sems, out_sems,
):
    core, bit, _ = mesh_place()
    partner = {"seq": 1 - core}
    width = in_ref.shape[2]
    groups = cg_ref.shape[1]

    weights = pltpu.make_async_copy(wc_ref, wc, wc_sem)
    weights.start()
    greet((partner,))
    moves = []
    for n, (src, dst) in enumerate(
        ((mem_ref, mem), (in_ref, x_in), (old_ref, x_old), (og_ref, x_og))
    ):
        for j in range(2):
            away = remote(
                src.at[1 - core + 2 * j], dst.at[j, core], (row_sems.at[0, n, j], row_sems.at[1, n, j]), partner
            )
            here = pltpu.make_async_copy(src.at[core + 2 * j], dst.at[j, core], row_sems.at[2, n, j])
            away.start()
            here.start()
            moves.append((away, here))
    new[...] = jnp.zeros_like(new)
    outs = []
    for j in range(2):
        moves[j][0].wait_recv()
        moves[j][1].wait()
    outs.append(pltpu.make_async_copy(mem, x_mem_ref, out_sems.at[0]))
    outs[-1].start()
    weights.wait()

    grouped = []
    for j in range(2):
        rows = mem[j].reshape(2 * mem.shape[2], width)
        group = lax.broadcasted_iota(jnp.int32, (groups, rows.shape[0]), 0)
        row = lax.broadcasted_iota(jnp.int32, (groups, rows.shape[0]), 1)
        keep = jnp.where(resets_ref[core + 2 * j] == 0, 1.0, 0.0)
        total = jnp.zeros((groups, width), F32)
        mine = []
        for r in range(RATE):
            pick = jnp.where(row == RATE * group + r, keep, 0.0).astype(BF16)
            mine.append(dot(pick, rows).astype(BF16))
            total = total + dot(mine[-1], wc[r * width : (r + 1) * width])
        grouped.append(mine)
        new[j, :groups] = total.astype(BF16)

    news = []
    for j in range(2):
        at = core + 2 * j
        news.append(remote(new.at[j], new_ref.at[at], (new_sems.at[0, j], new_sems.at[1, j]), partner))
        outs.append(pltpu.make_async_copy(new.at[j], new_ref.at[at], new_sems.at[2, j]))
        news[-1].start()
        outs[-1].start()

    half = width // 2

    def grad(r, side):
        cols = pl.ds(pl.multiple_of(side * half, half), half)
        return sum(dot(grouped[j][r], cg_ref[core + 2 * j, :, cols], TN) for j in range(2))

    crossing = []
    for r in range(RATE):
        core_out[r] = grad(r, 1 - core).astype(BF16)
        crossing.append(
            remote(core_out.at[r], core_in.at[r], (core_sems.at[0, r], core_sems.at[1, r]), partner)
        )
        crossing[-1].start()
    for n, (src, dst) in enumerate(((x_in, x_in_ref), (x_old, x_old_ref), (x_og, x_og_ref))):
        for away, here in moves[2 * n + 2 : 2 * n + 4]:
            away.wait_recv()
            here.wait()
        outs.append(pltpu.make_async_copy(src, dst, out_sems.at[1 + n]))
        outs[-1].start()
    fine = width // 16
    quarter = half // 2
    for r in range(RATE):
        total = grad(r, core)
        crossing[r].wait()
        total = (total + core_in[r].astype(F32)).astype(BF16)
        for which, (kept_ref, sent_ref) in enumerate(
            ((kept_p_ref, sent_p_ref), (kept_q_ref, sent_q_ref))
        ):
            for mine in range(2):

                @pl.when(bit(which) == mine)
                def _():
                    for t in range(16):
                        block, third = divmod(r * 16 + t, RATE)
                        place = (block >> 3, block >> 2 & 1, block >> (1 - which) & 1)
                        ref = kept_ref if block >> which & 1 == mine else sent_ref
                        ref[place + (slice(third * fine, (third + 1) * fine),)] = total[
                            t * fine : (t + 1) * fine, which * quarter : (which + 1) * quarter
                        ]
    for away, _ in moves:
        away.wait_send()
    for move in outs + news:
        move.wait()


def front(resets, inputs, memory, compressed, out_grad, w_compress, comp_grad):
    streams, half, width = inputs.shape
    anywhere = pl.BlockSpec(memory_space=pl.ANY)
    vmem = pl.BlockSpec(memory_space=pltpu.VMEM)
    pair = jax.ShapeDtypeStruct((2, 2, half, width), BF16)
    padded = -(-comp_grad.shape[1] // 16) * 16
    part = jax.ShapeDtypeStruct((2, 2, 2, RATE * width // 16, width // 4), BF16)
    return pl.pallas_call(
        front_kernel,
        out_shape=(
            pair, pair, pair, pair, jax.ShapeDtypeStruct((streams, padded, width), BF16),
            part, part, part, part,
        ),
        in_specs=[pl.BlockSpec(memory_space=pltpu.SMEM)] + [anywhere] * 5 + [vmem],
        out_specs=(anywhere,) * 5 + (vmem,) * 4,
        scratch_shapes=[
            pltpu.VMEM((2, 2, half, width), BF16),
            pltpu.VMEM((2, 2, half, width), BF16),
            pltpu.VMEM((2, 2, half, width), BF16),
            pltpu.VMEM((2, 2, half, width), BF16),
            pltpu.VMEM(w_compress.shape, BF16),
            pltpu.VMEM((2, padded, width), BF16),
            pltpu.VMEM((RATE, width, width // 2), BF16),
            pltpu.VMEM((RATE, width, width // 2), BF16),
            pltpu.SemaphoreType.DMA((3, 4, 2)),
            pltpu.SemaphoreType.DMA,
            pltpu.SemaphoreType.DMA((3, 2)),
            pltpu.SemaphoreType.DMA((2, RATE)),
            pltpu.SemaphoreType.DMA((4,)),
        ],
        compiler_params=pltpu.CompilerParams(
            vmem_limit_bytes=VMEM_LIMIT, collective_id=4, has_side_effects=True
        ),
        cost_estimate=cost(12e9, 24e6),
        name="front",
    )(resets, inputs, memory, compressed, out_grad, w_compress, comp_grad)


def project_kernel(
    pick_ref, old_ref, mem_ref, in_ref, og_ref, gain_ref, wq_ref, wk_ref, wv_ref,
    raw_ref, normed_ref, q_ref, k_ref, v_ref, og_out_ref,
):
    step = pl.program_id(0)
    raw = jnp.where(step < 2, old_ref[...], jnp.where(step < 4, mem_ref[...], in_ref[...]))
    raw_ref[...] = raw
    unit, _ = norm_parts(raw.astype(F32))
    normed = (unit * gain_ref[...]).astype(BF16)
    normed_ref[...] = normed
    k_ref[...] = dot(normed, wk_ref[...]).astype(BF16)
    v_ref[...] = dot(normed, wv_ref[...]).astype(BF16)

    @pl.when(step >= 4)
    def _():
        q_ref[...] = dot(normed, wq_ref[...]).astype(BF16)
        og_out_ref[...] = og_ref[...]


def project_rows(pick, old, mem, inputs, og, gain, wq, wk, wv):
    _, _, half, width = inputs.shape

    def from_pair(first):
        def index(i, pick_ref):
            at = jnp.clip(i - first, 0, 3 if first == 4 else 1)
            return pick_ref[at // 2], at % 2, 0, 0

        return pl.BlockSpec((None, None, half, width), index)

    keys = pl.BlockSpec((half, width), lambda i, _: (i, 0))
    rows = pl.BlockSpec((half, width), lambda i, _: (jnp.maximum(i - 4, 0), 0))
    key_shape = jax.ShapeDtypeStruct((8 * half, width), BF16)
    row_shape = jax.ShapeDtypeStruct((4 * half, width), BF16)
    return pl.pallas_call(
        project_kernel,
        out_shape=(key_shape, key_shape, row_shape, key_shape, key_shape, row_shape),
        grid_spec=pltpu.PrefetchScalarGridSpec(
            num_scalar_prefetch=1,
            grid=(8,),
            in_specs=[
                from_pair(0), from_pair(2), from_pair(4), from_pair(4),
                held(gain.shape), held(wq.shape), held(wk.shape), held(wv.shape),
            ],
            out_specs=(keys, keys, rows, keys, keys, rows),
        ),
        compiler_params=params(),
        cost_estimate=cost(14e9, 30e6),
        name="project",
    )(pick, old, mem, inputs, og, gain, wq, wk, wv)


def attn_fwd_kernel(
    off_ref, q_ref, k_ref, v_ref, in_ref, wo_ref, gain_ref, kept_p_ref, got_p_ref, kept_q_ref, got_q_ref,
    mixed_ref, hidden_ref, ffn_ref, lse_ref, compress_ref,
    packed, *scratch,
):
    step = pl.program_id(0)
    lands, chip_sems = scratch[:-1], scratch[-1]
    place = mesh_place()
    chunks = [
        Chunk(
            packed.at[which],
            tuple(b for b in BITS if b != ORDERS[which][0]),
            ORDERS[which][1:],
            lands[3 * which : 3 * which + 3],
            chip_sems.at[which],
            place,
        )
        for which in range(2)
    ]

    @pl.when(step == 0)
    def _():
        greet(tuple({"dp": place[2](b)} for b in range(4)))
        packed[0] = add_low(kept_p_ref[...], got_p_ref[...])
        packed[1] = add_low(kept_q_ref[...], got_q_ref[...])
        for part in chunks:
            part.start(0)

    for swap in range(2):

        @pl.when(step == swap + 2)
        def _():
            for part in chunks:
                part.settle(swap)
                part.start(swap + 1)

    half = q_ref.shape[0]
    seg = 2 * half

    def run(pieces):
        def one_head(h, stats):
            cols = pl.ds(pl.multiple_of(h * HEAD_DIM, HEAD_DIM), HEAD_DIM)
            q = q_ref[:, cols]
            scores = []
            for start, size, kind in pieces:
                s = dot(q, k_ref[start : start + size, cols], NT)
                if kind == "mem":
                    slot = lax.broadcasted_iota(jnp.int32, s.shape, 1)
                    s = jnp.where(slot >= off_ref[0], s, masked_score)
                if kind == "diag":
                    key = lax.broadcasted_iota(jnp.int32, s.shape, 1)
                    row = lax.broadcasted_iota(jnp.int32, s.shape, 0)
                    s = jnp.where(key <= row, s, masked_score)
                scores.append(s)
            top = functools.reduce(
                jnp.maximum, [jnp.max(s, axis=-1, keepdims=True) for s in scores]
            ) * EXP2_SCALE
            mix = jnp.zeros((half, 2 * HEAD_DIM), F32)
            for s, (start, size, _) in zip(scores, pieces):
                p = jnp.exp2(s * EXP2_SCALE - top).astype(BF16)
                ones = jnp.ones((size, HEAD_DIM), BF16)
                mix = mix + dot(p, jnp.concatenate([v_ref[start : start + size, cols], ones], axis=1))
            total = mix[:, HEAD_DIM:]
            mixed_ref[:, cols] = (mix[:, :HEAD_DIM] / total).astype(BF16)
            lane = lax.broadcasted_iota(jnp.int32, stats.shape, 1)
            return jnp.where(lane == h, top + jnp.log2(total), stats)

        stats = lax.fori_loop(0, HEADS, one_head, jnp.zeros((half, 128), F32), unroll=True)
        lse_ref[...] = stats.T[:HEADS]

    cases = (
        ((0, 2 * seg, "mem"), (2 * seg, half, "diag")),
        ((0, 2 * seg, "mem"), (2 * seg, half, "full"), (2 * seg + half, half, "diag")),
        ((3 * seg, half, "diag"),),
        ((3 * seg, half, "full"), (3 * seg + half, half, "diag")),
    )
    for i, pieces in enumerate(cases[2:] + cases[:2]):
        pl.when(step == i)(functools.partial(run, pieces))
    hidden = in_ref[...].astype(F32) + dot(mixed_ref[...], wo_ref[...])
    hidden_ref[...] = hidden
    unit, _ = norm_parts(hidden)
    ffn_ref[...] = (unit * gain_ref[...]).astype(BF16)

    @pl.when(step == 3)
    def _():
        cols = compress_ref.shape[1] // 2
        for which, part in enumerate(chunks):
            compress_ref[:, which * cols : (which + 1) * cols] = part.last(2)


def attn_fwd(first_slot, q, k, v, raw, wo, gain, kept_p, got_p, kept_q, got_q):
    rows, width = q.shape
    half = rows // 4
    by_block = pl.BlockSpec((half, width), lambda i: (lax.rem(i + 2, 4), 0))
    in_block = pl.BlockSpec((half, width), lambda i: (4 + lax.rem(i + 2, 4), 0))
    block = kept_p.shape[-2:]
    part = held(kept_p.shape)
    lands = []
    for which in range(2):
        lands += landings(BITS[1:], ORDERS[which][1:], block)
    out = (block[0], 2 * block[1])
    return pl.pallas_call(
        attn_fwd_kernel,
        grid=(4,),
        out_shape=(
            jax.ShapeDtypeStruct((rows, width), BF16),
            jax.ShapeDtypeStruct((rows, width), F32),
            jax.ShapeDtypeStruct((rows, width), BF16),
            jax.ShapeDtypeStruct((HEADS, rows), F32),
            jax.ShapeDtypeStruct(out, F32),
        ),
        in_specs=[
            pl.BlockSpec(memory_space=pltpu.SMEM),
            by_block, held(k.shape), held(v.shape), in_block, held(wo.shape), held(gain.shape),
            part, part, part, part,
        ],
        out_specs=(
            by_block, by_block, by_block, pl.BlockSpec((HEADS, half), lambda i: (0, lax.rem(i + 2, 4))), held(out),
        ),
        scratch_shapes=[pltpu.VMEM((2,) + kept_p.shape, BF16)] + lands + [pltpu.SemaphoreType.DMA((2, 2, 3))],
        compiler_params=pltpu.CompilerParams(
            vmem_limit_bytes=VMEM_LIMIT, dimension_semantics=("arbitrary",),
            collective_id=5, has_side_effects=True,
        ),
        cost_estimate=cost(20e9, 20e6),
        name="attn_fwd",
    )(first_slot, q, k, v, raw, wo, gain, kept_p, got_p, kept_q, got_q)


GELU_C = math.sqrt(2.0 / math.pi)
GELU_A = 0.044715
CHUNK = 512


def gelu_pair(pre, act_grad):
    square = pre * pre
    t = jnp.tanh(pre * (GELU_C + (GELU_C * GELU_A) * square))
    cdf = 0.5 + 0.5 * t
    slope = cdf + (0.5 * pre) * (1.0 - t * t) * (GELU_C + (3.0 * GELU_C * GELU_A) * square)
    return (pre * cdf).astype(BF16), (act_grad * slope).astype(BF16)


def ffn_kernel(
    x_ref, og_ref, hidden_ref, gain_ref, wo_ref, wh0_ref, wh1_ref, wr0_ref, wr1_ref,
    out_ref, attn_grad_ref, do_ref, gain_grad_ref, done_ref, part_ref, raw_ref,
    out_acc, in_acc, act_ref, pre_ref, core_out, core_in, own_ref, land0, land1, land2, land3,
    core_sems, chip_sems,
):
    step = pl.program_id(0)
    last = pl.num_programs(0) - 1
    rows, width = x_ref.shape
    chunks = rows // CHUNK
    place = mesh_place()
    core, _, across = place
    partner = {"seq": 1 - core}

    @pl.when(step == 0)
    def _():
        greet((partner,) + tuple({"dp": across(b)} for b in range(4)))
        out_acc[...] = jnp.zeros_like(out_acc)
        in_acc[...] = jnp.zeros_like(in_acc)

    def core_copy(which, index):
        return remote(
            core_out.at[which],
            core_in.at[which, lax.rem(index, 2)],
            (core_sems.at[0, which, index], core_sems.at[1, which, index]),
            partner,
        )

    def tile(which, index):
        slot = lax.rem(index, 2)
        return Chunk(
            own_ref.at[which, slot], BITS, ORDERS[which],
            [land.at[which, slot] for land in (land0, land1, land2, land3)],
            chip_sems.at[which, index], place,
        )

    def pass_on(index, swap):
        for which in range(2):
            part = tile(which, index)
            part.settle(swap)
            part.start(swap + 1)

    def tile_grads(wh_ref, wr_ref, between=None):
        for m in range(chunks):
            at = slice(m * CHUNK, (m + 1) * CHUNK)
            pre = dot(x_ref[at], wh_ref[...])
            act_grad = dot(og_ref[at], wr_ref[...], NT)
            act, pre_grad = gelu_pair(pre, act_grad)
            act_ref[at] = act
            pre_ref[at] = pre_grad
            out_acc[at] += dot(act, wr_ref[...])
            in_acc[at] += dot(pre_grad, wh_ref[...], NT)
            if m == 0 and between is not None:
                between()
        return (
            lambda: dot(x_ref[...], pre_ref[...], TN),
            lambda: dot(og_ref[...], act_ref[...], TN),
        )

    grads = tile_grads(wh0_ref, wr0_ref)
    for which in range(2):

        @pl.when(step > 0)
        def _():
            core_copy(which, step - 1).wait_send()

        core_out[which] = grads[which]().astype(BF16)
        core_copy(which, step).start()

    @pl.when(step > 1)
    def _():
        pass_on(step - 2, 2)

    def first_swap():
        @pl.when(step > 0)
        def _():
            pass_on(step - 1, 0)

    grads = tile_grads(wh1_ref, wr1_ref, first_swap)

    @pl.when((step > 0) & (step < last))
    def _():
        pass_on(step - 1, 1)

    @pl.when(step > 1)
    def _():
        for which in range(2):
            done_ref[which, step - 2] = tile(which, step - 2).last(3)

    def own_grad(which):
        total = grads[which]()
        core_copy(which, step).wait_recv()
        return (total + core_in[which, lax.rem(step, 2)].astype(F32)).astype(BF16).reshape(raw_ref.shape[1:])

    @pl.when(step < last)
    def _():
        for which in range(2):
            own_ref[which, lax.rem(step, 2)] = own_grad(which)
            tile(which, step).start(0)

    @pl.when(step == last)
    def _():
        def finish(m, gain_sum):
            at = pl.ds(pl.multiple_of(m * 256, 256), 256)
            hidden = hidden_ref[at, :]
            out_ref[at, :] = (hidden + out_acc[at, :]).astype(BF16)
            unit, inverse = norm_parts(hidden)
            grad = in_acc[at, :]
            hidden_grad = og_ref[at, :].astype(F32) + norm_back(
                grad * gain_ref[...], unit, inverse
            )
            low = hidden_grad.astype(BF16)
            attn_grad_ref[at, :] = low
            do_ref[at, :] = dot(low, wo_ref[...], NT).astype(BF16)
            return gain_sum + jnp.sum(grad * unit, axis=0, keepdims=True)

        gain_grad_ref[...] = lax.fori_loop(
            0, rows // 256, finish, jnp.zeros(gain_grad_ref.shape, F32)
        )
        for which in range(2):
            raw_ref[which] = own_grad(which)
            core_copy(which, step).wait_send()
            part = tile(which, last - 1)
            part.settle(1)
            part_ref[which] = part.data[part.rest(2)]


def ffn(x, og, hidden, gain, wo, wh0, wh1, wr0, wr1):
    rows, width = x.shape
    units = wh0.shape[1]
    tile = 512
    steps = units // tile
    count = lax.axis_size("dp")
    block = width // count
    col = pl.BlockSpec((width, tile), lambda i: (0, i))
    row = pl.BlockSpec((tile, width), lambda i: (i, 0))
    whole = held((rows, width))
    low_rows = jax.ShapeDtypeStruct((rows, width), BF16)
    raw = (2, 2, 2, 2, 2, block, tile)
    part = (2, 2, 2, block, tile)
    done = (2, steps - 2, block, tile)
    lands = [pltpu.VMEM((2, 2) + (2,) * n + (block, tile), BF16) for n in (3, 2, 1, 0)]
    return pl.pallas_call(
        ffn_kernel,
        grid=(steps,),
        out_shape=(
            low_rows, low_rows, low_rows, jax.ShapeDtypeStruct((1, width), F32),
            jax.ShapeDtypeStruct(done, F32),
            jax.ShapeDtypeStruct(part, BF16),
            jax.ShapeDtypeStruct(raw, BF16),
        ),
        in_specs=[whole, whole, whole, held(gain.shape), held(wo.shape), col, col, row, row],
        out_specs=(whole, whole, whole, held((1, width)), held(done), held(part), held(raw)),
        scratch_shapes=[
            pltpu.VMEM((rows, width), F32),
            pltpu.VMEM((rows, width), F32),
            pltpu.VMEM((rows, tile), BF16),
            pltpu.VMEM((rows, tile), BF16),
            pltpu.VMEM((2, width, tile), BF16),
            pltpu.VMEM((2, 2, width, tile), BF16),
            pltpu.VMEM((2, 2) + raw[1:], BF16),
        ] + lands + [
            pltpu.SemaphoreType.DMA((2, 2, steps)),
            pltpu.SemaphoreType.DMA((2, steps, 2, 4)),
        ],
        compiler_params=pltpu.CompilerParams(
            vmem_limit_bytes=VMEM_LIMIT, dimension_semantics=("arbitrary",),
            collective_id=1, has_side_effects=True,
        ),
        cost_estimate=cost(75e9, 50e6),
        name="ffn",
    )(x, og, hidden, gain, wo, wh0, wh1, wr0, wr1)


def attn_bwd_head(first_slot, q_ref, k_ref, v_ref, do_ref, mixed_ref, lse, dq_ref, dk_ref, dv_ref, cols):
    seg = q_ref.shape[0] // 2
    half = seg // 2
    for stream in range(2):
        base = stream * seg
        rows = slice(base, base + seg)
        lse_row = lse[:, rows]
        weight = do_ref[rows, cols].astype(F32) * mixed_ref[rows, cols].astype(F32)
        delta_row = jnp.sum(weight.T, axis=0, keepdims=True)
        key_base = 2 * seg + stream * seg
        pieces = []
        if stream == 0:
            pieces += [(start, half, 0, "mem") for start in range(0, 2 * seg, half)]
        pieces += [(key_base, half, 0, "diag"), (key_base + half, half, half, "diag")]
        dq_low = jnp.zeros((half, HEAD_DIM), F32)
        dq_high = jnp.zeros((half, HEAD_DIM), F32)
        for start, size, first, kind in pieces:
            q = q_ref[base + first : base + seg, cols]
            do = do_ref[base + first : base + seg, cols]
            k = k_ref[start : start + size, cols]
            s = dot(k, q, NT) * EXP2_SCALE - lse_row[:, first:]
            if kind == "mem":
                slot = start + lax.broadcasted_iota(jnp.int32, s.shape, 0)
                s = jnp.where(slot >= first_slot, s, masked_score)
            else:
                key = lax.broadcasted_iota(jnp.int32, s.shape, 0)
                row = lax.broadcasted_iota(jnp.int32, s.shape, 1)
                s = jnp.where(key <= row, s, masked_score)
            p = jnp.exp2(s)
            dp = dot(v_ref[start : start + size, cols], do, NT)
            ds = (p * (dp - delta_row[:, first:])).astype(BF16)
            dv_ref[start : start + size, cols] = dot(p.astype(BF16), do).astype(BF16)
            dk_ref[start : start + size, cols] = (dot(ds, q) * SCALE).astype(BF16)
            dq = dot(ds, k, TN)
            if first == 0:
                dq_low = dq_low + dq[:half]
                dq_high = dq_high + dq[half:]
            else:
                dq_high = dq_high + dq
        dq_ref[base : base + half, cols] = (dq_low * SCALE).astype(BF16)
        dq_ref[base + half : base + seg, cols] = (dq_high * SCALE).astype(BF16)


def attn_back_kernel(
    off_ref, q_ref, k_ref, v_ref, do_ref, mix_ref, lse_ref, normed_ref, mixed_ref, ag_ref,
    ffn_part_ref, ffn_raw_ref,
    dq_ref, dk_ref, dv_ref, early_ref, late_ref, ffn_done_ref,
    core_out, core_in, own_ref, *scratch,
):
    step = pl.program_id(0)
    last = pl.num_programs(0) - 1
    place = mesh_place()
    core, _, across = place
    partner = {"seq": 1 - core}
    lands, (core_sems, chip_sems) = list(scratch[:-2]), scratch[-2:]
    chunks, ffn_parts, ffn_raws = [], [], []

    def chunk(number, data, left, order):
        mine = [lands.pop(0) for _ in order]
        return Chunk(data, left, order, mine, chip_sems.at[number], place)

    for which in range(2):
        order = ORDERS[which]
        chunks.append(chunk(3 * which, own_ref.at[which], BITS, order[:2]))
        ffn_parts.append(chunk(3 * which + 1, ffn_part_ref.at[which], order[2:][::-1], order[2:]))
        ffn_raws.append(chunk(3 * which + 2, ffn_raw_ref.at[which], BITS, order))
    index = lax.div(step, 2)
    rows = q_ref.shape[0]
    keys = k_ref.shape[0]
    pair = q_ref.shape[1]

    @pl.when(step == 0)
    def _():
        greet((partner,) + tuple({"dp": across(b)} for b in range(4)))
        for part in ffn_raws + ffn_parts:
            part.start(0)

    for n in range(1, 4):

        @pl.when(step == n)
        def _():
            for part in ffn_raws:
                part.settle(n - 1)
                part.start(n)

    @pl.when(step == 1)
    def _():
        for part in ffn_parts:
            part.settle(0)
            part.start(1)

    @pl.when(step == 2)
    def _():
        for which in range(2):
            ffn_done_ref[which, 0] = ffn_parts[which].last(1)

    def core_copy(which, index):
        return remote(
            core_out.at[which, index],
            core_in.at[which, index],
            (core_sems.at[0, which, index], core_sems.at[1, which, index]),
            partner,
        )

    head = 4 * jnp.where(lax.rem(step, 2) == 0, 1 - core, core) + 2 * index
    for h in range(2):
        attn_bwd_head(
            off_ref[0], q_ref, k_ref, v_ref, do_ref, mix_ref, lse_ref[pl.ds(head + h, 1), :],
            dq_ref, dk_ref, dv_ref, slice(h * HEAD_DIM, (h + 1) * HEAD_DIM),
        )
    grads = (
        (
            lambda: dot(normed_ref[keys - rows :], dq_ref[...], TN),
            lambda: dot(normed_ref[...], dk_ref[...], TN),
        ),
        (
            lambda: dot(normed_ref[...], dv_ref[...], TN),
            lambda: dot(mixed_ref[...], ag_ref[...], TN),
        ),
    )

    @pl.when(lax.rem(step, 2) == 0)
    def _():
        for which in range(2):
            for side in range(2):
                core_out[which, index, :, side * pair : (side + 1) * pair] = grads[which][side]().astype(BF16)
            core_copy(which, index).start()

    @pl.when(step == 2)
    def _():
        for part in chunks:
            part.settle(0)
            part.start(1)

    def own_grads(which, index, out_ref):
        parts = [grads[which][side]() for side in range(2)]
        core_copy(which, index).wait()
        for side in range(2):
            cols = slice(side * pair, (side + 1) * pair)
            total = parts[side] + core_in[which, index, :, cols].astype(F32)
            out_ref[:, :, :, :, :, cols] = total.astype(BF16).reshape(out_ref.shape[:5] + (pair,))

    @pl.when(step == 1)
    def _():
        for which in range(2):
            own_grads(which, 0, own_ref.at[which])
            chunks[which].start(0)

    @pl.when(step == last)
    def _():
        for which in range(2):
            own_grads(which, 1, late_ref.at[which])
        for which in range(2):
            chunks[which].settle(1)
            early_ref[which] = own_ref[(which,) + chunks[which].rest(2)]
            ffn_done_ref[which, 1] = ffn_raws[which].last(3)


def attn_back(first_slot, q, k, v, do, mixed, lse, normed, attn_grad, ffn_part, ffn_raw):
    rows, width = q.shape
    keys = k.shape[0]
    pair = 2 * HEAD_DIM
    block = (width // 16, 2 * pair)

    def by_pair(count):
        def index(i):
            core = lax.axis_index("seq")
            half = jnp.where(lax.rem(i, 2) == 0, 1 - core, core)
            return 0, 2 * half + lax.div(i, 2)

        return pl.BlockSpec((count, pair), index)

    early, late = (2, 2, 2) + block, (2, 2, 2, 2, 2) + block
    ffn_block = ffn_raw.shape[-2:]
    done = (2, 2) + ffn_block
    lands = []
    for order in ORDERS:
        lands += landings(BITS, order[:2], block)
        lands += landings(order[2:], order[2:], ffn_block)
        lands += landings(BITS, order, ffn_block)
    return pl.pallas_call(
        attn_back_kernel,
        grid=(4,),
        out_shape=(
            jax.ShapeDtypeStruct((rows, width), BF16),
            jax.ShapeDtypeStruct((keys, width), BF16),
            jax.ShapeDtypeStruct((keys, width), BF16),
            jax.ShapeDtypeStruct(early, BF16),
            jax.ShapeDtypeStruct(late, BF16),
            jax.ShapeDtypeStruct(done, F32),
        ),
        in_specs=[
            pl.BlockSpec(memory_space=pltpu.SMEM),
            by_pair(rows), by_pair(keys), by_pair(keys), by_pair(rows), by_pair(rows),
            held(lse.shape), held(normed.shape), held(mixed.shape), by_pair(rows),
            held(ffn_part.shape), held(ffn_raw.shape),
        ],
        out_specs=(by_pair(rows), by_pair(keys), by_pair(keys), held(early), held(late), held(done)),
        scratch_shapes=[
            pltpu.VMEM((2, 2, width, 2 * pair), BF16),
            pltpu.VMEM((2, 2, width, 2 * pair), BF16),
            pltpu.VMEM(late, BF16),
        ] + lands + [
            pltpu.SemaphoreType.DMA((2, 2, 2)),
            pltpu.SemaphoreType.DMA((6, 2, 4)),
        ],
        compiler_params=pltpu.CompilerParams(
            vmem_limit_bytes=VMEM_LIMIT, dimension_semantics=("arbitrary",),
            collective_id=2, has_side_effects=True,
        ),
        cost_estimate=cost(45e9, 24e6),
        name="attn_back",
    )(first_slot, q, k, v, do, mixed, lse, normed, mixed, attn_grad, ffn_part, ffn_raw)


def rows_back_kernel(
    dq_ref, dk_ref, dv_ref, raw_ref, ag_ref, gain_ref, gain_ffn_ref, wq_ref, wk_ref, wv_ref,
    early_ref, late_ref,
    mine_ref, theirs_ref, gains_ref, early_out_ref, late_out_ref,
    rows_out, gain_acc, gain_in, *scratch,
):
    step = pl.program_id(0)
    last = pl.num_programs(0) - 1
    place = mesh_place()
    core, _, across = place
    partner = {"seq": 1 - core}
    lands, (row_sems, local_sems, gain_sems, chip_sems) = list(scratch[:-4]), scratch[-4:]

    chunks = []

    def chunk(data, left, order):
        number = len(chunks)
        mine = [lands.pop(0) for _ in order]
        chunks.append(Chunk(data, left, order, mine, chip_sems.at[number], place))
        return chunks[-1]

    early, late = [], []
    for which in range(2):
        early.append(chunk(early_ref.at[which], BITS[:2], ORDERS[which][2:]))
        late.append(chunk(late_ref.at[which], BITS, ORDERS[which]))

    def gain_copy(n):
        device = partner if n == 0 else {"dp": across(n - 1)}
        return remote(gain_acc.at[n], gain_in.at[n], (gain_sems.at[0, n], gain_sems.at[1, n]), device)

    def row_copy(block):
        stream = block // 2
        return remote(
            rows_out.at[block], theirs_ref.at[stream], (row_sems.at[0, stream], row_sems.at[1, stream]), partner
        )

    def row_keep(block):
        stream = block // 2
        return pltpu.make_async_copy(rows_out.at[block], mine_ref.at[stream], local_sems.at[stream])

    @pl.when(step == 0)
    def _():
        greet((partner,) + tuple({"dp": across(b)} for b in range(4)))
        for part in late + early:
            part.start(0)
        gain_acc[...] = jnp.zeros_like(gain_acc)

    def normed_grad():
        return dot(dk_ref[...], wk_ref[...], NT) + dot(dv_ref[...], wv_ref[...], NT)

    unit, inverse = norm_parts(raw_ref[...].astype(F32))

    @pl.when(step < 4)
    def _():
        gain_acc[0, 0:1] += jnp.sum(normed_grad() * unit, axis=0, keepdims=True)

    @pl.when(step >= 4)
    def _():
        grad = normed_grad() + dot(dq_ref[...], wq_ref[...], NT)
        gain_acc[0, 0:1] += jnp.sum(grad * unit, axis=0, keepdims=True)
        rows_grad = norm_back(grad * gain_ref[...], unit, inverse)
        rows_out[step - 4] = (rows_grad + ag_ref[...].astype(F32)).astype(BF16)

    for block in range(4):
        stays = core == block % 2
        pl.when((step == block + 4) & stays)(row_keep(block).start)
        pl.when((step == block + 4) & jnp.logical_not(stays))(row_copy(block).start)

    @pl.when(step == 4)
    def _():
        for part in early:
            part.settle(0)
            part.start(1)

    @pl.when(step == 6)
    def _():
        for part in late:
            part.settle(0)
            part.start(1)

    @pl.when(step == last)
    def _():
        def gain_step(n):
            gain_copy(n).wait()
            total = gain_acc[n] + gain_in[n]
            if n < 4:
                gain_acc[n + 1] = total
                gain_copy(n + 1).start()
            else:
                gains_ref[...] = total

        gain_acc[0, 1:2] = gain_ffn_ref[...]
        gain_copy(0).start()
        for which in range(2):
            early_out_ref[which] = early[which].last(1)
        gain_step(0)
        for part in late:
            part.settle(1)
            part.start(2)
        gain_step(1)
        gain_step(2)
        for part in late:
            part.settle(2)
            part.start(3)
        gain_step(3)
        gain_step(4)
        for which in range(2):
            late_out_ref[which] = late[which].last(3)
        for block in range(4):
            stays = core == block % 2
            pl.when(stays)(row_keep(block).wait)
            pl.when(jnp.logical_not(stays))(row_copy(block).wait_send)
        for stream in range(2):
            row_copy(2 * stream).wait_recv()


def rows_back(
    dq, dk, dv, raw, attn_grad, gain, gain_ffn, wq, wk, wv, early, late
):
    keys, width = dk.shape
    rows = dq.shape[0]
    size = keys // 8
    key_block = pl.BlockSpec((size, width), lambda i: (i, 0))
    row_block = pl.BlockSpec((size, width), lambda i: (jnp.maximum(i - 4, 0), 0))
    anywhere = pl.BlockSpec(memory_space=pl.ANY)
    rows_shape = jax.ShapeDtypeStruct((2, size, width), BF16)
    block = early.shape[-2:]
    lands = []
    for order in ORDERS:
        lands += landings(BITS[:2], order[2:], block)
        lands += landings(BITS, order, block)
    out = (2,) + block
    vector = (8, width)
    return pl.pallas_call(
        rows_back_kernel,
        grid=(8,),
        out_shape=(
            rows_shape, rows_shape,
            jax.ShapeDtypeStruct(vector, F32),
            jax.ShapeDtypeStruct(out, F32),
            jax.ShapeDtypeStruct(out, F32),
        ),
        in_specs=[
            row_block, key_block, key_block, key_block, row_block,
            held(gain.shape), held(gain_ffn.shape), held(wq.shape), held(wk.shape), held(wv.shape),
            held(early.shape), held(late.shape),
        ],
        out_specs=(
            anywhere, anywhere, held(vector), held(out), held(out),
        ),
        scratch_shapes=[
            pltpu.VMEM((4, size, width), BF16),
            pltpu.VMEM((5,) + vector, F32),
            pltpu.VMEM((5,) + vector, F32),
        ] + lands + [
            pltpu.SemaphoreType.DMA((2, 2)),
            pltpu.SemaphoreType.DMA((2,)),
            pltpu.SemaphoreType.DMA((2, 5)),
            pltpu.SemaphoreType.DMA((4, 2, 4)),
        ],
        compiler_params=pltpu.CompilerParams(
            vmem_limit_bytes=VMEM_LIMIT, dimension_semantics=("arbitrary",),
            collective_id=3, has_side_effects=True,
        ),
        cost_estimate=cost(20e9, 24e6),
        name="rows_back",
    )(
        dq, dk, dv, raw, attn_grad, gain, gain_ffn, wq, wk, wv,
        early, late,
    )


def swap_dp(block, bit):
    count = lax.axis_size("dp")
    return lax.ppermute(block, "dp", [(i, i ^ (1 << bit)) for i in range(count)])


def swap_core(block):
    return lax.ppermute(block, "seq", [(0, 1), (1, 0)])


def on_device_pair(
    inputs, memory, compressed, offsets, resets, w_query, w_key, w_value, w_output, w_hidden,
    w_return, w_compress, gain_attn, gain_ffn, out_grad, comp_grad,
):
    core = lax.axis_index("seq")
    dp_count = lax.axis_size("dp")
    streams, half, width = inputs.shape
    seg = 2 * half
    low_core = core == 0

    unused = (resets != 0) | (offsets >= 2 * seg)
    pick_a = lax.dynamic_index_in_dim(unused, core, 0, False).astype(jnp.int32)
    stream_a = core + 2 * pick_a
    reset_a = lax.dynamic_index_in_dim(resets, stream_a, 0, False)
    offset_a = lax.dynamic_index_in_dim(offsets, stream_a, 0, False)
    first_slot = jnp.where(reset_a != 0, 2 * seg, offset_a).reshape(1)
    gain_a = gain_attn.astype(F32).reshape(1, width)
    gain_f = gain_ffn.astype(F32).reshape(1, width)

    x_in, x_mem, x_old, x_og, new_rows, kept_p, sent_p, kept_q, sent_q = front(
        resets, inputs, memory, compressed, out_grad, w_compress, comp_grad
    )
    got_p, got_q = swap_dp(sent_p, 0), swap_dp(sent_q, 1)
    wh_late, wr_late, x_in = lax.optimization_barrier((w_hidden, w_return, x_in))
    wh_other, wr_other = swap_core(wh_late), swap_core(wr_late)
    all_rows, normed, q, k, v, og = project_rows(
        jnp.stack([pick_a, 1 - pick_a]), x_old, x_mem, x_in, x_og, gain_a, w_query, w_key, w_value
    )
    mixed, hidden, ffn_in, lse, grad_compress = attn_fwd(
        first_slot, q, k, v, all_rows, w_output, gain_f, kept_p, got_p, kept_q, got_q
    )
    outputs, attn_grad, mixed_grad, gain_ffn_grad, ffn_done, ffn_part, ffn_raw = ffn(
        ffn_in, og, hidden, gain_f, w_output, wh_other, w_hidden, wr_other, w_return
    )
    dq, dk, dv, early, late, ffn_rest = attn_back(
        first_slot, q, k, v, mixed_grad, mixed, lse, normed, attn_grad, ffn_part, ffn_raw
    )
    mine_rows, their_rows, gains, early_out, late_out = rows_back(
        dq, dk, dv, all_rows, attn_grad, gain_a, gain_ffn_grad, w_query, w_key, w_value, early, late
    )

    def tiles(which):
        parts = [ffn_done[which, i] for i in range(2)] + [ffn_rest[which, i] for i in range(2)]
        return jnp.concatenate(parts, axis=1)

    grad_hidden, grad_return = tiles(0), tiles(1).T
    pair = 2 * HEAD_DIM

    def weight_grad(which, side):
        cols = slice(side * pair, (side + 1) * pair)
        return jnp.concatenate([early_out[which, :, cols], late_out[which, :, cols]], axis=1)

    grad_query, grad_key = weight_grad(0, 0), weight_grad(0, 1)
    grad_value, grad_output = weight_grad(1, 0), weight_grad(1, 1)
    rank = lax.axis_index("dp")
    gains = lax.dynamic_slice_in_dim(gains[:2], rank * (width // dp_count), width // dp_count, 1)

    def to_streams(a, b, which):
        swapped = lax.dynamic_index_in_dim(unused, which, 0, False)
        return jnp.where(swapped, b, a), jnp.where(swapped, a, b)

    def spread(own_pair, other_pair):
        own = to_streams(own_pair[0], own_pair[1], core)
        other = to_streams(other_pair[0], other_pair[1], 1 - core)
        return jnp.stack(
            [
                jnp.where(low_core, own[0], other[0]),
                jnp.where(low_core, other[0], own[0]),
                jnp.where(low_core, own[1], other[1]),
                jnp.where(low_core, other[1], own[1]),
            ]
        )

    def place_rows(rows):
        halves = rows.reshape(2, 2, half, width)
        return spread(
            lax.dynamic_index_in_dim(halves, core, 1, False),
            swap_core(lax.dynamic_index_in_dim(halves, 1 - core, 1, False)),
        )

    return (
        place_rows(outputs),
        new_rows[:, : comp_grad.shape[1]],
        spread(mine_rows, their_rows),
        grad_query,
        grad_key,
        grad_value,
        grad_output,
        grad_hidden,
        grad_return,
        grad_compress,
        gains[0],
        gains[1],
    )


def solution(mesh):
    placed = (
        P("dp", "seq", None),
        P("dp", "seq", None),
        P("dp", "seq", None),
        P("dp"),
        P("dp"),
        P(),
        P(),
        P(),
        P(),
        P(None, "seq"),
        P("seq", None),
        P(),
        P(),
        P(),
        P("dp", "seq", None),
        P("dp", None, None),
    )
    fast = mesh.shape["seq"] == 2 and mesh.shape["dp"] == 16
    return jax.shard_map(
        on_device_pair if fast else on_device,
        mesh=mesh,
        in_specs=placed,
        out_specs=(
            P("dp", "seq", None),
            P("dp", None, None),
            P("dp", "seq", None),
            P("dp", "seq"),
            P("dp", "seq"),
            P("dp", "seq"),
            P("dp", "seq"),
            P("dp", "seq"),
            P("seq", "dp"),
            P("dp", "seq"),
            P("dp"),
            P("dp"),
        ),
        check_vma=False,
    )
```

```python
import functools
import math

import jax
import jax.numpy as jnp
from jax import lax
from jax.experimental import pallas as pl
from jax.experimental.pallas import tpu as pltpu
from jax.sharding import PartitionSpec as P

HEADS = 8
HEAD_DIM = 128
RATE = 3


epsilon = 1e-05
masked_score = -1e30


def shifted(block, axis, distance):
    devices = range(lax.axis_size(axis))
    route = [(i - distance, i) for i in devices if i - distance in devices]
    return lax.ppermute(block, axis, route)


def layer_norm(values, gain):
    centred = values - jnp.mean(values, axis=-1, keepdims=True)
    spread = jnp.mean(centred * centred, axis=-1, keepdims=True)
    return centred * lax.rsqrt(spread + epsilon) * gain


def project(left, right):
    return jnp.einsum("srd,de->sre", left, right, preferred_element_type=jnp.float32)


def project_back(left, right):
    return jnp.einsum("sre,de->srd", left, right, preferred_element_type=jnp.float32)


def weight_term(left, right):
    return jnp.einsum("srd,sre->de", left, right, preferred_element_type=jnp.float32)


def key_layout(key_index, local_rows, seg_len):
    key_owner = key_index // (3 * local_rows)
    inside = key_index % (3 * local_rows)
    key_kind = inside // local_rows
    key_place = key_owner * local_rows + inside % local_rows
    mem_slot = jnp.where(key_kind == 0, key_place, seg_len + key_place)
    return (key_kind, mem_slot, key_place)


def allowed_mask(key_kind, mem_slot, key_place, query_place, offsets, keep_flag):
    memory_ok = (mem_slot[None, :] >= offsets[:, None]) & keep_flag[:, None]
    causal = key_place[None, :] <= query_place[:, None]
    return jnp.where(key_kind[None, None, :] < 2, memory_ok[:, None, :], causal[None, :, :])


def score_block(query_heads, key_heads, allowed, score_scale):
    scores = (
        jnp.einsum("sthe,skhe->shtk", query_heads, key_heads, preferred_element_type=jnp.float32)
        * score_scale
    )
    return jnp.where(allowed[:, None], scores, masked_score)


def tile_matrix(matrix, dp_count, seq_count):
    rows_total, cols_total = matrix.shape
    blocks = matrix.reshape(dp_count, rows_total // dp_count, seq_count, cols_total // seq_count)
    return blocks.transpose(0, 2, 1, 3).reshape(
        dp_count * seq_count, rows_total // dp_count, cols_total // seq_count
    )


def tile_vector(vector, dp_count, seq_count):
    piece_len = vector.shape[0] // dp_count
    pieces = vector.reshape(dp_count, 1, piece_len)
    return jnp.broadcast_to(pieces, (dp_count, seq_count, piece_len)).reshape(
        dp_count * seq_count, piece_len
    )


def on_device(
    inputs,
    memory,
    compressed,
    offsets,
    resets,
    w_query,
    w_key,
    w_value,
    w_output,
    w_hidden,
    w_return,
    w_compress,
    gain_attn,
    gain_ffn,
    out_grad,
    comp_grad,
):
    seq_count = lax.axis_size("seq")
    dp_count = lax.axis_size("dp")
    seq_rank = lax.axis_index("seq")
    streams, local_rows, feat_width = inputs.shape
    seg_len = local_rows * seq_count
    score_scale = HEAD_DIM ** (-0.5)
    keep_flag = resets == 0
    all_rows = jnp.concatenate([compressed, memory, inputs], axis=1).astype(jnp.float32)
    normed, attn_norm_back = jax.vjp(layer_norm, all_rows, gain_attn.astype(jnp.float32))
    normed_low = normed.astype(jnp.bfloat16)
    query_in = normed_low[:, 2 * local_rows :]
    query_low = project(query_in, w_query).astype(jnp.bfloat16)
    key_low = project(normed_low, w_key).astype(jnp.bfloat16)
    value_low = project(normed_low, w_value).astype(jnp.bfloat16)
    key_all, value_all = (
        lax.all_gather(key_low, "seq", axis=1, tiled=True),
        lax.all_gather(value_low, "seq", axis=1, tiled=True),
    )
    total_keys = key_all.shape[1]
    key_kind, mem_slot, key_place = key_layout(
        jnp.arange(total_keys, dtype=jnp.int32), local_rows, seg_len
    )
    query_place = seq_rank * local_rows + jnp.arange(local_rows, dtype=jnp.int32)
    allowed = allowed_mask(key_kind, mem_slot, key_place, query_place, offsets, keep_flag)
    query_heads = query_low.reshape(streams, local_rows, HEADS, HEAD_DIM)
    key_heads = key_all.reshape(streams, total_keys, HEADS, HEAD_DIM)
    value_heads = value_all.reshape(streams, total_keys, HEADS, HEAD_DIM)
    scores = score_block(query_heads, key_heads, allowed, score_scale)
    row_top = jnp.max(scores, axis=-1, keepdims=True)
    exp_scores = jnp.exp(scores - row_top)
    row_total = jnp.sum(exp_scores, axis=-1, keepdims=True)
    attn_prob = exp_scores / row_total
    log_total = row_top + jnp.log(row_total)
    mixed_low = (
        jnp.einsum(
            "shtk,skhe->sthe",
            attn_prob.astype(jnp.bfloat16),
            value_heads,
            preferred_element_type=jnp.float32,
        )
        .reshape(streams, local_rows, feat_width)
        .astype(jnp.bfloat16)
    )
    hidden = inputs.astype(jnp.float32) + project(mixed_low, w_output)
    ffn_in, ffn_norm_back = jax.vjp(layer_norm, hidden, gain_ffn.astype(jnp.float32))
    ffn_low = ffn_in.astype(jnp.bfloat16)
    ffn_all = lax.all_gather(ffn_low, "seq", axis=1, tiled=True)
    pre_act = jnp.einsum("std,df->stf", ffn_all, w_hidden, preferred_element_type=jnp.float32)
    act_float, gelu_back = jax.vjp(jax.nn.gelu, pre_act)
    act_low = act_float.astype(jnp.bfloat16)
    partial_out = jnp.einsum("stf,fd->std", act_low, w_return, preferred_element_type=jnp.float32)
    ffn_out = lax.psum_scatter(
        partial_out.astype(jnp.bfloat16), "seq", scatter_dimension=1, tiled=True
    ).astype(jnp.float32)
    cot_all = lax.all_gather(out_grad, "seq", axis=1, tiled=True)
    act_grad = jnp.einsum("std,fd->stf", cot_all, w_return, preferred_element_type=jnp.float32)
    return_part = jnp.einsum("stf,std->fd", act_low, cot_all, preferred_element_type=jnp.float32)
    pre_grad = gelu_back(act_grad)[0].astype(jnp.bfloat16)
    hidden_part = jnp.einsum("std,stf->df", ffn_all, pre_grad, preferred_element_type=jnp.float32)
    in_part = jnp.einsum("stf,df->std", pre_grad, w_hidden, preferred_element_type=jnp.float32)
    ffn_in_grad = lax.psum_scatter(in_part, "seq", scatter_dimension=1, tiled=True)
    hidden_sum, return_sum = (
        lax.psum_scatter(
            hidden_part.astype(jnp.bfloat16), "dp", scatter_dimension=0, tiled=True
        ).astype(jnp.float32),
        lax.psum_scatter(
            return_part.T.astype(jnp.bfloat16), "dp", scatter_dimension=0, tiled=True
        ).astype(jnp.float32),
    )
    grad_return = return_sum.T
    outputs = (hidden + ffn_out).astype(jnp.bfloat16)
    hidden_grad, gain_ffn_grad = ffn_norm_back(ffn_in_grad)
    hidden_grad = hidden_grad + out_grad.astype(jnp.float32)
    attn_grad_low = hidden_grad.astype(jnp.bfloat16)
    output_part = weight_term(mixed_low, attn_grad_low)
    mixed_grad = project_back(attn_grad_low, w_output).astype(jnp.bfloat16)
    mixed_heads = mixed_grad.reshape(streams, local_rows, HEADS, HEAD_DIM)
    prob_again = jnp.exp(score_block(query_heads, key_heads, allowed, score_scale) - log_total)
    prob_grad = jnp.einsum(
        "sthe,skhe->shtk", mixed_heads, value_heads, preferred_element_type=jnp.float32
    )
    prob_delta = jnp.sum(prob_again * prob_grad, axis=-1)
    score_grad = (prob_again * (prob_grad - prob_delta[..., None])).astype(jnp.bfloat16)
    query_grad = (
        (
            jnp.einsum("shtk,skhe->sthe", score_grad, key_heads, preferred_element_type=jnp.float32)
            * score_scale
        )
        .reshape(streams, local_rows, feat_width)
        .astype(jnp.bfloat16)
    )
    key_part = (
        jnp.einsum("shtk,sthe->skhe", score_grad, query_heads, preferred_element_type=jnp.float32)
        * score_scale
    ).reshape(streams, total_keys, feat_width)
    value_part = jnp.einsum(
        "shtk,sthe->skhe",
        prob_again.astype(jnp.bfloat16),
        mixed_heads,
        preferred_element_type=jnp.float32,
    ).reshape(streams, total_keys, feat_width)
    key_sum, value_sum = (
        lax.psum_scatter(
            key_part.astype(jnp.bfloat16), "seq", scatter_dimension=1, tiled=True
        ).astype(jnp.float32),
        lax.psum_scatter(
            value_part.astype(jnp.bfloat16), "seq", scatter_dimension=1, tiled=True
        ).astype(jnp.float32),
    )
    key_grad = key_sum.astype(jnp.bfloat16)
    value_grad = value_sum.astype(jnp.bfloat16)
    query_part = weight_term(query_in, query_grad)
    key_wpart = weight_term(normed_low, key_grad)
    value_wpart = weight_term(normed_low, value_grad)
    query_back = project_back(query_grad, w_query)
    normed_grad = project_back(key_grad, w_key) + project_back(value_grad, w_value)
    normed_grad = normed_grad + jnp.concatenate(
        [jnp.zeros((streams, 2 * local_rows, feat_width), jnp.float32), query_back], axis=1
    )
    rows_grad, gain_attn_grad = attn_norm_back(normed_grad)
    input_grad = (rows_grad[:, 2 * local_rows :] + hidden_grad).astype(jnp.bfloat16)
    kept_memory = memory * keep_flag[:, None, None].astype(jnp.bfloat16)
    edge_rows = shifted(kept_memory[:, : 2 * (RATE - 1)], "seq", -1)
    extended = jnp.concatenate([kept_memory, edge_rows], axis=1)
    group_count = (local_rows + RATE - 1) // RATE
    first_group = (seq_rank * local_rows + RATE - 1) // RATE
    slice_start = RATE * first_group - seq_rank * local_rows
    grouped = lax.dynamic_slice_in_dim(extended, slice_start, RATE * group_count, 1).reshape(
        streams, group_count, RATE * feat_width
    )
    piece_rows = jnp.einsum(
        "sgc,cd->sgd", grouped, w_compress, preferred_element_type=jnp.float32
    ).astype(jnp.bfloat16)
    comp_all = lax.all_gather(piece_rows, "seq", axis=1, tiled=True)
    comp_count = comp_grad.shape[1]
    out_index = jnp.arange(comp_count, dtype=jnp.int32)
    holder = RATE * out_index // local_rows
    lookup = holder * group_count + out_index - (holder * local_rows + RATE - 1) // RATE
    new_compressed = jnp.take(comp_all, lookup, axis=1)
    slot_index = first_group + jnp.arange(group_count, dtype=jnp.int32)
    slot_valid = (RATE * slot_index < (seq_rank + 1) * local_rows) & (slot_index < comp_count)
    picked = jnp.take(comp_grad, jnp.minimum(slot_index, comp_count - 1), axis=1) * slot_valid[
        None, :, None
    ].astype(jnp.bfloat16)
    compress_part = jnp.einsum("sgc,sgd->cd", grouped, picked, preferred_element_type=jnp.float32)
    reduced = (
        lax.psum_scatter(
            tile_matrix(query_part, dp_count, seq_count),
            ("dp", "seq"),
            scatter_dimension=0,
            tiled=True,
        ),
        lax.psum_scatter(
            tile_matrix(key_wpart, dp_count, seq_count),
            ("dp", "seq"),
            scatter_dimension=0,
            tiled=True,
        ),
        lax.psum_scatter(
            tile_matrix(value_wpart, dp_count, seq_count),
            ("dp", "seq"),
            scatter_dimension=0,
            tiled=True,
        ),
        lax.psum_scatter(
            tile_matrix(output_part, dp_count, seq_count),
            ("dp", "seq"),
            scatter_dimension=0,
            tiled=True,
        ),
        lax.psum_scatter(
            tile_matrix(compress_part, dp_count, seq_count),
            ("dp", "seq"),
            scatter_dimension=0,
            tiled=True,
        ),
        lax.psum_scatter(
            tile_vector(gain_attn_grad, dp_count, seq_count),
            ("dp", "seq"),
            scatter_dimension=0,
            tiled=True,
        ),
        lax.psum_scatter(
            tile_vector(gain_ffn_grad, dp_count, seq_count),
            ("dp", "seq"),
            scatter_dimension=0,
            tiled=True,
        ),
    )
    return (
        outputs,
        new_compressed,
        input_grad,
        reduced[0][0],
        reduced[1][0],
        reduced[2][0],
        reduced[3][0],
        hidden_sum,
        grad_return,
        reduced[4][0],
        reduced[5][0],
        reduced[6][0],
    )


F32 = jnp.float32
BF16 = jnp.bfloat16
NN = (((1,), (0,)), ((), ()))
NT = (((1,), (1,)), ((), ()))
TN = (((0,), (0,)), ((), ()))
VMEM_LIMIT = 60 * 1024 * 1024
SCALE = HEAD_DIM ** (-0.5)
EXP2_SCALE = SCALE * math.log2(math.e)


def dot(left, right, dims=NN):
    return lax.dot_general(left, right, dims, preferred_element_type=F32)


def params(steps=1):
    return pltpu.CompilerParams(
        vmem_limit_bytes=VMEM_LIMIT, dimension_semantics=("arbitrary",) * steps
    )


def cost(flops, bytes_accessed=0, transcendentals=0):
    return pl.CostEstimate(
        flops=int(flops), bytes_accessed=int(bytes_accessed), transcendentals=int(transcendentals)
    )


def held(shape):
    zeros = (0,) * len(shape)
    return pl.BlockSpec(shape, lambda *_: zeros, pipeline_mode=pl.Buffered(1))


def norm_parts(rows):
    centred = rows - jnp.mean(rows, axis=-1, keepdims=True)
    inverse = lax.rsqrt(jnp.mean(centred * centred, axis=-1, keepdims=True) + epsilon)
    return centred * inverse, inverse


def norm_back(grad, unit, inverse):
    return inverse * (
        grad
        - jnp.mean(grad, axis=-1, keepdims=True)
        - unit * jnp.mean(grad * unit, axis=-1, keepdims=True)
    )


def add_low(left, right):
    return (left.astype(F32) + right.astype(F32)).astype(BF16)


def mesh_place():
    rank, core = lax.axis_index("dp"), lax.axis_index("seq")

    def bit(b):
        return lax.rem(lax.div(rank, 1 << b), 2)

    def across(b):
        return rank + (1 << b) * (1 - 2 * bit(b))

    return core, bit, across


def greet(devices):
    barrier = pltpu.get_barrier_semaphore()
    for device in devices:
        pl.semaphore_signal(
            barrier, inc=1, device_id=device, device_id_type=pl.DeviceIdType.MESH
        )
    pl.semaphore_wait(barrier, len(devices))


def remote(src, dst, sems, device):
    return pltpu.make_async_remote_copy(
        src_ref=src,
        dst_ref=dst,
        send_sem=sems[0],
        recv_sem=sems[1],
        device_id=device,
        device_id_type=pl.DeviceIdType.MESH,
    )


class Chunk:
    def __init__(self, data, left, order, landing, sems, place):
        self.data, self.left, self.order = data, left, order
        self.landing, self.sems = landing, sems
        _, self.bit, self.across = place

    def at(self, swap, away):
        index = []
        for b in self.left:
            if b in self.order[:swap]:
                index.append(self.bit(b))
            elif swap < len(self.order) and b == self.order[swap]:
                index.append(1 - self.bit(b) if away else self.bit(b))
            else:
                index.append(slice(None))
        return tuple(index)

    def rest(self, swap):
        done = self.order[:swap]
        return tuple(self.bit(b) if b in done else slice(None) for b in self.left)

    def copy(self, swap):
        return remote(
            self.data.at[self.at(swap, True)],
            self.landing[swap],
            (self.sems.at[0, swap], self.sems.at[1, swap]),
            {"dp": self.across(self.order[swap])},
        )

    def start(self, swap):
        self.copy(swap).start()

    def settle(self, swap):
        self.copy(swap).wait()
        here = self.at(swap, False)
        self.data[here] = add_low(self.data[here], self.landing[swap][...])

    def last(self, swap):
        self.copy(swap).wait()
        return self.data[self.at(swap, False)].astype(F32) + self.landing[swap][...].astype(F32)


def landings(left, order, block):
    shapes, count = [], len(left)
    for _ in order:
        count -= 1
        shapes.append(pltpu.VMEM((2,) * count + block, BF16))
    return shapes


BITS = (3, 2, 1, 0)
ORDERS = ((0, 1, 2, 3), (1, 0, 2, 3))


def front_kernel(
    resets_ref, in_ref, mem_ref, old_ref, og_ref, wc_ref, cg_ref,
    x_in_ref, x_mem_ref, x_old_ref, x_og_ref, new_ref, kept_p_ref, sent_p_ref, kept_q_ref, sent_q_ref,
    mem, x_in, x_old, x_og, wc, new, core_out, core_in, row_sems, wc_sem, new_sems, core_sems, out_sems,
):
    core, bit, _ = mesh_place()
    partner = {"seq": 1 - core}
    width = in_ref.shape[2]
    groups = cg_ref.shape[1]

    weights = pltpu.make_async_copy(wc_ref, wc, wc_sem)
    weights.start()
    greet((partner,))
    moves = []
    for n, (src, dst) in enumerate(
        ((mem_ref, mem), (in_ref, x_in), (old_ref, x_old), (og_ref, x_og))
    ):
        for j in range(2):
            away = remote(
                src.at[1 - core + 2 * j], dst.at[j, core], (row_sems.at[0, n, j], row_sems.at[1, n, j]), partner
            )
            here = pltpu.make_async_copy(src.at[core + 2 * j], dst.at[j, core], row_sems.at[2, n, j])
            away.start()
            here.start()
            moves.append((away, here))
    new[...] = jnp.zeros_like(new)
    outs = []
    for j in range(2):
        moves[j][0].wait_recv()
        moves[j][1].wait()
    outs.append(pltpu.make_async_copy(mem, x_mem_ref, out_sems.at[0]))
    outs[-1].start()
    weights.wait()

    grouped = []
    for j in range(2):
        rows = mem[j].reshape(2 * mem.shape[2], width)
        group = lax.broadcasted_iota(jnp.int32, (groups, rows.shape[0]), 0)
        row = lax.broadcasted_iota(jnp.int32, (groups, rows.shape[0]), 1)
        keep = jnp.where(resets_ref[core + 2 * j] == 0, 1.0, 0.0)
        total = jnp.zeros((groups, width), F32)
        mine = []
        for r in range(RATE):
            pick = jnp.where(row == RATE * group + r, keep, 0.0).astype(BF16)
            mine.append(dot(pick, rows).astype(BF16))
            total = total + dot(mine[-1], wc[r * width : (r + 1) * width])
        grouped.append(mine)
        new[j, :groups] = total.astype(BF16)

    news = []
    for j in range(2):
        at = core + 2 * j
        news.append(remote(new.at[j], new_ref.at[at], (new_sems.at[0, j], new_sems.at[1, j]), partner))
        outs.append(pltpu.make_async_copy(new.at[j], new_ref.at[at], new_sems.at[2, j]))
        news[-1].start()
        outs[-1].start()

    half = width // 2

    def grad(r, side):
        cols = pl.ds(pl.multiple_of(side * half, half), half)
        return sum(dot(grouped[j][r], cg_ref[core + 2 * j, :, cols], TN) for j in range(2))

    crossing = []
    for r in range(RATE):
        core_out[r] = grad(r, 1 - core).astype(BF16)
        crossing.append(
            remote(core_out.at[r], core_in.at[r], (core_sems.at[0, r], core_sems.at[1, r]), partner)
        )
        crossing[-1].start()
    for n, (src, dst) in enumerate(((x_in, x_in_ref), (x_old, x_old_ref), (x_og, x_og_ref))):
        for away, here in moves[2 * n + 2 : 2 * n + 4]:
            away.wait_recv()
            here.wait()
        outs.append(pltpu.make_async_copy(src, dst, out_sems.at[1 + n]))
        outs[-1].start()
    fine = width // 16
    quarter = half // 2
    for r in range(RATE):
        total = grad(r, core)
        crossing[r].wait()
        total = (total + core_in[r].astype(F32)).astype(BF16)
        for which, (kept_ref, sent_ref) in enumerate(
            ((kept_p_ref, sent_p_ref), (kept_q_ref, sent_q_ref))
        ):
            for mine in range(2):

                @pl.when(bit(which) == mine)
                def _():
                    for t in range(16):
                        block, third = divmod(r * 16 + t, RATE)
                        place = (block >> 3, block >> 2 & 1, block >> (1 - which) & 1)
                        ref = kept_ref if block >> which & 1 == mine else sent_ref
                        ref[place + (slice(third * fine, (third + 1) * fine),)] = total[
                            t * fine : (t + 1) * fine, which * quarter : (which + 1) * quarter
                        ]
    for away, _ in moves:
        away.wait_send()
    for move in outs + news:
        move.wait()


def front(resets, inputs, memory, compressed, out_grad, w_compress, comp_grad):
    streams, half, width = inputs.shape
    anywhere = pl.BlockSpec(memory_space=pl.ANY)
    vmem = pl.BlockSpec(memory_space=pltpu.VMEM)
    pair = jax.ShapeDtypeStruct((2, 2, half, width), BF16)
    padded = -(-comp_grad.shape[1] // 16) * 16
    part = jax.ShapeDtypeStruct((2, 2, 2, RATE * width // 16, width // 4), BF16)
    return pl.pallas_call(
        front_kernel,
        out_shape=(
            pair, pair, pair, pair, jax.ShapeDtypeStruct((streams, padded, width), BF16),
            part, part, part, part,
        ),
        in_specs=[pl.BlockSpec(memory_space=pltpu.SMEM)] + [anywhere] * 5 + [vmem],
        out_specs=(anywhere,) * 5 + (vmem,) * 4,
        scratch_shapes=[
            pltpu.VMEM((2, 2, half, width), BF16),
            pltpu.VMEM((2, 2, half, width), BF16),
            pltpu.VMEM((2, 2, half, width), BF16),
            pltpu.VMEM((2, 2, half, width), BF16),
            pltpu.VMEM(w_compress.shape, BF16),
            pltpu.VMEM((2, padded, width), BF16),
            pltpu.VMEM((RATE, width, width // 2), BF16),
            pltpu.VMEM((RATE, width, width // 2), BF16),
            pltpu.SemaphoreType.DMA((3, 4, 2)),
            pltpu.SemaphoreType.DMA,
            pltpu.SemaphoreType.DMA((3, 2)),
            pltpu.SemaphoreType.DMA((2, RATE)),
            pltpu.SemaphoreType.DMA((4,)),
        ],
        compiler_params=pltpu.CompilerParams(
            vmem_limit_bytes=VMEM_LIMIT, collective_id=4, has_side_effects=True
        ),
        cost_estimate=cost(12e9, 24e6),
        name="front",
    )(resets, inputs, memory, compressed, out_grad, w_compress, comp_grad)


def project_kernel(
    pick_ref, old_ref, mem_ref, in_ref, og_ref, gain_ref, wq_ref, wk_ref, wv_ref,
    raw_ref, normed_ref, q_ref, k_ref, v_ref, og_out_ref,
):
    step = pl.program_id(0)
    raw = jnp.where(step < 2, old_ref[...], jnp.where(step < 4, mem_ref[...], in_ref[...]))
    raw_ref[...] = raw
    unit, _ = norm_parts(raw.astype(F32))
    normed = (unit * gain_ref[...]).astype(BF16)
    normed_ref[...] = normed
    k_ref[...] = dot(normed, wk_ref[...]).astype(BF16)
    v_ref[...] = dot(normed, wv_ref[...]).astype(BF16)

    @pl.when(step >= 4)
    def _():
        q_ref[...] = dot(normed, wq_ref[...]).astype(BF16)
        og_out_ref[...] = og_ref[...]


def project_rows(pick, old, mem, inputs, og, gain, wq, wk, wv):
    _, _, half, width = inputs.shape

    def from_pair(first):
        def index(i, pick_ref):
            at = jnp.clip(i - first, 0, 3 if first == 4 else 1)
            return pick_ref[at // 2], at % 2, 0, 0

        return pl.BlockSpec((None, None, half, width), index)

    keys = pl.BlockSpec((half, width), lambda i, _: (i, 0))
    rows = pl.BlockSpec((half, width), lambda i, _: (jnp.maximum(i - 4, 0), 0))
    key_shape = jax.ShapeDtypeStruct((8 * half, width), BF16)
    row_shape = jax.ShapeDtypeStruct((4 * half, width), BF16)
    return pl.pallas_call(
        project_kernel,
        out_shape=(key_shape, key_shape, row_shape, key_shape, key_shape, row_shape),
        grid_spec=pltpu.PrefetchScalarGridSpec(
            num_scalar_prefetch=1,
            grid=(8,),
            in_specs=[
                from_pair(0), from_pair(2), from_pair(4), from_pair(4),
                held(gain.shape), held(wq.shape), held(wk.shape), held(wv.shape),
            ],
            out_specs=(keys, keys, rows, keys, keys, rows),
        ),
        compiler_params=params(),
        cost_estimate=cost(14e9, 30e6),
        name="project",
    )(pick, old, mem, inputs, og, gain, wq, wk, wv)


def attn_fwd_kernel(
    off_ref, q_ref, k_ref, v_ref, in_ref, wo_ref, gain_ref, kept_p_ref, got_p_ref, kept_q_ref, got_q_ref,
    mixed_ref, hidden_ref, ffn_ref, lse_ref, compress_ref,
    packed, *scratch,
):
    step = pl.program_id(0)
    lands, chip_sems = scratch[:-1], scratch[-1]
    place = mesh_place()
    chunks = [
        Chunk(
            packed.at[which],
            tuple(b for b in BITS if b != ORDERS[which][0]),
            ORDERS[which][1:],
            lands[3 * which : 3 * which + 3],
            chip_sems.at[which],
            place,
        )
        for which in range(2)
    ]

    @pl.when(step == 0)
    def _():
        greet(tuple({"dp": place[2](b)} for b in range(4)))
        packed[0] = add_low(kept_p_ref[...], got_p_ref[...])
        packed[1] = add_low(kept_q_ref[...], got_q_ref[...])
        for part in chunks:
            part.start(0)

    for swap in range(2):

        @pl.when(step == swap + 2)
        def _():
            for part in chunks:
                part.settle(swap)
                part.start(swap + 1)

    half = q_ref.shape[0]
    seg = 2 * half

    def run(pieces):
        def one_head(h, stats):
            cols = pl.ds(pl.multiple_of(h * HEAD_DIM, HEAD_DIM), HEAD_DIM)
            q = q_ref[:, cols]
            scores = []
            for start, size, kind in pieces:
                s = dot(q, k_ref[start : start + size, cols], NT)
                if kind == "mem":
                    slot = lax.broadcasted_iota(jnp.int32, s.shape, 1)
                    s = jnp.where(slot >= off_ref[0], s, masked_score)
                if kind == "diag":
                    key = lax.broadcasted_iota(jnp.int32, s.shape, 1)
                    row = lax.broadcasted_iota(jnp.int32, s.shape, 0)
                    s = jnp.where(key <= row, s, masked_score)
                scores.append(s)
            top = functools.reduce(
                jnp.maximum, [jnp.max(s, axis=-1, keepdims=True) for s in scores]
            ) * EXP2_SCALE
            mix = jnp.zeros((half, 2 * HEAD_DIM), F32)
            for s, (start, size, _) in zip(scores, pieces):
                p = jnp.exp2(s * EXP2_SCALE - top).astype(BF16)
                ones = jnp.ones((size, HEAD_DIM), BF16)
                mix = mix + dot(p, jnp.concatenate([v_ref[start : start + size, cols], ones], axis=1))
            total = mix[:, HEAD_DIM:]
            mixed_ref[:, cols] = (mix[:, :HEAD_DIM] / total).astype(BF16)
            lane = lax.broadcasted_iota(jnp.int32, stats.shape, 1)
            return jnp.where(lane == h, top + jnp.log2(total), stats)

        stats = lax.fori_loop(0, HEADS, one_head, jnp.zeros((half, 128), F32), unroll=True)
        lse_ref[...] = stats.T[:HEADS]

    cases = (
        ((0, 2 * seg, "mem"), (2 * seg, half, "diag")),
        ((0, 2 * seg, "mem"), (2 * seg, half, "full"), (2 * seg + half, half, "diag")),
        ((3 * seg, half, "diag"),),
        ((3 * seg, half, "full"), (3 * seg + half, half, "diag")),
    )
    for i, pieces in enumerate(cases[2:] + cases[:2]):
        pl.when(step == i)(functools.partial(run, pieces))
    hidden = in_ref[...].astype(F32) + dot(mixed_ref[...], wo_ref[...])
    hidden_ref[...] = hidden
    unit, _ = norm_parts(hidden)
    ffn_ref[...] = (unit * gain_ref[...]).astype(BF16)

    @pl.when(step == 3)
    def _():
        cols = compress_ref.shape[1] // 2
        for which, part in enumerate(chunks):
            compress_ref[:, which * cols : (which + 1) * cols] = part.last(2)


def attn_fwd(first_slot, q, k, v, raw, wo, gain, kept_p, got_p, kept_q, got_q):
    rows, width = q.shape
    half = rows // 4
    by_block = pl.BlockSpec((half, width), lambda i: (lax.rem(i + 2, 4), 0))
    in_block = pl.BlockSpec((half, width), lambda i: (4 + lax.rem(i + 2, 4), 0))
    block = kept_p.shape[-2:]
    part = held(kept_p.shape)
    lands = []
    for which in range(2):
        lands += landings(BITS[1:], ORDERS[which][1:], block)
    out = (block[0], 2 * block[1])
    return pl.pallas_call(
        attn_fwd_kernel,
        grid=(4,),
        out_shape=(
            jax.ShapeDtypeStruct((rows, width), BF16),
            jax.ShapeDtypeStruct((rows, width), F32),
            jax.ShapeDtypeStruct((rows, width), BF16),
            jax.ShapeDtypeStruct((HEADS, rows), F32),
            jax.ShapeDtypeStruct(out, F32),
        ),
        in_specs=[
            pl.BlockSpec(memory_space=pltpu.SMEM),
            by_block, held(k.shape), held(v.shape), in_block, held(wo.shape), held(gain.shape),
            part, part, part, part,
        ],
        out_specs=(
            by_block, by_block, by_block, pl.BlockSpec((HEADS, half), lambda i: (0, lax.rem(i + 2, 4))), held(out),
        ),
        scratch_shapes=[pltpu.VMEM((2,) + kept_p.shape, BF16)] + lands + [pltpu.SemaphoreType.DMA((2, 2, 3))],
        compiler_params=pltpu.CompilerParams(
            vmem_limit_bytes=VMEM_LIMIT, dimension_semantics=("arbitrary",),
            collective_id=5, has_side_effects=True,
        ),
        cost_estimate=cost(20e9, 20e6),
        name="attn_fwd",
    )(first_slot, q, k, v, raw, wo, gain, kept_p, got_p, kept_q, got_q)


GELU_C = math.sqrt(2.0 / math.pi)
GELU_A = 0.044715
CHUNK = 512


def gelu_pair(pre, act_grad):
    square = pre * pre
    t = jnp.tanh(pre * (GELU_C + (GELU_C * GELU_A) * square))
    cdf = 0.5 + 0.5 * t
    slope = cdf + (0.5 * pre) * (1.0 - t * t) * (GELU_C + (3.0 * GELU_C * GELU_A) * square)
    return (pre * cdf).astype(BF16), (act_grad * slope).astype(BF16)


def ffn_kernel(
    x_ref, og_ref, hidden_ref, gain_ref, wo_ref, wh0_ref, wh1_ref, wr0_ref, wr1_ref,
    out_ref, attn_grad_ref, do_ref, gain_grad_ref, done_ref, part_ref, raw_ref,
    wh, wr, out_acc, in_acc, act_ref, pre_ref, core_out, core_in, own_ref, land0, land1, land2, land3,
    weight_sems, core_sems, chip_sems,
):
    step = pl.program_id(0)
    last = pl.num_programs(0) - 1
    index = lax.div(step, 2)
    end = lax.div(last, 2)
    owned = lax.rem(step, 2) == 1
    rows, width = x_ref.shape
    units = wh.shape[2]
    chunks = rows // CHUNK
    place = mesh_place()
    core, _, across = place
    partner = {"seq": 1 - core}

    def fetch(at, side):
        cols = pl.ds(pl.multiple_of(at * units, units), units)
        wh_ref, wr_ref = ((wh0_ref, wr0_ref), (wh1_ref, wr1_ref))[side]
        return (
            pltpu.make_async_copy(wh_ref.at[:, cols], wh.at[side], weight_sems.at[0, side]),
            pltpu.make_async_copy(wr_ref.at[cols], wr.at[side], weight_sems.at[1, side]),
        )

    @pl.when(step == 0)
    def _():
        for copy in fetch(0, 0):
            copy.start()
        greet((partner,) + tuple({"dp": across(b)} for b in range(4)))
        out_acc[...] = jnp.zeros_like(out_acc)
        in_acc[...] = jnp.zeros_like(in_acc)

    @pl.when(jnp.logical_not(owned))
    def _():
        for copy in fetch(index, 1):
            copy.start()
        for copy in fetch(index, 0):
            copy.wait()

    @pl.when(owned)
    def _():
        @pl.when(index < end)
        def _():
            for copy in fetch(index + 1, 0):
                copy.start()

        for copy in fetch(index, 1):
            copy.wait()

    def core_copy(which, index):
        return remote(
            core_out.at[which],
            core_in.at[which, lax.rem(index, 2)],
            (core_sems.at[0, which, index], core_sems.at[1, which, index]),
            partner,
        )

    def tile(which, index):
        slot = lax.rem(index, 2)
        return Chunk(
            own_ref.at[which, slot], BITS, ORDERS[which],
            [land.at[which, slot] for land in (land0, land1, land2, land3)],
            chip_sems.at[which, index], place,
        )

    def pass_on(index, swap):
        for which in range(2):
            part = tile(which, index)
            part.settle(swap)
            part.start(swap + 1)

    side = lax.rem(step, 2)

    def rows_step(m, _):
        at = pl.ds(pl.multiple_of(m * CHUNK, CHUNK), CHUNK)
        pre = dot(x_ref[at, :], wh[side])
        act_grad = dot(og_ref[at, :], wr[side], NT)
        act, pre_grad = gelu_pair(pre, act_grad)
        act_ref[at, :] = act
        pre_ref[at, :] = pre_grad
        out_acc[at, :] += dot(act, wr[side])
        in_acc[at, :] += dot(pre_grad, wh[side], NT)

        @pl.when((m == 0) & owned & (index > 0))
        def _():
            pass_on(index - 1, 0)

        return 0

    lax.fori_loop(0, chunks, rows_step, 0)

    @pl.when(owned & (index > 0) & (index < end))
    def _():
        pass_on(index - 1, 1)

    @pl.when(owned & (index > 1))
    def _():
        for which in range(2):
            done_ref[which, index - 2] = tile(which, index - 2).last(3)

    for which, (left_ref, right_ref) in enumerate(((x_ref, pre_ref), (og_ref, act_ref))):
        grad = dot(left_ref[...], right_ref[...], TN)

        @pl.when(jnp.logical_not(owned))
        def _():
            @pl.when(index > 0)
            def _():
                core_copy(which, index - 1).wait_send()

            core_out[which] = grad.astype(BF16)
            core_copy(which, index).start()

        @pl.when(owned)
        def _():
            core_copy(which, index).wait_recv()
            total = grad + core_in[which, lax.rem(index, 2)].astype(F32)
            own_ref[which, lax.rem(index, 2)] = total.astype(BF16).reshape(own_ref.shape[2:])

            @pl.when(index < end)
            def _():
                tile(which, index).start(0)

    @pl.when(jnp.logical_not(owned) & (index > 1))
    def _():
        pass_on(index - 2, 2)

    @pl.when(step == last)
    def _():
        def finish(m, gain_sum):
            at = pl.ds(pl.multiple_of(m * 256, 256), 256)
            hidden = hidden_ref[at, :]
            out_ref[at, :] = (hidden + out_acc[at, :]).astype(BF16)
            unit, inverse = norm_parts(hidden)
            grad = in_acc[at, :]
            hidden_grad = og_ref[at, :].astype(F32) + norm_back(
                grad * gain_ref[...], unit, inverse
            )
            low = hidden_grad.astype(BF16)
            attn_grad_ref[at, :] = low
            do_ref[at, :] = dot(low, wo_ref[...], NT).astype(BF16)
            return gain_sum + jnp.sum(grad * unit, axis=0, keepdims=True)

        gain_grad_ref[...] = lax.fori_loop(
            0, rows // 256, finish, jnp.zeros(gain_grad_ref.shape, F32)
        )
        for which in range(2):
            raw_ref[which] = own_ref[which, lax.rem(end, 2)]
            core_copy(which, end).wait_send()
            part = tile(which, end - 1)
            part.settle(1)
            part_ref[which] = part.data[part.rest(2)]


def ffn(x, og, hidden, gain, wo, wh0, wh1, wr0, wr1):
    rows, width = x.shape
    units = wh0.shape[1]
    tile = 512
    steps = units // tile
    count = lax.axis_size("dp")
    block = width // count
    anywhere = pl.BlockSpec(memory_space=pl.ANY)
    whole = held((rows, width))
    low_rows = jax.ShapeDtypeStruct((rows, width), BF16)
    raw = (2, 2, 2, 2, 2, block, tile)
    part = (2, 2, 2, block, tile)
    done = (2, steps - 2, block, tile)
    lands = [pltpu.VMEM((2, 2) + (2,) * n + (block, tile), BF16) for n in (3, 2, 1, 0)]
    return pl.pallas_call(
        ffn_kernel,
        grid=(2 * steps,),
        out_shape=(
            low_rows, low_rows, low_rows, jax.ShapeDtypeStruct((1, width), F32),
            jax.ShapeDtypeStruct(done, F32),
            jax.ShapeDtypeStruct(part, BF16),
            jax.ShapeDtypeStruct(raw, BF16),
        ),
        in_specs=[whole, whole, whole, held(gain.shape), held(wo.shape)] + [anywhere] * 4,
        out_specs=(whole, whole, whole, held((1, width)), held(done), held(part), held(raw)),
        scratch_shapes=[
            pltpu.VMEM((2, width, tile), BF16),
            pltpu.VMEM((2, tile, width), BF16),
            pltpu.VMEM((rows, width), F32),
            pltpu.VMEM((rows, width), F32),
            pltpu.VMEM((rows, tile), BF16),
            pltpu.VMEM((rows, tile), BF16),
            pltpu.VMEM((2, width, tile), BF16),
            pltpu.VMEM((2, 2, width, tile), BF16),
            pltpu.VMEM((2, 2) + raw[1:], BF16),
        ] + lands + [
            pltpu.SemaphoreType.DMA((2, 2)),
            pltpu.SemaphoreType.DMA((2, 2, steps)),
            pltpu.SemaphoreType.DMA((2, steps, 2, 4)),
        ],
        compiler_params=pltpu.CompilerParams(
            vmem_limit_bytes=VMEM_LIMIT, dimension_semantics=("arbitrary",),
            collective_id=1, has_side_effects=True,
        ),
        cost_estimate=cost(75e9, 50e6),
        name="ffn",
    )(x, og, hidden, gain, wo, wh0, wh1, wr0, wr1)


def attn_bwd_head(first_slot, q_ref, k_ref, v_ref, do_ref, mixed_ref, lse, dq_ref, dk_ref, dv_ref, cols):
    seg = q_ref.shape[0] // 2
    half = seg // 2
    for stream in range(2):
        base = stream * seg
        rows = slice(base, base + seg)
        lse_row = lse[:, rows]
        weight = do_ref[rows, cols].astype(F32) * mixed_ref[rows, cols].astype(F32)
        delta_row = jnp.sum(weight.T, axis=0, keepdims=True)
        key_base = 2 * seg + stream * seg
        pieces = []
        if stream == 0:
            pieces += [(start, half, 0, "mem") for start in range(0, 2 * seg, half)]
        pieces += [(key_base, half, 0, "diag"), (key_base + half, half, half, "diag")]
        dq_low = jnp.zeros((half, HEAD_DIM), F32)
        dq_high = jnp.zeros((half, HEAD_DIM), F32)
        for start, size, first, kind in pieces:
            q = q_ref[base + first : base + seg, cols]
            do = do_ref[base + first : base + seg, cols]
            k = k_ref[start : start + size, cols]
            s = dot(k, q, NT) * EXP2_SCALE - lse_row[:, first:]
            if kind == "mem":
                slot = start + lax.broadcasted_iota(jnp.int32, s.shape, 0)
                s = jnp.where(slot >= first_slot, s, masked_score)
            else:
                key = lax.broadcasted_iota(jnp.int32, s.shape, 0)
                row = lax.broadcasted_iota(jnp.int32, s.shape, 1)
                s = jnp.where(key <= row, s, masked_score)
            p = jnp.exp2(s)
            dp = dot(v_ref[start : start + size, cols], do, NT)
            ds = (p * (dp - delta_row[:, first:])).astype(BF16)
            dv_ref[start : start + size, cols] = dot(p.astype(BF16), do).astype(BF16)
            dk_ref[start : start + size, cols] = (dot(ds, q) * SCALE).astype(BF16)
            dq = dot(ds, k, TN)
            if first == 0:
                dq_low = dq_low + dq[:half]
                dq_high = dq_high + dq[half:]
            else:
                dq_high = dq_high + dq
        dq_ref[base : base + half, cols] = (dq_low * SCALE).astype(BF16)
        dq_ref[base + half : base + seg, cols] = (dq_high * SCALE).astype(BF16)


def attn_back_kernel(
    off_ref, q_ref, k_ref, v_ref, do_ref, mix_ref, lse_ref, normed_ref, mixed_ref, ag_ref,
    ffn_part_ref, ffn_raw_ref,
    dq_ref, dk_ref, dv_ref, early_ref, late_ref, ffn_done_ref,
    grads_ref, core_out, core_in, own_ref, *scratch,
):
    step = pl.program_id(0)
    last = pl.num_programs(0) - 1
    place = mesh_place()
    core, _, across = place
    partner = {"seq": 1 - core}
    lands, (core_sems, chip_sems) = list(scratch[:-2]), scratch[-2:]
    chunks, ffn_parts, ffn_raws = [], [], []

    def chunk(number, data, left, order):
        mine = [lands.pop(0) for _ in order]
        return Chunk(data, left, order, mine, chip_sems.at[number], place)

    for which in range(2):
        order = ORDERS[which]
        chunks.append(chunk(3 * which, own_ref.at[which], BITS, order[:2]))
        ffn_parts.append(chunk(3 * which + 1, ffn_part_ref.at[which], order[2:][::-1], order[2:]))
        ffn_raws.append(chunk(3 * which + 2, ffn_raw_ref.at[which], BITS, order))
    index = lax.div(step, 2)
    rows = q_ref.shape[0]
    keys = k_ref.shape[0]
    pair = q_ref.shape[1]

    @pl.when(step == 0)
    def _():
        greet((partner,) + tuple({"dp": across(b)} for b in range(4)))
        for part in ffn_raws + ffn_parts:
            part.start(0)

    for n in range(1, 4):

        @pl.when(step == n)
        def _():
            for part in ffn_raws:
                part.settle(n - 1)
                part.start(n)

    @pl.when(step == 1)
    def _():
        for part in ffn_parts:
            part.settle(0)
            part.start(1)

    @pl.when(step == 2)
    def _():
        for which in range(2):
            ffn_done_ref[which, 0] = ffn_parts[which].last(1)

    def core_copy(which, index):
        return remote(
            core_out.at[which, index],
            core_in.at[which, index],
            (core_sems.at[0, which, index], core_sems.at[1, which, index]),
            partner,
        )

    head = 4 * jnp.where(lax.rem(step, 2) == 0, 1 - core, core) + 2 * index

    def one_head(h, _):
        attn_bwd_head(
            off_ref[0], q_ref, k_ref, v_ref, do_ref, mix_ref, lse_ref[pl.ds(head + h, 1), :],
            dq_ref, dk_ref, dv_ref, pl.ds(pl.multiple_of(h * HEAD_DIM, HEAD_DIM), HEAD_DIM),
        )
        return 0

    lax.fori_loop(0, 2, one_head, 0)
    grads_ref[0, :, :pair] = dot(normed_ref[keys - rows :], dq_ref[...], TN)
    grads_ref[0, :, pair:] = dot(normed_ref[...], dk_ref[...], TN)
    grads_ref[1, :, :pair] = dot(normed_ref[...], dv_ref[...], TN)
    grads_ref[1, :, pair:] = dot(mixed_ref[...], ag_ref[...], TN)

    @pl.when(lax.rem(step, 2) == 0)
    def _():
        for which in range(2):
            core_out[which, index] = grads_ref[which].astype(BF16)
            core_copy(which, index).start()

    @pl.when(step == 2)
    def _():
        for part in chunks:
            part.settle(0)
            part.start(1)

    def own_grads(which, index, out_ref):
        core_copy(which, index).wait()
        total = grads_ref[which] + core_in[which, index].astype(F32)
        out_ref[...] = total.astype(BF16).reshape(out_ref.shape)

    @pl.when(step == 1)
    def _():
        for which in range(2):
            own_grads(which, 0, own_ref.at[which])
            chunks[which].start(0)

    @pl.when(step == last)
    def _():
        for which in range(2):
            own_grads(which, 1, late_ref.at[which])
        for which in range(2):
            chunks[which].settle(1)
            early_ref[which] = own_ref[(which,) + chunks[which].rest(2)]
            ffn_done_ref[which, 1] = ffn_raws[which].last(3)


def attn_back(first_slot, q, k, v, do, mixed, lse, normed, attn_grad, ffn_part, ffn_raw):
    rows, width = q.shape
    keys = k.shape[0]
    pair = 2 * HEAD_DIM
    block = (width // 16, 2 * pair)

    def by_pair(count):
        def index(i):
            core = lax.axis_index("seq")
            half = jnp.where(lax.rem(i, 2) == 0, 1 - core, core)
            return 0, 2 * half + lax.div(i, 2)

        return pl.BlockSpec((count, pair), index)

    early, late = (2, 2, 2) + block, (2, 2, 2, 2, 2) + block
    ffn_block = ffn_raw.shape[-2:]
    done = (2, 2) + ffn_block
    lands = []
    for order in ORDERS:
        lands += landings(BITS, order[:2], block)
        lands += landings(order[2:], order[2:], ffn_block)
        lands += landings(BITS, order, ffn_block)
    return pl.pallas_call(
        attn_back_kernel,
        grid=(4,),
        out_shape=(
            jax.ShapeDtypeStruct((rows, width), BF16),
            jax.ShapeDtypeStruct((keys, width), BF16),
            jax.ShapeDtypeStruct((keys, width), BF16),
            jax.ShapeDtypeStruct(early, BF16),
            jax.ShapeDtypeStruct(late, BF16),
            jax.ShapeDtypeStruct(done, F32),
        ),
        in_specs=[
            pl.BlockSpec(memory_space=pltpu.SMEM),
            by_pair(rows), by_pair(keys), by_pair(keys), by_pair(rows), by_pair(rows),
            held(lse.shape), held(normed.shape), held(mixed.shape), by_pair(rows),
            held(ffn_part.shape), held(ffn_raw.shape),
        ],
        out_specs=(by_pair(rows), by_pair(keys), by_pair(keys), held(early), held(late), held(done)),
        scratch_shapes=[
            pltpu.VMEM((2, width, 2 * pair), F32),
            pltpu.VMEM((2, 2, width, 2 * pair), BF16),
            pltpu.VMEM((2, 2, width, 2 * pair), BF16),
            pltpu.VMEM(late, BF16),
        ] + lands + [
            pltpu.SemaphoreType.DMA((2, 2, 2)),
            pltpu.SemaphoreType.DMA((6, 2, 4)),
        ],
        compiler_params=pltpu.CompilerParams(
            vmem_limit_bytes=VMEM_LIMIT, dimension_semantics=("arbitrary",),
            collective_id=2, has_side_effects=True,
        ),
        cost_estimate=cost(45e9, 24e6),
        name="attn_back",
    )(first_slot, q, k, v, do, mixed, lse, normed, mixed, attn_grad, ffn_part, ffn_raw)


def rows_back_kernel(
    dq_ref, dk_ref, dv_ref, raw_ref, ag_ref, gain_ref, gain_ffn_ref, wq_ref, wk_ref, wv_ref,
    early_ref, late_ref,
    mine_ref, theirs_ref, gains_ref, early_out_ref, late_out_ref,
    rows_out, gain_acc, gain_in, *scratch,
):
    step = pl.program_id(0)
    last = pl.num_programs(0) - 1
    place = mesh_place()
    core, _, across = place
    partner = {"seq": 1 - core}
    lands, (row_sems, local_sems, gain_sems, chip_sems) = list(scratch[:-4]), scratch[-4:]

    chunks = []

    def chunk(data, left, order):
        number = len(chunks)
        mine = [lands.pop(0) for _ in order]
        chunks.append(Chunk(data, left, order, mine, chip_sems.at[number], place))
        return chunks[-1]

    early, late = [], []
    for which in range(2):
        early.append(chunk(early_ref.at[which], BITS[:2], ORDERS[which][2:]))
        late.append(chunk(late_ref.at[which], BITS, ORDERS[which]))

    def gain_copy(n):
        device = partner if n == 0 else {"dp": across(n - 1)}
        return remote(gain_acc.at[n], gain_in.at[n], (gain_sems.at[0, n], gain_sems.at[1, n]), device)

    def row_copy(block):
        stream = block // 2
        return remote(
            rows_out.at[block], theirs_ref.at[stream], (row_sems.at[0, stream], row_sems.at[1, stream]), partner
        )

    def row_keep(block):
        stream = block // 2
        return pltpu.make_async_copy(rows_out.at[block], mine_ref.at[stream], local_sems.at[stream])

    @pl.when(step == 0)
    def _():
        greet((partner,) + tuple({"dp": across(b)} for b in range(4)))
        for part in late + early:
            part.start(0)
        gain_acc[...] = jnp.zeros_like(gain_acc)

    def normed_grad():
        return dot(dk_ref[...], wk_ref[...], NT) + dot(dv_ref[...], wv_ref[...], NT)

    unit, inverse = norm_parts(raw_ref[...].astype(F32))

    @pl.when(step < 4)
    def _():
        gain_acc[0, 0:1] += jnp.sum(normed_grad() * unit, axis=0, keepdims=True)

    @pl.when(step >= 4)
    def _():
        grad = normed_grad() + dot(dq_ref[...], wq_ref[...], NT)
        gain_acc[0, 0:1] += jnp.sum(grad * unit, axis=0, keepdims=True)
        rows_grad = norm_back(grad * gain_ref[...], unit, inverse)
        rows_out[step - 4] = (rows_grad + ag_ref[...].astype(F32)).astype(BF16)

    for block in range(4):
        stays = core == block % 2
        pl.when((step == block + 4) & stays)(row_keep(block).start)
        pl.when((step == block + 4) & jnp.logical_not(stays))(row_copy(block).start)

    @pl.when(step == 4)
    def _():
        for part in early:
            part.settle(0)
            part.start(1)

    @pl.when(step == 6)
    def _():
        for part in late:
            part.settle(0)
            part.start(1)

    @pl.when(step == last)
    def _():
        def gain_step(n):
            gain_copy(n).wait()
            total = gain_acc[n] + gain_in[n]
            if n < 4:
                gain_acc[n + 1] = total
                gain_copy(n + 1).start()
            else:
                gains_ref[...] = total

        gain_acc[0, 1:2] = gain_ffn_ref[...]
        gain_copy(0).start()
        for which in range(2):
            early_out_ref[which] = early[which].last(1)
        gain_step(0)
        for part in late:
            part.settle(1)
            part.start(2)
        gain_step(1)
        gain_step(2)
        for part in late:
            part.settle(2)
            part.start(3)
        gain_step(3)
        gain_step(4)
        for which in range(2):
            late_out_ref[which] = late[which].last(3)
        for block in range(4):
            stays = core == block % 2
            pl.when(stays)(row_keep(block).wait)
            pl.when(jnp.logical_not(stays))(row_copy(block).wait_send)
        for stream in range(2):
            row_copy(2 * stream).wait_recv()


def rows_back(
    dq, dk, dv, raw, attn_grad, gain, gain_ffn, wq, wk, wv, early, late
):
    keys, width = dk.shape
    rows = dq.shape[0]
    size = keys // 8
    key_block = pl.BlockSpec((size, width), lambda i: (i, 0))
    row_block = pl.BlockSpec((size, width), lambda i: (jnp.maximum(i - 4, 0), 0))
    anywhere = pl.BlockSpec(memory_space=pl.ANY)
    rows_shape = jax.ShapeDtypeStruct((2, size, width), BF16)
    block = early.shape[-2:]
    lands = []
    for order in ORDERS:
        lands += landings(BITS[:2], order[2:], block)
        lands += landings(BITS, order, block)
    out = (2,) + block
    vector = (8, width)
    return pl.pallas_call(
        rows_back_kernel,
        grid=(8,),
        out_shape=(
            rows_shape, rows_shape,
            jax.ShapeDtypeStruct(vector, F32),
            jax.ShapeDtypeStruct(out, F32),
            jax.ShapeDtypeStruct(out, F32),
        ),
        in_specs=[
            row_block, key_block, key_block, key_block, row_block,
            held(gain.shape), held(gain_ffn.shape), held(wq.shape), held(wk.shape), held(wv.shape),
            held(early.shape), held(late.shape),
        ],
        out_specs=(
            anywhere, anywhere, held(vector), held(out), held(out),
        ),
        scratch_shapes=[
            pltpu.VMEM((4, size, width), BF16),
            pltpu.VMEM((5,) + vector, F32),
            pltpu.VMEM((5,) + vector, F32),
        ] + lands + [
            pltpu.SemaphoreType.DMA((2, 2)),
            pltpu.SemaphoreType.DMA((2,)),
            pltpu.SemaphoreType.DMA((2, 5)),
            pltpu.SemaphoreType.DMA((4, 2, 4)),
        ],
        compiler_params=pltpu.CompilerParams(
            vmem_limit_bytes=VMEM_LIMIT, dimension_semantics=("arbitrary",),
            collective_id=3, has_side_effects=True,
        ),
        cost_estimate=cost(20e9, 24e6),
        name="rows_back",
    )(
        dq, dk, dv, raw, attn_grad, gain, gain_ffn, wq, wk, wv,
        early, late,
    )


def swap_dp(block, bit):
    count = lax.axis_size("dp")
    return lax.ppermute(block, "dp", [(i, i ^ (1 << bit)) for i in range(count)])


def swap_core(block):
    return lax.ppermute(block, "seq", [(0, 1), (1, 0)])


def on_device_pair(
    inputs, memory, compressed, offsets, resets, w_query, w_key, w_value, w_output, w_hidden,
    w_return, w_compress, gain_attn, gain_ffn, out_grad, comp_grad,
):
    core = lax.axis_index("seq")
    dp_count = lax.axis_size("dp")
    streams, half, width = inputs.shape
    seg = 2 * half
    low_core = core == 0

    unused = (resets != 0) | (offsets >= 2 * seg)
    pick_a = lax.dynamic_index_in_dim(unused, core, 0, False).astype(jnp.int32)
    stream_a = core + 2 * pick_a
    reset_a = lax.dynamic_index_in_dim(resets, stream_a, 0, False)
    offset_a = lax.dynamic_index_in_dim(offsets, stream_a, 0, False)
    first_slot = jnp.where(reset_a != 0, 2 * seg, offset_a).reshape(1)
    gain_a = gain_attn.astype(F32).reshape(1, width)
    gain_f = gain_ffn.astype(F32).reshape(1, width)

    x_in, x_mem, x_old, x_og, new_rows, kept_p, sent_p, kept_q, sent_q = front(
        resets, inputs, memory, compressed, out_grad, w_compress, comp_grad
    )
    got_p, got_q = swap_dp(sent_p, 0), swap_dp(sent_q, 1)
    wh_late, wr_late, x_in = lax.optimization_barrier((w_hidden, w_return, x_in))
    wh_other, wr_other = swap_core(wh_late), swap_core(wr_late)
    all_rows, normed, q, k, v, og = project_rows(
        jnp.stack([pick_a, 1 - pick_a]), x_old, x_mem, x_in, x_og, gain_a, w_query, w_key, w_value
    )
    mixed, hidden, ffn_in, lse, grad_compress = attn_fwd(
        first_slot, q, k, v, all_rows, w_output, gain_f, kept_p, got_p, kept_q, got_q
    )
    outputs, attn_grad, mixed_grad, gain_ffn_grad, ffn_done, ffn_part, ffn_raw = ffn(
        ffn_in, og, hidden, gain_f, w_output, wh_other, w_hidden, wr_other, w_return
    )
    dq, dk, dv, early, late, ffn_rest = attn_back(
        first_slot, q, k, v, mixed_grad, mixed, lse, normed, attn_grad, ffn_part, ffn_raw
    )
    mine_rows, their_rows, gains, early_out, late_out = rows_back(
        dq, dk, dv, all_rows, attn_grad, gain_a, gain_ffn_grad, w_query, w_key, w_value, early, late
    )

    def tiles(which):
        parts = [ffn_done[which, i] for i in range(2)] + [ffn_rest[which, i] for i in range(2)]
        return jnp.concatenate(parts, axis=1)

    grad_hidden, grad_return = tiles(0), tiles(1).T
    pair = 2 * HEAD_DIM

    def weight_grad(which, side):
        cols = slice(side * pair, (side + 1) * pair)
        return jnp.concatenate([early_out[which, :, cols], late_out[which, :, cols]], axis=1)

    grad_query, grad_key = weight_grad(0, 0), weight_grad(0, 1)
    grad_value, grad_output = weight_grad(1, 0), weight_grad(1, 1)
    rank = lax.axis_index("dp")
    gains = lax.dynamic_slice_in_dim(gains[:2], rank * (width // dp_count), width // dp_count, 1)

    def to_streams(a, b, which):
        swapped = lax.dynamic_index_in_dim(unused, which, 0, False)
        return jnp.where(swapped, b, a), jnp.where(swapped, a, b)

    def spread(own_pair, other_pair):
        own = to_streams(own_pair[0], own_pair[1], core)
        other = to_streams(other_pair[0], other_pair[1], 1 - core)
        return jnp.stack(
            [
                jnp.where(low_core, own[0], other[0]),
                jnp.where(low_core, other[0], own[0]),
                jnp.where(low_core, own[1], other[1]),
                jnp.where(low_core, other[1], own[1]),
            ]
        )

    def place_rows(rows):
        halves = rows.reshape(2, 2, half, width)
        return spread(
            lax.dynamic_index_in_dim(halves, core, 1, False),
            swap_core(lax.dynamic_index_in_dim(halves, 1 - core, 1, False)),
        )

    return (
        place_rows(outputs),
        new_rows[:, : comp_grad.shape[1]],
        spread(mine_rows, their_rows),
        grad_query,
        grad_key,
        grad_value,
        grad_output,
        grad_hidden,
        grad_return,
        grad_compress,
        gains[0],
        gains[1],
    )


def solution(mesh):
    placed = (
        P("dp", "seq", None),
        P("dp", "seq", None),
        P("dp", "seq", None),
        P("dp"),
        P("dp"),
        P(),
        P(),
        P(),
        P(),
        P(None, "seq"),
        P("seq", None),
        P(),
        P(),
        P(),
        P("dp", "seq", None),
        P("dp", None, None),
    )
    fast = mesh.shape["seq"] == 2 and mesh.shape["dp"] == 16
    return jax.shard_map(
        on_device_pair if fast else on_device,
        mesh=mesh,
        in_specs=placed,
        out_specs=(
            P("dp", "seq", None),
            P("dp", None, None),
            P("dp", "seq", None),
            P("dp", "seq"),
            P("dp", "seq"),
            P("dp", "seq"),
            P("dp", "seq"),
            P("dp", "seq"),
            P("seq", "dp"),
            P("dp", "seq"),
            P("dp"),
            P("dp"),
        ),
        check_vma=False,
    )
```

```python
import functools
import math

import jax
import jax.numpy as jnp
from jax import lax
from jax.experimental import pallas as pl
from jax.experimental.pallas import tpu as pltpu
from jax.sharding import PartitionSpec as P

HEADS = 8
HEAD_DIM = 128
RATE = 3


epsilon = 1e-05
masked_score = -1e30


def shifted(block, axis, distance):
    devices = range(lax.axis_size(axis))
    route = [(i - distance, i) for i in devices if i - distance in devices]
    return lax.ppermute(block, axis, route)


def layer_norm(values, gain):
    centred = values - jnp.mean(values, axis=-1, keepdims=True)
    spread = jnp.mean(centred * centred, axis=-1, keepdims=True)
    return centred * lax.rsqrt(spread + epsilon) * gain


def project(left, right):
    return jnp.einsum("srd,de->sre", left, right, preferred_element_type=jnp.float32)


def project_back(left, right):
    return jnp.einsum("sre,de->srd", left, right, preferred_element_type=jnp.float32)


def weight_term(left, right):
    return jnp.einsum("srd,sre->de", left, right, preferred_element_type=jnp.float32)


def key_layout(key_index, local_rows, seg_len):
    key_owner = key_index // (3 * local_rows)
    inside = key_index % (3 * local_rows)
    key_kind = inside // local_rows
    key_place = key_owner * local_rows + inside % local_rows
    mem_slot = jnp.where(key_kind == 0, key_place, seg_len + key_place)
    return (key_kind, mem_slot, key_place)


def allowed_mask(key_kind, mem_slot, key_place, query_place, offsets, keep_flag):
    memory_ok = (mem_slot[None, :] >= offsets[:, None]) & keep_flag[:, None]
    causal = key_place[None, :] <= query_place[:, None]
    return jnp.where(key_kind[None, None, :] < 2, memory_ok[:, None, :], causal[None, :, :])


def score_block(query_heads, key_heads, allowed, score_scale):
    scores = (
        jnp.einsum("sthe,skhe->shtk", query_heads, key_heads, preferred_element_type=jnp.float32)
        * score_scale
    )
    return jnp.where(allowed[:, None], scores, masked_score)


def tile_matrix(matrix, dp_count, seq_count):
    rows_total, cols_total = matrix.shape
    blocks = matrix.reshape(dp_count, rows_total // dp_count, seq_count, cols_total // seq_count)
    return blocks.transpose(0, 2, 1, 3).reshape(
        dp_count * seq_count, rows_total // dp_count, cols_total // seq_count
    )


def tile_vector(vector, dp_count, seq_count):
    piece_len = vector.shape[0] // dp_count
    pieces = vector.reshape(dp_count, 1, piece_len)
    return jnp.broadcast_to(pieces, (dp_count, seq_count, piece_len)).reshape(
        dp_count * seq_count, piece_len
    )


def on_device(
    inputs,
    memory,
    compressed,
    offsets,
    resets,
    w_query,
    w_key,
    w_value,
    w_output,
    w_hidden,
    w_return,
    w_compress,
    gain_attn,
    gain_ffn,
    out_grad,
    comp_grad,
):
    seq_count = lax.axis_size("seq")
    dp_count = lax.axis_size("dp")
    seq_rank = lax.axis_index("seq")
    streams, local_rows, feat_width = inputs.shape
    seg_len = local_rows * seq_count
    score_scale = HEAD_DIM ** (-0.5)
    keep_flag = resets == 0
    all_rows = jnp.concatenate([compressed, memory, inputs], axis=1).astype(jnp.float32)
    normed, attn_norm_back = jax.vjp(layer_norm, all_rows, gain_attn.astype(jnp.float32))
    normed_low = normed.astype(jnp.bfloat16)
    query_in = normed_low[:, 2 * local_rows :]
    query_low = project(query_in, w_query).astype(jnp.bfloat16)
    key_low = project(normed_low, w_key).astype(jnp.bfloat16)
    value_low = project(normed_low, w_value).astype(jnp.bfloat16)
    key_all, value_all = (
        lax.all_gather(key_low, "seq", axis=1, tiled=True),
        lax.all_gather(value_low, "seq", axis=1, tiled=True),
    )
    total_keys = key_all.shape[1]
    key_kind, mem_slot, key_place = key_layout(
        jnp.arange(total_keys, dtype=jnp.int32), local_rows, seg_len
    )
    query_place = seq_rank * local_rows + jnp.arange(local_rows, dtype=jnp.int32)
    allowed = allowed_mask(key_kind, mem_slot, key_place, query_place, offsets, keep_flag)
    query_heads = query_low.reshape(streams, local_rows, HEADS, HEAD_DIM)
    key_heads = key_all.reshape(streams, total_keys, HEADS, HEAD_DIM)
    value_heads = value_all.reshape(streams, total_keys, HEADS, HEAD_DIM)
    scores = score_block(query_heads, key_heads, allowed, score_scale)
    row_top = jnp.max(scores, axis=-1, keepdims=True)
    exp_scores = jnp.exp(scores - row_top)
    row_total = jnp.sum(exp_scores, axis=-1, keepdims=True)
    attn_prob = exp_scores / row_total
    log_total = row_top + jnp.log(row_total)
    mixed_low = (
        jnp.einsum(
            "shtk,skhe->sthe",
            attn_prob.astype(jnp.bfloat16),
            value_heads,
            preferred_element_type=jnp.float32,
        )
        .reshape(streams, local_rows, feat_width)
        .astype(jnp.bfloat16)
    )
    hidden = inputs.astype(jnp.float32) + project(mixed_low, w_output)
    ffn_in, ffn_norm_back = jax.vjp(layer_norm, hidden, gain_ffn.astype(jnp.float32))
    ffn_low = ffn_in.astype(jnp.bfloat16)
    ffn_all = lax.all_gather(ffn_low, "seq", axis=1, tiled=True)
    pre_act = jnp.einsum("std,df->stf", ffn_all, w_hidden, preferred_element_type=jnp.float32)
    act_float, gelu_back = jax.vjp(jax.nn.gelu, pre_act)
    act_low = act_float.astype(jnp.bfloat16)
    partial_out = jnp.einsum("stf,fd->std", act_low, w_return, preferred_element_type=jnp.float32)
    ffn_out = lax.psum_scatter(
        partial_out.astype(jnp.bfloat16), "seq", scatter_dimension=1, tiled=True
    ).astype(jnp.float32)
    cot_all = lax.all_gather(out_grad, "seq", axis=1, tiled=True)
    act_grad = jnp.einsum("std,fd->stf", cot_all, w_return, preferred_element_type=jnp.float32)
    return_part = jnp.einsum("stf,std->fd", act_low, cot_all, preferred_element_type=jnp.float32)
    pre_grad = gelu_back(act_grad)[0].astype(jnp.bfloat16)
    hidden_part = jnp.einsum("std,stf->df", ffn_all, pre_grad, preferred_element_type=jnp.float32)
    in_part = jnp.einsum("stf,df->std", pre_grad, w_hidden, preferred_element_type=jnp.float32)
    ffn_in_grad = lax.psum_scatter(in_part, "seq", scatter_dimension=1, tiled=True)
    hidden_sum, return_sum = (
        lax.psum_scatter(
            hidden_part.astype(jnp.bfloat16), "dp", scatter_dimension=0, tiled=True
        ).astype(jnp.float32),
        lax.psum_scatter(
            return_part.T.astype(jnp.bfloat16), "dp", scatter_dimension=0, tiled=True
        ).astype(jnp.float32),
    )
    grad_return = return_sum.T
    outputs = (hidden + ffn_out).astype(jnp.bfloat16)
    hidden_grad, gain_ffn_grad = ffn_norm_back(ffn_in_grad)
    hidden_grad = hidden_grad + out_grad.astype(jnp.float32)
    attn_grad_low = hidden_grad.astype(jnp.bfloat16)
    output_part = weight_term(mixed_low, attn_grad_low)
    mixed_grad = project_back(attn_grad_low, w_output).astype(jnp.bfloat16)
    mixed_heads = mixed_grad.reshape(streams, local_rows, HEADS, HEAD_DIM)
    prob_again = jnp.exp(score_block(query_heads, key_heads, allowed, score_scale) - log_total)
    prob_grad = jnp.einsum(
        "sthe,skhe->shtk", mixed_heads, value_heads, preferred_element_type=jnp.float32
    )
    prob_delta = jnp.sum(prob_again * prob_grad, axis=-1)
    score_grad = (prob_again * (prob_grad - prob_delta[..., None])).astype(jnp.bfloat16)
    query_grad = (
        (
            jnp.einsum("shtk,skhe->sthe", score_grad, key_heads, preferred_element_type=jnp.float32)
            * score_scale
        )
        .reshape(streams, local_rows, feat_width)
        .astype(jnp.bfloat16)
    )
    key_part = (
        jnp.einsum("shtk,sthe->skhe", score_grad, query_heads, preferred_element_type=jnp.float32)
        * score_scale
    ).reshape(streams, total_keys, feat_width)
    value_part = jnp.einsum(
        "shtk,sthe->skhe",
        prob_again.astype(jnp.bfloat16),
        mixed_heads,
        preferred_element_type=jnp.float32,
    ).reshape(streams, total_keys, feat_width)
    key_sum, value_sum = (
        lax.psum_scatter(
            key_part.astype(jnp.bfloat16), "seq", scatter_dimension=1, tiled=True
        ).astype(jnp.float32),
        lax.psum_scatter(
            value_part.astype(jnp.bfloat16), "seq", scatter_dimension=1, tiled=True
        ).astype(jnp.float32),
    )
    key_grad = key_sum.astype(jnp.bfloat16)
    value_grad = value_sum.astype(jnp.bfloat16)
    query_part = weight_term(query_in, query_grad)
    key_wpart = weight_term(normed_low, key_grad)
    value_wpart = weight_term(normed_low, value_grad)
    query_back = project_back(query_grad, w_query)
    normed_grad = project_back(key_grad, w_key) + project_back(value_grad, w_value)
    normed_grad = normed_grad + jnp.concatenate(
        [jnp.zeros((streams, 2 * local_rows, feat_width), jnp.float32), query_back], axis=1
    )
    rows_grad, gain_attn_grad = attn_norm_back(normed_grad)
    input_grad = (rows_grad[:, 2 * local_rows :] + hidden_grad).astype(jnp.bfloat16)
    kept_memory = memory * keep_flag[:, None, None].astype(jnp.bfloat16)
    edge_rows = shifted(kept_memory[:, : 2 * (RATE - 1)], "seq", -1)
    extended = jnp.concatenate([kept_memory, edge_rows], axis=1)
    group_count = (local_rows + RATE - 1) // RATE
    first_group = (seq_rank * local_rows + RATE - 1) // RATE
    slice_start = RATE * first_group - seq_rank * local_rows
    grouped = lax.dynamic_slice_in_dim(extended, slice_start, RATE * group_count, 1).reshape(
        streams, group_count, RATE * feat_width
    )
    piece_rows = jnp.einsum(
        "sgc,cd->sgd", grouped, w_compress, preferred_element_type=jnp.float32
    ).astype(jnp.bfloat16)
    comp_all = lax.all_gather(piece_rows, "seq", axis=1, tiled=True)
    comp_count = comp_grad.shape[1]
    out_index = jnp.arange(comp_count, dtype=jnp.int32)
    holder = RATE * out_index // local_rows
    lookup = holder * group_count + out_index - (holder * local_rows + RATE - 1) // RATE
    new_compressed = jnp.take(comp_all, lookup, axis=1)
    slot_index = first_group + jnp.arange(group_count, dtype=jnp.int32)
    slot_valid = (RATE * slot_index < (seq_rank + 1) * local_rows) & (slot_index < comp_count)
    picked = jnp.take(comp_grad, jnp.minimum(slot_index, comp_count - 1), axis=1) * slot_valid[
        None, :, None
    ].astype(jnp.bfloat16)
    compress_part = jnp.einsum("sgc,sgd->cd", grouped, picked, preferred_element_type=jnp.float32)
    reduced = (
        lax.psum_scatter(
            tile_matrix(query_part, dp_count, seq_count),
            ("dp", "seq"),
            scatter_dimension=0,
            tiled=True,
        ),
        lax.psum_scatter(
            tile_matrix(key_wpart, dp_count, seq_count),
            ("dp", "seq"),
            scatter_dimension=0,
            tiled=True,
        ),
        lax.psum_scatter(
            tile_matrix(value_wpart, dp_count, seq_count),
            ("dp", "seq"),
            scatter_dimension=0,
            tiled=True,
        ),
        lax.psum_scatter(
            tile_matrix(output_part, dp_count, seq_count),
            ("dp", "seq"),
            scatter_dimension=0,
            tiled=True,
        ),
        lax.psum_scatter(
            tile_matrix(compress_part, dp_count, seq_count),
            ("dp", "seq"),
            scatter_dimension=0,
            tiled=True,
        ),
        lax.psum_scatter(
            tile_vector(gain_attn_grad, dp_count, seq_count),
            ("dp", "seq"),
            scatter_dimension=0,
            tiled=True,
        ),
        lax.psum_scatter(
            tile_vector(gain_ffn_grad, dp_count, seq_count),
            ("dp", "seq"),
            scatter_dimension=0,
            tiled=True,
        ),
    )
    return (
        outputs,
        new_compressed,
        input_grad,
        reduced[0][0],
        reduced[1][0],
        reduced[2][0],
        reduced[3][0],
        hidden_sum,
        grad_return,
        reduced[4][0],
        reduced[5][0],
        reduced[6][0],
    )


F32 = jnp.float32
BF16 = jnp.bfloat16
NN = (((1,), (0,)), ((), ()))
NT = (((1,), (1,)), ((), ()))
TN = (((0,), (0,)), ((), ()))
VMEM_LIMIT = 60 * 1024 * 1024
SCALE = HEAD_DIM ** (-0.5)
EXP2_SCALE = SCALE * math.log2(math.e)


def dot(left, right, dims=NN):
    return lax.dot_general(left, right, dims, preferred_element_type=F32)


def params(steps=1):
    return pltpu.CompilerParams(
        vmem_limit_bytes=VMEM_LIMIT, dimension_semantics=("arbitrary",) * steps
    )


def cost(flops, bytes_accessed=0, transcendentals=0):
    return pl.CostEstimate(
        flops=int(flops), bytes_accessed=int(bytes_accessed), transcendentals=int(transcendentals)
    )


def held(shape):
    zeros = (0,) * len(shape)
    return pl.BlockSpec(shape, lambda *_: zeros, pipeline_mode=pl.Buffered(1))


def norm_parts(rows):
    centred = rows - jnp.mean(rows, axis=-1, keepdims=True)
    inverse = lax.rsqrt(jnp.mean(centred * centred, axis=-1, keepdims=True) + epsilon)
    return centred * inverse, inverse


def norm_back(grad, unit, inverse):
    return inverse * (
        grad
        - jnp.mean(grad, axis=-1, keepdims=True)
        - unit * jnp.mean(grad * unit, axis=-1, keepdims=True)
    )


def add_low(left, right):
    return (left.astype(F32) + right.astype(F32)).astype(BF16)


def mesh_place():
    rank, core = lax.axis_index("dp"), lax.axis_index("seq")

    def bit(b):
        return lax.rem(lax.div(rank, 1 << b), 2)

    def across(b):
        return rank + (1 << b) * (1 - 2 * bit(b))

    return core, bit, across


def first_slots(resets_ref, offsets_ref, core, total):
    return [
        jnp.where(resets_ref[core + 2 * j] != 0, total, offsets_ref[core + 2 * j]) for j in range(2)
    ]


def stream_a_slot(resets_ref, offsets_ref, core, total):
    first, second = first_slots(resets_ref, offsets_ref, core, total)
    return jnp.where(first >= total, second, first)


def greet(devices):
    barrier = pltpu.get_barrier_semaphore()
    for device in devices:
        pl.semaphore_signal(
            barrier, inc=1, device_id=device, device_id_type=pl.DeviceIdType.MESH
        )
    pl.semaphore_wait(barrier, len(devices))


def remote(src, dst, sems, device):
    return pltpu.make_async_remote_copy(
        src_ref=src,
        dst_ref=dst,
        send_sem=sems[0],
        recv_sem=sems[1],
        device_id=device,
        device_id_type=pl.DeviceIdType.MESH,
    )


class Chunk:
    def __init__(self, data, left, order, landing, sems, place):
        self.data, self.left, self.order = data, left, order
        self.landing, self.sems = landing, sems
        _, self.bit, self.across = place

    def at(self, swap, away):
        index = []
        for b in self.left:
            if b in self.order[:swap]:
                index.append(self.bit(b))
            elif swap < len(self.order) and b == self.order[swap]:
                index.append(1 - self.bit(b) if away else self.bit(b))
            else:
                index.append(slice(None))
        return tuple(index)

    def rest(self, swap):
        done = self.order[:swap]
        return tuple(self.bit(b) if b in done else slice(None) for b in self.left)

    def copy(self, swap):
        return remote(
            self.data.at[self.at(swap, True)],
            self.landing[swap],
            (self.sems.at[0, swap], self.sems.at[1, swap]),
            {"dp": self.across(self.order[swap])},
        )

    def start(self, swap):
        self.copy(swap).start()

    def settle(self, swap):
        self.copy(swap).wait()
        here = self.at(swap, False)
        self.data[here] = add_low(self.data[here], self.landing[swap][...])

    def last(self, swap):
        self.copy(swap).wait()
        return self.data[self.at(swap, False)].astype(F32) + self.landing[swap][...].astype(F32)


def landings(left, order, block):
    shapes, count = [], len(left)
    for _ in order:
        count -= 1
        shapes.append(pltpu.VMEM((2,) * count + block, BF16))
    return shapes


BITS = (3, 2, 1, 0)
ORDERS = ((0, 1, 2, 3), (1, 0, 2, 3))


def front_kernel(
    resets_ref, in_ref, mem_ref, old_ref, og_ref, wc_ref, cg_ref,
    x_in_ref, x_mem_ref, x_old_ref, x_og_ref, new_ref, kept_p_ref, sent_p_ref, kept_q_ref, sent_q_ref,
    mem, x_in, x_old, x_og, wc, new, core_out, core_in, row_sems, wc_sem, new_sems, core_sems, out_sems,
):
    core, bit, _ = mesh_place()
    partner = {"seq": 1 - core}
    width = in_ref.shape[2]
    groups = cg_ref.shape[1]

    weights = pltpu.make_async_copy(wc_ref, wc, wc_sem)
    weights.start()
    greet((partner,))
    moves = []
    for n, (src, dst) in enumerate(
        ((mem_ref, mem), (in_ref, x_in), (old_ref, x_old), (og_ref, x_og))
    ):
        for j in range(2):
            away = remote(
                src.at[1 - core + 2 * j], dst.at[j, core], (row_sems.at[0, n, j], row_sems.at[1, n, j]), partner
            )
            here = pltpu.make_async_copy(src.at[core + 2 * j], dst.at[j, core], row_sems.at[2, n, j])
            away.start()
            here.start()
            moves.append((away, here))
    new[...] = jnp.zeros_like(new)
    outs = []
    for j in range(2):
        moves[j][0].wait_recv()
        moves[j][1].wait()
    outs.append(pltpu.make_async_copy(mem, x_mem_ref, out_sems.at[0]))
    outs[-1].start()
    weights.wait()

    grouped = []
    for j in range(2):
        rows = mem[j].reshape(2 * mem.shape[2], width)
        group = lax.broadcasted_iota(jnp.int32, (groups, rows.shape[0]), 0)
        row = lax.broadcasted_iota(jnp.int32, (groups, rows.shape[0]), 1)
        keep = jnp.where(resets_ref[core + 2 * j] == 0, 1.0, 0.0)
        total = jnp.zeros((groups, width), F32)
        mine = []
        for r in range(RATE):
            pick = jnp.where(row == RATE * group + r, keep, 0.0).astype(BF16)
            mine.append(dot(pick, rows).astype(BF16))
            total = total + dot(mine[-1], wc[r * width : (r + 1) * width])
        grouped.append(mine)
        new[j, :groups] = total.astype(BF16)

    news = []
    for j in range(2):
        at = core + 2 * j
        news.append(remote(new.at[j], new_ref.at[at], (new_sems.at[0, j], new_sems.at[1, j]), partner))
        outs.append(pltpu.make_async_copy(new.at[j], new_ref.at[at], new_sems.at[2, j]))
        news[-1].start()
        outs[-1].start()

    half = width // 2

    def grad(r, side):
        cols = pl.ds(pl.multiple_of(side * half, half), half)
        return sum(dot(grouped[j][r], cg_ref[core + 2 * j, :, cols], TN) for j in range(2))

    crossing = []
    for r in range(RATE):
        core_out[r] = grad(r, 1 - core).astype(BF16)
        crossing.append(
            remote(core_out.at[r], core_in.at[r], (core_sems.at[0, r], core_sems.at[1, r]), partner)
        )
        crossing[-1].start()
    for n, (src, dst) in enumerate(((x_in, x_in_ref), (x_old, x_old_ref), (x_og, x_og_ref))):
        for away, here in moves[2 * n + 2 : 2 * n + 4]:
            away.wait_recv()
            here.wait()
        outs.append(pltpu.make_async_copy(src, dst, out_sems.at[1 + n]))
        outs[-1].start()
    fine = width // 16
    quarter = half // 2
    for r in range(RATE):
        total = grad(r, core)
        crossing[r].wait()
        total = (total + core_in[r].astype(F32)).astype(BF16)
        for which, (kept_ref, sent_ref) in enumerate(
            ((kept_p_ref, sent_p_ref), (kept_q_ref, sent_q_ref))
        ):
            for mine in range(2):

                @pl.when(bit(which) == mine)
                def _():
                    for t in range(16):
                        block, third = divmod(r * 16 + t, RATE)
                        place = (block >> 3, block >> 2 & 1, block >> (1 - which) & 1)
                        ref = kept_ref if block >> which & 1 == mine else sent_ref
                        ref[place + (slice(third * fine, (third + 1) * fine),)] = total[
                            t * fine : (t + 1) * fine, which * quarter : (which + 1) * quarter
                        ]
    for away, _ in moves:
        away.wait_send()
    for move in outs + news:
        move.wait()


def front(resets, inputs, memory, compressed, out_grad, w_compress, comp_grad):
    streams, half, width = inputs.shape
    anywhere = pl.BlockSpec(memory_space=pl.ANY)
    vmem = pl.BlockSpec(memory_space=pltpu.VMEM)
    pair = jax.ShapeDtypeStruct((2, 2, half, width), BF16)
    padded = -(-comp_grad.shape[1] // 16) * 16
    part = jax.ShapeDtypeStruct((2, 2, 2, RATE * width // 16, width // 4), BF16)
    return pl.pallas_call(
        front_kernel,
        out_shape=(
            pair, pair, pair, pair, jax.ShapeDtypeStruct((streams, padded, width), BF16),
            part, part, part, part,
        ),
        in_specs=[pl.BlockSpec(memory_space=pltpu.SMEM)] + [anywhere] * 5 + [vmem],
        out_specs=(anywhere,) * 5 + (vmem,) * 4,
        scratch_shapes=[
            pltpu.VMEM((2, 2, half, width), BF16),
            pltpu.VMEM((2, 2, half, width), BF16),
            pltpu.VMEM((2, 2, half, width), BF16),
            pltpu.VMEM((2, 2, half, width), BF16),
            pltpu.VMEM(w_compress.shape, BF16),
            pltpu.VMEM((2, padded, width), BF16),
            pltpu.VMEM((RATE, width, width // 2), BF16),
            pltpu.VMEM((RATE, width, width // 2), BF16),
            pltpu.SemaphoreType.DMA((3, 4, 2)),
            pltpu.SemaphoreType.DMA,
            pltpu.SemaphoreType.DMA((3, 2)),
            pltpu.SemaphoreType.DMA((2, RATE)),
            pltpu.SemaphoreType.DMA((4,)),
        ],
        compiler_params=pltpu.CompilerParams(
            vmem_limit_bytes=VMEM_LIMIT, collective_id=4, has_side_effects=True
        ),
        cost_estimate=cost(12e9, 24e6),
        name="front",
    )(resets, inputs, memory, compressed, out_grad, w_compress, comp_grad)


def project_kernel(
    resets_ref, offsets_ref, old_ref, mem_ref, in_ref, og_ref, gain_ref, wq_ref, wk_ref, wv_ref,
    raw_ref, normed_ref, q_ref, k_ref, v_ref, og_out_ref,
):
    step = pl.program_id(0)
    raw = jnp.where(step < 2, old_ref[...], jnp.where(step < 4, mem_ref[...], in_ref[...]))
    raw_ref[...] = raw
    unit, _ = norm_parts(raw.astype(F32))
    normed = (unit * gain_ref[...]).astype(BF16)
    normed_ref[...] = normed
    k_ref[...] = dot(normed, wk_ref[...]).astype(BF16)
    v_ref[...] = dot(normed, wv_ref[...]).astype(BF16)

    @pl.when(step >= 4)
    def _():
        q_ref[...] = dot(normed, wq_ref[...]).astype(BF16)
        og_out_ref[...] = og_ref[...]


def project_rows(resets, offsets, old, mem, inputs, og, gain, wq, wk, wv):
    _, _, half, width = inputs.shape

    def from_pair(first):
        def index(i, resets_ref, offsets_ref):
            at = jnp.clip(i - first, 0, 3 if first == 4 else 1)
            slots = first_slots(resets_ref, offsets_ref, lax.axis_index("seq"), 4 * half)
            stream_a = jnp.where(slots[0] >= 4 * half, 1, 0)
            return jnp.where(at < 2, stream_a, 1 - stream_a), lax.rem(at, 2), 0, 0

        return pl.BlockSpec((None, None, half, width), index)

    keys = pl.BlockSpec((half, width), lambda i, *_: (i, 0))
    rows = pl.BlockSpec((half, width), lambda i, *_: (jnp.maximum(i - 4, 0), 0))
    key_shape = jax.ShapeDtypeStruct((8 * half, width), BF16)
    row_shape = jax.ShapeDtypeStruct((4 * half, width), BF16)
    return pl.pallas_call(
        project_kernel,
        out_shape=(key_shape, key_shape, row_shape, key_shape, key_shape, row_shape),
        grid_spec=pltpu.PrefetchScalarGridSpec(
            num_scalar_prefetch=2,
            grid=(8,),
            in_specs=[
                from_pair(0), from_pair(2), from_pair(4), from_pair(4),
                held(gain.shape), held(wq.shape), held(wk.shape), held(wv.shape),
            ],
            out_specs=(keys, keys, rows, keys, keys, rows),
        ),
        compiler_params=params(),
        cost_estimate=cost(14e9, 30e6),
        name="project",
    )(resets, offsets, old, mem, inputs, og, gain, wq, wk, wv)


def attn_fwd_kernel(
    resets_ref, offsets_ref, q_ref, k_ref, v_ref, in_ref, wo_ref, gain_ref, kept_p_ref, got_p_ref, kept_q_ref, got_q_ref,
    mixed_ref, hidden_ref, ffn_ref, lse_ref, compress_ref,
    packed, *scratch,
):
    step = pl.program_id(0)
    lands, chip_sems = scratch[:-1], scratch[-1]
    place = mesh_place()
    half = q_ref.shape[0]
    seg = 2 * half
    first_slot = stream_a_slot(resets_ref, offsets_ref, place[0], 2 * seg)
    chunks = [
        Chunk(
            packed.at[which],
            tuple(b for b in BITS if b != ORDERS[which][0]),
            ORDERS[which][1:2],
            lands[which : which + 1],
            chip_sems.at[which],
            place,
        )
        for which in range(2)
    ]

    @pl.when(step == 0)
    def _():
        greet(tuple({"dp": place[2](b)} for b in range(2)))
        packed[0] = add_low(kept_p_ref[...], got_p_ref[...])
        packed[1] = add_low(kept_q_ref[...], got_q_ref[...])
        for part in chunks:
            part.start(0)

    def run(pieces):
        def one_head(h, stats):
            cols = pl.ds(pl.multiple_of(h * HEAD_DIM, HEAD_DIM), HEAD_DIM)
            q = q_ref[:, cols]
            scores = []
            for start, size, kind in pieces:
                s = dot(q, k_ref[start : start + size, cols], NT)
                if kind == "mem":
                    slot = lax.broadcasted_iota(jnp.int32, s.shape, 1)
                    s = jnp.where(slot >= first_slot, s, masked_score)
                if kind == "diag":
                    key = lax.broadcasted_iota(jnp.int32, s.shape, 1)
                    row = lax.broadcasted_iota(jnp.int32, s.shape, 0)
                    s = jnp.where(key <= row, s, masked_score)
                scores.append(s)
            top = functools.reduce(
                jnp.maximum, [jnp.max(s, axis=-1, keepdims=True) for s in scores]
            ) * EXP2_SCALE
            mix = jnp.zeros((half, 2 * HEAD_DIM), F32)
            for s, (start, size, _) in zip(scores, pieces):
                p = jnp.exp2(s * EXP2_SCALE - top).astype(BF16)
                ones = jnp.ones((size, HEAD_DIM), BF16)
                mix = mix + dot(p, jnp.concatenate([v_ref[start : start + size, cols], ones], axis=1))
            total = mix[:, HEAD_DIM:]
            mixed_ref[:, cols] = (mix[:, :HEAD_DIM] / total).astype(BF16)
            lane = lax.broadcasted_iota(jnp.int32, stats.shape, 1)
            return jnp.where(lane == h, top + jnp.log2(total), stats)

        stats = lax.fori_loop(0, HEADS, one_head, jnp.zeros((half, 128), F32), unroll=True)
        lse_ref[...] = stats.T[:HEADS]

    cases = (
        ((0, 2 * seg, "mem"), (2 * seg, half, "diag")),
        ((0, 2 * seg, "mem"), (2 * seg, half, "full"), (2 * seg + half, half, "diag")),
        ((3 * seg, half, "diag"),),
        ((3 * seg, half, "full"), (3 * seg + half, half, "diag")),
    )
    for i, pieces in enumerate(cases[2:] + cases[:2]):
        pl.when(step == i)(functools.partial(run, pieces))
    hidden = in_ref[...].astype(F32) + dot(mixed_ref[...], wo_ref[...])
    hidden_ref[...] = hidden
    unit, _ = norm_parts(hidden)
    ffn_ref[...] = (unit * gain_ref[...]).astype(BF16)

    @pl.when(step == 3)
    def _():
        for which, part in enumerate(chunks):
            part.settle(0)
            compress_ref[which] = packed[(which,) + part.rest(1)]


def attn_fwd(resets, offsets, q, k, v, raw, wo, gain, kept_p, got_p, kept_q, got_q):
    rows, width = q.shape
    half = rows // 4
    by_block = pl.BlockSpec((half, width), lambda i: (lax.rem(i + 2, 4), 0))
    in_block = pl.BlockSpec((half, width), lambda i: (4 + lax.rem(i + 2, 4), 0))
    block = kept_p.shape[-2:]
    part = held(kept_p.shape)
    lands = []
    for which in range(2):
        lands += landings(BITS[1:], ORDERS[which][1:2], block)
    out = (2, 2, 2) + block
    return pl.pallas_call(
        attn_fwd_kernel,
        grid=(4,),
        out_shape=(
            jax.ShapeDtypeStruct((rows, width), BF16),
            jax.ShapeDtypeStruct((rows, width), F32),
            jax.ShapeDtypeStruct((rows, width), BF16),
            jax.ShapeDtypeStruct((HEADS, rows), F32),
            jax.ShapeDtypeStruct(out, BF16),
        ),
        in_specs=[
            pl.BlockSpec(memory_space=pltpu.SMEM),
            pl.BlockSpec(memory_space=pltpu.SMEM),
            by_block, held(k.shape), held(v.shape), in_block, held(wo.shape), held(gain.shape),
            part, part, part, part,
        ],
        out_specs=(
            by_block, by_block, by_block, pl.BlockSpec((HEADS, half), lambda i: (0, lax.rem(i + 2, 4))), held(out),
        ),
        scratch_shapes=[pltpu.VMEM((2,) + kept_p.shape, BF16)] + lands + [pltpu.SemaphoreType.DMA((2, 2, 1))],
        compiler_params=pltpu.CompilerParams(
            vmem_limit_bytes=VMEM_LIMIT, dimension_semantics=("arbitrary",),
            collective_id=5, has_side_effects=True,
        ),
        cost_estimate=cost(20e9, 20e6),
        name="attn_fwd",
    )(resets, offsets, q, k, v, raw, wo, gain, kept_p, got_p, kept_q, got_q)


GELU_C = math.sqrt(2.0 / math.pi)
GELU_A = 0.044715
CHUNK = 512


def gelu_pair(pre, act_grad):
    square = pre * pre
    t = jnp.tanh(pre * (GELU_C + (GELU_C * GELU_A) * square))
    cdf = 0.5 + 0.5 * t
    slope = cdf + (0.5 * pre) * (1.0 - t * t) * (GELU_C + (3.0 * GELU_C * GELU_A) * square)
    return (pre * cdf).astype(BF16), (act_grad * slope).astype(BF16)


def ffn_kernel(
    x_ref, og_ref, gain_ref, packed_ref, hidden_hbm, wo_hbm, wh0_ref, wh1_ref, wr0_ref, wr1_ref,
    out_ref, attn_grad_ref, do_ref, gain_grad_ref, done_ref, part_ref, raw_ref, compress_ref,
    hidden_ref, wo_ref, held_sems, pack0, pack1, pack_sems, wh, wr, out_acc, in_acc, act_ref, pre_ref, core_out, core_in, own_ref, land0, land1, land2, land3,
    weight_sems, core_sems, chip_sems,
):
    step = pl.program_id(0)
    last = pl.num_programs(0) - 1
    index = lax.div(step, 2)
    end = lax.div(last, 2)
    owned = lax.rem(step, 2) == 1
    rows, width = x_ref.shape
    units = wh.shape[2]
    chunks = rows // CHUNK
    place = mesh_place()
    core, _, across = place
    partner = {"seq": 1 - core}

    def fetch(at, side):
        cols = pl.ds(pl.multiple_of(at * units, units), units)
        wh_ref, wr_ref = ((wh0_ref, wr0_ref), (wh1_ref, wr1_ref))[side]
        return (
            pltpu.make_async_copy(wh_ref.at[:, cols], wh.at[side], weight_sems.at[0, side]),
            pltpu.make_async_copy(wr_ref.at[cols], wr.at[side], weight_sems.at[1, side]),
        )

    held_copies = (
        pltpu.make_async_copy(hidden_hbm, hidden_ref, held_sems.at[0]),
        pltpu.make_async_copy(wo_hbm, wo_ref, held_sems.at[1]),
    )
    packs = [
        Chunk(
            packed_ref.at[which], (3, 2), (2, 3), [pack0.at[which], pack1.at[which]],
            pack_sems.at[which], place,
        )
        for which in range(2)
    ]

    @pl.when(step == 0)
    def _():
        for copy in fetch(0, 0) + held_copies:
            copy.start()
        greet((partner,) + tuple({"dp": across(b)} for b in range(4)))
        for part in packs:
            part.start(0)
        out_acc[...] = jnp.zeros_like(out_acc)
        in_acc[...] = jnp.zeros_like(in_acc)

    @pl.when(step == 2)
    def _():
        for part in packs:
            part.settle(0)
            part.start(1)

    @pl.when(step == 4)
    def _():
        cols = compress_ref.shape[1] // 2
        for which, part in enumerate(packs):
            compress_ref[:, which * cols : (which + 1) * cols] = part.last(1)

    @pl.when(jnp.logical_not(owned))
    def _():
        for copy in fetch(index, 1):
            copy.start()
        for copy in fetch(index, 0):
            copy.wait()

    @pl.when(owned)
    def _():
        @pl.when(index < end)
        def _():
            for copy in fetch(index + 1, 0):
                copy.start()

        for copy in fetch(index, 1):
            copy.wait()

    def core_copy(which, index):
        return remote(
            core_out.at[which],
            core_in.at[which, lax.rem(index, 2)],
            (core_sems.at[0, which, index], core_sems.at[1, which, index]),
            partner,
        )

    def tile(which, index):
        return Chunk(
            own_ref.at[which, index], BITS, ORDERS[which],
            [land.at[which, index] for land in (land0, land1, land2, land3)],
            chip_sems.at[which, index], place,
        )

    def pass_on(index, swap):
        for which in range(2):
            part = tile(which, index)
            part.settle(swap)
            part.start(swap + 1)

    def finish_tile(index):
        for which in range(2):
            done_ref[which, index] = tile(which, index).last(3)

    side = lax.rem(step, 2)

    def rows_step(m, _):
        at = pl.ds(pl.multiple_of(m * CHUNK, CHUNK), CHUNK)
        pre = dot(x_ref[at, :], wh[side])
        act_grad = dot(og_ref[at, :], wr[side], NT)
        act, pre_grad = gelu_pair(pre, act_grad)
        act_ref[at, :] = act
        pre_ref[at, :] = pre_grad
        out_acc[at, :] += dot(act, wr[side])
        in_acc[at, :] += dot(pre_grad, wh[side], NT)

        @pl.when((m == 0) & owned & (index > 0))
        def _():
            pass_on(index - 1, 0)

        @pl.when((m == 0) & owned & (index > 1))
        def _():
            pass_on(index - 2, 2)

        @pl.when((m == 0) & jnp.logical_not(owned) & (index > 1))
        def _():
            pass_on(index - 2, 1)

        @pl.when((m == 0) & jnp.logical_not(owned) & (index > 2))
        def _():
            finish_tile(index - 3)

        return 0

    lax.fori_loop(0, chunks, rows_step, 0)

    for which, (left_ref, right_ref) in enumerate(((x_ref, pre_ref), (og_ref, act_ref))):
        grad = dot(left_ref[...], right_ref[...], TN)

        @pl.when(jnp.logical_not(owned))
        def _():
            @pl.when(index > 0)
            def _():
                core_copy(which, index - 1).wait_send()

            core_out[which] = grad.astype(BF16)
            core_copy(which, index).start()

        @pl.when(owned)
        def _():
            core_copy(which, index).wait_recv()
            total = grad + core_in[which, lax.rem(index, 2)].astype(F32)
            total = total.astype(BF16).reshape(own_ref.shape[2:])

            @pl.when(index < end)
            def _():
                own_ref[which, index] = total
                tile(which, index).start(0)

            @pl.when(index == end)
            def _():
                raw_ref[which] = total

    @pl.when(step == last)
    def _():
        for copy in held_copies:
            copy.wait()

        def finish(m, gain_sum):
            at = pl.ds(pl.multiple_of(m * 256, 256), 256)
            hidden = hidden_ref[at, :]
            out_ref[at, :] = (hidden + out_acc[at, :]).astype(BF16)
            unit, inverse = norm_parts(hidden)
            grad = in_acc[at, :]
            hidden_grad = og_ref[at, :].astype(F32) + norm_back(
                grad * gain_ref[...], unit, inverse
            )
            low = hidden_grad.astype(BF16)
            attn_grad_ref[at, :] = low
            do_ref[at, :] = dot(low, wo_ref[...], NT).astype(BF16)
            return gain_sum + jnp.sum(grad * unit, axis=0, keepdims=True)

        gain_grad_ref[...] = lax.fori_loop(
            0, rows // 256, finish, jnp.zeros(gain_grad_ref.shape, F32)
        )
        finish_tile(end - 2)
        for which in range(2):
            core_copy(which, end).wait_send()
            part = tile(which, end - 1)
            part.settle(1)
            part_ref[which] = part.data[part.rest(2)]


def ffn(x, og, gain, packed, hidden, wo, wh0, wh1, wr0, wr1):
    rows, width = x.shape
    units = wh0.shape[1]
    tile = 512
    steps = units // tile
    count = lax.axis_size("dp")
    block = width // count
    anywhere = pl.BlockSpec(memory_space=pl.ANY)
    whole = held((rows, width))
    low_rows = jax.ShapeDtypeStruct((rows, width), BF16)
    raw = (2, 2, 2, 2, 2, block, tile)
    part = (2, 2, 2, block, tile)
    done = (2, steps - 2, block, tile)
    tiles = (2, steps - 1)
    lands = [pltpu.VMEM(tiles + (2,) * n + (block, tile), BF16) for n in (3, 2, 1, 0)]
    pack = packed.shape[-2:]
    compress = (pack[0], 2 * pack[1])
    return pl.pallas_call(
        ffn_kernel,
        grid=(2 * steps,),
        out_shape=(
            low_rows, low_rows, low_rows, jax.ShapeDtypeStruct((1, width), F32),
            jax.ShapeDtypeStruct(done, F32),
            jax.ShapeDtypeStruct(part, BF16),
            jax.ShapeDtypeStruct(raw, BF16),
            jax.ShapeDtypeStruct(compress, F32),
        ),
        in_specs=[whole, whole, held(gain.shape), held(packed.shape)] + [anywhere] * 6,
        out_specs=(whole, whole, whole, held((1, width)), held(done), held(part), held(raw), held(compress)),
        scratch_shapes=[
            pltpu.VMEM((rows, width), F32),
            pltpu.VMEM(wo.shape, BF16),
            pltpu.SemaphoreType.DMA((2,)),
            pltpu.VMEM((2, 2) + pack, BF16),
            pltpu.VMEM((2,) + pack, BF16),
            pltpu.SemaphoreType.DMA((2, 2, 2)),
            pltpu.VMEM((2, width, tile), BF16),
            pltpu.VMEM((2, tile, width), BF16),
            pltpu.VMEM((rows, width), F32),
            pltpu.VMEM((rows, width), F32),
            pltpu.VMEM((rows, tile), BF16),
            pltpu.VMEM((rows, tile), BF16),
            pltpu.VMEM((2, width, tile), BF16),
            pltpu.VMEM((2, 2, width, tile), BF16),
            pltpu.VMEM(tiles + raw[1:], BF16),
        ] + lands + [
            pltpu.SemaphoreType.DMA((2, 2)),
            pltpu.SemaphoreType.DMA((2, 2, steps)),
            pltpu.SemaphoreType.DMA((2, steps, 2, 4)),
        ],
        compiler_params=pltpu.CompilerParams(
            vmem_limit_bytes=VMEM_LIMIT, dimension_semantics=("arbitrary",),
            collective_id=1, has_side_effects=True,
        ),
        cost_estimate=cost(75e9, 50e6),
        name="ffn",
    )(x, og, gain, packed, hidden, wo, wh0, wh1, wr0, wr1)


def attn_bwd_head(first_slot, q_ref, k_ref, v_ref, do_ref, mixed_ref, lse, dq_ref, dk_ref, dv_ref, cols):
    seg = q_ref.shape[0] // 2
    half = seg // 2
    for stream in range(2):
        base = stream * seg
        rows = slice(base, base + seg)
        lse_row = lse[:, rows]
        weight = do_ref[rows, cols].astype(F32) * mixed_ref[rows, cols].astype(F32)
        delta_row = jnp.sum(weight.T, axis=0, keepdims=True)
        key_base = 2 * seg + stream * seg
        pieces = []
        if stream == 0:
            pieces += [(start, half, 0, "mem") for start in range(0, 2 * seg, half)]
        pieces += [(key_base, half, 0, "diag"), (key_base + half, half, half, "diag")]
        dq_low = jnp.zeros((half, HEAD_DIM), F32)
        dq_high = jnp.zeros((half, HEAD_DIM), F32)
        for start, size, first, kind in pieces:
            q = q_ref[base + first : base + seg, cols]
            do = do_ref[base + first : base + seg, cols]
            k = k_ref[start : start + size, cols]
            s = dot(k, q, NT) * EXP2_SCALE - lse_row[:, first:]
            if kind == "mem":
                slot = start + lax.broadcasted_iota(jnp.int32, s.shape, 0)
                s = jnp.where(slot >= first_slot, s, masked_score)
            else:
                key = lax.broadcasted_iota(jnp.int32, s.shape, 0)
                row = lax.broadcasted_iota(jnp.int32, s.shape, 1)
                s = jnp.where(key <= row, s, masked_score)
            p = jnp.exp2(s)
            dp = dot(v_ref[start : start + size, cols], do, NT)
            ds = (p * (dp - delta_row[:, first:])).astype(BF16)
            dv_ref[start : start + size, cols] = dot(p.astype(BF16), do).astype(BF16)
            dk_ref[start : start + size, cols] = (dot(ds, q) * SCALE).astype(BF16)
            dq = dot(ds, k, TN)
            if first == 0:
                dq_low = dq_low + dq[:half]
                dq_high = dq_high + dq[half:]
            else:
                dq_high = dq_high + dq
        dq_ref[base : base + half, cols] = (dq_low * SCALE).astype(BF16)
        dq_ref[base + half : base + seg, cols] = (dq_high * SCALE).astype(BF16)


def attn_back_kernel(
    resets_ref, offsets_ref, q_ref, k_ref, v_ref, do_ref, mix_ref, lse_ref, normed_hbm, mixed_hbm, ag_ref,
    ffn_part_ref, ffn_raw_ref,
    dq_ref, dk_ref, dv_ref, early_ref, late_ref, ffn_done_ref,
    normed_ref, mixed_ref, held_sems, grads_ref, core_out, core_in, own_ref, *scratch,
):
    step = pl.program_id(0)
    last = pl.num_programs(0) - 1
    place = mesh_place()
    core, _, across = place
    partner = {"seq": 1 - core}
    lands, (core_sems, chip_sems) = list(scratch[:-2]), scratch[-2:]
    chunks, ffn_parts, ffn_raws = [], [], []
    first_slot = stream_a_slot(resets_ref, offsets_ref, core, q_ref.shape[0])
    held_copies = (
        pltpu.make_async_copy(normed_hbm, normed_ref, held_sems.at[0]),
        pltpu.make_async_copy(mixed_hbm, mixed_ref, held_sems.at[1]),
    )

    def chunk(number, data, left, order):
        mine = [lands.pop(0) for _ in order]
        return Chunk(data, left, order, mine, chip_sems.at[number], place)

    for which in range(2):
        order = ORDERS[which]
        chunks.append(chunk(3 * which, own_ref.at[which], BITS, order[:2]))
        ffn_parts.append(chunk(3 * which + 1, ffn_part_ref.at[which], order[2:][::-1], order[2:]))
        ffn_raws.append(chunk(3 * which + 2, ffn_raw_ref.at[which], BITS, order))
    index = lax.div(step, 2)
    rows = q_ref.shape[0]
    keys = k_ref.shape[0]
    pair = q_ref.shape[1]

    @pl.when(step == 0)
    def _():
        for copy in held_copies:
            copy.start()
        greet((partner,) + tuple({"dp": across(b)} for b in range(4)))
        for part in ffn_raws + ffn_parts:
            part.start(0)

    for n in range(1, 4):

        @pl.when(step == n)
        def _():
            for part in ffn_raws:
                part.settle(n - 1)
                part.start(n)

    @pl.when(step == 1)
    def _():
        for part in ffn_parts:
            part.settle(0)
            part.start(1)

    @pl.when(step == 2)
    def _():
        for which in range(2):
            ffn_done_ref[which, 0] = ffn_parts[which].last(1)

    def core_copy(which, index):
        return remote(
            core_out.at[which, index],
            core_in.at[which, index],
            (core_sems.at[0, which, index], core_sems.at[1, which, index]),
            partner,
        )

    head = 4 * jnp.where(lax.rem(step, 2) == 0, 1 - core, core) + 2 * index

    def one_head(h, _):
        attn_bwd_head(
            first_slot, q_ref, k_ref, v_ref, do_ref, mix_ref, lse_ref[pl.ds(head + h, 1), :],
            dq_ref, dk_ref, dv_ref, pl.ds(pl.multiple_of(h * HEAD_DIM, HEAD_DIM), HEAD_DIM),
        )
        return 0

    lax.fori_loop(0, 2, one_head, 0)

    @pl.when(step == 0)
    def _():
        for copy in held_copies:
            copy.wait()

    grads_ref[0, :, :pair] = dot(normed_ref[keys - rows :], dq_ref[...], TN)
    grads_ref[0, :, pair:] = dot(normed_ref[...], dk_ref[...], TN)
    grads_ref[1, :, :pair] = dot(normed_ref[...], dv_ref[...], TN)
    grads_ref[1, :, pair:] = dot(mixed_ref[...], ag_ref[...], TN)

    @pl.when(lax.rem(step, 2) == 0)
    def _():
        for which in range(2):
            core_out[which, index] = grads_ref[which].astype(BF16)
            core_copy(which, index).start()

    @pl.when(step == 2)
    def _():
        for part in chunks:
            part.settle(0)
            part.start(1)

    def own_grads(which, index, out_ref):
        core_copy(which, index).wait()
        total = grads_ref[which] + core_in[which, index].astype(F32)
        out_ref[...] = total.astype(BF16).reshape(out_ref.shape)

    @pl.when(step == 1)
    def _():
        for which in range(2):
            own_grads(which, 0, own_ref.at[which])
            chunks[which].start(0)

    @pl.when(step == last)
    def _():
        for which in range(2):
            own_grads(which, 1, late_ref.at[which])
        for which in range(2):
            chunks[which].settle(1)
            early_ref[which] = own_ref[(which,) + chunks[which].rest(2)]
            ffn_done_ref[which, 1] = ffn_raws[which].last(3)


def attn_back(resets, offsets, q, k, v, do, mixed, lse, normed, attn_grad, ffn_part, ffn_raw):
    rows, width = q.shape
    keys = k.shape[0]
    pair = 2 * HEAD_DIM
    block = (width // 16, 2 * pair)

    def by_pair(count):
        def index(i):
            core = lax.axis_index("seq")
            half = jnp.where(lax.rem(i, 2) == 0, 1 - core, core)
            return 0, 2 * half + lax.div(i, 2)

        return pl.BlockSpec((count, pair), index)

    early, late = (2, 2, 2) + block, (2, 2, 2, 2, 2) + block
    ffn_block = ffn_raw.shape[-2:]
    done = (2, 2) + ffn_block
    lands = []
    for order in ORDERS:
        lands += landings(BITS, order[:2], block)
        lands += landings(order[2:], order[2:], ffn_block)
        lands += landings(BITS, order, ffn_block)
    return pl.pallas_call(
        attn_back_kernel,
        grid=(4,),
        out_shape=(
            jax.ShapeDtypeStruct((rows, width), BF16),
            jax.ShapeDtypeStruct((keys, width), BF16),
            jax.ShapeDtypeStruct((keys, width), BF16),
            jax.ShapeDtypeStruct(early, BF16),
            jax.ShapeDtypeStruct(late, BF16),
            jax.ShapeDtypeStruct(done, F32),
        ),
        in_specs=[
            pl.BlockSpec(memory_space=pltpu.SMEM),
            pl.BlockSpec(memory_space=pltpu.SMEM),
            by_pair(rows), by_pair(keys), by_pair(keys), by_pair(rows), by_pair(rows),
            held(lse.shape), pl.BlockSpec(memory_space=pl.ANY), pl.BlockSpec(memory_space=pl.ANY), by_pair(rows),
            held(ffn_part.shape), held(ffn_raw.shape),
        ],
        out_specs=(by_pair(rows), by_pair(keys), by_pair(keys), held(early), held(late), held(done)),
        scratch_shapes=[
            pltpu.VMEM(normed.shape, BF16),
            pltpu.VMEM(mixed.shape, BF16),
            pltpu.SemaphoreType.DMA((2,)),
            pltpu.VMEM((2, width, 2 * pair), F32),
            pltpu.VMEM((2, 2, width, 2 * pair), BF16),
            pltpu.VMEM((2, 2, width, 2 * pair), BF16),
            pltpu.VMEM(late, BF16),
        ] + lands + [
            pltpu.SemaphoreType.DMA((2, 2, 2)),
            pltpu.SemaphoreType.DMA((6, 2, 4)),
        ],
        compiler_params=pltpu.CompilerParams(
            vmem_limit_bytes=VMEM_LIMIT, dimension_semantics=("arbitrary",),
            collective_id=2, has_side_effects=True,
        ),
        cost_estimate=cost(45e9, 24e6),
        name="attn_back",
    )(resets, offsets, q, k, v, do, mixed, lse, normed, mixed, attn_grad, ffn_part, ffn_raw)


def rows_back_kernel(
    dq_ref, dk_ref, dv_ref, raw_ref, ag_ref, gain_ref, gain_ffn_ref, wq_ref, wk_ref, wv_ref,
    early_ref, late_ref,
    mine_ref, theirs_ref, gains_ref, early_out_ref, late_out_ref,
    rows_out, gain_acc, gain_in, *scratch,
):
    step = pl.program_id(0)
    last = pl.num_programs(0) - 1
    place = mesh_place()
    core, _, across = place
    partner = {"seq": 1 - core}
    lands, (row_sems, local_sems, gain_sems, chip_sems) = list(scratch[:-4]), scratch[-4:]

    chunks = []

    def chunk(data, left, order):
        number = len(chunks)
        mine = [lands.pop(0) for _ in order]
        chunks.append(Chunk(data, left, order, mine, chip_sems.at[number], place))
        return chunks[-1]

    early, late = [], []
    for which in range(2):
        early.append(chunk(early_ref.at[which], BITS[:2], ORDERS[which][2:]))
        late.append(chunk(late_ref.at[which], BITS, ORDERS[which]))

    def gain_copy(n):
        device = partner if n == 0 else {"dp": across(n - 1)}
        return remote(gain_acc.at[n], gain_in.at[n], (gain_sems.at[0, n], gain_sems.at[1, n]), device)

    def row_copy(block):
        stream = block // 2
        return remote(
            rows_out.at[block], theirs_ref.at[stream], (row_sems.at[0, stream], row_sems.at[1, stream]), partner
        )

    def row_keep(block):
        stream = block // 2
        return pltpu.make_async_copy(rows_out.at[block], mine_ref.at[stream], local_sems.at[stream])

    @pl.when(step == 0)
    def _():
        greet((partner,) + tuple({"dp": across(b)} for b in range(4)))
        for part in late + early:
            part.start(0)
        gain_acc[...] = jnp.zeros_like(gain_acc)

    def normed_grad():
        return dot(dk_ref[...], wk_ref[...], NT) + dot(dv_ref[...], wv_ref[...], NT)

    unit, inverse = norm_parts(raw_ref[...].astype(F32))

    @pl.when(step < 4)
    def _():
        gain_acc[0, 0:1] += jnp.sum(normed_grad() * unit, axis=0, keepdims=True)

    @pl.when(step >= 4)
    def _():
        grad = normed_grad() + dot(dq_ref[...], wq_ref[...], NT)
        gain_acc[0, 0:1] += jnp.sum(grad * unit, axis=0, keepdims=True)
        rows_grad = norm_back(grad * gain_ref[...], unit, inverse)
        rows_out[step - 4] = (rows_grad + ag_ref[...].astype(F32)).astype(BF16)

    for block in range(4):
        stays = core == block % 2
        pl.when((step == block + 4) & stays)(row_keep(block).start)
        pl.when((step == block + 4) & jnp.logical_not(stays))(row_copy(block).start)

    @pl.when(step == 4)
    def _():
        for part in early:
            part.settle(0)
            part.start(1)

    @pl.when(step == 6)
    def _():
        for part in late:
            part.settle(0)
            part.start(1)

    @pl.when(step == last)
    def _():
        def gain_step(n):
            gain_copy(n).wait()
            total = gain_acc[n] + gain_in[n]
            if n < 4:
                gain_acc[n + 1] = total
                gain_copy(n + 1).start()
            else:
                gains_ref[...] = total

        gain_acc[0, 1:2] = gain_ffn_ref[...]
        gain_copy(0).start()
        for which in range(2):
            early_out_ref[which] = early[which].last(1)
        gain_step(0)
        for part in late:
            part.settle(1)
            part.start(2)
        gain_step(1)
        gain_step(2)
        for part in late:
            part.settle(2)
            part.start(3)
        gain_step(3)
        gain_step(4)
        for which in range(2):
            late_out_ref[which] = late[which].last(3)
        for block in range(4):
            stays = core == block % 2
            pl.when(stays)(row_keep(block).wait)
            pl.when(jnp.logical_not(stays))(row_copy(block).wait_send)
        for stream in range(2):
            row_copy(2 * stream).wait_recv()


def rows_back(
    dq, dk, dv, raw, attn_grad, gain, gain_ffn, wq, wk, wv, early, late
):
    keys, width = dk.shape
    rows = dq.shape[0]
    size = keys // 8
    key_block = pl.BlockSpec((size, width), lambda i: (i, 0))
    row_block = pl.BlockSpec((size, width), lambda i: (jnp.maximum(i - 4, 0), 0))
    anywhere = pl.BlockSpec(memory_space=pl.ANY)
    rows_shape = jax.ShapeDtypeStruct((2, size, width), BF16)
    block = early.shape[-2:]
    lands = []
    for order in ORDERS:
        lands += landings(BITS[:2], order[2:], block)
        lands += landings(BITS, order, block)
    out = (2,) + block
    vector = (8, width)
    return pl.pallas_call(
        rows_back_kernel,
        grid=(8,),
        out_shape=(
            rows_shape, rows_shape,
            jax.ShapeDtypeStruct(vector, F32),
            jax.ShapeDtypeStruct(out, F32),
            jax.ShapeDtypeStruct(out, F32),
        ),
        in_specs=[
            row_block, key_block, key_block, key_block, row_block,
            held(gain.shape), held(gain_ffn.shape), held(wq.shape), held(wk.shape), held(wv.shape),
            held(early.shape), held(late.shape),
        ],
        out_specs=(
            anywhere, anywhere, held(vector), held(out), held(out),
        ),
        scratch_shapes=[
            pltpu.VMEM((4, size, width), BF16),
            pltpu.VMEM((5,) + vector, F32),
            pltpu.VMEM((5,) + vector, F32),
        ] + lands + [
            pltpu.SemaphoreType.DMA((2, 2)),
            pltpu.SemaphoreType.DMA((2,)),
            pltpu.SemaphoreType.DMA((2, 5)),
            pltpu.SemaphoreType.DMA((4, 2, 4)),
        ],
        compiler_params=pltpu.CompilerParams(
            vmem_limit_bytes=VMEM_LIMIT, dimension_semantics=("arbitrary",),
            collective_id=3, has_side_effects=True,
        ),
        cost_estimate=cost(20e9, 24e6),
        name="rows_back",
    )(
        dq, dk, dv, raw, attn_grad, gain, gain_ffn, wq, wk, wv,
        early, late,
    )


def swap_dp(block, bit):
    count = lax.axis_size("dp")
    return lax.ppermute(block, "dp", [(i, i ^ (1 << bit)) for i in range(count)])


def swap_core(block):
    return lax.ppermute(block, "seq", [(0, 1), (1, 0)])


def on_device_pair(
    inputs, memory, compressed, offsets, resets, w_query, w_key, w_value, w_output, w_hidden,
    w_return, w_compress, gain_attn, gain_ffn, out_grad, comp_grad,
):
    core = lax.axis_index("seq")
    dp_count = lax.axis_size("dp")
    streams, half, width = inputs.shape
    seg = 2 * half
    low_core = core == 0

    unused = (resets != 0) | (offsets >= 2 * seg)
    gain_a = gain_attn.astype(F32).reshape(1, width)
    gain_f = gain_ffn.astype(F32).reshape(1, width)

    x_in, x_mem, x_old, x_og, new_rows, kept_p, sent_p, kept_q, sent_q = front(
        resets, inputs, memory, compressed, out_grad, w_compress, comp_grad
    )
    got_p, got_q = swap_dp(sent_p, 0), swap_dp(sent_q, 1)
    wh_late, wr_late, x_in = lax.optimization_barrier((w_hidden, w_return, x_in))
    wh_other, wr_other = swap_core(wh_late), swap_core(wr_late)
    all_rows, normed, q, k, v, og = project_rows(
        resets, offsets, x_old, x_mem, x_in, x_og, gain_a, w_query, w_key, w_value
    )
    mixed, hidden, ffn_in, lse, packed = attn_fwd(
        resets, offsets, q, k, v, all_rows, w_output, gain_f, kept_p, got_p, kept_q, got_q
    )
    outputs, attn_grad, mixed_grad, gain_ffn_grad, ffn_done, ffn_part, ffn_raw, grad_compress = ffn(
        ffn_in, og, gain_f, packed, hidden, w_output, wh_other, w_hidden, wr_other, w_return
    )
    dq, dk, dv, early, late, ffn_rest = attn_back(
        resets, offsets, q, k, v, mixed_grad, mixed, lse, normed, attn_grad, ffn_part, ffn_raw
    )
    mine_rows, their_rows, gains, early_out, late_out = rows_back(
        dq, dk, dv, all_rows, attn_grad, gain_a, gain_ffn_grad, w_query, w_key, w_value, early, late
    )

    def tiles(which):
        parts = [ffn_done[which, i] for i in range(2)] + [ffn_rest[which, i] for i in range(2)]
        return jnp.concatenate(parts, axis=1)

    grad_hidden, grad_return = tiles(0), tiles(1).T
    pair = 2 * HEAD_DIM

    def weight_grad(which, side):
        cols = slice(side * pair, (side + 1) * pair)
        return jnp.concatenate([early_out[which, :, cols], late_out[which, :, cols]], axis=1)

    grad_query, grad_key = weight_grad(0, 0), weight_grad(0, 1)
    grad_value, grad_output = weight_grad(1, 0), weight_grad(1, 1)
    rank = lax.axis_index("dp")
    gains = lax.dynamic_slice_in_dim(gains[:2], rank * (width // dp_count), width // dp_count, 1)

    def to_streams(a, b, which):
        swapped = lax.dynamic_index_in_dim(unused, which, 0, False)
        return jnp.where(swapped, b, a), jnp.where(swapped, a, b)

    def spread(own_pair, other_pair):
        own = to_streams(own_pair[0], own_pair[1], core)
        other = to_streams(other_pair[0], other_pair[1], 1 - core)
        return jnp.stack(
            [
                jnp.where(low_core, own[0], other[0]),
                jnp.where(low_core, other[0], own[0]),
                jnp.where(low_core, own[1], other[1]),
                jnp.where(low_core, other[1], own[1]),
            ]
        )

    def place_rows(rows):
        halves = rows.reshape(2, 2, half, width)
        return spread(
            lax.dynamic_index_in_dim(halves, core, 1, False),
            swap_core(lax.dynamic_index_in_dim(halves, 1 - core, 1, False)),
        )

    return (
        place_rows(outputs),
        new_rows[:, : comp_grad.shape[1]],
        spread(mine_rows, their_rows),
        grad_query,
        grad_key,
        grad_value,
        grad_output,
        grad_hidden,
        grad_return,
        grad_compress,
        gains[0],
        gains[1],
    )


def solution(mesh):
    placed = (
        P("dp", "seq", None),
        P("dp", "seq", None),
        P("dp", "seq", None),
        P("dp"),
        P("dp"),
        P(),
        P(),
        P(),
        P(),
        P(None, "seq"),
        P("seq", None),
        P(),
        P(),
        P(),
        P("dp", "seq", None),
        P("dp", None, None),
    )
    fast = mesh.shape["seq"] == 2 and mesh.shape["dp"] == 16
    return jax.shard_map(
        on_device_pair if fast else on_device,
        mesh=mesh,
        in_specs=placed,
        out_specs=(
            P("dp", "seq", None),
            P("dp", None, None),
            P("dp", "seq", None),
            P("dp", "seq"),
            P("dp", "seq"),
            P("dp", "seq"),
            P("dp", "seq"),
            P("dp", "seq"),
            P("seq", "dp"),
            P("dp", "seq"),
            P("dp"),
            P("dp"),
        ),
        check_vma=False,
    )
```

```python
import functools
import math

import jax
import jax.numpy as jnp
from jax import lax
from jax.experimental import pallas as pl
from jax.experimental.pallas import tpu as pltpu
from jax.sharding import PartitionSpec as P

HEADS = 8
HEAD_DIM = 128
RATE = 3


epsilon = 1e-05
masked_score = -1e30


def shifted(block, axis, distance):
    devices = range(lax.axis_size(axis))
    route = [(i - distance, i) for i in devices if i - distance in devices]
    return lax.ppermute(block, axis, route)


def layer_norm(values, gain):
    centred = values - jnp.mean(values, axis=-1, keepdims=True)
    spread = jnp.mean(centred * centred, axis=-1, keepdims=True)
    return centred * lax.rsqrt(spread + epsilon) * gain


def project(left, right):
    return jnp.einsum("srd,de->sre", left, right, preferred_element_type=jnp.float32)


def project_back(left, right):
    return jnp.einsum("sre,de->srd", left, right, preferred_element_type=jnp.float32)


def weight_term(left, right):
    return jnp.einsum("srd,sre->de", left, right, preferred_element_type=jnp.float32)


def key_layout(key_index, local_rows, seg_len):
    key_owner = key_index // (3 * local_rows)
    inside = key_index % (3 * local_rows)
    key_kind = inside // local_rows
    key_place = key_owner * local_rows + inside % local_rows
    mem_slot = jnp.where(key_kind == 0, key_place, seg_len + key_place)
    return (key_kind, mem_slot, key_place)


def allowed_mask(key_kind, mem_slot, key_place, query_place, offsets, keep_flag):
    memory_ok = (mem_slot[None, :] >= offsets[:, None]) & keep_flag[:, None]
    causal = key_place[None, :] <= query_place[:, None]
    return jnp.where(key_kind[None, None, :] < 2, memory_ok[:, None, :], causal[None, :, :])


def score_block(query_heads, key_heads, allowed, score_scale):
    scores = (
        jnp.einsum("sthe,skhe->shtk", query_heads, key_heads, preferred_element_type=jnp.float32)
        * score_scale
    )
    return jnp.where(allowed[:, None], scores, masked_score)


def tile_matrix(matrix, dp_count, seq_count):
    rows_total, cols_total = matrix.shape
    blocks = matrix.reshape(dp_count, rows_total // dp_count, seq_count, cols_total // seq_count)
    return blocks.transpose(0, 2, 1, 3).reshape(
        dp_count * seq_count, rows_total // dp_count, cols_total // seq_count
    )


def tile_vector(vector, dp_count, seq_count):
    piece_len = vector.shape[0] // dp_count
    pieces = vector.reshape(dp_count, 1, piece_len)
    return jnp.broadcast_to(pieces, (dp_count, seq_count, piece_len)).reshape(
        dp_count * seq_count, piece_len
    )


def on_device(
    inputs,
    memory,
    compressed,
    offsets,
    resets,
    w_query,
    w_key,
    w_value,
    w_output,
    w_hidden,
    w_return,
    w_compress,
    gain_attn,
    gain_ffn,
    out_grad,
    comp_grad,
):
    seq_count = lax.axis_size("seq")
    dp_count = lax.axis_size("dp")
    seq_rank = lax.axis_index("seq")
    streams, local_rows, feat_width = inputs.shape
    seg_len = local_rows * seq_count
    score_scale = HEAD_DIM ** (-0.5)
    keep_flag = resets == 0
    all_rows = jnp.concatenate([compressed, memory, inputs], axis=1).astype(jnp.float32)
    normed, attn_norm_back = jax.vjp(layer_norm, all_rows, gain_attn.astype(jnp.float32))
    normed_low = normed.astype(jnp.bfloat16)
    query_in = normed_low[:, 2 * local_rows :]
    query_low = project(query_in, w_query).astype(jnp.bfloat16)
    key_low = project(normed_low, w_key).astype(jnp.bfloat16)
    value_low = project(normed_low, w_value).astype(jnp.bfloat16)
    key_all, value_all = (
        lax.all_gather(key_low, "seq", axis=1, tiled=True),
        lax.all_gather(value_low, "seq", axis=1, tiled=True),
    )
    total_keys = key_all.shape[1]
    key_kind, mem_slot, key_place = key_layout(
        jnp.arange(total_keys, dtype=jnp.int32), local_rows, seg_len
    )
    query_place = seq_rank * local_rows + jnp.arange(local_rows, dtype=jnp.int32)
    allowed = allowed_mask(key_kind, mem_slot, key_place, query_place, offsets, keep_flag)
    query_heads = query_low.reshape(streams, local_rows, HEADS, HEAD_DIM)
    key_heads = key_all.reshape(streams, total_keys, HEADS, HEAD_DIM)
    value_heads = value_all.reshape(streams, total_keys, HEADS, HEAD_DIM)
    scores = score_block(query_heads, key_heads, allowed, score_scale)
    row_top = jnp.max(scores, axis=-1, keepdims=True)
    exp_scores = jnp.exp(scores - row_top)
    row_total = jnp.sum(exp_scores, axis=-1, keepdims=True)
    attn_prob = exp_scores / row_total
    log_total = row_top + jnp.log(row_total)
    mixed_low = (
        jnp.einsum(
            "shtk,skhe->sthe",
            attn_prob.astype(jnp.bfloat16),
            value_heads,
            preferred_element_type=jnp.float32,
        )
        .reshape(streams, local_rows, feat_width)
        .astype(jnp.bfloat16)
    )
    hidden = inputs.astype(jnp.float32) + project(mixed_low, w_output)
    ffn_in, ffn_norm_back = jax.vjp(layer_norm, hidden, gain_ffn.astype(jnp.float32))
    ffn_low = ffn_in.astype(jnp.bfloat16)
    ffn_all = lax.all_gather(ffn_low, "seq", axis=1, tiled=True)
    pre_act = jnp.einsum("std,df->stf", ffn_all, w_hidden, preferred_element_type=jnp.float32)
    act_float, gelu_back = jax.vjp(jax.nn.gelu, pre_act)
    act_low = act_float.astype(jnp.bfloat16)
    partial_out = jnp.einsum("stf,fd->std", act_low, w_return, preferred_element_type=jnp.float32)
    ffn_out = lax.psum_scatter(
        partial_out.astype(jnp.bfloat16), "seq", scatter_dimension=1, tiled=True
    ).astype(jnp.float32)
    cot_all = lax.all_gather(out_grad, "seq", axis=1, tiled=True)
    act_grad = jnp.einsum("std,fd->stf", cot_all, w_return, preferred_element_type=jnp.float32)
    return_part = jnp.einsum("stf,std->fd", act_low, cot_all, preferred_element_type=jnp.float32)
    pre_grad = gelu_back(act_grad)[0].astype(jnp.bfloat16)
    hidden_part = jnp.einsum("std,stf->df", ffn_all, pre_grad, preferred_element_type=jnp.float32)
    in_part = jnp.einsum("stf,df->std", pre_grad, w_hidden, preferred_element_type=jnp.float32)
    ffn_in_grad = lax.psum_scatter(in_part, "seq", scatter_dimension=1, tiled=True)
    hidden_sum, return_sum = (
        lax.psum_scatter(
            hidden_part.astype(jnp.bfloat16), "dp", scatter_dimension=0, tiled=True
        ).astype(jnp.float32),
        lax.psum_scatter(
            return_part.T.astype(jnp.bfloat16), "dp", scatter_dimension=0, tiled=True
        ).astype(jnp.float32),
    )
    grad_return = return_sum.T
    outputs = (hidden + ffn_out).astype(jnp.bfloat16)
    hidden_grad, gain_ffn_grad = ffn_norm_back(ffn_in_grad)
    hidden_grad = hidden_grad + out_grad.astype(jnp.float32)
    attn_grad_low = hidden_grad.astype(jnp.bfloat16)
    output_part = weight_term(mixed_low, attn_grad_low)
    mixed_grad = project_back(attn_grad_low, w_output).astype(jnp.bfloat16)
    mixed_heads = mixed_grad.reshape(streams, local_rows, HEADS, HEAD_DIM)
    prob_again = jnp.exp(score_block(query_heads, key_heads, allowed, score_scale) - log_total)
    prob_grad = jnp.einsum(
        "sthe,skhe->shtk", mixed_heads, value_heads, preferred_element_type=jnp.float32
    )
    prob_delta = jnp.sum(prob_again * prob_grad, axis=-1)
    score_grad = (prob_again * (prob_grad - prob_delta[..., None])).astype(jnp.bfloat16)
    query_grad = (
        (
            jnp.einsum("shtk,skhe->sthe", score_grad, key_heads, preferred_element_type=jnp.float32)
            * score_scale
        )
        .reshape(streams, local_rows, feat_width)
        .astype(jnp.bfloat16)
    )
    key_part = (
        jnp.einsum("shtk,sthe->skhe", score_grad, query_heads, preferred_element_type=jnp.float32)
        * score_scale
    ).reshape(streams, total_keys, feat_width)
    value_part = jnp.einsum(
        "shtk,sthe->skhe",
        prob_again.astype(jnp.bfloat16),
        mixed_heads,
        preferred_element_type=jnp.float32,
    ).reshape(streams, total_keys, feat_width)
    key_sum, value_sum = (
        lax.psum_scatter(
            key_part.astype(jnp.bfloat16), "seq", scatter_dimension=1, tiled=True
        ).astype(jnp.float32),
        lax.psum_scatter(
            value_part.astype(jnp.bfloat16), "seq", scatter_dimension=1, tiled=True
        ).astype(jnp.float32),
    )
    key_grad = key_sum.astype(jnp.bfloat16)
    value_grad = value_sum.astype(jnp.bfloat16)
    query_part = weight_term(query_in, query_grad)
    key_wpart = weight_term(normed_low, key_grad)
    value_wpart = weight_term(normed_low, value_grad)
    query_back = project_back(query_grad, w_query)
    normed_grad = project_back(key_grad, w_key) + project_back(value_grad, w_value)
    normed_grad = normed_grad + jnp.concatenate(
        [jnp.zeros((streams, 2 * local_rows, feat_width), jnp.float32), query_back], axis=1
    )
    rows_grad, gain_attn_grad = attn_norm_back(normed_grad)
    input_grad = (rows_grad[:, 2 * local_rows :] + hidden_grad).astype(jnp.bfloat16)
    kept_memory = memory * keep_flag[:, None, None].astype(jnp.bfloat16)
    edge_rows = shifted(kept_memory[:, : 2 * (RATE - 1)], "seq", -1)
    extended = jnp.concatenate([kept_memory, edge_rows], axis=1)
    group_count = (local_rows + RATE - 1) // RATE
    first_group = (seq_rank * local_rows + RATE - 1) // RATE
    slice_start = RATE * first_group - seq_rank * local_rows
    grouped = lax.dynamic_slice_in_dim(extended, slice_start, RATE * group_count, 1).reshape(
        streams, group_count, RATE * feat_width
    )
    piece_rows = jnp.einsum(
        "sgc,cd->sgd", grouped, w_compress, preferred_element_type=jnp.float32
    ).astype(jnp.bfloat16)
    comp_all = lax.all_gather(piece_rows, "seq", axis=1, tiled=True)
    comp_count = comp_grad.shape[1]
    out_index = jnp.arange(comp_count, dtype=jnp.int32)
    holder = RATE * out_index // local_rows
    lookup = holder * group_count + out_index - (holder * local_rows + RATE - 1) // RATE
    new_compressed = jnp.take(comp_all, lookup, axis=1)
    slot_index = first_group + jnp.arange(group_count, dtype=jnp.int32)
    slot_valid = (RATE * slot_index < (seq_rank + 1) * local_rows) & (slot_index < comp_count)
    picked = jnp.take(comp_grad, jnp.minimum(slot_index, comp_count - 1), axis=1) * slot_valid[
        None, :, None
    ].astype(jnp.bfloat16)
    compress_part = jnp.einsum("sgc,sgd->cd", grouped, picked, preferred_element_type=jnp.float32)
    reduced = (
        lax.psum_scatter(
            tile_matrix(query_part, dp_count, seq_count),
            ("dp", "seq"),
            scatter_dimension=0,
            tiled=True,
        ),
        lax.psum_scatter(
            tile_matrix(key_wpart, dp_count, seq_count),
            ("dp", "seq"),
            scatter_dimension=0,
            tiled=True,
        ),
        lax.psum_scatter(
            tile_matrix(value_wpart, dp_count, seq_count),
            ("dp", "seq"),
            scatter_dimension=0,
            tiled=True,
        ),
        lax.psum_scatter(
            tile_matrix(output_part, dp_count, seq_count),
            ("dp", "seq"),
            scatter_dimension=0,
            tiled=True,
        ),
        lax.psum_scatter(
            tile_matrix(compress_part, dp_count, seq_count),
            ("dp", "seq"),
            scatter_dimension=0,
            tiled=True,
        ),
        lax.psum_scatter(
            tile_vector(gain_attn_grad, dp_count, seq_count),
            ("dp", "seq"),
            scatter_dimension=0,
            tiled=True,
        ),
        lax.psum_scatter(
            tile_vector(gain_ffn_grad, dp_count, seq_count),
            ("dp", "seq"),
            scatter_dimension=0,
            tiled=True,
        ),
    )
    return (
        outputs,
        new_compressed,
        input_grad,
        reduced[0][0],
        reduced[1][0],
        reduced[2][0],
        reduced[3][0],
        hidden_sum,
        grad_return,
        reduced[4][0],
        reduced[5][0],
        reduced[6][0],
    )


F32 = jnp.float32
BF16 = jnp.bfloat16
NN = (((1,), (0,)), ((), ()))
NT = (((1,), (1,)), ((), ()))
TN = (((0,), (0,)), ((), ()))
VMEM_LIMIT = 60 * 1024 * 1024
SCALE = HEAD_DIM ** (-0.5)
EXP2_SCALE = SCALE * math.log2(math.e)


def dot(left, right, dims=NN):
    return lax.dot_general(left, right, dims, preferred_element_type=F32)


def params(steps=1):
    return pltpu.CompilerParams(
        vmem_limit_bytes=VMEM_LIMIT, dimension_semantics=("arbitrary",) * steps
    )


def cost(flops, bytes_accessed=0, transcendentals=0):
    return pl.CostEstimate(
        flops=int(flops), bytes_accessed=int(bytes_accessed), transcendentals=int(transcendentals)
    )


def held(shape):
    zeros = (0,) * len(shape)
    return pl.BlockSpec(shape, lambda *_: zeros, pipeline_mode=pl.Buffered(1))


def norm_parts(rows):
    centred = rows - jnp.mean(rows, axis=-1, keepdims=True)
    inverse = lax.rsqrt(jnp.mean(centred * centred, axis=-1, keepdims=True) + epsilon)
    return centred * inverse, inverse


def norm_back(grad, unit, inverse):
    return inverse * (
        grad
        - jnp.mean(grad, axis=-1, keepdims=True)
        - unit * jnp.mean(grad * unit, axis=-1, keepdims=True)
    )


def add_low(left, right):
    return (left.astype(F32) + right.astype(F32)).astype(BF16)


def mesh_place():
    rank, core = lax.axis_index("dp"), lax.axis_index("seq")

    def bit(b):
        return lax.rem(lax.div(rank, 1 << b), 2)

    def across(b):
        return rank + (1 << b) * (1 - 2 * bit(b))

    return core, bit, across


def first_slots(resets_ref, offsets_ref, core, total):
    return [
        jnp.where(resets_ref[core + 2 * j] != 0, total, offsets_ref[core + 2 * j]) for j in range(2)
    ]


def stream_a_slot(resets_ref, offsets_ref, core, total):
    first, second = first_slots(resets_ref, offsets_ref, core, total)
    return jnp.where(first >= total, second, first)


def greet(devices):
    barrier = pltpu.get_barrier_semaphore()
    for device in devices:
        pl.semaphore_signal(
            barrier, inc=1, device_id=device, device_id_type=pl.DeviceIdType.MESH
        )
    pl.semaphore_wait(barrier, len(devices))


def remote(src, dst, sems, device):
    return pltpu.make_async_remote_copy(
        src_ref=src,
        dst_ref=dst,
        send_sem=sems[0],
        recv_sem=sems[1],
        device_id=device,
        device_id_type=pl.DeviceIdType.MESH,
    )


class Chunk:
    def __init__(self, data, left, order, landing, sems, place):
        self.data, self.left, self.order = data, left, order
        self.landing, self.sems = landing, sems
        _, self.bit, self.across = place

    def at(self, swap, away):
        index = []
        for b in self.left:
            if b in self.order[:swap]:
                index.append(self.bit(b))
            elif swap < len(self.order) and b == self.order[swap]:
                index.append(1 - self.bit(b) if away else self.bit(b))
            else:
                index.append(slice(None))
        return tuple(index)

    def rest(self, swap):
        done = self.order[:swap]
        return tuple(self.bit(b) if b in done else slice(None) for b in self.left)

    def copy(self, swap):
        return remote(
            self.data.at[self.at(swap, True)],
            self.landing[swap],
            (self.sems.at[0, swap], self.sems.at[1, swap]),
            {"dp": self.across(self.order[swap])},
        )

    def start(self, swap):
        self.copy(swap).start()

    def settle(self, swap):
        self.copy(swap).wait()
        here = self.at(swap, False)
        self.data[here] = add_low(self.data[here], self.landing[swap][...])

    def last(self, swap):
        self.copy(swap).wait()
        return self.data[self.at(swap, False)].astype(F32) + self.landing[swap][...].astype(F32)


def landings(left, order, block):
    shapes, count = [], len(left)
    for _ in order:
        count -= 1
        shapes.append(pltpu.VMEM((2,) * count + block, BF16))
    return shapes


BITS = (3, 2, 1, 0)
ORDERS = ((0, 1, 2, 3), (1, 0, 2, 3))


def front_kernel(
    resets_ref, in_ref, mem_ref, old_ref, og_ref, wc_ref, cg_ref,
    x_in_ref, x_mem_ref, x_old_ref, x_og_ref, new_ref, kept_p_ref, sent_p_ref, kept_q_ref, sent_q_ref,
    mem, x_in, x_old, x_og, wc, new, core_out, core_in, row_sems, wc_sem, new_sems, core_sems, out_sems,
):
    core, bit, _ = mesh_place()
    partner = {"seq": 1 - core}
    width = in_ref.shape[2]
    groups = cg_ref.shape[1]

    weights = pltpu.make_async_copy(wc_ref, wc, wc_sem)
    weights.start()
    greet((partner,))
    moves = []
    for n, (src, dst) in enumerate(
        ((mem_ref, mem), (in_ref, x_in), (old_ref, x_old), (og_ref, x_og))
    ):
        for j in range(2):
            away = remote(
                src.at[1 - core + 2 * j], dst.at[j, core], (row_sems.at[0, n, j], row_sems.at[1, n, j]), partner
            )
            here = pltpu.make_async_copy(src.at[core + 2 * j], dst.at[j, core], row_sems.at[2, n, j])
            away.start()
            here.start()
            moves.append((away, here))
    new[...] = jnp.zeros_like(new)
    outs = []
    for j in range(2):
        moves[j][0].wait_recv()
        moves[j][1].wait()
    outs.append(pltpu.make_async_copy(mem, x_mem_ref, out_sems.at[0]))
    outs[-1].start()
    weights.wait()

    grouped = []
    for j in range(2):
        rows = mem[j].reshape(2 * mem.shape[2], width)
        group = lax.broadcasted_iota(jnp.int32, (groups, rows.shape[0]), 0)
        row = lax.broadcasted_iota(jnp.int32, (groups, rows.shape[0]), 1)
        keep = jnp.where(resets_ref[core + 2 * j] == 0, 1.0, 0.0)
        total = jnp.zeros((groups, width), F32)
        mine = []
        for r in range(RATE):
            pick = jnp.where(row == RATE * group + r, keep, 0.0).astype(BF16)
            mine.append(dot(pick, rows).astype(BF16))
            total = total + dot(mine[-1], wc[r * width : (r + 1) * width])
        grouped.append(mine)
        new[j, :groups] = total.astype(BF16)

    news = []
    for j in range(2):
        at = core + 2 * j
        news.append(remote(new.at[j], new_ref.at[at], (new_sems.at[0, j], new_sems.at[1, j]), partner))
        outs.append(pltpu.make_async_copy(new.at[j], new_ref.at[at], new_sems.at[2, j]))
        news[-1].start()
        outs[-1].start()

    half = width // 2

    def grad(r, side):
        cols = pl.ds(pl.multiple_of(side * half, half), half)
        return sum(dot(grouped[j][r], cg_ref[core + 2 * j, :, cols], TN) for j in range(2))

    crossing = []
    for r in range(RATE):
        core_out[r] = grad(r, 1 - core).astype(BF16)
        crossing.append(
            remote(core_out.at[r], core_in.at[r], (core_sems.at[0, r], core_sems.at[1, r]), partner)
        )
        crossing[-1].start()
    for n, (src, dst) in enumerate(((x_in, x_in_ref), (x_old, x_old_ref), (x_og, x_og_ref))):
        for away, here in moves[2 * n + 2 : 2 * n + 4]:
            away.wait_recv()
            here.wait()
        outs.append(pltpu.make_async_copy(src, dst, out_sems.at[1 + n]))
        outs[-1].start()
    fine = width // 16
    quarter = half // 2
    for r in range(RATE):
        total = grad(r, core)
        crossing[r].wait()
        total = (total + core_in[r].astype(F32)).astype(BF16)
        for which, (kept_ref, sent_ref) in enumerate(
            ((kept_p_ref, sent_p_ref), (kept_q_ref, sent_q_ref))
        ):
            for mine in range(2):

                @pl.when(bit(which) == mine)
                def _():
                    for t in range(16):
                        block, third = divmod(r * 16 + t, RATE)
                        place = (block >> 3, block >> 2 & 1, block >> (1 - which) & 1)
                        ref = kept_ref if block >> which & 1 == mine else sent_ref
                        ref[place + (slice(third * fine, (third + 1) * fine),)] = total[
                            t * fine : (t + 1) * fine, which * quarter : (which + 1) * quarter
                        ]
    for away, _ in moves:
        away.wait_send()
    for move in outs + news:
        move.wait()


def front(resets, inputs, memory, compressed, out_grad, w_compress, comp_grad):
    streams, half, width = inputs.shape
    anywhere = pl.BlockSpec(memory_space=pl.ANY)
    vmem = pl.BlockSpec(memory_space=pltpu.VMEM)
    pair = jax.ShapeDtypeStruct((2, 2, half, width), BF16)
    padded = -(-comp_grad.shape[1] // 16) * 16
    part = jax.ShapeDtypeStruct((2, 2, 2, RATE * width // 16, width // 4), BF16)
    return pl.pallas_call(
        front_kernel,
        out_shape=(
            pair, pair, pair, pair, jax.ShapeDtypeStruct((streams, padded, width), BF16),
            part, part, part, part,
        ),
        in_specs=[pl.BlockSpec(memory_space=pltpu.SMEM)] + [anywhere] * 5 + [vmem],
        out_specs=(anywhere,) * 5 + (vmem,) * 4,
        scratch_shapes=[
            pltpu.VMEM((2, 2, half, width), BF16),
            pltpu.VMEM((2, 2, half, width), BF16),
            pltpu.VMEM((2, 2, half, width), BF16),
            pltpu.VMEM((2, 2, half, width), BF16),
            pltpu.VMEM(w_compress.shape, BF16),
            pltpu.VMEM((2, padded, width), BF16),
            pltpu.VMEM((RATE, width, width // 2), BF16),
            pltpu.VMEM((RATE, width, width // 2), BF16),
            pltpu.SemaphoreType.DMA((3, 4, 2)),
            pltpu.SemaphoreType.DMA,
            pltpu.SemaphoreType.DMA((3, 2)),
            pltpu.SemaphoreType.DMA((2, RATE)),
            pltpu.SemaphoreType.DMA((4,)),
        ],
        compiler_params=pltpu.CompilerParams(
            vmem_limit_bytes=VMEM_LIMIT, collective_id=4, has_side_effects=True
        ),
        cost_estimate=cost(12e9, 24e6),
        name="front",
    )(resets, inputs, memory, compressed, out_grad, w_compress, comp_grad)


def project_kernel(
    resets_ref, offsets_ref, old_ref, mem_ref, in_ref, og_ref, gain_ref, wq_hbm, wk_hbm, wv_hbm,
    raw_ref, normed_ref, q_ref, k_ref, v_ref, og_out_ref,
    wq_ref, wk_ref, wv_ref, sems,
):
    step = pl.program_id(0)
    weights = [
        pltpu.make_async_copy(src, dst, sems.at[n])
        for n, (src, dst) in enumerate(((wk_hbm, wk_ref), (wv_hbm, wv_ref), (wq_hbm, wq_ref)))
    ]

    @pl.when(step == 0)
    def _():
        for copy in weights:
            copy.start()

    half, width = in_ref.shape[1:]
    size = 2 * half // 2
    for n in range(2):
        at = slice(n * size, (n + 1) * size)
        pick = lambda ref: ref[...].reshape(2 * half, width)[at]
        raw = jnp.where(step == 0, pick(old_ref), jnp.where(step == 1, pick(mem_ref), pick(in_ref)))
        raw_ref[at] = raw
        unit, _ = norm_parts(raw.astype(F32))
        normed_ref[at] = (unit * gain_ref[...]).astype(BF16)
        if n == 0:

            @pl.when(step == 0)
            def _():
                for copy in weights[:2]:
                    copy.wait()

        k_ref[at] = dot(normed_ref[at], wk_ref[...]).astype(BF16)
        v_ref[at] = dot(normed_ref[at], wv_ref[...]).astype(BF16)

    @pl.when(step == 2)
    def _():
        weights[2].wait()

    @pl.when(step >= 2)
    def _():
        q_ref[...] = dot(normed_ref[...], wq_ref[...]).astype(BF16)
        og_out_ref[...] = og_ref[...].reshape(og_out_ref.shape)


def project_rows(resets, offsets, old, mem, inputs, og, gain, wq, wk, wv):
    _, _, half, width = inputs.shape
    seg = 2 * half

    def from_pair(first):
        def index(i, resets_ref, offsets_ref):
            slots = first_slots(resets_ref, offsets_ref, lax.axis_index("seq"), 2 * seg)
            stream_a = jnp.where(slots[0] >= 2 * seg, 1, 0)
            return jnp.where(i < first + 1, stream_a, 1 - stream_a), 0, 0, 0

        return pl.BlockSpec((None, 2, half, width), index)

    keys = pl.BlockSpec((seg, width), lambda i, *_: (i, 0))
    rows = pl.BlockSpec((seg, width), lambda i, *_: (jnp.maximum(i - 2, 0), 0))
    key_shape = jax.ShapeDtypeStruct((4 * seg, width), BF16)
    row_shape = jax.ShapeDtypeStruct((2 * seg, width), BF16)
    anywhere = pl.BlockSpec(memory_space=pl.ANY)
    return pl.pallas_call(
        project_kernel,
        out_shape=(key_shape, key_shape, row_shape, key_shape, key_shape, row_shape),
        grid_spec=pltpu.PrefetchScalarGridSpec(
            num_scalar_prefetch=2,
            grid=(4,),
            in_specs=[
                from_pair(4), from_pair(4), from_pair(2), from_pair(2),
                held(gain.shape), anywhere, anywhere, anywhere,
            ],
            out_specs=(keys, keys, rows, keys, keys, rows),
            scratch_shapes=[
                pltpu.VMEM(wq.shape, BF16),
                pltpu.VMEM(wk.shape, BF16),
                pltpu.VMEM(wv.shape, BF16),
                pltpu.SemaphoreType.DMA((3,)),
            ],
        ),
        compiler_params=params(),
        cost_estimate=cost(14e9, 30e6),
        name="project",
    )(resets, offsets, old, mem, inputs, og, gain, wq, wk, wv)


def attn_fwd_kernel(
    resets_ref, offsets_ref, q_ref, k_ref, v_ref, in_ref, wo_ref, gain_ref, kept_p_ref, got_p_ref, kept_q_ref, got_q_ref,
    mixed_ref, hidden_ref, ffn_ref, lse_ref, compress_ref,
    packed, *scratch,
):
    step = pl.program_id(0)
    lands, chip_sems = scratch[:-1], scratch[-1]
    place = mesh_place()
    half = q_ref.shape[0]
    seg = 2 * half
    first_slot = stream_a_slot(resets_ref, offsets_ref, place[0], 2 * seg)
    chunks = [
        Chunk(
            packed.at[which],
            tuple(b for b in BITS if b != ORDERS[which][0]),
            ORDERS[which][1:2],
            lands[which : which + 1],
            chip_sems.at[which],
            place,
        )
        for which in range(2)
    ]

    @pl.when(step == 0)
    def _():
        greet(tuple({"dp": place[2](b)} for b in range(2)))
        packed[0] = add_low(kept_p_ref[...], got_p_ref[...])
        packed[1] = add_low(kept_q_ref[...], got_q_ref[...])
        for part in chunks:
            part.start(0)

    def run(pieces):
        def one_head(h, stats):
            cols = pl.ds(pl.multiple_of(h * HEAD_DIM, HEAD_DIM), HEAD_DIM)
            q = q_ref[:, cols]
            scores = []
            for start, size, kind in pieces:
                s = dot(q, k_ref[start : start + size, cols], NT)
                if kind == "mem":
                    slot = lax.broadcasted_iota(jnp.int32, s.shape, 1)
                    s = jnp.where(slot >= first_slot, s, masked_score)
                if kind == "diag":
                    key = lax.broadcasted_iota(jnp.int32, s.shape, 1)
                    row = lax.broadcasted_iota(jnp.int32, s.shape, 0)
                    s = jnp.where(key <= row, s, masked_score)
                scores.append(s)
            top = functools.reduce(
                jnp.maximum, [jnp.max(s, axis=-1, keepdims=True) for s in scores]
            ) * EXP2_SCALE
            mix = jnp.zeros((half, 2 * HEAD_DIM), F32)
            for s, (start, size, _) in zip(scores, pieces):
                p = jnp.exp2(s * EXP2_SCALE - top).astype(BF16)
                ones = jnp.ones((size, HEAD_DIM), BF16)
                mix = mix + dot(p, jnp.concatenate([v_ref[start : start + size, cols], ones], axis=1))
            total = mix[:, HEAD_DIM:]
            mixed_ref[:, cols] = (mix[:, :HEAD_DIM] / total).astype(BF16)
            lane = lax.broadcasted_iota(jnp.int32, stats.shape, 1)
            return jnp.where(lane == h, top + jnp.log2(total), stats)

        stats = lax.fori_loop(0, HEADS, one_head, jnp.zeros((half, 128), F32), unroll=True)
        lse_ref[...] = stats.T[:HEADS]

    cases = (
        ((0, 2 * seg, "mem"), (2 * seg, half, "diag")),
        ((0, 2 * seg, "mem"), (2 * seg, half, "full"), (2 * seg + half, half, "diag")),
        ((3 * seg, half, "diag"),),
        ((3 * seg, half, "full"), (3 * seg + half, half, "diag")),
    )
    for i, pieces in enumerate(cases[2:] + cases[:2]):
        pl.when(step == i)(functools.partial(run, pieces))
    hidden = in_ref[...].astype(F32) + dot(mixed_ref[...], wo_ref[...])
    hidden_ref[...] = hidden
    unit, _ = norm_parts(hidden)
    ffn_ref[...] = (unit * gain_ref[...]).astype(BF16)

    @pl.when(step == 3)
    def _():
        for which, part in enumerate(chunks):
            part.settle(0)
            compress_ref[which] = packed[(which,) + part.rest(1)]


def attn_fwd(resets, offsets, q, k, v, raw, wo, gain, kept_p, got_p, kept_q, got_q):
    rows, width = q.shape
    half = rows // 4
    by_block = pl.BlockSpec((half, width), lambda i: (lax.rem(i + 2, 4), 0))
    in_block = pl.BlockSpec((half, width), lambda i: (4 + lax.rem(i + 2, 4), 0))
    block = kept_p.shape[-2:]
    part = held(kept_p.shape)
    lands = []
    for which in range(2):
        lands += landings(BITS[1:], ORDERS[which][1:2], block)
    out = (2, 2, 2) + block
    return pl.pallas_call(
        attn_fwd_kernel,
        grid=(4,),
        out_shape=(
            jax.ShapeDtypeStruct((rows, width), BF16),
            jax.ShapeDtypeStruct((rows, width), F32),
            jax.ShapeDtypeStruct((rows, width), BF16),
            jax.ShapeDtypeStruct((HEADS, rows), F32),
            jax.ShapeDtypeStruct(out, BF16),
        ),
        in_specs=[
            pl.BlockSpec(memory_space=pltpu.SMEM),
            pl.BlockSpec(memory_space=pltpu.SMEM),
            by_block, held(k.shape), held(v.shape), in_block, held(wo.shape), held(gain.shape),
            part, part, part, part,
        ],
        out_specs=(
            by_block, by_block, by_block, pl.BlockSpec((HEADS, half), lambda i: (0, lax.rem(i + 2, 4))), held(out),
        ),
        scratch_shapes=[pltpu.VMEM((2,) + kept_p.shape, BF16)] + lands + [pltpu.SemaphoreType.DMA((2, 2, 1))],
        compiler_params=pltpu.CompilerParams(
            vmem_limit_bytes=VMEM_LIMIT, dimension_semantics=("arbitrary",),
            collective_id=5, has_side_effects=True,
        ),
        cost_estimate=cost(20e9, 20e6),
        name="attn_fwd",
    )(resets, offsets, q, k, v, raw, wo, gain, kept_p, got_p, kept_q, got_q)


GELU_C = math.sqrt(2.0 / math.pi)
GELU_A = 0.044715
CHUNK = 512


def gelu_pair(pre, act_grad):
    square = pre * pre
    t = jnp.tanh(pre * (GELU_C + (GELU_C * GELU_A) * square))
    cdf = 0.5 + 0.5 * t
    slope = cdf + (0.5 * pre) * (1.0 - t * t) * (GELU_C + (3.0 * GELU_C * GELU_A) * square)
    return (pre * cdf).astype(BF16), (act_grad * slope).astype(BF16)


def ffn_kernel(
    x_ref, og_ref, gain_ref, packed_ref, hidden_hbm, wo_hbm, wh0_ref, wh1_ref, wr0_ref, wr1_ref,
    out_ref, attn_grad_ref, do_ref, gain_grad_ref, done_ref, part_ref, raw_ref, compress_ref,
    hidden_ref, wo_ref, held_sems, pack0, pack1, pack_sems, wh, wr, out_acc, in_acc, act_ref, pre_ref, core_out, core_in, own_ref, land0, land1, land2, land3,
    weight_sems, core_sems, chip_sems,
):
    step = pl.program_id(0)
    last = pl.num_programs(0) - 1
    index = lax.div(step, 2)
    end = lax.div(last, 2)
    owned = lax.rem(step, 2) == 1
    rows, width = x_ref.shape
    units = wh.shape[2]
    chunks = rows // CHUNK
    place = mesh_place()
    core, _, across = place
    partner = {"seq": 1 - core}

    def fetch(at, side):
        cols = pl.ds(pl.multiple_of(at * units, units), units)
        wh_ref, wr_ref = ((wh0_ref, wr0_ref), (wh1_ref, wr1_ref))[side]
        return (
            pltpu.make_async_copy(wh_ref.at[:, cols], wh.at[side], weight_sems.at[0, side]),
            pltpu.make_async_copy(wr_ref.at[cols], wr.at[side], weight_sems.at[1, side]),
        )

    held_copies = (
        pltpu.make_async_copy(hidden_hbm, hidden_ref, held_sems.at[0]),
        pltpu.make_async_copy(wo_hbm, wo_ref, held_sems.at[1]),
    )
    packs = [
        Chunk(
            packed_ref.at[which], (3, 2), (2, 3), [pack0.at[which], pack1.at[which]],
            pack_sems.at[which], place,
        )
        for which in range(2)
    ]

    @pl.when(step == 0)
    def _():
        for copy in fetch(0, 0) + held_copies:
            copy.start()
        greet((partner,) + tuple({"dp": across(b)} for b in range(4)))
        for part in packs:
            part.start(0)
        out_acc[...] = jnp.zeros_like(out_acc)
        in_acc[...] = jnp.zeros_like(in_acc)

    @pl.when(step == 2)
    def _():
        for part in packs:
            part.settle(0)
            part.start(1)

    @pl.when(step == 4)
    def _():
        cols = compress_ref.shape[1] // 2
        for which, part in enumerate(packs):
            compress_ref[:, which * cols : (which + 1) * cols] = part.last(1)

    @pl.when(jnp.logical_not(owned))
    def _():
        for copy in fetch(index, 1):
            copy.start()
        for copy in fetch(index, 0):
            copy.wait()

    @pl.when(owned)
    def _():
        @pl.when(index < end)
        def _():
            for copy in fetch(index + 1, 0):
                copy.start()

        for copy in fetch(index, 1):
            copy.wait()

    def core_copy(which, index):
        return remote(
            core_out.at[which],
            core_in.at[which, lax.rem(index, 2)],
            (core_sems.at[0, which, index], core_sems.at[1, which, index]),
            partner,
        )

    def tile(which, index):
        return Chunk(
            own_ref.at[which, index], BITS, ORDERS[which],
            [land.at[which, index] for land in (land0, land1, land2, land3)],
            chip_sems.at[which, index], place,
        )

    def pass_on(index, swap):
        for which in range(2):
            part = tile(which, index)
            part.settle(swap)
            part.start(swap + 1)

    def finish_tile(index):
        for which in range(2):
            done_ref[which, index] = tile(which, index).last(3)

    side = lax.rem(step, 2)

    def rows_step(m, _):
        at = pl.ds(pl.multiple_of(m * CHUNK, CHUNK), CHUNK)
        pre = dot(x_ref[at, :], wh[side])
        act_grad = dot(og_ref[at, :], wr[side], NT)
        act, pre_grad = gelu_pair(pre, act_grad)
        act_ref[at, :] = act
        pre_ref[at, :] = pre_grad
        out_acc[at, :] += dot(act, wr[side])
        in_acc[at, :] += dot(pre_grad, wh[side], NT)

        return 0

    lax.fori_loop(0, chunks, rows_step, 0)

    @pl.when(owned & (index > 0))
    def _():
        pass_on(index - 1, 0)

    @pl.when(owned & (index > 1))
    def _():
        pass_on(index - 2, 2)

    @pl.when(jnp.logical_not(owned) & (index > 1))
    def _():
        pass_on(index - 2, 1)

    @pl.when(jnp.logical_not(owned) & (index > 2))
    def _():
        finish_tile(index - 3)

    for which, (left_ref, right_ref) in enumerate(((x_ref, pre_ref), (og_ref, act_ref))):
        grad = dot(left_ref[...], right_ref[...], TN)

        @pl.when(jnp.logical_not(owned))
        def _():
            @pl.when(index > 0)
            def _():
                core_copy(which, index - 1).wait_send()

            core_out[which] = grad.astype(BF16)
            core_copy(which, index).start()

        @pl.when(owned)
        def _():
            core_copy(which, index).wait_recv()
            total = grad + core_in[which, lax.rem(index, 2)].astype(F32)
            total = total.astype(BF16).reshape(own_ref.shape[2:])

            @pl.when(index < end)
            def _():
                own_ref[which, index] = total
                tile(which, index).start(0)

            @pl.when(index == end)
            def _():
                raw_ref[which] = total

    @pl.when(step == last)
    def _():
        for copy in held_copies:
            copy.wait()

        def finish(m, gain_sum):
            at = pl.ds(pl.multiple_of(m * 256, 256), 256)
            hidden = hidden_ref[at, :]
            out_ref[at, :] = (hidden + out_acc[at, :]).astype(BF16)
            unit, inverse = norm_parts(hidden)
            grad = in_acc[at, :]
            hidden_grad = og_ref[at, :].astype(F32) + norm_back(
                grad * gain_ref[...], unit, inverse
            )
            low = hidden_grad.astype(BF16)
            attn_grad_ref[at, :] = low
            do_ref[at, :] = dot(low, wo_ref[...], NT).astype(BF16)
            return gain_sum + jnp.sum(grad * unit, axis=0, keepdims=True)

        gain_grad_ref[...] = lax.fori_loop(
            0, rows // 256, finish, jnp.zeros(gain_grad_ref.shape, F32)
        )
        finish_tile(end - 2)
        for which in range(2):
            core_copy(which, end).wait_send()
            part = tile(which, end - 1)
            part.settle(1)
            part_ref[which] = part.data[part.rest(2)]


def ffn(x, og, gain, packed, hidden, wo, wh0, wh1, wr0, wr1):
    rows, width = x.shape
    units = wh0.shape[1]
    tile = 512
    steps = units // tile
    count = lax.axis_size("dp")
    block = width // count
    anywhere = pl.BlockSpec(memory_space=pl.ANY)
    whole = held((rows, width))
    low_rows = jax.ShapeDtypeStruct((rows, width), BF16)
    raw = (2, 2, 2, 2, 2, block, tile)
    part = (2, 2, 2, block, tile)
    done = (2, steps - 2, block, tile)
    tiles = (2, steps - 1)
    lands = [pltpu.VMEM(tiles + (2,) * n + (block, tile), BF16) for n in (3, 2, 1, 0)]
    pack = packed.shape[-2:]
    compress = (pack[0], 2 * pack[1])
    return pl.pallas_call(
        ffn_kernel,
        grid=(2 * steps,),
        out_shape=(
            low_rows, low_rows, low_rows, jax.ShapeDtypeStruct((1, width), F32),
            jax.ShapeDtypeStruct(done, F32),
            jax.ShapeDtypeStruct(part, BF16),
            jax.ShapeDtypeStruct(raw, BF16),
            jax.ShapeDtypeStruct(compress, F32),
        ),
        in_specs=[whole, whole, held(gain.shape), held(packed.shape)] + [anywhere] * 6,
        out_specs=(whole, whole, whole, held((1, width)), held(done), held(part), held(raw), held(compress)),
        scratch_shapes=[
            pltpu.VMEM((rows, width), F32),
            pltpu.VMEM(wo.shape, BF16),
            pltpu.SemaphoreType.DMA((2,)),
            pltpu.VMEM((2, 2) + pack, BF16),
            pltpu.VMEM((2,) + pack, BF16),
            pltpu.SemaphoreType.DMA((2, 2, 2)),
            pltpu.VMEM((2, width, tile), BF16),
            pltpu.VMEM((2, tile, width), BF16),
            pltpu.VMEM((rows, width), F32),
            pltpu.VMEM((rows, width), F32),
            pltpu.VMEM((rows, tile), BF16),
            pltpu.VMEM((rows, tile), BF16),
            pltpu.VMEM((2, width, tile), BF16),
            pltpu.VMEM((2, 2, width, tile), BF16),
            pltpu.VMEM(tiles + raw[1:], BF16),
        ] + lands + [
            pltpu.SemaphoreType.DMA((2, 2)),
            pltpu.SemaphoreType.DMA((2, 2, steps)),
            pltpu.SemaphoreType.DMA((2, steps, 2, 4)),
        ],
        compiler_params=pltpu.CompilerParams(
            vmem_limit_bytes=VMEM_LIMIT, dimension_semantics=("arbitrary",),
            collective_id=1, has_side_effects=True,
        ),
        cost_estimate=cost(75e9, 50e6),
        name="ffn",
    )(x, og, gain, packed, hidden, wo, wh0, wh1, wr0, wr1)


def attn_bwd_head(first_slot, q_ref, k_ref, v_ref, do_ref, mixed_ref, lse, dq_ref, dk_ref, dv_ref, cols):
    seg = q_ref.shape[0] // 2
    half = seg // 2
    for stream in range(2):
        base = stream * seg
        rows = slice(base, base + seg)
        lse_row = lse[:, rows]
        weight = do_ref[rows, cols].astype(F32) * mixed_ref[rows, cols].astype(F32)
        delta_row = jnp.sum(weight.T, axis=0, keepdims=True)
        key_base = 2 * seg + stream * seg
        pieces = []
        if stream == 0:
            pieces += [(start, half, 0, "mem") for start in range(0, 2 * seg, half)]
        pieces += [(key_base, half, 0, "diag"), (key_base + half, half, half, "diag")]
        dq_low = jnp.zeros((half, HEAD_DIM), F32)
        dq_high = jnp.zeros((half, HEAD_DIM), F32)
        for start, size, first, kind in pieces:
            q = q_ref[base + first : base + seg, cols]
            do = do_ref[base + first : base + seg, cols]
            k = k_ref[start : start + size, cols]
            s = dot(k, q, NT) * EXP2_SCALE - lse_row[:, first:]
            if kind == "mem":
                slot = start + lax.broadcasted_iota(jnp.int32, s.shape, 0)
                s = jnp.where(slot >= first_slot, s, masked_score)
            else:
                key = lax.broadcasted_iota(jnp.int32, s.shape, 0)
                row = lax.broadcasted_iota(jnp.int32, s.shape, 1)
                s = jnp.where(key <= row, s, masked_score)
            p = jnp.exp2(s)
            dp = dot(v_ref[start : start + size, cols], do, NT)
            ds = (p * (dp - delta_row[:, first:])).astype(BF16)
            dv_ref[start : start + size, cols] = dot(p.astype(BF16), do).astype(BF16)
            dk_ref[start : start + size, cols] = (dot(ds, q) * SCALE).astype(BF16)
            dq = dot(ds, k, TN)
            if first == 0:
                dq_low = dq_low + dq[:half]
                dq_high = dq_high + dq[half:]
            else:
                dq_high = dq_high + dq
        dq_ref[base : base + half, cols] = (dq_low * SCALE).astype(BF16)
        dq_ref[base + half : base + seg, cols] = (dq_high * SCALE).astype(BF16)


def attn_back_kernel(
    resets_ref, offsets_ref, q_ref, k_ref, v_ref, do_ref, mix_ref, lse_ref, normed_hbm, mixed_hbm, ag_ref,
    ffn_part_ref, ffn_raw_ref,
    dq_ref, dk_ref, dv_ref, early_ref, late_ref, ffn_done_ref,
    normed_ref, mixed_ref, held_sems, grads_ref, core_out0, core_in0, core_out1, core_in1, own_ref,
    *scratch,
):
    step = pl.program_id(0)
    last = pl.num_programs(0) - 1
    place = mesh_place()
    core, _, across = place
    partner = {"seq": 1 - core}
    lands, (core_sems, chip_sems) = list(scratch[:-2]), scratch[-2:]
    chunks, ffn_parts, ffn_raws = [], [], []
    first_slot = stream_a_slot(resets_ref, offsets_ref, core, q_ref.shape[0])
    held_copies = (
        pltpu.make_async_copy(normed_hbm, normed_ref, held_sems.at[0]),
        pltpu.make_async_copy(mixed_hbm, mixed_ref, held_sems.at[1]),
    )

    def chunk(number, data, left, order):
        mine = [lands.pop(0) for _ in order]
        return Chunk(data, left, order, mine, chip_sems.at[number], place)

    for which in range(2):
        order = ORDERS[which]
        chunks.append(chunk(3 * which, own_ref.at[which], BITS, order[:2]))
        ffn_parts.append(chunk(3 * which + 1, ffn_part_ref.at[which], order[2:][::-1], order[2:]))
        ffn_raws.append(chunk(3 * which + 2, ffn_raw_ref.at[which], BITS, order))
    index = lax.div(step, 2)
    rows = q_ref.shape[0]
    keys = k_ref.shape[0]
    pair = q_ref.shape[1]

    @pl.when(step == 0)
    def _():
        for copy in held_copies:
            copy.start()
        greet((partner,) + tuple({"dp": across(b)} for b in range(4)))
        for part in ffn_raws + ffn_parts:
            part.start(0)

    @pl.when(step == 1)
    def _():
        for part in ffn_parts:
            part.settle(0)
            part.start(1)

    @pl.when(step == 2)
    def _():
        for which in range(2):
            ffn_done_ref[which, 0] = ffn_parts[which].last(1)

    crossing = ((core_out0, core_in0), (core_out1, core_in1))

    def core_copy(which, index):
        sent, got = crossing[index]
        return remote(
            sent.at[which],
            got.at[which],
            (core_sems.at[0, which, index], core_sems.at[1, which, index]),
            partner,
        )

    head = 4 * jnp.where(lax.rem(step, 2) == 0, 1 - core, core) + 2 * index

    def one_head(h, _):
        attn_bwd_head(
            first_slot, q_ref, k_ref, v_ref, do_ref, mix_ref, lse_ref[pl.ds(head + h, 1), :],
            dq_ref, dk_ref, dv_ref, pl.ds(pl.multiple_of(h * HEAD_DIM, HEAD_DIM), HEAD_DIM),
        )
        for n in range(1, 4):

            @pl.when((step == n) & (h == 0))
            def _():
                for part in ffn_raws + (chunks if n == 3 else []):
                    swap = 0 if part in chunks else n - 1
                    part.settle(swap)
                    part.start(swap + 1)

        return 0

    lax.fori_loop(0, 2, one_head, 0)

    @pl.when(step == 0)
    def _():
        for copy in held_copies:
            copy.wait()

    less = pair + pair // 2
    grads_ref[0, :, :pair] = dot(normed_ref[keys - rows :], dq_ref[...], TN)
    grads_ref[1, :, :pair] = dot(normed_ref[...], dv_ref[...], TN)
    key_grads = dot(normed_ref[...], dk_ref[...], TN)
    grads_ref[0, :, pair:less] = key_grads[:, : pair // 2]
    grads_ref[1, :, pair:less] = key_grads[:, pair // 2 :]

    @pl.when(step < 2)
    def _():
        output_grads = dot(mixed_ref[...], ag_ref[...], TN)
        grads_ref[0, :, less:] = output_grads[:, :pair]
        grads_ref[1, :, less:] = output_grads[:, pair:]

    for n in range(2):

        @pl.when(step == 2 * n)
        def _():
            sent = crossing[n][0]
            for which in range(2):
                sent[which] = grads_ref[which, :, : sent.shape[2]].astype(BF16)
                core_copy(which, n).start()

    def own_grads(which, index, out_ref):
        core_copy(which, index).wait()
        got = crossing[index][1]
        total = grads_ref[which, :, : got.shape[2]] + got[which].astype(F32)
        out_ref[...] = total.astype(BF16).reshape(out_ref.shape)

    @pl.when(step == 1)
    def _():
        for which in range(2):
            own_grads(which, 0, own_ref.at[which])
            chunks[which].start(0)

    @pl.when(step == last)
    def _():
        for which in range(2):
            own_grads(which, 1, late_ref.at[which])
        for which in range(2):
            chunks[which].settle(1)
            early_ref[which] = own_ref[(which,) + chunks[which].rest(2)]
            ffn_done_ref[which, 1] = ffn_raws[which].last(3)


def attn_back(resets, offsets, q, k, v, do, mixed, lse, normed, attn_grad, ffn_part, ffn_raw):
    rows, width = q.shape
    keys = k.shape[0]
    pair = 2 * HEAD_DIM
    more, less = 2 * pair + pair // 2, pair + pair // 2
    block = (width // 16, more)

    def by_pair(count):
        def index(i):
            core = lax.axis_index("seq")
            half = jnp.where(lax.rem(i, 2) == 0, 1 - core, core)
            return 0, 2 * half + lax.div(i, 2)

        return pl.BlockSpec((count, pair), index)

    def output_half(i):
        core = lax.axis_index("seq")
        return 0, jnp.where(i == 0, 1 - core, core)

    early, late = (2, 2, 2) + block, (2, 2, 2, 2, 2, width // 16, less)
    ffn_block = ffn_raw.shape[-2:]
    done = (2, 2) + ffn_block
    lands = []
    for order in ORDERS:
        lands += landings(BITS, order[:2], block)
        lands += landings(order[2:], order[2:], ffn_block)
        lands += landings(BITS, order, ffn_block)
    return pl.pallas_call(
        attn_back_kernel,
        grid=(4,),
        out_shape=(
            jax.ShapeDtypeStruct((rows, width), BF16),
            jax.ShapeDtypeStruct((keys, width), BF16),
            jax.ShapeDtypeStruct((keys, width), BF16),
            jax.ShapeDtypeStruct(early, BF16),
            jax.ShapeDtypeStruct(late, BF16),
            jax.ShapeDtypeStruct(done, F32),
        ),
        in_specs=[
            pl.BlockSpec(memory_space=pltpu.SMEM),
            pl.BlockSpec(memory_space=pltpu.SMEM),
            by_pair(rows), by_pair(keys), by_pair(keys), by_pair(rows), by_pair(rows),
            held(lse.shape), pl.BlockSpec(memory_space=pl.ANY), pl.BlockSpec(memory_space=pl.ANY),
            pl.BlockSpec((rows, 2 * pair), output_half),
            held(ffn_part.shape), held(ffn_raw.shape),
        ],
        out_specs=(by_pair(rows), by_pair(keys), by_pair(keys), held(early), held(late), held(done)),
        scratch_shapes=[
            pltpu.VMEM(normed.shape, BF16),
            pltpu.VMEM(mixed.shape, BF16),
            pltpu.SemaphoreType.DMA((2,)),
            pltpu.VMEM((2, width, more), F32),
            pltpu.VMEM((2, width, more), BF16),
            pltpu.VMEM((2, width, more), BF16),
            pltpu.VMEM((2, width, less), BF16),
            pltpu.VMEM((2, width, less), BF16),
            pltpu.VMEM((2, 2, 2, 2, 2) + block, BF16),
        ] + lands + [
            pltpu.SemaphoreType.DMA((2, 2, 2)),
            pltpu.SemaphoreType.DMA((6, 2, 4)),
        ],
        compiler_params=pltpu.CompilerParams(
            vmem_limit_bytes=VMEM_LIMIT, dimension_semantics=("arbitrary",),
            collective_id=2, has_side_effects=True,
        ),
        cost_estimate=cost(45e9, 24e6),
        name="attn_back",
    )(resets, offsets, q, k, v, do, mixed, lse, normed, mixed, attn_grad, ffn_part, ffn_raw)


def rows_back_kernel(
    dq_ref, dk_ref, dv_ref, raw_ref, ag_ref, gain_ref, gain_ffn_ref, wq_hbm, wk_hbm, wv_hbm,
    early_ref, late_ref,
    mine_ref, theirs_ref, gains_ref, early_out_ref, late_out_ref,
    wq_ref, wk_ref, wv_ref, weight_sems, rows_out, gain_acc, gain_out, gain_in, *scratch,
):
    step = pl.program_id(0)
    last = pl.num_programs(0) - 1
    place = mesh_place()
    core, _, across = place
    partner = {"seq": 1 - core}
    lands, (row_sems, local_sems, gain_sems, chip_sems) = list(scratch[:-4]), scratch[-4:]

    chunks = []

    def chunk(data, left, order):
        number = len(chunks)
        mine = [lands.pop(0) for _ in order]
        chunks.append(Chunk(data, left, order, mine, chip_sems.at[number], place))
        return chunks[-1]

    early, late = [], []
    for which in range(2):
        early.append(chunk(early_ref.at[which], BITS[:2], ORDERS[which][2:]))
        late.append(chunk(late_ref.at[which], BITS, ORDERS[which]))

    rank = lax.axis_index("dp")

    def flipped(n, bits):
        return rank + sum(across(b) - rank for i, b in enumerate(bits) if n >> i & 1)

    gain_groups = (
        [{"dp": flipped(n >> 1, (0, 1)), "seq": 1 - core if n & 1 else core} for n in range(1, 8)],
        [{"dp": flipped(n, (2, 3))} for n in range(1, 4)],
    )

    def gain_copies(stage):
        first = 7 * stage
        return [
            remote(
                gain_out.at[stage],
                gain_in.at[first + n],
                (gain_sems.at[0, first + n], gain_sems.at[1, first + n]),
                device,
            )
            for n, device in enumerate(gain_groups[stage])
        ]

    def gain_total(stage):
        for copy in gain_copies(stage):
            copy.wait()
        return gain_out[stage] + sum(gain_in[7 * stage + n] for n in range(len(gain_groups[stage])))

    def row_copy(block):
        stream = block // 2
        return remote(
            rows_out.at[block], theirs_ref.at[stream], (row_sems.at[0, stream], row_sems.at[1, stream]), partner
        )

    def row_keep(block):
        stream = block // 2
        return pltpu.make_async_copy(rows_out.at[block], mine_ref.at[stream], local_sems.at[stream])

    weights = [
        pltpu.make_async_copy(src, dst, weight_sems.at[n])
        for n, (src, dst) in enumerate(((wk_hbm, wk_ref), (wv_hbm, wv_ref), (wq_hbm, wq_ref)))
    ]

    @pl.when(step == 0)
    def _():
        for copy in weights:
            copy.start()
        greet(gain_groups[0] + gain_groups[1])
        for part in late + early:
            part.start(0)
        for copy in weights[:2]:
            copy.wait()
        gain_acc[...] = jnp.zeros_like(gain_acc)

    def normed_grad():
        return dot(dk_ref[...], wk_ref[...], NT) + dot(dv_ref[...], wv_ref[...], NT)

    unit, inverse = norm_parts(raw_ref[...].astype(F32))

    @pl.when(step < 4)
    def _():
        gain_acc[0:1] += jnp.sum(normed_grad() * unit, axis=0, keepdims=True)

    @pl.when(step == 4)
    def _():
        weights[2].wait()

    @pl.when(step >= 4)
    def _():
        grad = normed_grad() + dot(dq_ref[...], wq_ref[...], NT)
        gain_acc[0:1] += jnp.sum(grad * unit, axis=0, keepdims=True)
        rows_grad = norm_back(grad * gain_ref[...], unit, inverse)
        rows_out[step - 4] = (rows_grad + ag_ref[...].astype(F32)).astype(BF16)

    for block in range(4):
        stays = core == block % 2
        pl.when((step == block + 4) & stays)(row_keep(block).start)
        pl.when((step == block + 4) & jnp.logical_not(stays))(row_copy(block).start)

    @pl.when(step == 4)
    def _():
        for part in early:
            part.settle(0)
            part.start(1)

    @pl.when(step == 5)
    def _():
        for part in late:
            part.settle(0)
            part.start(1)

    @pl.when(step == last)
    def _():
        lanes = gain_out.shape[2]
        for n in range(8):
            cols = slice(n * lanes, (n + 1) * lanes)
            gain_out[0, n : n + 1] = gain_acc[0:1, cols]
            gain_out[0, 8 + n : 9 + n] = gain_ffn_ref[:, cols]
        for copy in gain_copies(0):
            copy.start()
        for which in range(2):
            early_out_ref[which] = early[which].last(1)
        for part in late:
            part.settle(1)
            part.start(2)
        gain_out[1] = gain_total(0)
        for copy in gain_copies(1):
            copy.start()
        for part in late:
            part.settle(2)
            part.start(3)
        gains_ref[...] = gain_total(1)
        for which in range(2):
            late_out_ref[which] = late[which].last(3)
        for block in range(4):
            stays = core == block % 2
            pl.when(stays)(row_keep(block).wait)
            pl.when(jnp.logical_not(stays))(row_copy(block).wait_send)
        for stream in range(2):
            row_copy(2 * stream).wait_recv()


def rows_back(
    dq, dk, dv, raw, attn_grad, gain, gain_ffn, wq, wk, wv, early, late
):
    keys, width = dk.shape
    rows = dq.shape[0]
    size = keys // 8
    key_block = pl.BlockSpec((size, width), lambda i: (i, 0))
    row_block = pl.BlockSpec((size, width), lambda i: (jnp.maximum(i - 4, 0), 0))
    anywhere = pl.BlockSpec(memory_space=pl.ANY)
    rows_shape = jax.ShapeDtypeStruct((2, size, width), BF16)
    early_block, late_block = early.shape[-2:], late.shape[-2:]
    lands = []
    for order in ORDERS:
        lands += landings(BITS[:2], order[2:], early_block)
        lands += landings(BITS, order, late_block)
    early_out, late_out = (2,) + early_block, (2,) + late_block
    vector = (16, width // 8)
    return pl.pallas_call(
        rows_back_kernel,
        grid=(8,),
        out_shape=(
            rows_shape, rows_shape,
            jax.ShapeDtypeStruct(vector, F32),
            jax.ShapeDtypeStruct(early_out, F32),
            jax.ShapeDtypeStruct(late_out, F32),
        ),
        in_specs=[
            row_block, key_block, key_block, key_block, row_block,
            held(gain.shape), held(gain_ffn.shape), anywhere, anywhere, anywhere,
            held(early.shape), held(late.shape),
        ],
        out_specs=(
            anywhere, anywhere, held(vector), held(early_out), held(late_out),
        ),
        scratch_shapes=[
            pltpu.VMEM(wq.shape, BF16),
            pltpu.VMEM(wk.shape, BF16),
            pltpu.VMEM(wv.shape, BF16),
            pltpu.SemaphoreType.DMA((3,)),
            pltpu.VMEM((4, size, width), BF16),
            pltpu.VMEM((8, width), F32),
            pltpu.VMEM((2,) + vector, F32),
            pltpu.VMEM((10,) + vector, F32),
        ] + lands + [
            pltpu.SemaphoreType.DMA((2, 2)),
            pltpu.SemaphoreType.DMA((2,)),
            pltpu.SemaphoreType.DMA((2, 10)),
            pltpu.SemaphoreType.DMA((4, 2, 4)),
        ],
        compiler_params=pltpu.CompilerParams(
            vmem_limit_bytes=VMEM_LIMIT, dimension_semantics=("arbitrary",),
            collective_id=3, has_side_effects=True,
        ),
        cost_estimate=cost(20e9, 24e6),
        name="rows_back",
    )(
        dq, dk, dv, raw, attn_grad, gain, gain_ffn, wq, wk, wv,
        early, late,
    )


def swap_dp(block, bit):
    count = lax.axis_size("dp")
    return lax.ppermute(block, "dp", [(i, i ^ (1 << bit)) for i in range(count)])


def swap_core(block):
    return lax.ppermute(block, "seq", [(0, 1), (1, 0)])


def on_device_pair(
    inputs, memory, compressed, offsets, resets, w_query, w_key, w_value, w_output, w_hidden,
    w_return, w_compress, gain_attn, gain_ffn, out_grad, comp_grad,
):
    core = lax.axis_index("seq")
    dp_count = lax.axis_size("dp")
    streams, half, width = inputs.shape
    seg = 2 * half
    low_core = core == 0

    unused = (resets != 0) | (offsets >= 2 * seg)
    gain_a = gain_attn.astype(F32).reshape(1, width)
    gain_f = gain_ffn.astype(F32).reshape(1, width)

    x_in, x_mem, x_old, x_og, new_rows, kept_p, sent_p, kept_q, sent_q = front(
        resets, inputs, memory, compressed, out_grad, w_compress, comp_grad
    )
    got_p, got_q = swap_dp(sent_p, 0), swap_dp(sent_q, 1)
    wh_late, wr_late, x_in = lax.optimization_barrier((w_hidden, w_return, x_in))
    wh_other, wr_other = swap_core(wh_late), swap_core(wr_late)
    all_rows, normed, q, k, v, og = project_rows(
        resets, offsets, x_old, x_mem, x_in, x_og, gain_a, w_query, w_key, w_value
    )
    mixed, hidden, ffn_in, lse, packed = attn_fwd(
        resets, offsets, q, k, v, all_rows, w_output, gain_f, kept_p, got_p, kept_q, got_q
    )
    outputs, attn_grad, mixed_grad, gain_ffn_grad, ffn_done, ffn_part, ffn_raw, grad_compress = ffn(
        ffn_in, og, gain_f, packed, hidden, w_output, wh_other, w_hidden, wr_other, w_return
    )
    dq, dk, dv, early, late, ffn_rest = attn_back(
        resets, offsets, q, k, v, mixed_grad, mixed, lse, normed, attn_grad, ffn_part, ffn_raw
    )
    mine_rows, their_rows, gains, early_out, late_out = rows_back(
        dq, dk, dv, all_rows, attn_grad, gain_a, gain_ffn_grad, w_query, w_key, w_value, early, late
    )

    def tiles(which):
        parts = [ffn_done[which, i] for i in range(2)] + [ffn_rest[which, i] for i in range(2)]
        return jnp.concatenate(parts, axis=1)

    grad_hidden, grad_return = tiles(0), tiles(1).T
    pair = 2 * HEAD_DIM
    less = pair + HEAD_DIM
    low, high = slice(0, pair), slice(pair, less)

    def weight_grad(*parts):
        return jnp.concatenate([part[which, :, cols] for part, which, cols in parts], axis=1)

    grad_query = weight_grad((early_out, 0, low), (late_out, 0, low))
    grad_key = weight_grad(
        (early_out, 0, high), (early_out, 1, high), (late_out, 0, high), (late_out, 1, high)
    )
    grad_value = weight_grad((early_out, 1, low), (late_out, 1, low))
    grad_output = weight_grad((early_out, 0, slice(less, None)), (early_out, 1, slice(less, None)))
    rank = lax.axis_index("dp")
    gains = lax.dynamic_slice_in_dim(gains.reshape(2, width), rank * (width // dp_count), width // dp_count, 1)

    def to_streams(a, b, which):
        swapped = lax.dynamic_index_in_dim(unused, which, 0, False)
        return jnp.where(swapped, b, a), jnp.where(swapped, a, b)

    def spread(own_pair, other_pair):
        own = to_streams(own_pair[0], own_pair[1], core)
        other = to_streams(other_pair[0], other_pair[1], 1 - core)
        return jnp.stack(
            [
                jnp.where(low_core, own[0], other[0]),
                jnp.where(low_core, other[0], own[0]),
                jnp.where(low_core, own[1], other[1]),
                jnp.where(low_core, other[1], own[1]),
            ]
        )

    def place_rows(rows):
        halves = rows.reshape(2, 2, half, width)
        return spread(
            lax.dynamic_index_in_dim(halves, core, 1, False),
            swap_core(lax.dynamic_index_in_dim(halves, 1 - core, 1, False)),
        )

    return (
        place_rows(outputs),
        new_rows[:, : comp_grad.shape[1]],
        spread(mine_rows, their_rows),
        grad_query,
        grad_key,
        grad_value,
        grad_output,
        grad_hidden,
        grad_return,
        grad_compress,
        gains[0],
        gains[1],
    )


def solution(mesh):
    placed = (
        P("dp", "seq", None),
        P("dp", "seq", None),
        P("dp", "seq", None),
        P("dp"),
        P("dp"),
        P(),
        P(),
        P(),
        P(),
        P(None, "seq"),
        P("seq", None),
        P(),
        P(),
        P(),
        P("dp", "seq", None),
        P("dp", None, None),
    )
    fast = mesh.shape["seq"] == 2 and mesh.shape["dp"] == 16
    return jax.shard_map(
        on_device_pair if fast else on_device,
        mesh=mesh,
        in_specs=placed,
        out_specs=(
            P("dp", "seq", None),
            P("dp", None, None),
            P("dp", "seq", None),
            P("dp", "seq"),
            P("dp", "seq"),
            P("dp", "seq"),
            P("dp", "seq"),
            P("dp", "seq"),
            P("seq", "dp"),
            P("dp", "seq"),
            P("dp"),
            P("dp"),
        ),
        check_vma=False,
    )
```

```python
import functools
import math

import jax
import jax.numpy as jnp
from jax import lax
from jax.experimental import pallas as pl
from jax.experimental.pallas import tpu as pltpu
from jax.sharding import PartitionSpec as P

HEADS = 8
HEAD_DIM = 128
RATE = 3


epsilon = 1e-05
masked_score = -1e30


def shifted(block, axis, distance):
    devices = range(lax.axis_size(axis))
    route = [(i - distance, i) for i in devices if i - distance in devices]
    return lax.ppermute(block, axis, route)


def layer_norm(values, gain):
    centred = values - jnp.mean(values, axis=-1, keepdims=True)
    spread = jnp.mean(centred * centred, axis=-1, keepdims=True)
    return centred * lax.rsqrt(spread + epsilon) * gain


def project(left, right):
    return jnp.einsum("srd,de->sre", left, right, preferred_element_type=jnp.float32)


def project_back(left, right):
    return jnp.einsum("sre,de->srd", left, right, preferred_element_type=jnp.float32)


def weight_term(left, right):
    return jnp.einsum("srd,sre->de", left, right, preferred_element_type=jnp.float32)


def key_layout(key_index, local_rows, seg_len):
    key_owner = key_index // (3 * local_rows)
    inside = key_index % (3 * local_rows)
    key_kind = inside // local_rows
    key_place = key_owner * local_rows + inside % local_rows
    mem_slot = jnp.where(key_kind == 0, key_place, seg_len + key_place)
    return (key_kind, mem_slot, key_place)


def allowed_mask(key_kind, mem_slot, key_place, query_place, offsets, keep_flag):
    memory_ok = (mem_slot[None, :] >= offsets[:, None]) & keep_flag[:, None]
    causal = key_place[None, :] <= query_place[:, None]
    return jnp.where(key_kind[None, None, :] < 2, memory_ok[:, None, :], causal[None, :, :])


def score_block(query_heads, key_heads, allowed, score_scale):
    scores = (
        jnp.einsum("sthe,skhe->shtk", query_heads, key_heads, preferred_element_type=jnp.float32)
        * score_scale
    )
    return jnp.where(allowed[:, None], scores, masked_score)


def tile_matrix(matrix, dp_count, seq_count):
    rows_total, cols_total = matrix.shape
    blocks = matrix.reshape(dp_count, rows_total // dp_count, seq_count, cols_total // seq_count)
    return blocks.transpose(0, 2, 1, 3).reshape(
        dp_count * seq_count, rows_total // dp_count, cols_total // seq_count
    )


def tile_vector(vector, dp_count, seq_count):
    piece_len = vector.shape[0] // dp_count
    pieces = vector.reshape(dp_count, 1, piece_len)
    return jnp.broadcast_to(pieces, (dp_count, seq_count, piece_len)).reshape(
        dp_count * seq_count, piece_len
    )


def on_device(
    inputs,
    memory,
    compressed,
    offsets,
    resets,
    w_query,
    w_key,
    w_value,
    w_output,
    w_hidden,
    w_return,
    w_compress,
    gain_attn,
    gain_ffn,
    out_grad,
    comp_grad,
):
    seq_count = lax.axis_size("seq")
    dp_count = lax.axis_size("dp")
    seq_rank = lax.axis_index("seq")
    streams, local_rows, feat_width = inputs.shape
    seg_len = local_rows * seq_count
    score_scale = HEAD_DIM ** (-0.5)
    keep_flag = resets == 0
    all_rows = jnp.concatenate([compressed, memory, inputs], axis=1).astype(jnp.float32)
    normed, attn_norm_back = jax.vjp(layer_norm, all_rows, gain_attn.astype(jnp.float32))
    normed_low = normed.astype(jnp.bfloat16)
    query_in = normed_low[:, 2 * local_rows :]
    query_low = project(query_in, w_query).astype(jnp.bfloat16)
    key_low = project(normed_low, w_key).astype(jnp.bfloat16)
    value_low = project(normed_low, w_value).astype(jnp.bfloat16)
    key_all, value_all = (
        lax.all_gather(key_low, "seq", axis=1, tiled=True),
        lax.all_gather(value_low, "seq", axis=1, tiled=True),
    )
    total_keys = key_all.shape[1]
    key_kind, mem_slot, key_place = key_layout(
        jnp.arange(total_keys, dtype=jnp.int32), local_rows, seg_len
    )
    query_place = seq_rank * local_rows + jnp.arange(local_rows, dtype=jnp.int32)
    allowed = allowed_mask(key_kind, mem_slot, key_place, query_place, offsets, keep_flag)
    query_heads = query_low.reshape(streams, local_rows, HEADS, HEAD_DIM)
    key_heads = key_all.reshape(streams, total_keys, HEADS, HEAD_DIM)
    value_heads = value_all.reshape(streams, total_keys, HEADS, HEAD_DIM)
    scores = score_block(query_heads, key_heads, allowed, score_scale)
    row_top = jnp.max(scores, axis=-1, keepdims=True)
    exp_scores = jnp.exp(scores - row_top)
    row_total = jnp.sum(exp_scores, axis=-1, keepdims=True)
    attn_prob = exp_scores / row_total
    log_total = row_top + jnp.log(row_total)
    mixed_low = (
        jnp.einsum(
            "shtk,skhe->sthe",
            attn_prob.astype(jnp.bfloat16),
            value_heads,
            preferred_element_type=jnp.float32,
        )
        .reshape(streams, local_rows, feat_width)
        .astype(jnp.bfloat16)
    )
    hidden = inputs.astype(jnp.float32) + project(mixed_low, w_output)
    ffn_in, ffn_norm_back = jax.vjp(layer_norm, hidden, gain_ffn.astype(jnp.float32))
    ffn_low = ffn_in.astype(jnp.bfloat16)
    ffn_all = lax.all_gather(ffn_low, "seq", axis=1, tiled=True)
    pre_act = jnp.einsum("std,df->stf", ffn_all, w_hidden, preferred_element_type=jnp.float32)
    act_float, gelu_back = jax.vjp(jax.nn.gelu, pre_act)
    act_low = act_float.astype(jnp.bfloat16)
    partial_out = jnp.einsum("stf,fd->std", act_low, w_return, preferred_element_type=jnp.float32)
    ffn_out = lax.psum_scatter(
        partial_out.astype(jnp.bfloat16), "seq", scatter_dimension=1, tiled=True
    ).astype(jnp.float32)
    cot_all = lax.all_gather(out_grad, "seq", axis=1, tiled=True)
    act_grad = jnp.einsum("std,fd->stf", cot_all, w_return, preferred_element_type=jnp.float32)
    return_part = jnp.einsum("stf,std->fd", act_low, cot_all, preferred_element_type=jnp.float32)
    pre_grad = gelu_back(act_grad)[0].astype(jnp.bfloat16)
    hidden_part = jnp.einsum("std,stf->df", ffn_all, pre_grad, preferred_element_type=jnp.float32)
    in_part = jnp.einsum("stf,df->std", pre_grad, w_hidden, preferred_element_type=jnp.float32)
    ffn_in_grad = lax.psum_scatter(in_part, "seq", scatter_dimension=1, tiled=True)
    hidden_sum, return_sum = (
        lax.psum_scatter(
            hidden_part.astype(jnp.bfloat16), "dp", scatter_dimension=0, tiled=True
        ).astype(jnp.float32),
        lax.psum_scatter(
            return_part.T.astype(jnp.bfloat16), "dp", scatter_dimension=0, tiled=True
        ).astype(jnp.float32),
    )
    grad_return = return_sum.T
    outputs = (hidden + ffn_out).astype(jnp.bfloat16)
    hidden_grad, gain_ffn_grad = ffn_norm_back(ffn_in_grad)
    hidden_grad = hidden_grad + out_grad.astype(jnp.float32)
    attn_grad_low = hidden_grad.astype(jnp.bfloat16)
    output_part = weight_term(mixed_low, attn_grad_low)
    mixed_grad = project_back(attn_grad_low, w_output).astype(jnp.bfloat16)
    mixed_heads = mixed_grad.reshape(streams, local_rows, HEADS, HEAD_DIM)
    prob_again = jnp.exp(score_block(query_heads, key_heads, allowed, score_scale) - log_total)
    prob_grad = jnp.einsum(
        "sthe,skhe->shtk", mixed_heads, value_heads, preferred_element_type=jnp.float32
    )
    prob_delta = jnp.sum(prob_again * prob_grad, axis=-1)
    score_grad = (prob_again * (prob_grad - prob_delta[..., None])).astype(jnp.bfloat16)
    query_grad = (
        (
            jnp.einsum("shtk,skhe->sthe", score_grad, key_heads, preferred_element_type=jnp.float32)
            * score_scale
        )
        .reshape(streams, local_rows, feat_width)
        .astype(jnp.bfloat16)
    )
    key_part = (
        jnp.einsum("shtk,sthe->skhe", score_grad, query_heads, preferred_element_type=jnp.float32)
        * score_scale
    ).reshape(streams, total_keys, feat_width)
    value_part = jnp.einsum(
        "shtk,sthe->skhe",
        prob_again.astype(jnp.bfloat16),
        mixed_heads,
        preferred_element_type=jnp.float32,
    ).reshape(streams, total_keys, feat_width)
    key_sum, value_sum = (
        lax.psum_scatter(
            key_part.astype(jnp.bfloat16), "seq", scatter_dimension=1, tiled=True
        ).astype(jnp.float32),
        lax.psum_scatter(
            value_part.astype(jnp.bfloat16), "seq", scatter_dimension=1, tiled=True
        ).astype(jnp.float32),
    )
    key_grad = key_sum.astype(jnp.bfloat16)
    value_grad = value_sum.astype(jnp.bfloat16)
    query_part = weight_term(query_in, query_grad)
    key_wpart = weight_term(normed_low, key_grad)
    value_wpart = weight_term(normed_low, value_grad)
    query_back = project_back(query_grad, w_query)
    normed_grad = project_back(key_grad, w_key) + project_back(value_grad, w_value)
    normed_grad = normed_grad + jnp.concatenate(
        [jnp.zeros((streams, 2 * local_rows, feat_width), jnp.float32), query_back], axis=1
    )
    rows_grad, gain_attn_grad = attn_norm_back(normed_grad)
    input_grad = (rows_grad[:, 2 * local_rows :] + hidden_grad).astype(jnp.bfloat16)
    kept_memory = memory * keep_flag[:, None, None].astype(jnp.bfloat16)
    edge_rows = shifted(kept_memory[:, : 2 * (RATE - 1)], "seq", -1)
    extended = jnp.concatenate([kept_memory, edge_rows], axis=1)
    group_count = (local_rows + RATE - 1) // RATE
    first_group = (seq_rank * local_rows + RATE - 1) // RATE
    slice_start = RATE * first_group - seq_rank * local_rows
    grouped = lax.dynamic_slice_in_dim(extended, slice_start, RATE * group_count, 1).reshape(
        streams, group_count, RATE * feat_width
    )
    piece_rows = jnp.einsum(
        "sgc,cd->sgd", grouped, w_compress, preferred_element_type=jnp.float32
    ).astype(jnp.bfloat16)
    comp_all = lax.all_gather(piece_rows, "seq", axis=1, tiled=True)
    comp_count = comp_grad.shape[1]
    out_index = jnp.arange(comp_count, dtype=jnp.int32)
    holder = RATE * out_index // local_rows
    lookup = holder * group_count + out_index - (holder * local_rows + RATE - 1) // RATE
    new_compressed = jnp.take(comp_all, lookup, axis=1)
    slot_index = first_group + jnp.arange(group_count, dtype=jnp.int32)
    slot_valid = (RATE * slot_index < (seq_rank + 1) * local_rows) & (slot_index < comp_count)
    picked = jnp.take(comp_grad, jnp.minimum(slot_index, comp_count - 1), axis=1) * slot_valid[
        None, :, None
    ].astype(jnp.bfloat16)
    compress_part = jnp.einsum("sgc,sgd->cd", grouped, picked, preferred_element_type=jnp.float32)
    reduced = (
        lax.psum_scatter(
            tile_matrix(query_part, dp_count, seq_count),
            ("dp", "seq"),
            scatter_dimension=0,
            tiled=True,
        ),
        lax.psum_scatter(
            tile_matrix(key_wpart, dp_count, seq_count),
            ("dp", "seq"),
            scatter_dimension=0,
            tiled=True,
        ),
        lax.psum_scatter(
            tile_matrix(value_wpart, dp_count, seq_count),
            ("dp", "seq"),
            scatter_dimension=0,
            tiled=True,
        ),
        lax.psum_scatter(
            tile_matrix(output_part, dp_count, seq_count),
            ("dp", "seq"),
            scatter_dimension=0,
            tiled=True,
        ),
        lax.psum_scatter(
            tile_matrix(compress_part, dp_count, seq_count),
            ("dp", "seq"),
            scatter_dimension=0,
            tiled=True,
        ),
        lax.psum_scatter(
            tile_vector(gain_attn_grad, dp_count, seq_count),
            ("dp", "seq"),
            scatter_dimension=0,
            tiled=True,
        ),
        lax.psum_scatter(
            tile_vector(gain_ffn_grad, dp_count, seq_count),
            ("dp", "seq"),
            scatter_dimension=0,
            tiled=True,
        ),
    )
    return (
        outputs,
        new_compressed,
        input_grad,
        reduced[0][0],
        reduced[1][0],
        reduced[2][0],
        reduced[3][0],
        hidden_sum,
        grad_return,
        reduced[4][0],
        reduced[5][0],
        reduced[6][0],
    )


F32 = jnp.float32
BF16 = jnp.bfloat16
NN = (((1,), (0,)), ((), ()))
NT = (((1,), (1,)), ((), ()))
TN = (((0,), (0,)), ((), ()))
VMEM_LIMIT = 60 * 1024 * 1024
SCALE = HEAD_DIM ** (-0.5)
EXP2_SCALE = SCALE * math.log2(math.e)


def dot(left, right, dims=NN):
    return lax.dot_general(left, right, dims, preferred_element_type=F32)


def params(steps=1):
    return pltpu.CompilerParams(
        vmem_limit_bytes=VMEM_LIMIT, dimension_semantics=("arbitrary",) * steps
    )


def cost(flops, bytes_accessed=0, transcendentals=0):
    return pl.CostEstimate(
        flops=int(flops), bytes_accessed=int(bytes_accessed), transcendentals=int(transcendentals)
    )


def held(shape):
    zeros = (0,) * len(shape)
    return pl.BlockSpec(shape, lambda *_: zeros, pipeline_mode=pl.Buffered(1))


def norm_parts(rows):
    centred = rows - jnp.mean(rows, axis=-1, keepdims=True)
    inverse = lax.rsqrt(jnp.mean(centred * centred, axis=-1, keepdims=True) + epsilon)
    return centred * inverse, inverse


def norm_back(grad, unit, inverse):
    return inverse * (
        grad
        - jnp.mean(grad, axis=-1, keepdims=True)
        - unit * jnp.mean(grad * unit, axis=-1, keepdims=True)
    )


def add_low(left, right):
    return (left.astype(F32) + right.astype(F32)).astype(BF16)


def mesh_place():
    rank, core = lax.axis_index("dp"), lax.axis_index("seq")

    def bit(b):
        return lax.rem(lax.div(rank, 1 << b), 2)

    def across(b):
        return rank + (1 << b) * (1 - 2 * bit(b))

    return core, bit, across


def first_slots(resets_ref, offsets_ref, core, total):
    return [
        jnp.where(resets_ref[core + 2 * j] != 0, total, offsets_ref[core + 2 * j]) for j in range(2)
    ]


def stream_a_slot(resets_ref, offsets_ref, core, total):
    first, second = first_slots(resets_ref, offsets_ref, core, total)
    return jnp.where(first >= total, second, first)


def greet(devices):
    barrier = pltpu.get_barrier_semaphore()
    for device in devices:
        pl.semaphore_signal(
            barrier, inc=1, device_id=device, device_id_type=pl.DeviceIdType.MESH
        )
    pl.semaphore_wait(barrier, len(devices))


def remote(src, dst, sems, device):
    return pltpu.make_async_remote_copy(
        src_ref=src,
        dst_ref=dst,
        send_sem=sems[0],
        recv_sem=sems[1],
        device_id=device,
        device_id_type=pl.DeviceIdType.MESH,
    )


class Chunk:
    def __init__(self, data, left, order, landing, sems, place):
        self.data, self.left, self.order = data, left, order
        self.landing, self.sems = landing, sems
        _, self.bit, self.across = place

    def at(self, swap, away):
        index = []
        for b in self.left:
            if b in self.order[:swap]:
                index.append(self.bit(b))
            elif swap < len(self.order) and b == self.order[swap]:
                index.append(1 - self.bit(b) if away else self.bit(b))
            else:
                index.append(slice(None))
        return tuple(index)

    def rest(self, swap):
        done = self.order[:swap]
        return tuple(self.bit(b) if b in done else slice(None) for b in self.left)

    def copy(self, swap):
        return remote(
            self.data.at[self.at(swap, True)],
            self.landing[swap],
            (self.sems.at[0, swap], self.sems.at[1, swap]),
            {"dp": self.across(self.order[swap])},
        )

    def start(self, swap):
        self.copy(swap).start()

    def settle(self, swap):
        self.copy(swap).wait()
        here = self.at(swap, False)
        self.data[here] = add_low(self.data[here], self.landing[swap][...])

    def last(self, swap):
        self.copy(swap).wait()
        return self.data[self.at(swap, False)].astype(F32) + self.landing[swap][...].astype(F32)


def landings(left, order, block):
    shapes, count = [], len(left)
    for _ in order:
        count -= 1
        shapes.append(pltpu.VMEM((2,) * count + block, BF16))
    return shapes


BITS = (3, 2, 1, 0)
ORDERS = ((0, 1, 2, 3), (1, 0, 2, 3))


def front_kernel(
    resets_ref, in_ref, mem_ref, old_ref, og_ref, wc_ref, cg_ref,
    x_in_ref, x_mem_ref, x_old_ref, x_og_ref, new_ref, kept_p_ref, sent_p_ref, kept_q_ref, sent_q_ref,
    mem, x_in, x_old, x_og, wc, new, core_out, core_in, row_sems, wc_sem, new_sems, core_sems, out_sems,
):
    core, bit, _ = mesh_place()
    partner = {"seq": 1 - core}
    width = in_ref.shape[2]
    groups = cg_ref.shape[1]

    weights = pltpu.make_async_copy(wc_ref, wc, wc_sem)
    weights.start()
    greet((partner,))
    moves = []
    for n, (src, dst) in enumerate(
        ((mem_ref, mem), (in_ref, x_in), (old_ref, x_old), (og_ref, x_og))
    ):
        for j in range(2):
            away = remote(
                src.at[1 - core + 2 * j], dst.at[j, core], (row_sems.at[0, n, j], row_sems.at[1, n, j]), partner
            )
            here = pltpu.make_async_copy(src.at[core + 2 * j], dst.at[j, core], row_sems.at[2, n, j])
            away.start()
            here.start()
            moves.append((away, here))
    new[...] = jnp.zeros_like(new)
    outs = []
    for j in range(2):
        moves[j][0].wait_recv()
        moves[j][1].wait()
    outs.append(pltpu.make_async_copy(mem, x_mem_ref, out_sems.at[0]))
    outs[-1].start()
    weights.wait()

    grouped = []
    for j in range(2):
        rows = mem[j].reshape(2 * mem.shape[2], width)
        group = lax.broadcasted_iota(jnp.int32, (groups, rows.shape[0]), 0)
        row = lax.broadcasted_iota(jnp.int32, (groups, rows.shape[0]), 1)
        keep = jnp.where(resets_ref[core + 2 * j] == 0, 1.0, 0.0)
        total = jnp.zeros((groups, width), F32)
        mine = []
        for r in range(RATE):
            pick = jnp.where(row == RATE * group + r, keep, 0.0).astype(BF16)
            mine.append(dot(pick, rows).astype(BF16))
            total = total + dot(mine[-1], wc[r * width : (r + 1) * width])
        grouped.append(mine)
        new[j, :groups] = total.astype(BF16)

    news = []
    for j in range(2):
        at = core + 2 * j
        news.append(remote(new.at[j], new_ref.at[at], (new_sems.at[0, j], new_sems.at[1, j]), partner))
        outs.append(pltpu.make_async_copy(new.at[j], new_ref.at[at], new_sems.at[2, j]))
        news[-1].start()
        outs[-1].start()

    half = width // 2

    def grad(r, side):
        cols = pl.ds(pl.multiple_of(side * half, half), half)
        return sum(dot(grouped[j][r], cg_ref[core + 2 * j, :, cols], TN) for j in range(2))

    crossing = []
    for r in range(RATE):
        core_out[r] = grad(r, 1 - core).astype(BF16)
        crossing.append(
            remote(core_out.at[r], core_in.at[r], (core_sems.at[0, r], core_sems.at[1, r]), partner)
        )
        crossing[-1].start()
    for n, (src, dst) in enumerate(((x_in, x_in_ref), (x_old, x_old_ref), (x_og, x_og_ref))):
        for away, here in moves[2 * n + 2 : 2 * n + 4]:
            away.wait_recv()
            here.wait()
        outs.append(pltpu.make_async_copy(src, dst, out_sems.at[1 + n]))
        outs[-1].start()
    fine = width // 16
    quarter = half // 2
    for r in range(RATE):
        total = grad(r, core)
        crossing[r].wait()
        total = (total + core_in[r].astype(F32)).astype(BF16)
        for which, (kept_ref, sent_ref) in enumerate(
            ((kept_p_ref, sent_p_ref), (kept_q_ref, sent_q_ref))
        ):
            for mine in range(2):

                @pl.when(bit(which) == mine)
                def _():
                    for t in range(16):
                        block, third = divmod(r * 16 + t, RATE)
                        place = (block >> 3, block >> 2 & 1, block >> (1 - which) & 1)
                        ref = kept_ref if block >> which & 1 == mine else sent_ref
                        ref[place + (slice(third * fine, (third + 1) * fine),)] = total[
                            t * fine : (t + 1) * fine, which * quarter : (which + 1) * quarter
                        ]
    for away, _ in moves:
        away.wait_send()
    for move in outs + news:
        move.wait()


def front(resets, inputs, memory, compressed, out_grad, w_compress, comp_grad):
    streams, half, width = inputs.shape
    anywhere = pl.BlockSpec(memory_space=pl.ANY)
    vmem = pl.BlockSpec(memory_space=pltpu.VMEM)
    pair = jax.ShapeDtypeStruct((2, 2, half, width), BF16)
    padded = -(-comp_grad.shape[1] // 16) * 16
    part = jax.ShapeDtypeStruct((2, 2, 2, RATE * width // 16, width // 4), BF16)
    return pl.pallas_call(
        front_kernel,
        out_shape=(
            pair, pair, pair, pair, jax.ShapeDtypeStruct((streams, padded, width), BF16),
            part, part, part, part,
        ),
        in_specs=[pl.BlockSpec(memory_space=pltpu.SMEM)] + [anywhere] * 5 + [vmem],
        out_specs=(anywhere,) * 5 + (vmem,) * 4,
        scratch_shapes=[
            pltpu.VMEM((2, 2, half, width), BF16),
            pltpu.VMEM((2, 2, half, width), BF16),
            pltpu.VMEM((2, 2, half, width), BF16),
            pltpu.VMEM((2, 2, half, width), BF16),
            pltpu.VMEM(w_compress.shape, BF16),
            pltpu.VMEM((2, padded, width), BF16),
            pltpu.VMEM((RATE, width, width // 2), BF16),
            pltpu.VMEM((RATE, width, width // 2), BF16),
            pltpu.SemaphoreType.DMA((3, 4, 2)),
            pltpu.SemaphoreType.DMA,
            pltpu.SemaphoreType.DMA((3, 2)),
            pltpu.SemaphoreType.DMA((2, RATE)),
            pltpu.SemaphoreType.DMA((4,)),
        ],
        compiler_params=pltpu.CompilerParams(
            vmem_limit_bytes=VMEM_LIMIT, collective_id=4, has_side_effects=True
        ),
        cost_estimate=cost(12e9, 24e6),
        name="front",
    )(resets, inputs, memory, compressed, out_grad, w_compress, comp_grad)


def project_kernel(
    resets_ref, offsets_ref, old_ref, mem_ref, in_ref, og_ref, gain_ref, wq_hbm, wk_hbm, wv_hbm,
    raw_ref, normed_ref, q_ref, k_ref, v_ref, og_out_ref,
    wq_ref, wk_ref, wv_ref, sems,
):
    step = pl.program_id(0)
    weights = [
        pltpu.make_async_copy(src, dst, sems.at[n])
        for n, (src, dst) in enumerate(((wk_hbm, wk_ref), (wv_hbm, wv_ref), (wq_hbm, wq_ref)))
    ]

    @pl.when(step == 0)
    def _():
        for copy in weights:
            copy.start()

    half, width = in_ref.shape[1:]
    size = 2 * half // 2
    for n in range(2):
        at = slice(n * size, (n + 1) * size)
        pick = lambda ref: ref[...].reshape(2 * half, width)[at]
        raw = jnp.where(step == 0, pick(old_ref), jnp.where(step == 1, pick(mem_ref), pick(in_ref)))
        raw_ref[at] = raw
        unit, _ = norm_parts(raw.astype(F32))
        normed_ref[at] = (unit * gain_ref[...]).astype(BF16)
        if n == 0:

            @pl.when(step == 0)
            def _():
                for copy in weights[:2]:
                    copy.wait()

        k_ref[at] = dot(normed_ref[at], wk_ref[...]).astype(BF16)
        v_ref[at] = dot(normed_ref[at], wv_ref[...]).astype(BF16)

    @pl.when(step == 2)
    def _():
        weights[2].wait()

    @pl.when(step >= 2)
    def _():
        q_ref[...] = dot(normed_ref[...], wq_ref[...]).astype(BF16)
        og_out_ref[...] = og_ref[...].reshape(og_out_ref.shape)


def project_rows(resets, offsets, old, mem, inputs, og, gain, wq, wk, wv):
    _, _, half, width = inputs.shape
    seg = 2 * half

    def from_pair(first):
        def index(i, resets_ref, offsets_ref):
            slots = first_slots(resets_ref, offsets_ref, lax.axis_index("seq"), 2 * seg)
            stream_a = jnp.where(slots[0] >= 2 * seg, 1, 0)
            return jnp.where(i < first + 1, stream_a, 1 - stream_a), 0, 0, 0

        return pl.BlockSpec((None, 2, half, width), index)

    keys = pl.BlockSpec((seg, width), lambda i, *_: (i, 0))
    rows = pl.BlockSpec((seg, width), lambda i, *_: (jnp.maximum(i - 2, 0), 0))
    key_shape = jax.ShapeDtypeStruct((4 * seg, width), BF16)
    row_shape = jax.ShapeDtypeStruct((2 * seg, width), BF16)
    anywhere = pl.BlockSpec(memory_space=pl.ANY)
    return pl.pallas_call(
        project_kernel,
        out_shape=(key_shape, key_shape, row_shape, key_shape, key_shape, row_shape),
        grid_spec=pltpu.PrefetchScalarGridSpec(
            num_scalar_prefetch=2,
            grid=(4,),
            in_specs=[
                from_pair(4), from_pair(4), from_pair(2), from_pair(2),
                held(gain.shape), anywhere, anywhere, anywhere,
            ],
            out_specs=(keys, keys, rows, keys, keys, rows),
            scratch_shapes=[
                pltpu.VMEM(wq.shape, BF16),
                pltpu.VMEM(wk.shape, BF16),
                pltpu.VMEM(wv.shape, BF16),
                pltpu.SemaphoreType.DMA((3,)),
            ],
        ),
        compiler_params=params(),
        cost_estimate=cost(14e9, 30e6),
        name="project",
    )(resets, offsets, old, mem, inputs, og, gain, wq, wk, wv)


def attn_fwd_kernel(
    resets_ref, offsets_ref, q_ref, k_ref, v_ref, in_ref, wo_ref, gain_ref, kept_p_ref, got_p_ref, kept_q_ref, got_q_ref,
    wh_hbm, wr_hbm,
    mixed_ref, hidden_ref, ffn_ref, lse_ref, compress_ref, wh_got, wr_got,
    weight_sems, packed, *scratch,
):
    step = pl.program_id(0)
    lands, chip_sems = scratch[:-1], scratch[-1]
    place = mesh_place()
    half = q_ref.shape[0]
    seg = 2 * half
    first_slot = stream_a_slot(resets_ref, offsets_ref, place[0], 2 * seg)
    partner = {"seq": 1 - place[0]}
    weights = [
        remote(src, dst, (weight_sems.at[0, n], weight_sems.at[1, n]), partner)
        for n, (src, dst) in enumerate(((wh_hbm, wh_got), (wr_hbm, wr_got)))
    ]
    chunks = [
        Chunk(
            packed.at[which],
            tuple(b for b in BITS if b != ORDERS[which][0]),
            ORDERS[which][1:2],
            lands[which : which + 1],
            chip_sems.at[which],
            place,
        )
        for which in range(2)
    ]

    @pl.when(step == 0)
    def _():
        greet((partner,) + tuple({"dp": place[2](b)} for b in range(2)))
        for copy in weights:
            copy.start()
        packed[0] = add_low(kept_p_ref[...], got_p_ref[...])
        packed[1] = add_low(kept_q_ref[...], got_q_ref[...])
        for part in chunks:
            part.start(0)

    def run(pieces):
        def one_head(h, stats):
            cols = pl.ds(pl.multiple_of(h * HEAD_DIM, HEAD_DIM), HEAD_DIM)
            q = q_ref[:, cols]
            scores = []
            for start, size, kind in pieces:
                s = dot(q, k_ref[start : start + size, cols], NT)
                if kind == "mem":
                    slot = lax.broadcasted_iota(jnp.int32, s.shape, 1)
                    s = jnp.where(slot >= first_slot, s, masked_score)
                if kind == "diag":
                    key = lax.broadcasted_iota(jnp.int32, s.shape, 1)
                    row = lax.broadcasted_iota(jnp.int32, s.shape, 0)
                    s = jnp.where(key <= row, s, masked_score)
                scores.append(s)
            top = functools.reduce(
                jnp.maximum, [jnp.max(s, axis=-1, keepdims=True) for s in scores]
            ) * EXP2_SCALE
            mix = jnp.zeros((half, 2 * HEAD_DIM), F32)
            for s, (start, size, _) in zip(scores, pieces):
                p = jnp.exp2(s * EXP2_SCALE - top).astype(BF16)
                ones = jnp.ones((size, HEAD_DIM), BF16)
                mix = mix + dot(p, jnp.concatenate([v_ref[start : start + size, cols], ones], axis=1))
            total = mix[:, HEAD_DIM:]
            mixed_ref[:, cols] = (mix[:, :HEAD_DIM] / total).astype(BF16)
            lane = lax.broadcasted_iota(jnp.int32, stats.shape, 1)
            return jnp.where(lane == h, top + jnp.log2(total), stats)

        stats = lax.fori_loop(0, HEADS, one_head, jnp.zeros((half, 128), F32), unroll=True)
        lse_ref[...] = stats.T[:HEADS]

    cases = (
        ((0, 2 * seg, "mem"), (2 * seg, half, "diag")),
        ((0, 2 * seg, "mem"), (2 * seg, half, "full"), (2 * seg + half, half, "diag")),
        ((3 * seg, half, "diag"),),
        ((3 * seg, half, "full"), (3 * seg + half, half, "diag")),
    )
    for i, pieces in enumerate(cases[2:] + cases[:2]):
        pl.when(step == i)(functools.partial(run, pieces))
    hidden = in_ref[...].astype(F32) + dot(mixed_ref[...], wo_ref[...])
    hidden_ref[...] = hidden
    unit, _ = norm_parts(hidden)
    ffn_ref[...] = (unit * gain_ref[...]).astype(BF16)

    @pl.when(step == 3)
    def _():
        for which, part in enumerate(chunks):
            part.settle(0)
            compress_ref[which] = packed[(which,) + part.rest(1)]
        for copy in weights:
            copy.wait()


def attn_fwd(resets, offsets, q, k, v, raw, wo, gain, kept_p, got_p, kept_q, got_q, wh, wr):
    rows, width = q.shape
    half = rows // 4
    by_block = pl.BlockSpec((half, width), lambda i: (lax.rem(i + 2, 4), 0))
    in_block = pl.BlockSpec((half, width), lambda i: (4 + lax.rem(i + 2, 4), 0))
    anywhere = pl.BlockSpec(memory_space=pl.ANY)
    block = kept_p.shape[-2:]
    part = held(kept_p.shape)
    lands = []
    for which in range(2):
        lands += landings(BITS[1:], ORDERS[which][1:2], block)
    out = (2, 2, 2) + block
    return pl.pallas_call(
        attn_fwd_kernel,
        grid=(4,),
        out_shape=(
            jax.ShapeDtypeStruct((rows, width), BF16),
            jax.ShapeDtypeStruct((rows, width), F32),
            jax.ShapeDtypeStruct((rows, width), BF16),
            jax.ShapeDtypeStruct((HEADS, rows), F32),
            jax.ShapeDtypeStruct(out, BF16),
            jax.ShapeDtypeStruct(wh.shape, BF16),
            jax.ShapeDtypeStruct(wr.shape, BF16),
        ),
        in_specs=[
            pl.BlockSpec(memory_space=pltpu.SMEM),
            pl.BlockSpec(memory_space=pltpu.SMEM),
            by_block, held(k.shape), held(v.shape), in_block, held(wo.shape), held(gain.shape),
            part, part, part, part, anywhere, anywhere,
        ],
        out_specs=(
            by_block, by_block, by_block, pl.BlockSpec((HEADS, half), lambda i: (0, lax.rem(i + 2, 4))), held(out),
            anywhere, anywhere,
        ),
        scratch_shapes=[pltpu.SemaphoreType.DMA((2, 2)), pltpu.VMEM((2,) + kept_p.shape, BF16)] + lands + [pltpu.SemaphoreType.DMA((2, 2, 1))],
        compiler_params=pltpu.CompilerParams(
            vmem_limit_bytes=VMEM_LIMIT, dimension_semantics=("arbitrary",),
            collective_id=5, has_side_effects=True,
        ),
        cost_estimate=cost(20e9, 20e6),
        name="attn_fwd",
    )(resets, offsets, q, k, v, raw, wo, gain, kept_p, got_p, kept_q, got_q, wh, wr)


GELU_C = math.sqrt(2.0 / math.pi)
GELU_A = 0.044715
CHUNK = 512


def gelu_pair(pre, act_grad):
    square = pre * pre
    t = jnp.tanh(pre * (GELU_C + (GELU_C * GELU_A) * square))
    cdf = 0.5 + 0.5 * t
    slope = cdf + (0.5 * pre) * (1.0 - t * t) * (GELU_C + (3.0 * GELU_C * GELU_A) * square)
    return (pre * cdf).astype(BF16), (act_grad * slope).astype(BF16)


def ffn_kernel(
    x_ref, og_ref, gain_ref, packed_ref, hidden_hbm, wo_hbm, wh0_ref, wh1_ref, wr0_ref, wr1_ref,
    out_ref, attn_grad_ref, do_ref, gain_grad_ref, done_ref, part_ref, raw_ref, compress_ref,
    hidden_ref, wo_ref, held_sems, pack0, pack1, pack_sems, wh, wr, out_acc, in_acc, act_ref, pre_ref, core_out, core_in, own_ref, land0, land1, land2, land3,
    weight_sems, core_sems, chip_sems,
):
    step = pl.program_id(0)
    last = pl.num_programs(0) - 1
    index = lax.div(step, 2)
    end = lax.div(last, 2)
    owned = lax.rem(step, 2) == 1
    rows, width = x_ref.shape
    units = wh.shape[2]
    chunks = rows // CHUNK
    place = mesh_place()
    core, _, across = place
    partner = {"seq": 1 - core}

    def fetch(at, side):
        cols = pl.ds(pl.multiple_of(at * units, units), units)
        wh_ref, wr_ref = ((wh0_ref, wr0_ref), (wh1_ref, wr1_ref))[side]
        return (
            pltpu.make_async_copy(wh_ref.at[:, cols], wh.at[side], weight_sems.at[0, side]),
            pltpu.make_async_copy(wr_ref.at[cols], wr.at[side], weight_sems.at[1, side]),
        )

    held_copies = (
        pltpu.make_async_copy(hidden_hbm, hidden_ref, held_sems.at[0]),
        pltpu.make_async_copy(wo_hbm, wo_ref, held_sems.at[1]),
    )
    packs = [
        Chunk(
            packed_ref.at[which], (3, 2), (2, 3), [pack0.at[which], pack1.at[which]],
            pack_sems.at[which], place,
        )
        for which in range(2)
    ]

    @pl.when(step == 0)
    def _():
        for copy in fetch(0, 0) + held_copies:
            copy.start()
        greet((partner,) + tuple({"dp": across(b)} for b in range(4)))
        for part in packs:
            part.start(0)
        out_acc[...] = jnp.zeros_like(out_acc)
        in_acc[...] = jnp.zeros_like(in_acc)

    @pl.when(step == 2)
    def _():
        for part in packs:
            part.settle(0)
            part.start(1)

    @pl.when(step == 4)
    def _():
        cols = compress_ref.shape[1] // 2
        for which, part in enumerate(packs):
            compress_ref[:, which * cols : (which + 1) * cols] = part.last(1)

    @pl.when(jnp.logical_not(owned))
    def _():
        for copy in fetch(index, 1):
            copy.start()
        for copy in fetch(index, 0):
            copy.wait()

    @pl.when(owned)
    def _():
        @pl.when(index < end)
        def _():
            for copy in fetch(index + 1, 0):
                copy.start()

        for copy in fetch(index, 1):
            copy.wait()

    def core_copy(which, index):
        return remote(
            core_out.at[which],
            core_in.at[which, lax.rem(index, 2)],
            (core_sems.at[0, which, index], core_sems.at[1, which, index]),
            partner,
        )

    def tile(which, index):
        return Chunk(
            own_ref.at[which, index], BITS, ORDERS[which],
            [land.at[which, index] for land in (land0, land1, land2, land3)],
            chip_sems.at[which, index], place,
        )

    def pass_on(index, swap):
        for which in range(2):
            part = tile(which, index)
            part.settle(swap)
            part.start(swap + 1)

    def finish_tile(index):
        for which in range(2):
            done_ref[which, index] = tile(which, index).last(3)

    side = lax.rem(step, 2)

    def rows_step(m, _):
        at = pl.ds(pl.multiple_of(m * CHUNK, CHUNK), CHUNK)
        pre = dot(x_ref[at, :], wh[side])
        act_grad = dot(og_ref[at, :], wr[side], NT)
        act, pre_grad = gelu_pair(pre, act_grad)
        act_ref[at, :] = act
        pre_ref[at, :] = pre_grad
        out_acc[at, :] += dot(act, wr[side])
        in_acc[at, :] += dot(pre_grad, wh[side], NT)

        return 0

    lax.fori_loop(0, chunks, rows_step, 0)

    @pl.when(owned & (index > 0))
    def _():
        pass_on(index - 1, 0)

    @pl.when(owned & (index > 1))
    def _():
        pass_on(index - 2, 2)

    @pl.when(jnp.logical_not(owned) & (index > 1))
    def _():
        pass_on(index - 2, 1)

    @pl.when(jnp.logical_not(owned) & (index > 2))
    def _():
        finish_tile(index - 3)

    for which, (left_ref, right_ref) in enumerate(((x_ref, pre_ref), (og_ref, act_ref))):
        grad = dot(left_ref[...], right_ref[...], TN)

        @pl.when(jnp.logical_not(owned))
        def _():
            @pl.when(index > 0)
            def _():
                core_copy(which, index - 1).wait_send()

            core_out[which] = grad.astype(BF16)
            core_copy(which, index).start()

        @pl.when(owned)
        def _():
            core_copy(which, index).wait_recv()
            total = grad + core_in[which, lax.rem(index, 2)].astype(F32)
            total = total.astype(BF16).reshape(own_ref.shape[2:])

            @pl.when(index < end)
            def _():
                own_ref[which, index] = total
                tile(which, index).start(0)

            @pl.when(index == end)
            def _():
                raw_ref[which] = total

    @pl.when(step == last)
    def _():
        for copy in held_copies:
            copy.wait()

        def finish(m, gain_sum):
            at = pl.ds(pl.multiple_of(m * 256, 256), 256)
            hidden = hidden_ref[at, :]
            out_ref[at, :] = (hidden + out_acc[at, :]).astype(BF16)
            unit, inverse = norm_parts(hidden)
            grad = in_acc[at, :]
            hidden_grad = og_ref[at, :].astype(F32) + norm_back(
                grad * gain_ref[...], unit, inverse
            )
            low = hidden_grad.astype(BF16)
            attn_grad_ref[at, :] = low
            do_ref[at, :] = dot(low, wo_ref[...], NT).astype(BF16)
            return gain_sum + jnp.sum(grad * unit, axis=0, keepdims=True)

        gain_grad_ref[...] = lax.fori_loop(
            0, rows // 256, finish, jnp.zeros(gain_grad_ref.shape, F32)
        )
        finish_tile(end - 2)
        for which in range(2):
            core_copy(which, end).wait_send()
            part = tile(which, end - 1)
            part.settle(1)
            part_ref[which] = part.data[part.rest(2)]


def ffn(x, og, gain, packed, hidden, wo, wh0, wh1, wr0, wr1):
    rows, width = x.shape
    units = wh0.shape[1]
    tile = 512
    steps = units // tile
    count = lax.axis_size("dp")
    block = width // count
    anywhere = pl.BlockSpec(memory_space=pl.ANY)
    whole = held((rows, width))
    low_rows = jax.ShapeDtypeStruct((rows, width), BF16)
    raw = (2, 2, 2, 2, 2, block, tile)
    part = (2, 2, 2, block, tile)
    done = (2, steps - 2, block, tile)
    tiles = (2, steps - 1)
    lands = [pltpu.VMEM(tiles + (2,) * n + (block, tile), BF16) for n in (3, 2, 1, 0)]
    pack = packed.shape[-2:]
    compress = (pack[0], 2 * pack[1])
    return pl.pallas_call(
        ffn_kernel,
        grid=(2 * steps,),
        out_shape=(
            low_rows, low_rows, low_rows, jax.ShapeDtypeStruct((1, width), F32),
            jax.ShapeDtypeStruct(done, F32),
            jax.ShapeDtypeStruct(part, BF16),
            jax.ShapeDtypeStruct(raw, BF16),
            jax.ShapeDtypeStruct(compress, F32),
        ),
        in_specs=[whole, whole, held(gain.shape), held(packed.shape)] + [anywhere] * 6,
        out_specs=(whole, whole, whole, held((1, width)), held(done), held(part), held(raw), held(compress)),
        scratch_shapes=[
            pltpu.VMEM((rows, width), F32),
            pltpu.VMEM(wo.shape, BF16),
            pltpu.SemaphoreType.DMA((2,)),
            pltpu.VMEM((2, 2) + pack, BF16),
            pltpu.VMEM((2,) + pack, BF16),
            pltpu.SemaphoreType.DMA((2, 2, 2)),
            pltpu.VMEM((2, width, tile), BF16),
            pltpu.VMEM((2, tile, width), BF16),
            pltpu.VMEM((rows, width), F32),
            pltpu.VMEM((rows, width), F32),
            pltpu.VMEM((rows, tile), BF16),
            pltpu.VMEM((rows, tile), BF16),
            pltpu.VMEM((2, width, tile), BF16),
            pltpu.VMEM((2, 2, width, tile), BF16),
            pltpu.VMEM(tiles + raw[1:], BF16),
        ] + lands + [
            pltpu.SemaphoreType.DMA((2, 2)),
            pltpu.SemaphoreType.DMA((2, 2, steps)),
            pltpu.SemaphoreType.DMA((2, steps, 2, 4)),
        ],
        compiler_params=pltpu.CompilerParams(
            vmem_limit_bytes=VMEM_LIMIT, dimension_semantics=("arbitrary",),
            collective_id=1, has_side_effects=True,
        ),
        cost_estimate=cost(75e9, 50e6),
        name="ffn",
    )(x, og, gain, packed, hidden, wo, wh0, wh1, wr0, wr1)


def attn_bwd_head(first_slot, q_ref, k_ref, v_ref, do_ref, mixed_ref, lse, dq_ref, dk_ref, dv_ref, cols):
    seg = q_ref.shape[0] // 2
    half = seg // 2
    for stream in range(2):
        base = stream * seg
        rows = slice(base, base + seg)
        lse_row = lse[:, rows]
        weight = do_ref[rows, cols].astype(F32) * mixed_ref[rows, cols].astype(F32)
        delta_row = jnp.sum(weight.T, axis=0, keepdims=True)
        key_base = 2 * seg + stream * seg
        pieces = []
        if stream == 0:
            pieces += [(start, half, 0, "mem") for start in range(0, 2 * seg, half)]
        pieces += [(key_base, half, 0, "diag"), (key_base + half, half, half, "diag")]
        dq_low = jnp.zeros((half, HEAD_DIM), F32)
        dq_high = jnp.zeros((half, HEAD_DIM), F32)
        for start, size, first, kind in pieces:
            q = q_ref[base + first : base + seg, cols]
            do = do_ref[base + first : base + seg, cols]
            k = k_ref[start : start + size, cols]
            s = dot(k, q, NT) * EXP2_SCALE - lse_row[:, first:]
            if kind == "mem":
                slot = start + lax.broadcasted_iota(jnp.int32, s.shape, 0)
                s = jnp.where(slot >= first_slot, s, masked_score)
            else:
                key = lax.broadcasted_iota(jnp.int32, s.shape, 0)
                row = lax.broadcasted_iota(jnp.int32, s.shape, 1)
                s = jnp.where(key <= row, s, masked_score)
            p = jnp.exp2(s)
            dp = dot(v_ref[start : start + size, cols], do, NT)
            ds = (p * (dp - delta_row[:, first:])).astype(BF16)
            dv_ref[start : start + size, cols] = dot(p.astype(BF16), do).astype(BF16)
            dk_ref[start : start + size, cols] = (dot(ds, q) * SCALE).astype(BF16)
            dq = dot(ds, k, TN)
            if first == 0:
                dq_low = dq_low + dq[:half]
                dq_high = dq_high + dq[half:]
            else:
                dq_high = dq_high + dq
        dq_ref[base : base + half, cols] = (dq_low * SCALE).astype(BF16)
        dq_ref[base + half : base + seg, cols] = (dq_high * SCALE).astype(BF16)


def attn_back_kernel(
    resets_ref, offsets_ref, q_ref, k_ref, v_ref, do_ref, mix_ref, lse_ref, normed_hbm, mixed_hbm, ag_ref,
    ffn_part_ref, ffn_raw_ref, outputs_hbm,
    dq_ref, dk_ref, dv_ref, early_ref, late_ref, ffn_done_ref, outputs_got, outputs_sems,
    normed_ref, mixed_ref, held_sems, grads_ref, core_out0, core_in0, core_out1, core_in1, own_ref,
    *scratch,
):
    step = pl.program_id(0)
    last = pl.num_programs(0) - 1
    place = mesh_place()
    core, _, across = place
    partner = {"seq": 1 - core}
    lands, (core_sems, chip_sems) = list(scratch[:-2]), scratch[-2:]
    chunks, ffn_parts, ffn_raws = [], [], []
    first_slot = stream_a_slot(resets_ref, offsets_ref, core, q_ref.shape[0])
    outputs_copies = [
        remote(
            outputs_hbm.at[j, 1 - core], outputs_got.at[j],
            (outputs_sems.at[0, j], outputs_sems.at[1, j]), partner,
        )
        for j in range(2)
    ]
    held_copies = (
        pltpu.make_async_copy(normed_hbm, normed_ref, held_sems.at[0]),
        pltpu.make_async_copy(mixed_hbm, mixed_ref, held_sems.at[1]),
    )

    def chunk(number, data, left, order):
        mine = [lands.pop(0) for _ in order]
        return Chunk(data, left, order, mine, chip_sems.at[number], place)

    for which in range(2):
        order = ORDERS[which]
        chunks.append(chunk(3 * which, own_ref.at[which], BITS, order[:2]))
        ffn_parts.append(chunk(3 * which + 1, ffn_part_ref.at[which], order[2:][::-1], order[2:]))
        ffn_raws.append(chunk(3 * which + 2, ffn_raw_ref.at[which], BITS, order))
    index = lax.div(step, 2)
    rows = q_ref.shape[0]
    keys = k_ref.shape[0]
    pair = q_ref.shape[1]

    @pl.when(step == 0)
    def _():
        for copy in held_copies:
            copy.start()
        greet((partner,) + tuple({"dp": across(b)} for b in range(4)))
        for part in ffn_raws + ffn_parts:
            part.start(0)
        for copy in outputs_copies:
            copy.start()

    @pl.when(step == 1)
    def _():
        for part in ffn_parts:
            part.settle(0)
            part.start(1)

    @pl.when(step == 2)
    def _():
        for which in range(2):
            ffn_done_ref[which, 0] = ffn_parts[which].last(1)

    crossing = ((core_out0, core_in0), (core_out1, core_in1))

    def core_copy(which, index):
        sent, got = crossing[index]
        return remote(
            sent.at[which],
            got.at[which],
            (core_sems.at[0, which, index], core_sems.at[1, which, index]),
            partner,
        )

    head = 4 * jnp.where(lax.rem(step, 2) == 0, 1 - core, core) + 2 * index

    def one_head(h, _):
        attn_bwd_head(
            first_slot, q_ref, k_ref, v_ref, do_ref, mix_ref, lse_ref[pl.ds(head + h, 1), :],
            dq_ref, dk_ref, dv_ref, pl.ds(pl.multiple_of(h * HEAD_DIM, HEAD_DIM), HEAD_DIM),
        )
        for n in range(1, 4):

            @pl.when((step == n) & (h == 0))
            def _():
                for part in ffn_raws + (chunks if n == 3 else []):
                    swap = 0 if part in chunks else n - 1
                    part.settle(swap)
                    part.start(swap + 1)

        return 0

    lax.fori_loop(0, 2, one_head, 0)

    @pl.when(step == 0)
    def _():
        for copy in held_copies:
            copy.wait()

    less = pair + pair // 2
    grads_ref[0, :, :pair] = dot(normed_ref[keys - rows :], dq_ref[...], TN)
    grads_ref[1, :, :pair] = dot(normed_ref[...], dv_ref[...], TN)
    key_grads = dot(normed_ref[...], dk_ref[...], TN)
    grads_ref[0, :, pair:less] = key_grads[:, : pair // 2]
    grads_ref[1, :, pair:less] = key_grads[:, pair // 2 :]

    @pl.when(step < 2)
    def _():
        output_grads = dot(mixed_ref[...], ag_ref[...], TN)
        grads_ref[0, :, less:] = output_grads[:, :pair]
        grads_ref[1, :, less:] = output_grads[:, pair:]

    for n in range(2):

        @pl.when(step == 2 * n)
        def _():
            sent = crossing[n][0]
            for which in range(2):
                sent[which] = grads_ref[which, :, : sent.shape[2]].astype(BF16)
                core_copy(which, n).start()

    def own_grads(which, index, out_ref):
        core_copy(which, index).wait()
        got = crossing[index][1]
        total = grads_ref[which, :, : got.shape[2]] + got[which].astype(F32)
        out_ref[...] = total.astype(BF16).reshape(out_ref.shape)

    @pl.when(step == 1)
    def _():
        for which in range(2):
            own_grads(which, 0, own_ref.at[which])
            chunks[which].start(0)

    @pl.when(step == last)
    def _():
        for which in range(2):
            own_grads(which, 1, late_ref.at[which])
        for which in range(2):
            chunks[which].settle(1)
            early_ref[which] = own_ref[(which,) + chunks[which].rest(2)]
            ffn_done_ref[which, 1] = ffn_raws[which].last(3)
        for copy in outputs_copies:
            copy.wait()


def attn_back(resets, offsets, q, k, v, do, mixed, lse, normed, attn_grad, ffn_part, ffn_raw, outputs):
    rows, width = q.shape
    keys = k.shape[0]
    pair = 2 * HEAD_DIM
    more, less = 2 * pair + pair // 2, pair + pair // 2
    block = (width // 16, more)

    def by_pair(count):
        def index(i):
            core = lax.axis_index("seq")
            half = jnp.where(lax.rem(i, 2) == 0, 1 - core, core)
            return 0, 2 * half + lax.div(i, 2)

        return pl.BlockSpec((count, pair), index)

    def output_half(i):
        core = lax.axis_index("seq")
        return 0, jnp.where(i == 0, 1 - core, core)

    early, late = (2, 2, 2) + block, (2, 2, 2, 2, 2, width // 16, less)
    ffn_block = ffn_raw.shape[-2:]
    done = (2, 2) + ffn_block
    lands = []
    for order in ORDERS:
        lands += landings(BITS, order[:2], block)
        lands += landings(order[2:], order[2:], ffn_block)
        lands += landings(BITS, order, ffn_block)
    return pl.pallas_call(
        attn_back_kernel,
        grid=(4,),
        out_shape=(
            jax.ShapeDtypeStruct((rows, width), BF16),
            jax.ShapeDtypeStruct((keys, width), BF16),
            jax.ShapeDtypeStruct((keys, width), BF16),
            jax.ShapeDtypeStruct(early, BF16),
            jax.ShapeDtypeStruct(late, BF16),
            jax.ShapeDtypeStruct(done, F32),
            jax.ShapeDtypeStruct((2,) + outputs.shape[2:], BF16),
        ),
        in_specs=[
            pl.BlockSpec(memory_space=pltpu.SMEM),
            pl.BlockSpec(memory_space=pltpu.SMEM),
            by_pair(rows), by_pair(keys), by_pair(keys), by_pair(rows), by_pair(rows),
            held(lse.shape), pl.BlockSpec(memory_space=pl.ANY), pl.BlockSpec(memory_space=pl.ANY),
            pl.BlockSpec((rows, 2 * pair), output_half),
            held(ffn_part.shape), held(ffn_raw.shape), pl.BlockSpec(memory_space=pl.ANY),
        ],
        out_specs=(by_pair(rows), by_pair(keys), by_pair(keys), held(early), held(late), held(done),
            pl.BlockSpec(memory_space=pl.ANY),
        ),
        scratch_shapes=[
            pltpu.SemaphoreType.DMA((2, 2)),
            pltpu.VMEM(normed.shape, BF16),
            pltpu.VMEM(mixed.shape, BF16),
            pltpu.SemaphoreType.DMA((2,)),
            pltpu.VMEM((2, width, more), F32),
            pltpu.VMEM((2, width, more), BF16),
            pltpu.VMEM((2, width, more), BF16),
            pltpu.VMEM((2, width, less), BF16),
            pltpu.VMEM((2, width, less), BF16),
            pltpu.VMEM((2, 2, 2, 2, 2) + block, BF16),
        ] + lands + [
            pltpu.SemaphoreType.DMA((2, 2, 2)),
            pltpu.SemaphoreType.DMA((6, 2, 4)),
        ],
        compiler_params=pltpu.CompilerParams(
            vmem_limit_bytes=VMEM_LIMIT, dimension_semantics=("arbitrary",),
            collective_id=2, has_side_effects=True,
        ),
        cost_estimate=cost(45e9, 24e6),
        name="attn_back",
    )(resets, offsets, q, k, v, do, mixed, lse, normed, mixed, attn_grad, ffn_part, ffn_raw, outputs)


def rows_back_kernel(
    dq_ref, dk_ref, dv_ref, raw_ref, ag_ref, gain_ref, gain_ffn_ref, wq_hbm, wk_hbm, wv_hbm,
    early_ref, late_ref,
    mine_ref, theirs_ref, gains_ref, query_ref, key_ref, value_ref, output_ref,
    wq_ref, wk_ref, wv_ref, weight_sems, rows_out, gain_acc, gain_out, gain_in, *scratch,
):
    step = pl.program_id(0)
    last = pl.num_programs(0) - 1
    place = mesh_place()
    core, _, across = place
    partner = {"seq": 1 - core}
    lands, (row_sems, local_sems, gain_sems, chip_sems) = list(scratch[:-4]), scratch[-4:]

    chunks = []

    def chunk(data, left, order):
        number = len(chunks)
        mine = [lands.pop(0) for _ in order]
        chunks.append(Chunk(data, left, order, mine, chip_sems.at[number], place))
        return chunks[-1]

    early, late = [], []
    for which in range(2):
        early.append(chunk(early_ref.at[which], BITS[:2], ORDERS[which][2:]))
        late.append(chunk(late_ref.at[which], BITS, ORDERS[which]))

    rank = lax.axis_index("dp")

    def flipped(n, bits):
        return rank + sum(across(b) - rank for i, b in enumerate(bits) if n >> i & 1)

    gain_groups = (
        [{"dp": flipped(n >> 1, (0, 1)), "seq": 1 - core if n & 1 else core} for n in range(1, 8)],
        [{"dp": flipped(n, (2, 3))} for n in range(1, 4)],
    )

    def gain_copies(stage):
        first = 7 * stage
        return [
            remote(
                gain_out.at[stage],
                gain_in.at[first + n],
                (gain_sems.at[0, first + n], gain_sems.at[1, first + n]),
                device,
            )
            for n, device in enumerate(gain_groups[stage])
        ]

    def gain_total(stage):
        for copy in gain_copies(stage):
            copy.wait()
        return gain_out[stage] + sum(gain_in[7 * stage + n] for n in range(len(gain_groups[stage])))

    def row_copy(block):
        stream = block // 2
        return remote(
            rows_out.at[block], theirs_ref.at[stream], (row_sems.at[0, stream], row_sems.at[1, stream]), partner
        )

    def row_keep(block):
        stream = block // 2
        return pltpu.make_async_copy(rows_out.at[block], mine_ref.at[stream], local_sems.at[stream])

    weights = [
        pltpu.make_async_copy(src, dst, weight_sems.at[n])
        for n, (src, dst) in enumerate(((wk_hbm, wk_ref), (wv_hbm, wv_ref), (wq_hbm, wq_ref)))
    ]

    @pl.when(step == 0)
    def _():
        for copy in weights:
            copy.start()
        greet(gain_groups[0] + gain_groups[1])
        for part in late + early:
            part.start(0)
        for copy in weights[:2]:
            copy.wait()
        gain_acc[...] = jnp.zeros_like(gain_acc)

    def normed_grad():
        return dot(dk_ref[...], wk_ref[...], NT) + dot(dv_ref[...], wv_ref[...], NT)

    unit, inverse = norm_parts(raw_ref[...].astype(F32))

    @pl.when(step < 4)
    def _():
        gain_acc[0:1] += jnp.sum(normed_grad() * unit, axis=0, keepdims=True)

    @pl.when(step == 4)
    def _():
        weights[2].wait()

    @pl.when(step >= 4)
    def _():
        grad = normed_grad() + dot(dq_ref[...], wq_ref[...], NT)
        gain_acc[0:1] += jnp.sum(grad * unit, axis=0, keepdims=True)
        rows_grad = norm_back(grad * gain_ref[...], unit, inverse)
        rows_out[step - 4] = (rows_grad + ag_ref[...].astype(F32)).astype(BF16)

    for block in range(4):
        stays = core == block % 2
        pl.when((step == block + 4) & stays)(row_keep(block).start)
        pl.when((step == block + 4) & jnp.logical_not(stays))(row_copy(block).start)

    @pl.when(step == 4)
    def _():
        for part in early:
            part.settle(0)
            part.start(1)

    @pl.when(step == 5)
    def _():
        for part in late:
            part.settle(0)
            part.start(1)

    @pl.when(step == last)
    def _():
        lanes = gain_out.shape[2]
        for n in range(8):
            cols = slice(n * lanes, (n + 1) * lanes)
            gain_out[0, n : n + 1] = gain_acc[0:1, cols]
            gain_out[0, 8 + n : 9 + n] = gain_ffn_ref[:, cols]
        for copy in gain_copies(0):
            copy.start()
        pair = 2 * HEAD_DIM
        for which, ref in enumerate((query_ref, value_ref)):
            total = early[which].last(1)
            ref[:, :pair] = total[:, :pair]
            key_ref[:, which * HEAD_DIM : (which + 1) * HEAD_DIM] = total[:, pair : pair + HEAD_DIM]
            output_ref[:, which * pair : (which + 1) * pair] = total[:, pair + HEAD_DIM :]
        for part in late:
            part.settle(1)
            part.start(2)
        gain_out[1] = gain_total(0)
        for copy in gain_copies(1):
            copy.start()
        for part in late:
            part.settle(2)
            part.start(3)
        gains_ref[...] = gain_total(1)
        for which, ref in enumerate((query_ref, value_ref)):
            total = late[which].last(3)
            ref[:, pair:] = total[:, :pair]
            key_ref[:, pair + which * HEAD_DIM : pair + (which + 1) * HEAD_DIM] = total[:, pair:]
        for block in range(4):
            stays = core == block % 2
            pl.when(stays)(row_keep(block).wait)
            pl.when(jnp.logical_not(stays))(row_copy(block).wait_send)
        for stream in range(2):
            row_copy(2 * stream).wait_recv()


def rows_back(
    dq, dk, dv, raw, attn_grad, gain, gain_ffn, wq, wk, wv, early, late
):
    keys, width = dk.shape
    rows = dq.shape[0]
    size = keys // 8
    key_block = pl.BlockSpec((size, width), lambda i: (i, 0))
    row_block = pl.BlockSpec((size, width), lambda i: (jnp.maximum(i - 4, 0), 0))
    anywhere = pl.BlockSpec(memory_space=pl.ANY)
    rows_shape = jax.ShapeDtypeStruct((2, size, width), BF16)
    early_block, late_block = early.shape[-2:], late.shape[-2:]
    lands = []
    for order in ORDERS:
        lands += landings(BITS[:2], order[2:], early_block)
        lands += landings(BITS, order, late_block)
    out = (early_block[0], 4 * HEAD_DIM)
    vector = (16, width // 8)
    return pl.pallas_call(
        rows_back_kernel,
        grid=(8,),
        out_shape=(
            rows_shape, rows_shape,
            jax.ShapeDtypeStruct(vector, F32),
        ) + (jax.ShapeDtypeStruct(out, F32),) * 4,
        in_specs=[
            row_block, key_block, key_block, key_block, row_block,
            held(gain.shape), held(gain_ffn.shape), anywhere, anywhere, anywhere,
            held(early.shape), held(late.shape),
        ],
        out_specs=(
            anywhere, anywhere, held(vector),
        ) + (held(out),) * 4,
        scratch_shapes=[
            pltpu.VMEM(wq.shape, BF16),
            pltpu.VMEM(wk.shape, BF16),
            pltpu.VMEM(wv.shape, BF16),
            pltpu.SemaphoreType.DMA((3,)),
            pltpu.VMEM((4, size, width), BF16),
            pltpu.VMEM((8, width), F32),
            pltpu.VMEM((2,) + vector, F32),
            pltpu.VMEM((10,) + vector, F32),
        ] + lands + [
            pltpu.SemaphoreType.DMA((2, 2)),
            pltpu.SemaphoreType.DMA((2,)),
            pltpu.SemaphoreType.DMA((2, 10)),
            pltpu.SemaphoreType.DMA((4, 2, 4)),
        ],
        compiler_params=pltpu.CompilerParams(
            vmem_limit_bytes=VMEM_LIMIT, dimension_semantics=("arbitrary",),
            collective_id=3, has_side_effects=True,
        ),
        cost_estimate=cost(20e9, 24e6),
        name="rows_back",
    )(
        dq, dk, dv, raw, attn_grad, gain, gain_ffn, wq, wk, wv,
        early, late,
    )


def place_kernel(
    resets_ref, offsets_ref, own_a_ref, got_a_ref, own_b_ref, got_b_ref, out_a_ref, out_b_ref
):
    mine = lax.rem(pl.program_id(0), 2) == lax.axis_index("seq")
    out_a_ref[...] = jnp.where(mine, own_a_ref[...], got_a_ref[...])
    out_b_ref[...] = jnp.where(mine, own_b_ref[...], got_b_ref[...])


def place_rows(resets, offsets, outputs, outputs_got, mine_rows, their_rows):
    _, _, half, width = outputs.shape

    def slot(i, resets_ref, offsets_ref, core):
        first = first_slots(resets_ref, offsets_ref, core, 4 * half)[0]
        return jnp.where(lax.div(i, 2) == jnp.where(first >= 4 * half, 1, 0), 0, 1)

    def own(i, *refs):
        return slot(i, *refs, lax.axis_index("seq"))

    def got(i, *refs):
        return slot(i, *refs, 1 - lax.axis_index("seq"))

    block = (None, half, width)
    out = jax.ShapeDtypeStruct((4, half, width), BF16)
    return pl.pallas_call(
        place_kernel,
        out_shape=(out, out),
        grid_spec=pltpu.PrefetchScalarGridSpec(
            num_scalar_prefetch=2,
            grid=(4,),
            in_specs=[
                pl.BlockSpec(
                    (None, None, half, width), lambda *a: (own(*a), lax.axis_index("seq"), 0, 0)
                ),
                pl.BlockSpec(block, lambda *a: (got(*a), 0, 0)),
                pl.BlockSpec(block, lambda *a: (own(*a), 0, 0)),
                pl.BlockSpec(block, lambda *a: (got(*a), 0, 0)),
            ],
            out_specs=(pl.BlockSpec(block, lambda i, *_: (i, 0, 0)),) * 2,
        ),
        compiler_params=params(),
        cost_estimate=cost(0, 8e6),
        name="place",
    )(resets, offsets, outputs, outputs_got, mine_rows, their_rows)


def swap_dp(block, bit):
    count = lax.axis_size("dp")
    return lax.ppermute(block, "dp", [(i, i ^ (1 << bit)) for i in range(count)])


def swap_core(block):
    return lax.ppermute(block, "seq", [(0, 1), (1, 0)])


def on_device_pair(
    inputs, memory, compressed, offsets, resets, w_query, w_key, w_value, w_output, w_hidden,
    w_return, w_compress, gain_attn, gain_ffn, out_grad, comp_grad,
):
    core = lax.axis_index("seq")
    dp_count = lax.axis_size("dp")
    streams, half, width = inputs.shape
    seg = 2 * half
    low_core = core == 0

    unused = (resets != 0) | (offsets >= 2 * seg)
    gain_a = gain_attn.astype(F32).reshape(1, width)
    gain_f = gain_ffn.astype(F32).reshape(1, width)

    x_in, x_mem, x_old, x_og, new_rows, kept_p, sent_p, kept_q, sent_q = front(
        resets, inputs, memory, compressed, out_grad, w_compress, comp_grad
    )
    got_p, got_q = swap_dp(sent_p, 0), swap_dp(sent_q, 1)
    all_rows, normed, q, k, v, og = project_rows(
        resets, offsets, x_old, x_mem, x_in, x_og, gain_a, w_query, w_key, w_value
    )
    mixed, hidden, ffn_in, lse, packed, wh_other, wr_other = attn_fwd(
        resets, offsets, q, k, v, all_rows, w_output, gain_f, kept_p, got_p, kept_q, got_q,
        w_hidden, w_return,
    )
    outputs, attn_grad, mixed_grad, gain_ffn_grad, ffn_done, ffn_part, ffn_raw, grad_compress = ffn(
        ffn_in, og, gain_f, packed, hidden, w_output, wh_other, w_hidden, wr_other, w_return
    )
    outputs = outputs.reshape(2, 2, half, width)
    dq, dk, dv, early, late, ffn_rest, outputs_got = attn_back(
        resets, offsets, q, k, v, mixed_grad, mixed, lse, normed, attn_grad, ffn_part, ffn_raw,
        outputs,
    )
    mine_rows, their_rows, gains, grad_query, grad_key, grad_value, grad_output = rows_back(
        dq, dk, dv, all_rows, attn_grad, gain_a, gain_ffn_grad, w_query, w_key, w_value, early, late
    )

    def tiles(which):
        parts = [ffn_done[which, i] for i in range(2)] + [ffn_rest[which, i] for i in range(2)]
        return jnp.concatenate(parts, axis=1)

    grad_hidden, grad_return = tiles(0), tiles(1).T
    rank = lax.axis_index("dp")
    gains = lax.dynamic_slice_in_dim(gains.reshape(2, width), rank * (width // dp_count), width // dp_count, 1)

    placed_outputs, input_grad = place_rows(
        resets, offsets, outputs, outputs_got, mine_rows, their_rows
    )
    return (
        placed_outputs,
        new_rows[:, : comp_grad.shape[1]],
        input_grad,
        grad_query,
        grad_key,
        grad_value,
        grad_output,
        grad_hidden,
        grad_return,
        grad_compress,
        gains[0],
        gains[1],
    )


def solution(mesh):
    placed = (
        P("dp", "seq", None),
        P("dp", "seq", None),
        P("dp", "seq", None),
        P("dp"),
        P("dp"),
        P(),
        P(),
        P(),
        P(),
        P(None, "seq"),
        P("seq", None),
        P(),
        P(),
        P(),
        P("dp", "seq", None),
        P("dp", None, None),
    )
    fast = mesh.shape["seq"] == 2 and mesh.shape["dp"] == 16
    return jax.shard_map(
        on_device_pair if fast else on_device,
        mesh=mesh,
        in_specs=placed,
        out_specs=(
            P("dp", "seq", None),
            P("dp", None, None),
            P("dp", "seq", None),
            P("dp", "seq"),
            P("dp", "seq"),
            P("dp", "seq"),
            P("dp", "seq"),
            P("dp", "seq"),
            P("seq", "dp"),
            P("dp", "seq"),
            P("dp"),
            P("dp"),
        ),
        check_vma=False,
    )
```

```python
import functools
import math

import jax
import jax.numpy as jnp
from jax import lax
from jax.experimental import pallas as pl
from jax.experimental.pallas import tpu as pltpu
from jax.sharding import PartitionSpec as P

HEADS = 8
HEAD_DIM = 128
RATE = 3


epsilon = 1e-05
masked_score = -1e30


def shifted(block, axis, distance):
    devices = range(lax.axis_size(axis))
    route = [(i - distance, i) for i in devices if i - distance in devices]
    return lax.ppermute(block, axis, route)


def layer_norm(values, gain):
    centred = values - jnp.mean(values, axis=-1, keepdims=True)
    spread = jnp.mean(centred * centred, axis=-1, keepdims=True)
    return centred * lax.rsqrt(spread + epsilon) * gain


def project(left, right):
    return jnp.einsum("srd,de->sre", left, right, preferred_element_type=jnp.float32)


def project_back(left, right):
    return jnp.einsum("sre,de->srd", left, right, preferred_element_type=jnp.float32)


def weight_term(left, right):
    return jnp.einsum("srd,sre->de", left, right, preferred_element_type=jnp.float32)


def key_layout(key_index, local_rows, seg_len):
    key_owner = key_index // (3 * local_rows)
    inside = key_index % (3 * local_rows)
    key_kind = inside // local_rows
    key_place = key_owner * local_rows + inside % local_rows
    mem_slot = jnp.where(key_kind == 0, key_place, seg_len + key_place)
    return (key_kind, mem_slot, key_place)


def allowed_mask(key_kind, mem_slot, key_place, query_place, offsets, keep_flag):
    memory_ok = (mem_slot[None, :] >= offsets[:, None]) & keep_flag[:, None]
    causal = key_place[None, :] <= query_place[:, None]
    return jnp.where(key_kind[None, None, :] < 2, memory_ok[:, None, :], causal[None, :, :])


def score_block(query_heads, key_heads, allowed, score_scale):
    scores = (
        jnp.einsum("sthe,skhe->shtk", query_heads, key_heads, preferred_element_type=jnp.float32)
        * score_scale
    )
    return jnp.where(allowed[:, None], scores, masked_score)


def tile_matrix(matrix, dp_count, seq_count):
    rows_total, cols_total = matrix.shape
    blocks = matrix.reshape(dp_count, rows_total // dp_count, seq_count, cols_total // seq_count)
    return blocks.transpose(0, 2, 1, 3).reshape(
        dp_count * seq_count, rows_total // dp_count, cols_total // seq_count
    )


def tile_vector(vector, dp_count, seq_count):
    piece_len = vector.shape[0] // dp_count
    pieces = vector.reshape(dp_count, 1, piece_len)
    return jnp.broadcast_to(pieces, (dp_count, seq_count, piece_len)).reshape(
        dp_count * seq_count, piece_len
    )


def on_device(
    inputs,
    memory,
    compressed,
    offsets,
    resets,
    w_query,
    w_key,
    w_value,
    w_output,
    w_hidden,
    w_return,
    w_compress,
    gain_attn,
    gain_ffn,
    out_grad,
    comp_grad,
):
    seq_count = lax.axis_size("seq")
    dp_count = lax.axis_size("dp")
    seq_rank = lax.axis_index("seq")
    streams, local_rows, feat_width = inputs.shape
    seg_len = local_rows * seq_count
    score_scale = HEAD_DIM ** (-0.5)
    keep_flag = resets == 0
    all_rows = jnp.concatenate([compressed, memory, inputs], axis=1).astype(jnp.float32)
    normed, attn_norm_back = jax.vjp(layer_norm, all_rows, gain_attn.astype(jnp.float32))
    normed_low = normed.astype(jnp.bfloat16)
    query_in = normed_low[:, 2 * local_rows :]
    query_low = project(query_in, w_query).astype(jnp.bfloat16)
    key_low = project(normed_low, w_key).astype(jnp.bfloat16)
    value_low = project(normed_low, w_value).astype(jnp.bfloat16)
    key_all, value_all = (
        lax.all_gather(key_low, "seq", axis=1, tiled=True),
        lax.all_gather(value_low, "seq", axis=1, tiled=True),
    )
    total_keys = key_all.shape[1]
    key_kind, mem_slot, key_place = key_layout(
        jnp.arange(total_keys, dtype=jnp.int32), local_rows, seg_len
    )
    query_place = seq_rank * local_rows + jnp.arange(local_rows, dtype=jnp.int32)
    allowed = allowed_mask(key_kind, mem_slot, key_place, query_place, offsets, keep_flag)
    query_heads = query_low.reshape(streams, local_rows, HEADS, HEAD_DIM)
    key_heads = key_all.reshape(streams, total_keys, HEADS, HEAD_DIM)
    value_heads = value_all.reshape(streams, total_keys, HEADS, HEAD_DIM)
    scores = score_block(query_heads, key_heads, allowed, score_scale)
    row_top = jnp.max(scores, axis=-1, keepdims=True)
    exp_scores = jnp.exp(scores - row_top)
    row_total = jnp.sum(exp_scores, axis=-1, keepdims=True)
    attn_prob = exp_scores / row_total
    log_total = row_top + jnp.log(row_total)
    mixed_low = (
        jnp.einsum(
            "shtk,skhe->sthe",
            attn_prob.astype(jnp.bfloat16),
            value_heads,
            preferred_element_type=jnp.float32,
        )
        .reshape(streams, local_rows, feat_width)
        .astype(jnp.bfloat16)
    )
    hidden = inputs.astype(jnp.float32) + project(mixed_low, w_output)
    ffn_in, ffn_norm_back = jax.vjp(layer_norm, hidden, gain_ffn.astype(jnp.float32))
    ffn_low = ffn_in.astype(jnp.bfloat16)
    ffn_all = lax.all_gather(ffn_low, "seq", axis=1, tiled=True)
    pre_act = jnp.einsum("std,df->stf", ffn_all, w_hidden, preferred_element_type=jnp.float32)
    act_float, gelu_back = jax.vjp(jax.nn.gelu, pre_act)
    act_low = act_float.astype(jnp.bfloat16)
    partial_out = jnp.einsum("stf,fd->std", act_low, w_return, preferred_element_type=jnp.float32)
    ffn_out = lax.psum_scatter(
        partial_out.astype(jnp.bfloat16), "seq", scatter_dimension=1, tiled=True
    ).astype(jnp.float32)
    cot_all = lax.all_gather(out_grad, "seq", axis=1, tiled=True)
    act_grad = jnp.einsum("std,fd->stf", cot_all, w_return, preferred_element_type=jnp.float32)
    return_part = jnp.einsum("stf,std->fd", act_low, cot_all, preferred_element_type=jnp.float32)
    pre_grad = gelu_back(act_grad)[0].astype(jnp.bfloat16)
    hidden_part = jnp.einsum("std,stf->df", ffn_all, pre_grad, preferred_element_type=jnp.float32)
    in_part = jnp.einsum("stf,df->std", pre_grad, w_hidden, preferred_element_type=jnp.float32)
    ffn_in_grad = lax.psum_scatter(in_part, "seq", scatter_dimension=1, tiled=True)
    hidden_sum, return_sum = (
        lax.psum_scatter(
            hidden_part.astype(jnp.bfloat16), "dp", scatter_dimension=0, tiled=True
        ).astype(jnp.float32),
        lax.psum_scatter(
            return_part.T.astype(jnp.bfloat16), "dp", scatter_dimension=0, tiled=True
        ).astype(jnp.float32),
    )
    grad_return = return_sum.T
    outputs = (hidden + ffn_out).astype(jnp.bfloat16)
    hidden_grad, gain_ffn_grad = ffn_norm_back(ffn_in_grad)
    hidden_grad = hidden_grad + out_grad.astype(jnp.float32)
    attn_grad_low = hidden_grad.astype(jnp.bfloat16)
    output_part = weight_term(mixed_low, attn_grad_low)
    mixed_grad = project_back(attn_grad_low, w_output).astype(jnp.bfloat16)
    mixed_heads = mixed_grad.reshape(streams, local_rows, HEADS, HEAD_DIM)
    prob_again = jnp.exp(score_block(query_heads, key_heads, allowed, score_scale) - log_total)
    prob_grad = jnp.einsum(
        "sthe,skhe->shtk", mixed_heads, value_heads, preferred_element_type=jnp.float32
    )
    prob_delta = jnp.sum(prob_again * prob_grad, axis=-1)
    score_grad = (prob_again * (prob_grad - prob_delta[..., None])).astype(jnp.bfloat16)
    query_grad = (
        (
            jnp.einsum("shtk,skhe->sthe", score_grad, key_heads, preferred_element_type=jnp.float32)
            * score_scale
        )
        .reshape(streams, local_rows, feat_width)
        .astype(jnp.bfloat16)
    )
    key_part = (
        jnp.einsum("shtk,sthe->skhe", score_grad, query_heads, preferred_element_type=jnp.float32)
        * score_scale
    ).reshape(streams, total_keys, feat_width)
    value_part = jnp.einsum(
        "shtk,sthe->skhe",
        prob_again.astype(jnp.bfloat16),
        mixed_heads,
        preferred_element_type=jnp.float32,
    ).reshape(streams, total_keys, feat_width)
    key_sum, value_sum = (
        lax.psum_scatter(
            key_part.astype(jnp.bfloat16), "seq", scatter_dimension=1, tiled=True
        ).astype(jnp.float32),
        lax.psum_scatter(
            value_part.astype(jnp.bfloat16), "seq", scatter_dimension=1, tiled=True
        ).astype(jnp.float32),
    )
    key_grad = key_sum.astype(jnp.bfloat16)
    value_grad = value_sum.astype(jnp.bfloat16)
    query_part = weight_term(query_in, query_grad)
    key_wpart = weight_term(normed_low, key_grad)
    value_wpart = weight_term(normed_low, value_grad)
    query_back = project_back(query_grad, w_query)
    normed_grad = project_back(key_grad, w_key) + project_back(value_grad, w_value)
    normed_grad = normed_grad + jnp.concatenate(
        [jnp.zeros((streams, 2 * local_rows, feat_width), jnp.float32), query_back], axis=1
    )
    rows_grad, gain_attn_grad = attn_norm_back(normed_grad)
    input_grad = (rows_grad[:, 2 * local_rows :] + hidden_grad).astype(jnp.bfloat16)
    kept_memory = memory * keep_flag[:, None, None].astype(jnp.bfloat16)
    edge_rows = shifted(kept_memory[:, : 2 * (RATE - 1)], "seq", -1)
    extended = jnp.concatenate([kept_memory, edge_rows], axis=1)
    group_count = (local_rows + RATE - 1) // RATE
    first_group = (seq_rank * local_rows + RATE - 1) // RATE
    slice_start = RATE * first_group - seq_rank * local_rows
    grouped = lax.dynamic_slice_in_dim(extended, slice_start, RATE * group_count, 1).reshape(
        streams, group_count, RATE * feat_width
    )
    piece_rows = jnp.einsum(
        "sgc,cd->sgd", grouped, w_compress, preferred_element_type=jnp.float32
    ).astype(jnp.bfloat16)
    comp_all = lax.all_gather(piece_rows, "seq", axis=1, tiled=True)
    comp_count = comp_grad.shape[1]
    out_index = jnp.arange(comp_count, dtype=jnp.int32)
    holder = RATE * out_index // local_rows
    lookup = holder * group_count + out_index - (holder * local_rows + RATE - 1) // RATE
    new_compressed = jnp.take(comp_all, lookup, axis=1)
    slot_index = first_group + jnp.arange(group_count, dtype=jnp.int32)
    slot_valid = (RATE * slot_index < (seq_rank + 1) * local_rows) & (slot_index < comp_count)
    picked = jnp.take(comp_grad, jnp.minimum(slot_index, comp_count - 1), axis=1) * slot_valid[
        None, :, None
    ].astype(jnp.bfloat16)
    compress_part = jnp.einsum("sgc,sgd->cd", grouped, picked, preferred_element_type=jnp.float32)
    reduced = (
        lax.psum_scatter(
            tile_matrix(query_part, dp_count, seq_count),
            ("dp", "seq"),
            scatter_dimension=0,
            tiled=True,
        ),
        lax.psum_scatter(
            tile_matrix(key_wpart, dp_count, seq_count),
            ("dp", "seq"),
            scatter_dimension=0,
            tiled=True,
        ),
        lax.psum_scatter(
            tile_matrix(value_wpart, dp_count, seq_count),
            ("dp", "seq"),
            scatter_dimension=0,
            tiled=True,
        ),
        lax.psum_scatter(
            tile_matrix(output_part, dp_count, seq_count),
            ("dp", "seq"),
            scatter_dimension=0,
            tiled=True,
        ),
        lax.psum_scatter(
            tile_matrix(compress_part, dp_count, seq_count),
            ("dp", "seq"),
            scatter_dimension=0,
            tiled=True,
        ),
        lax.psum_scatter(
            tile_vector(gain_attn_grad, dp_count, seq_count),
            ("dp", "seq"),
            scatter_dimension=0,
            tiled=True,
        ),
        lax.psum_scatter(
            tile_vector(gain_ffn_grad, dp_count, seq_count),
            ("dp", "seq"),
            scatter_dimension=0,
            tiled=True,
        ),
    )
    return (
        outputs,
        new_compressed,
        input_grad,
        reduced[0][0],
        reduced[1][0],
        reduced[2][0],
        reduced[3][0],
        hidden_sum,
        grad_return,
        reduced[4][0],
        reduced[5][0],
        reduced[6][0],
    )


F32 = jnp.float32
BF16 = jnp.bfloat16
NN = (((1,), (0,)), ((), ()))
NT = (((1,), (1,)), ((), ()))
TN = (((0,), (0,)), ((), ()))
VMEM_LIMIT = 60 * 1024 * 1024
SCALE = HEAD_DIM ** (-0.5)
EXP2_SCALE = SCALE * math.log2(math.e)


def dot(left, right, dims=NN):
    return lax.dot_general(left, right, dims, preferred_element_type=F32)


def params(steps=1):
    return pltpu.CompilerParams(
        vmem_limit_bytes=VMEM_LIMIT, dimension_semantics=("arbitrary",) * steps
    )


def cost(flops, bytes_accessed=0, transcendentals=0):
    return pl.CostEstimate(
        flops=int(flops), bytes_accessed=int(bytes_accessed), transcendentals=int(transcendentals)
    )


def held(shape):
    zeros = (0,) * len(shape)
    return pl.BlockSpec(shape, lambda *_: zeros, pipeline_mode=pl.Buffered(1))


def norm_parts(rows):
    centred = rows - jnp.mean(rows, axis=-1, keepdims=True)
    inverse = lax.rsqrt(jnp.mean(centred * centred, axis=-1, keepdims=True) + epsilon)
    return centred * inverse, inverse


def norm_back(grad, unit, inverse):
    return inverse * (
        grad
        - jnp.mean(grad, axis=-1, keepdims=True)
        - unit * jnp.mean(grad * unit, axis=-1, keepdims=True)
    )


def add_low(left, right):
    return (left.astype(F32) + right.astype(F32)).astype(BF16)


def mesh_place():
    rank, core = lax.axis_index("dp"), lax.axis_index("seq")

    def bit(b):
        return lax.rem(lax.div(rank, 1 << b), 2)

    def across(b):
        return rank + (1 << b) * (1 - 2 * bit(b))

    return core, bit, across


def first_slots(resets_ref, offsets_ref, core, total):
    return [
        jnp.where(resets_ref[core + 2 * j] != 0, total, offsets_ref[core + 2 * j]) for j in range(2)
    ]


def stream_a_slot(resets_ref, offsets_ref, core, total):
    first, second = first_slots(resets_ref, offsets_ref, core, total)
    return jnp.where(first >= total, second, first)


def greet(devices):
    barrier = pltpu.get_barrier_semaphore()
    for device in devices:
        pl.semaphore_signal(
            barrier, inc=1, device_id=device, device_id_type=pl.DeviceIdType.MESH
        )
    pl.semaphore_wait(barrier, len(devices))


def remote(src, dst, sems, device):
    return pltpu.make_async_remote_copy(
        src_ref=src,
        dst_ref=dst,
        send_sem=sems[0],
        recv_sem=sems[1],
        device_id=device,
        device_id_type=pl.DeviceIdType.MESH,
    )


class Chunk:
    def __init__(self, data, left, order, landing, sems, place):
        self.data, self.left, self.order = data, left, order
        self.landing, self.sems = landing, sems
        _, self.bit, self.across = place

    def at(self, swap, away):
        index = []
        for b in self.left:
            if b in self.order[:swap]:
                index.append(self.bit(b))
            elif swap < len(self.order) and b == self.order[swap]:
                index.append(1 - self.bit(b) if away else self.bit(b))
            else:
                index.append(slice(None))
        return tuple(index)

    def rest(self, swap):
        done = self.order[:swap]
        return tuple(self.bit(b) if b in done else slice(None) for b in self.left)

    def copy(self, swap):
        return remote(
            self.data.at[self.at(swap, True)],
            self.landing[swap],
            (self.sems.at[0, swap], self.sems.at[1, swap]),
            {"dp": self.across(self.order[swap])},
        )

    def start(self, swap):
        self.copy(swap).start()

    def settle(self, swap):
        self.copy(swap).wait()
        here = self.at(swap, False)
        self.data[here] = add_low(self.data[here], self.landing[swap][...])

    def last(self, swap):
        self.copy(swap).wait()
        return self.data[self.at(swap, False)].astype(F32) + self.landing[swap][...].astype(F32)


def landings(left, order, block):
    shapes, count = [], len(left)
    for _ in order:
        count -= 1
        shapes.append(pltpu.VMEM((2,) * count + block, BF16))
    return shapes


BITS = (3, 2, 1, 0)
ORDERS = ((0, 1, 2, 3), (1, 0, 2, 3))


def front_kernel(
    resets_ref, in_ref, mem_ref, old_ref, og_ref, wc_ref, cg_ref,
    x_in_ref, x_mem_ref, x_old_ref, x_og_ref, new_ref, kept_p_ref, sent_p_ref, kept_q_ref, sent_q_ref,
    mem, x_in, x_old, x_og, wc, new, core_out, core_in, row_sems, wc_sem, new_sems, core_sems, out_sems,
):
    core, bit, _ = mesh_place()
    partner = {"seq": 1 - core}
    width = in_ref.shape[2]
    groups = cg_ref.shape[1]

    weights = pltpu.make_async_copy(wc_ref, wc, wc_sem)
    weights.start()
    greet((partner,))
    moves = []
    for n, (src, dst) in enumerate(
        ((mem_ref, mem), (in_ref, x_in), (old_ref, x_old), (og_ref, x_og))
    ):
        for j in range(2):
            away = remote(
                src.at[1 - core + 2 * j], dst.at[j, core], (row_sems.at[0, n, j], row_sems.at[1, n, j]), partner
            )
            here = pltpu.make_async_copy(src.at[core + 2 * j], dst.at[j, core], row_sems.at[2, n, j])
            away.start()
            here.start()
            moves.append((away, here))
    new[...] = jnp.zeros_like(new)
    outs = []
    for j in range(2):
        moves[j][0].wait_recv()
        moves[j][1].wait()
    outs.append(pltpu.make_async_copy(mem, x_mem_ref, out_sems.at[0]))
    outs[-1].start()
    weights.wait()

    grouped = []
    for j in range(2):
        rows = mem[j].reshape(2 * mem.shape[2], width)
        group = lax.broadcasted_iota(jnp.int32, (groups, rows.shape[0]), 0)
        row = lax.broadcasted_iota(jnp.int32, (groups, rows.shape[0]), 1)
        keep = jnp.where(resets_ref[core + 2 * j] == 0, 1.0, 0.0)
        total = jnp.zeros((groups, width), F32)
        mine = []
        for r in range(RATE):
            pick = jnp.where(row == RATE * group + r, keep, 0.0).astype(BF16)
            mine.append(dot(pick, rows).astype(BF16))
            total = total + dot(mine[-1], wc[r * width : (r + 1) * width])
        grouped.append(mine)
        new[j, :groups] = total.astype(BF16)

    news = []
    for j in range(2):
        at = core + 2 * j
        news.append(remote(new.at[j], new_ref.at[at], (new_sems.at[0, j], new_sems.at[1, j]), partner))
        outs.append(pltpu.make_async_copy(new.at[j], new_ref.at[at], new_sems.at[2, j]))
        news[-1].start()
        outs[-1].start()

    half = width // 2

    def grad(r, side):
        cols = pl.ds(pl.multiple_of(side * half, half), half)
        return sum(dot(grouped[j][r], cg_ref[core + 2 * j, :, cols], TN) for j in range(2))

    crossing = []
    for r in range(RATE):
        core_out[r] = grad(r, 1 - core).astype(BF16)
        crossing.append(
            remote(core_out.at[r], core_in.at[r], (core_sems.at[0, r], core_sems.at[1, r]), partner)
        )
        crossing[-1].start()
    for n, (src, dst) in enumerate(((x_in, x_in_ref), (x_old, x_old_ref), (x_og, x_og_ref))):
        for away, here in moves[2 * n + 2 : 2 * n + 4]:
            away.wait_recv()
            here.wait()
        outs.append(pltpu.make_async_copy(src, dst, out_sems.at[1 + n]))
        outs[-1].start()
    fine = width // 16
    quarter = half // 2
    for r in range(RATE):
        total = grad(r, core)
        crossing[r].wait()
        total = (total + core_in[r].astype(F32)).astype(BF16)
        for which, (kept_ref, sent_ref) in enumerate(
            ((kept_p_ref, sent_p_ref), (kept_q_ref, sent_q_ref))
        ):
            for mine in range(2):

                @pl.when(bit(which) == mine)
                def _():
                    for t in range(16):
                        block, third = divmod(r * 16 + t, RATE)
                        place = (block >> 3, block >> 2 & 1, block >> (1 - which) & 1)
                        ref = kept_ref if block >> which & 1 == mine else sent_ref
                        ref[place + (slice(third * fine, (third + 1) * fine),)] = total[
                            t * fine : (t + 1) * fine, which * quarter : (which + 1) * quarter
                        ]
    for away, _ in moves:
        away.wait_send()
    for move in outs + news:
        move.wait()


def front(resets, inputs, memory, compressed, out_grad, w_compress, comp_grad):
    streams, half, width = inputs.shape
    anywhere = pl.BlockSpec(memory_space=pl.ANY)
    vmem = pl.BlockSpec(memory_space=pltpu.VMEM)
    pair = jax.ShapeDtypeStruct((2, 2, half, width), BF16)
    padded = -(-comp_grad.shape[1] // 16) * 16
    part = jax.ShapeDtypeStruct((2, 2, 2, RATE * width // 16, width // 4), BF16)
    return pl.pallas_call(
        front_kernel,
        out_shape=(
            pair, pair, pair, pair, jax.ShapeDtypeStruct((streams, padded, width), BF16),
            part, part, part, part,
        ),
        in_specs=[pl.BlockSpec(memory_space=pltpu.SMEM)] + [anywhere] * 5 + [vmem],
        out_specs=(anywhere,) * 5 + (vmem,) * 4,
        scratch_shapes=[
            pltpu.VMEM((2, 2, half, width), BF16),
            pltpu.VMEM((2, 2, half, width), BF16),
            pltpu.VMEM((2, 2, half, width), BF16),
            pltpu.VMEM((2, 2, half, width), BF16),
            pltpu.VMEM(w_compress.shape, BF16),
            pltpu.VMEM((2, padded, width), BF16),
            pltpu.VMEM((RATE, width, width // 2), BF16),
            pltpu.VMEM((RATE, width, width // 2), BF16),
            pltpu.SemaphoreType.DMA((3, 4, 2)),
            pltpu.SemaphoreType.DMA,
            pltpu.SemaphoreType.DMA((3, 2)),
            pltpu.SemaphoreType.DMA((2, RATE)),
            pltpu.SemaphoreType.DMA((4,)),
        ],
        compiler_params=pltpu.CompilerParams(
            vmem_limit_bytes=VMEM_LIMIT, collective_id=4, has_side_effects=True
        ),
        cost_estimate=cost(12e9, 24e6),
        name="front",
    )(resets, inputs, memory, compressed, out_grad, w_compress, comp_grad)


def project_kernel(
    resets_ref, offsets_ref, old_ref, mem_ref, in_ref, og_ref, gain_ref, wq_hbm, wk_hbm, wv_hbm,
    raw_ref, normed_ref, q_ref, k_ref, v_ref, og_out_ref,
    wq_ref, wk_ref, wv_ref, sems,
):
    step = pl.program_id(0)
    weights = [
        pltpu.make_async_copy(src, dst, sems.at[n])
        for n, (src, dst) in enumerate(((wk_hbm, wk_ref), (wv_hbm, wv_ref), (wq_hbm, wq_ref)))
    ]

    @pl.when(step == 0)
    def _():
        for copy in weights:
            copy.start()

    half, width = in_ref.shape[1:]
    size = 2 * half // 2
    for n in range(2):
        at = slice(n * size, (n + 1) * size)
        pick = lambda ref: ref[...].reshape(2 * half, width)[at]
        raw = jnp.where(step == 0, pick(old_ref), jnp.where(step == 1, pick(mem_ref), pick(in_ref)))
        raw_ref[at] = raw
        unit, _ = norm_parts(raw.astype(F32))
        normed_ref[at] = (unit * gain_ref[...]).astype(BF16)
        if n == 0:

            @pl.when(step == 0)
            def _():
                for copy in weights[:2]:
                    copy.wait()

        k_ref[at] = dot(normed_ref[at], wk_ref[...]).astype(BF16)
        v_ref[at] = dot(normed_ref[at], wv_ref[...]).astype(BF16)

    @pl.when(step == 2)
    def _():
        weights[2].wait()

    @pl.when(step >= 2)
    def _():
        q_ref[...] = dot(normed_ref[...], wq_ref[...]).astype(BF16)
        og_out_ref[...] = og_ref[...].reshape(og_out_ref.shape)


def project_rows(resets, offsets, old, mem, inputs, og, gain, wq, wk, wv):
    _, _, half, width = inputs.shape
    seg = 2 * half

    def from_pair(first):
        def index(i, resets_ref, offsets_ref):
            slots = first_slots(resets_ref, offsets_ref, lax.axis_index("seq"), 2 * seg)
            stream_a = jnp.where(slots[0] >= 2 * seg, 1, 0)
            return jnp.where(i < first + 1, stream_a, 1 - stream_a), 0, 0, 0

        return pl.BlockSpec((None, 2, half, width), index)

    keys = pl.BlockSpec((seg, width), lambda i, *_: (i, 0))
    rows = pl.BlockSpec((seg, width), lambda i, *_: (jnp.maximum(i - 2, 0), 0))
    key_shape = jax.ShapeDtypeStruct((4 * seg, width), BF16)
    row_shape = jax.ShapeDtypeStruct((2 * seg, width), BF16)
    anywhere = pl.BlockSpec(memory_space=pl.ANY)
    return pl.pallas_call(
        project_kernel,
        out_shape=(key_shape, key_shape, row_shape, key_shape, key_shape, row_shape),
        grid_spec=pltpu.PrefetchScalarGridSpec(
            num_scalar_prefetch=2,
            grid=(4,),
            in_specs=[
                from_pair(4), from_pair(4), from_pair(2), from_pair(2),
                held(gain.shape), anywhere, anywhere, anywhere,
            ],
            out_specs=(keys, keys, rows, keys, keys, rows),
            scratch_shapes=[
                pltpu.VMEM(wq.shape, BF16),
                pltpu.VMEM(wk.shape, BF16),
                pltpu.VMEM(wv.shape, BF16),
                pltpu.SemaphoreType.DMA((3,)),
            ],
        ),
        compiler_params=params(),
        cost_estimate=cost(14e9, 30e6),
        name="project",
    )(resets, offsets, old, mem, inputs, og, gain, wq, wk, wv)


def attn_fwd_kernel(
    resets_ref, offsets_ref, q_ref, k_ref, v_ref, in_ref, wo_ref, gain_ref, kept_p_ref, got_p_ref, kept_q_ref, got_q_ref,
    wh_hbm, wr_hbm,
    mixed_ref, hidden_ref, ffn_ref, lse_ref, compress_ref, wh_got, wr_got,
    weight_sems, packed, *scratch,
):
    step = pl.program_id(0)
    lands, chip_sems = scratch[:-1], scratch[-1]
    place = mesh_place()
    half = q_ref.shape[0]
    seg = 2 * half
    first_slot = stream_a_slot(resets_ref, offsets_ref, place[0], 2 * seg)
    partner = {"seq": 1 - place[0]}
    weights = [
        remote(src, dst, (weight_sems.at[0, n], weight_sems.at[1, n]), partner)
        for n, (src, dst) in enumerate(((wh_hbm, wh_got), (wr_hbm, wr_got)))
    ]
    chunks = [
        Chunk(
            packed.at[which],
            tuple(b for b in BITS if b != ORDERS[which][0]),
            ORDERS[which][1:2],
            lands[which : which + 1],
            chip_sems.at[which],
            place,
        )
        for which in range(2)
    ]

    @pl.when(step == 0)
    def _():
        greet((partner,) + tuple({"dp": place[2](b)} for b in range(2)))
        for copy in weights:
            copy.start()
        packed[0] = add_low(kept_p_ref[...], got_p_ref[...])
        packed[1] = add_low(kept_q_ref[...], got_q_ref[...])
        for part in chunks:
            part.start(0)

    def run(pieces):
        def one_head(h, stats):
            cols = pl.ds(pl.multiple_of(h * HEAD_DIM, HEAD_DIM), HEAD_DIM)
            q = q_ref[:, cols]
            scores = []
            for start, size, kind in pieces:
                s = dot(q, k_ref[start : start + size, cols], NT)
                if kind == "mem":
                    slot = lax.broadcasted_iota(jnp.int32, s.shape, 1)
                    s = jnp.where(slot >= first_slot, s, masked_score)
                if kind == "diag":
                    key = lax.broadcasted_iota(jnp.int32, s.shape, 1)
                    row = lax.broadcasted_iota(jnp.int32, s.shape, 0)
                    s = jnp.where(key <= row, s, masked_score)
                scores.append(s)
            top = functools.reduce(
                jnp.maximum, [jnp.max(s, axis=-1, keepdims=True) for s in scores]
            ) * EXP2_SCALE
            mix = jnp.zeros((half, 2 * HEAD_DIM), F32)
            for s, (start, size, _) in zip(scores, pieces):
                p = jnp.exp2(s * EXP2_SCALE - top).astype(BF16)
                ones = jnp.ones((size, HEAD_DIM), BF16)
                mix = mix + dot(p, jnp.concatenate([v_ref[start : start + size, cols], ones], axis=1))
            total = mix[:, HEAD_DIM:]
            mixed_ref[:, cols] = (mix[:, :HEAD_DIM] / total).astype(BF16)
            lane = lax.broadcasted_iota(jnp.int32, stats.shape, 1)
            return jnp.where(lane == h, top + jnp.log2(total), stats)

        stats = lax.fori_loop(0, HEADS, one_head, jnp.zeros((half, 128), F32), unroll=True)
        lse_ref[...] = stats.T[:HEADS]

    cases = (
        ((0, 2 * seg, "mem"), (2 * seg, half, "diag")),
        ((0, 2 * seg, "mem"), (2 * seg, half, "full"), (2 * seg + half, half, "diag")),
        ((3 * seg, half, "diag"),),
        ((3 * seg, half, "full"), (3 * seg + half, half, "diag")),
    )
    for i, pieces in enumerate(cases[2:] + cases[:2]):
        pl.when(step == i)(functools.partial(run, pieces))
    hidden = in_ref[...].astype(F32) + dot(mixed_ref[...], wo_ref[...])
    hidden_ref[...] = hidden
    unit, _ = norm_parts(hidden)
    ffn_ref[...] = (unit * gain_ref[...]).astype(BF16)

    @pl.when(step == 3)
    def _():
        for which, part in enumerate(chunks):
            part.settle(0)
            compress_ref[which] = packed[(which,) + part.rest(1)]
        for copy in weights:
            copy.wait()


def attn_fwd(resets, offsets, q, k, v, raw, wo, gain, kept_p, got_p, kept_q, got_q, wh, wr):
    rows, width = q.shape
    half = rows // 4
    by_block = pl.BlockSpec((half, width), lambda i: (lax.rem(i + 2, 4), 0))
    in_block = pl.BlockSpec((half, width), lambda i: (4 + lax.rem(i + 2, 4), 0))
    anywhere = pl.BlockSpec(memory_space=pl.ANY)
    block = kept_p.shape[-2:]
    part = held(kept_p.shape)
    lands = []
    for which in range(2):
        lands += landings(BITS[1:], ORDERS[which][1:2], block)
    out = (2, 2, 2) + block
    return pl.pallas_call(
        attn_fwd_kernel,
        grid=(4,),
        out_shape=(
            jax.ShapeDtypeStruct((rows, width), BF16),
            jax.ShapeDtypeStruct((rows, width), F32),
            jax.ShapeDtypeStruct((rows, width), BF16),
            jax.ShapeDtypeStruct((HEADS, rows), F32),
            jax.ShapeDtypeStruct(out, BF16),
            jax.ShapeDtypeStruct(wh.shape, BF16),
            jax.ShapeDtypeStruct(wr.shape, BF16),
        ),
        in_specs=[
            pl.BlockSpec(memory_space=pltpu.SMEM),
            pl.BlockSpec(memory_space=pltpu.SMEM),
            by_block, held(k.shape), held(v.shape), in_block, held(wo.shape), held(gain.shape),
            part, part, part, part, anywhere, anywhere,
        ],
        out_specs=(
            by_block, by_block, by_block, pl.BlockSpec((HEADS, half), lambda i: (0, lax.rem(i + 2, 4))), held(out),
            anywhere, anywhere,
        ),
        scratch_shapes=[pltpu.SemaphoreType.DMA((2, 2)), pltpu.VMEM((2,) + kept_p.shape, BF16)] + lands + [pltpu.SemaphoreType.DMA((2, 2, 1))],
        compiler_params=pltpu.CompilerParams(
            vmem_limit_bytes=VMEM_LIMIT, dimension_semantics=("arbitrary",),
            collective_id=5, has_side_effects=True,
        ),
        cost_estimate=cost(20e9, 20e6),
        name="attn_fwd",
    )(resets, offsets, q, k, v, raw, wo, gain, kept_p, got_p, kept_q, got_q, wh, wr)


GELU_C = math.sqrt(2.0 / math.pi)
GELU_A = 0.044715
CHUNK = 512


def gelu_pair(pre, act_grad):
    square = pre * pre
    t = jnp.tanh(pre * (GELU_C + (GELU_C * GELU_A) * square))
    cdf = 0.5 + 0.5 * t
    slope = cdf + (0.5 * pre) * (1.0 - t * t) * (GELU_C + (3.0 * GELU_C * GELU_A) * square)
    return (pre * cdf).astype(BF16), (act_grad * slope).astype(BF16)


def ffn_kernel(
    x_ref, og_ref, gain_ref, packed_ref, hidden_hbm, wo_hbm, wh0_ref, wh1_ref, wr0_ref, wr1_ref,
    out_ref, attn_grad_ref, do_ref, gain_grad_ref, done_ref, part_ref, raw_ref, compress_ref,
    hidden_ref, wo_ref, held_sems, pack0, pack1, pack_sems, wh, wr, out_acc, in_acc, act_ref, pre_ref, core_out, core_in, own_ref, land0, land1, land2, land3,
    weight_sems, core_sems, chip_sems,
):
    step = pl.program_id(0)
    last = pl.num_programs(0) - 1
    index = lax.div(step, 2)
    end = lax.div(last, 2)
    owned = lax.rem(step, 2) == 1
    rows, width = x_ref.shape
    units = wh.shape[2]
    chunks = rows // CHUNK
    place = mesh_place()
    core, _, across = place
    partner = {"seq": 1 - core}

    def fetch(at, side):
        cols = pl.ds(pl.multiple_of(at * units, units), units)
        wh_ref, wr_ref = ((wh0_ref, wr0_ref), (wh1_ref, wr1_ref))[side]
        return (
            pltpu.make_async_copy(wh_ref.at[:, cols], wh.at[side], weight_sems.at[0, side]),
            pltpu.make_async_copy(wr_ref.at[cols], wr.at[side], weight_sems.at[1, side]),
        )

    held_copies = (
        pltpu.make_async_copy(hidden_hbm, hidden_ref, held_sems.at[0]),
        pltpu.make_async_copy(wo_hbm, wo_ref, held_sems.at[1]),
    )
    packs = [
        Chunk(
            packed_ref.at[which], (3, 2), (2, 3), [pack0.at[which], pack1.at[which]],
            pack_sems.at[which], place,
        )
        for which in range(2)
    ]

    @pl.when(step == 0)
    def _():
        for copy in fetch(0, 0) + held_copies:
            copy.start()
        greet((partner,) + tuple({"dp": across(b)} for b in range(4)))
        for part in packs:
            part.start(0)
        out_acc[...] = jnp.zeros_like(out_acc)
        in_acc[...] = jnp.zeros_like(in_acc)

    @pl.when(step == 2)
    def _():
        for part in packs:
            part.settle(0)
            part.start(1)

    @pl.when(step == 4)
    def _():
        cols = compress_ref.shape[1] // 2
        for which, part in enumerate(packs):
            compress_ref[:, which * cols : (which + 1) * cols] = part.last(1)

    @pl.when(jnp.logical_not(owned))
    def _():
        for copy in fetch(index, 1):
            copy.start()
        for copy in fetch(index, 0):
            copy.wait()

    @pl.when(owned)
    def _():
        @pl.when(index < end)
        def _():
            for copy in fetch(index + 1, 0):
                copy.start()

        for copy in fetch(index, 1):
            copy.wait()

    def core_copy(which, index):
        return remote(
            core_out.at[which],
            core_in.at[which, lax.rem(index, 2)],
            (core_sems.at[0, which, index], core_sems.at[1, which, index]),
            partner,
        )

    def tile(which, index):
        return Chunk(
            own_ref.at[which, index], BITS, ORDERS[which],
            [land.at[which, index] for land in (land0, land1, land2, land3)],
            chip_sems.at[which, index], place,
        )

    def pass_on(index, swap):
        for which in range(2):
            part = tile(which, index)
            part.settle(swap)
            part.start(swap + 1)

    def finish_tile(index):
        for which in range(2):
            done_ref[which, index] = tile(which, index).last(3)

    side = lax.rem(step, 2)

    def rows_step(m, _):
        at = pl.ds(pl.multiple_of(m * CHUNK, CHUNK), CHUNK)
        pre = dot(x_ref[at, :], wh[side])
        act_grad = dot(og_ref[at, :], wr[side], NT)
        act, pre_grad = gelu_pair(pre, act_grad)
        act_ref[at, :] = act
        pre_ref[at, :] = pre_grad
        out_acc[at, :] += dot(act, wr[side])
        in_acc[at, :] += dot(pre_grad, wh[side], NT)

        return 0

    lax.fori_loop(0, chunks, rows_step, 0)

    @pl.when(owned & (index > 0))
    def _():
        pass_on(index - 1, 0)

    @pl.when(owned & (index > 1))
    def _():
        pass_on(index - 2, 2)

    @pl.when(jnp.logical_not(owned) & (index > 1))
    def _():
        pass_on(index - 2, 1)

    @pl.when(jnp.logical_not(owned) & (index > 2))
    def _():
        finish_tile(index - 3)

    for which, (left_ref, right_ref) in enumerate(((x_ref, pre_ref), (og_ref, act_ref))):
        grad = dot(left_ref[...], right_ref[...], TN)

        @pl.when(jnp.logical_not(owned))
        def _():
            @pl.when(index > 0)
            def _():
                core_copy(which, index - 1).wait_send()

            core_out[which] = grad.astype(BF16)
            core_copy(which, index).start()

        @pl.when(owned)
        def _():
            core_copy(which, index).wait_recv()
            total = grad + core_in[which, lax.rem(index, 2)].astype(F32)
            total = total.astype(BF16).reshape(own_ref.shape[2:])

            @pl.when(index < end)
            def _():
                own_ref[which, index] = total
                tile(which, index).start(0)

            @pl.when(index == end)
            def _():
                raw_ref[which] = total

    @pl.when(step == last)
    def _():
        for copy in held_copies:
            copy.wait()

        def finish(m, gain_sum):
            at = pl.ds(pl.multiple_of(m * 256, 256), 256)
            hidden = hidden_ref[at, :]
            out_ref[at, :] = (hidden + out_acc[at, :]).astype(BF16)
            unit, inverse = norm_parts(hidden)
            grad = in_acc[at, :]
            hidden_grad = og_ref[at, :].astype(F32) + norm_back(
                grad * gain_ref[...], unit, inverse
            )
            low = hidden_grad.astype(BF16)
            attn_grad_ref[at, :] = low
            do_ref[at, :] = dot(low, wo_ref[...], NT).astype(BF16)
            return gain_sum + jnp.sum(grad * unit, axis=0, keepdims=True)

        gain_grad_ref[...] = lax.fori_loop(
            0, rows // 256, finish, jnp.zeros(gain_grad_ref.shape, F32)
        )
        finish_tile(end - 2)
        for which in range(2):
            core_copy(which, end).wait_send()
            part = tile(which, end - 1)
            part.settle(1)
            part_ref[which] = part.data[part.rest(2)]


def ffn(x, og, gain, packed, hidden, wo, wh0, wh1, wr0, wr1):
    rows, width = x.shape
    units = wh0.shape[1]
    tile = 512
    steps = units // tile
    count = lax.axis_size("dp")
    block = width // count
    anywhere = pl.BlockSpec(memory_space=pl.ANY)
    whole = held((rows, width))
    low_rows = jax.ShapeDtypeStruct((rows, width), BF16)
    raw = (2, 2, 2, 2, 2, block, tile)
    part = (2, 2, 2, block, tile)
    done = (2, steps - 2, block, tile)
    tiles = (2, steps - 1)
    lands = [pltpu.VMEM(tiles + (2,) * n + (block, tile), BF16) for n in (3, 2, 1, 0)]
    pack = packed.shape[-2:]
    compress = (pack[0], 2 * pack[1])
    return pl.pallas_call(
        ffn_kernel,
        grid=(2 * steps,),
        out_shape=(
            low_rows, low_rows, low_rows, jax.ShapeDtypeStruct((1, width), F32),
            jax.ShapeDtypeStruct(done, F32),
            jax.ShapeDtypeStruct(part, BF16),
            jax.ShapeDtypeStruct(raw, BF16),
            jax.ShapeDtypeStruct(compress, F32),
        ),
        in_specs=[whole, whole, held(gain.shape), held(packed.shape)] + [anywhere] * 6,
        out_specs=(whole, whole, whole, held((1, width)), held(done), held(part), held(raw), held(compress)),
        scratch_shapes=[
            pltpu.VMEM((rows, width), F32),
            pltpu.VMEM(wo.shape, BF16),
            pltpu.SemaphoreType.DMA((2,)),
            pltpu.VMEM((2, 2) + pack, BF16),
            pltpu.VMEM((2,) + pack, BF16),
            pltpu.SemaphoreType.DMA((2, 2, 2)),
            pltpu.VMEM((2, width, tile), BF16),
            pltpu.VMEM((2, tile, width), BF16),
            pltpu.VMEM((rows, width), F32),
            pltpu.VMEM((rows, width), F32),
            pltpu.VMEM((rows, tile), BF16),
            pltpu.VMEM((rows, tile), BF16),
            pltpu.VMEM((2, width, tile), BF16),
            pltpu.VMEM((2, 2, width, tile), BF16),
            pltpu.VMEM(tiles + raw[1:], BF16),
        ] + lands + [
            pltpu.SemaphoreType.DMA((2, 2)),
            pltpu.SemaphoreType.DMA((2, 2, steps)),
            pltpu.SemaphoreType.DMA((2, steps, 2, 4)),
        ],
        compiler_params=pltpu.CompilerParams(
            vmem_limit_bytes=VMEM_LIMIT, dimension_semantics=("arbitrary",),
            collective_id=1, has_side_effects=True,
        ),
        cost_estimate=cost(75e9, 50e6),
        name="ffn",
    )(x, og, gain, packed, hidden, wo, wh0, wh1, wr0, wr1)


def attn_bwd_head(first_slot, q_ref, k_ref, v_ref, do_ref, mixed_ref, lse, dq_ref, dk_ref, dv_ref, cols):
    seg = q_ref.shape[0] // 2
    half = seg // 2
    for stream in range(2):
        base = stream * seg
        rows = slice(base, base + seg)
        lse_row = lse[:, rows]
        weight = do_ref[rows, cols].astype(F32) * mixed_ref[rows, cols].astype(F32)
        delta_row = jnp.sum(weight.T, axis=0, keepdims=True)
        key_base = 2 * seg + stream * seg
        pieces = []
        if stream == 0:
            pieces += [(start, half, 0, "mem") for start in range(0, 2 * seg, half)]
        pieces += [(key_base, half, 0, "diag"), (key_base + half, half, half, "diag")]
        dq_low = jnp.zeros((half, HEAD_DIM), F32)
        dq_high = jnp.zeros((half, HEAD_DIM), F32)
        for start, size, first, kind in pieces:
            q = q_ref[base + first : base + seg, cols]
            do = do_ref[base + first : base + seg, cols]
            k = k_ref[start : start + size, cols]
            s = dot(k, q, NT) * EXP2_SCALE - lse_row[:, first:]
            if kind == "mem":
                slot = start + lax.broadcasted_iota(jnp.int32, s.shape, 0)
                s = jnp.where(slot >= first_slot, s, masked_score)
            else:
                key = lax.broadcasted_iota(jnp.int32, s.shape, 0)
                row = lax.broadcasted_iota(jnp.int32, s.shape, 1)
                s = jnp.where(key <= row, s, masked_score)
            p = jnp.exp2(s)
            dp = dot(v_ref[start : start + size, cols], do, NT)
            ds = (p * (dp - delta_row[:, first:])).astype(BF16)
            dv_ref[start : start + size, cols] = dot(p.astype(BF16), do).astype(BF16)
            dk_ref[start : start + size, cols] = (dot(ds, q) * SCALE).astype(BF16)
            dq = dot(ds, k, TN)
            if first == 0:
                dq_low = dq_low + dq[:half]
                dq_high = dq_high + dq[half:]
            else:
                dq_high = dq_high + dq
        dq_ref[base : base + half, cols] = (dq_low * SCALE).astype(BF16)
        dq_ref[base + half : base + seg, cols] = (dq_high * SCALE).astype(BF16)


def attn_back_kernel(
    resets_ref, offsets_ref, q_ref, k_ref, v_ref, do_ref, mix_ref, lse_ref, normed_hbm, mixed_hbm, ag_ref,
    ffn_part_ref, ffn_raw_ref, outputs_hbm,
    dq_ref, dk_ref, dv_ref, early_ref, late_ref, ffn_done_ref, outputs_got, outputs_sems,
    normed_ref, mixed_ref, held_sems, grads_ref, core_out0, core_in0, core_out1, core_in1, own_ref,
    *scratch,
):
    step = pl.program_id(0)
    last = pl.num_programs(0) - 1
    place = mesh_place()
    core, _, across = place
    partner = {"seq": 1 - core}
    lands, (core_sems, chip_sems) = list(scratch[:-2]), scratch[-2:]
    chunks, ffn_parts, ffn_raws = [], [], []
    first_slot = stream_a_slot(resets_ref, offsets_ref, core, q_ref.shape[0])
    outputs_copies = [
        remote(
            outputs_hbm.at[j, 1 - core], outputs_got.at[j],
            (outputs_sems.at[0, j], outputs_sems.at[1, j]), partner,
        )
        for j in range(2)
    ]
    held_copies = (
        pltpu.make_async_copy(normed_hbm, normed_ref, held_sems.at[0]),
        pltpu.make_async_copy(mixed_hbm, mixed_ref, held_sems.at[1]),
    )

    def chunk(number, data, left, order):
        mine = [lands.pop(0) for _ in order]
        return Chunk(data, left, order, mine, chip_sems.at[number], place)

    for which in range(2):
        order = ORDERS[which]
        chunks.append(chunk(3 * which, own_ref.at[which], BITS, order[:2]))
        ffn_parts.append(chunk(3 * which + 1, ffn_part_ref.at[which], order[2:][::-1], order[2:]))
        ffn_raws.append(chunk(3 * which + 2, ffn_raw_ref.at[which], BITS, order))
    index = lax.div(step, 2)
    rows = q_ref.shape[0]
    keys = k_ref.shape[0]
    pair = q_ref.shape[1]

    @pl.when(step == 0)
    def _():
        for copy in held_copies:
            copy.start()
        greet((partner,) + tuple({"dp": across(b)} for b in range(4)))
        for part in ffn_raws + ffn_parts:
            part.start(0)
        for copy in outputs_copies:
            copy.start()

    @pl.when(step == 1)
    def _():
        for part in ffn_parts:
            part.settle(0)
            part.start(1)

    @pl.when(step == 2)
    def _():
        for which in range(2):
            ffn_done_ref[which, 0] = ffn_parts[which].last(1)

    crossing = ((core_out0, core_in0), (core_out1, core_in1))

    def core_copy(which, index):
        sent, got = crossing[index]
        return remote(
            sent.at[which],
            got.at[which],
            (core_sems.at[0, which, index], core_sems.at[1, which, index]),
            partner,
        )

    head = 4 * jnp.where(lax.rem(step, 2) == 0, 1 - core, core) + 2 * index

    def one_head(h, _):
        attn_bwd_head(
            first_slot, q_ref, k_ref, v_ref, do_ref, mix_ref, lse_ref[pl.ds(head + h, 1), :],
            dq_ref, dk_ref, dv_ref, pl.ds(pl.multiple_of(h * HEAD_DIM, HEAD_DIM), HEAD_DIM),
        )
        for n in range(1, 4):

            @pl.when((step == n) & (h == 0))
            def _():
                for part in ffn_raws + (chunks if n == 3 else []):
                    swap = 0 if part in chunks else n - 1
                    part.settle(swap)
                    part.start(swap + 1)

        return 0

    lax.fori_loop(0, 2, one_head, 0)

    @pl.when(step == 0)
    def _():
        for copy in held_copies:
            copy.wait()

    less = pair + pair // 2
    grads_ref[0, :, :pair] = dot(normed_ref[keys - rows :], dq_ref[...], TN)
    grads_ref[1, :, :pair] = dot(normed_ref[...], dv_ref[...], TN)
    key_grads = dot(normed_ref[...], dk_ref[...], TN)
    grads_ref[0, :, pair:less] = key_grads[:, : pair // 2]
    grads_ref[1, :, pair:less] = key_grads[:, pair // 2 :]

    @pl.when(step < 2)
    def _():
        output_grads = dot(mixed_ref[...], ag_ref[...], TN)
        grads_ref[0, :, less:] = output_grads[:, :pair]
        grads_ref[1, :, less:] = output_grads[:, pair:]

    for n in range(2):

        @pl.when(step == 2 * n)
        def _():
            sent = crossing[n][0]
            for which in range(2):
                sent[which] = grads_ref[which, :, : sent.shape[2]].astype(BF16)
                core_copy(which, n).start()

    def own_grads(which, index, out_ref):
        core_copy(which, index).wait()
        got = crossing[index][1]
        total = grads_ref[which, :, : got.shape[2]] + got[which].astype(F32)
        out_ref[...] = total.astype(BF16).reshape(out_ref.shape)

    @pl.when(step == 1)
    def _():
        for which in range(2):
            own_grads(which, 0, own_ref.at[which])
            chunks[which].start(0)

    @pl.when(step == last)
    def _():
        for which in range(2):
            own_grads(which, 1, late_ref.at[which])
        for which in range(2):
            chunks[which].settle(1)
            early_ref[which] = own_ref[(which,) + chunks[which].rest(2)]
            ffn_done_ref[which, 1] = ffn_raws[which].last(3)
        for copy in outputs_copies:
            copy.wait()


def attn_back(resets, offsets, q, k, v, do, mixed, lse, normed, attn_grad, ffn_part, ffn_raw, outputs):
    rows, width = q.shape
    keys = k.shape[0]
    pair = 2 * HEAD_DIM
    more, less = 2 * pair + pair // 2, pair + pair // 2
    block = (width // 16, more)

    def by_pair(count):
        def index(i):
            core = lax.axis_index("seq")
            half = jnp.where(lax.rem(i, 2) == 0, 1 - core, core)
            return 0, 2 * half + lax.div(i, 2)

        return pl.BlockSpec((count, pair), index)

    def output_half(i):
        core = lax.axis_index("seq")
        return 0, jnp.where(i == 0, 1 - core, core)

    early, late = (2, 2, 2) + block, (2, 2, 2, 2, 2, width // 16, less)
    ffn_block = ffn_raw.shape[-2:]
    done = (2, 2) + ffn_block
    lands = []
    for order in ORDERS:
        lands += landings(BITS, order[:2], block)
        lands += landings(order[2:], order[2:], ffn_block)
        lands += landings(BITS, order, ffn_block)
    return pl.pallas_call(
        attn_back_kernel,
        grid=(4,),
        out_shape=(
            jax.ShapeDtypeStruct((rows, width), BF16),
            jax.ShapeDtypeStruct((keys, width), BF16),
            jax.ShapeDtypeStruct((keys, width), BF16),
            jax.ShapeDtypeStruct(early, BF16),
            jax.ShapeDtypeStruct(late, BF16),
            jax.ShapeDtypeStruct(done, F32),
            jax.ShapeDtypeStruct((2,) + outputs.shape[2:], BF16),
        ),
        in_specs=[
            pl.BlockSpec(memory_space=pltpu.SMEM),
            pl.BlockSpec(memory_space=pltpu.SMEM),
            by_pair(rows), by_pair(keys), by_pair(keys), by_pair(rows), by_pair(rows),
            held(lse.shape), pl.BlockSpec(memory_space=pl.ANY), pl.BlockSpec(memory_space=pl.ANY),
            pl.BlockSpec((rows, 2 * pair), output_half),
            held(ffn_part.shape), held(ffn_raw.shape), pl.BlockSpec(memory_space=pl.ANY),
        ],
        out_specs=(by_pair(rows), by_pair(keys), by_pair(keys), held(early), held(late), held(done),
            pl.BlockSpec(memory_space=pl.ANY),
        ),
        scratch_shapes=[
            pltpu.SemaphoreType.DMA((2, 2)),
            pltpu.VMEM(normed.shape, BF16),
            pltpu.VMEM(mixed.shape, BF16),
            pltpu.SemaphoreType.DMA((2,)),
            pltpu.VMEM((2, width, more), F32),
            pltpu.VMEM((2, width, more), BF16),
            pltpu.VMEM((2, width, more), BF16),
            pltpu.VMEM((2, width, less), BF16),
            pltpu.VMEM((2, width, less), BF16),
            pltpu.VMEM((2, 2, 2, 2, 2) + block, BF16),
        ] + lands + [
            pltpu.SemaphoreType.DMA((2, 2, 2)),
            pltpu.SemaphoreType.DMA((6, 2, 4)),
        ],
        compiler_params=pltpu.CompilerParams(
            vmem_limit_bytes=VMEM_LIMIT, dimension_semantics=("arbitrary",),
            collective_id=2, has_side_effects=True,
        ),
        cost_estimate=cost(45e9, 24e6),
        name="attn_back",
    )(resets, offsets, q, k, v, do, mixed, lse, normed, mixed, attn_grad, ffn_part, ffn_raw, outputs)


def rows_back_kernel(
    dq_ref, dk_ref, dv_ref, raw_ref, ag_ref, gain_ref, gain_ffn_ref, wq_hbm, wk_hbm, wv_hbm,
    early_ref, late_ref,
    mine_ref, theirs_ref, gains_ref, query_ref, key_ref, value_ref, output_ref,
    wq_ref, wk_ref, wv_ref, weight_sems, rows_out, gain_acc, gain_out, gain_in, *scratch,
):
    step = pl.program_id(0)
    last = pl.num_programs(0) - 1
    place = mesh_place()
    core, _, across = place
    partner = {"seq": 1 - core}
    lands, (row_sems, local_sems, gain_sems, chip_sems) = list(scratch[:-4]), scratch[-4:]

    chunks = []

    def chunk(data, left, order):
        number = len(chunks)
        mine = [lands.pop(0) for _ in order]
        chunks.append(Chunk(data, left, order, mine, chip_sems.at[number], place))
        return chunks[-1]

    early, late = [], []
    for which in range(2):
        early.append(chunk(early_ref.at[which], BITS[:2], ORDERS[which][2:]))
        late.append(chunk(late_ref.at[which], BITS, ORDERS[which]))

    rank = lax.axis_index("dp")

    def flipped(n, bits):
        return rank + sum(across(b) - rank for i, b in enumerate(bits) if n >> i & 1)

    gain_groups = (
        [{"dp": flipped(n >> 1, (0, 1)), "seq": 1 - core if n & 1 else core} for n in range(1, 8)],
        [{"dp": flipped(n, (2, 3))} for n in range(1, 4)],
    )

    def gain_copies(stage):
        first = 7 * stage
        return [
            remote(
                gain_out.at[stage],
                gain_in.at[first + n],
                (gain_sems.at[0, first + n], gain_sems.at[1, first + n]),
                device,
            )
            for n, device in enumerate(gain_groups[stage])
        ]

    def gain_total(stage):
        for copy in gain_copies(stage):
            copy.wait()
        return gain_out[stage] + sum(gain_in[7 * stage + n] for n in range(len(gain_groups[stage])))

    def row_copy(block):
        stream = block // 2
        return remote(
            rows_out.at[block], theirs_ref.at[stream], (row_sems.at[0, stream], row_sems.at[1, stream]), partner
        )

    def row_keep(block):
        stream = block // 2
        return pltpu.make_async_copy(rows_out.at[block], mine_ref.at[stream], local_sems.at[stream])

    weights = [
        pltpu.make_async_copy(src, dst, weight_sems.at[n])
        for n, (src, dst) in enumerate(((wk_hbm, wk_ref), (wv_hbm, wv_ref), (wq_hbm, wq_ref)))
    ]

    @pl.when(step == 0)
    def _():
        for copy in weights:
            copy.start()
        greet(gain_groups[0] + gain_groups[1])
        for part in late + early:
            part.start(0)
        for copy in weights[:2]:
            copy.wait()
        gain_acc[...] = jnp.zeros_like(gain_acc)

    def normed_grad():
        return dot(dk_ref[...], wk_ref[...], NT) + dot(dv_ref[...], wv_ref[...], NT)

    unit, inverse = norm_parts(raw_ref[...].astype(F32))

    @pl.when(step < 4)
    def _():
        gain_acc[0:1] += jnp.sum(normed_grad() * unit, axis=0, keepdims=True)

    @pl.when(step == 4)
    def _():
        weights[2].wait()

    @pl.when(step >= 4)
    def _():
        grad = normed_grad() + dot(dq_ref[...], wq_ref[...], NT)
        gain_acc[0:1] += jnp.sum(grad * unit, axis=0, keepdims=True)
        rows_grad = norm_back(grad * gain_ref[...], unit, inverse)
        rows_out[step - 4] = (rows_grad + ag_ref[...].astype(F32)).astype(BF16)

    for block in range(4):
        stays = core == block % 2
        pl.when((step == block + 4) & stays)(row_keep(block).start)
        pl.when((step == block + 4) & jnp.logical_not(stays))(row_copy(block).start)

    @pl.when(step == 4)
    def _():
        for part in early:
            part.settle(0)
            part.start(1)

    @pl.when(step == 5)
    def _():
        for part in late:
            part.settle(0)
            part.start(1)

    @pl.when(step == last)
    def _():
        lanes = gain_out.shape[2]
        for n in range(8):
            cols = slice(n * lanes, (n + 1) * lanes)
            gain_out[0, n : n + 1] = gain_acc[0:1, cols]
            gain_out[0, 8 + n : 9 + n] = gain_ffn_ref[:, cols]
        for copy in gain_copies(0):
            copy.start()
        pair = 2 * HEAD_DIM
        for which, ref in enumerate((query_ref, value_ref)):
            total = early[which].last(1)
            ref[:, :pair] = total[:, :pair]
            key_ref[:, which * HEAD_DIM : (which + 1) * HEAD_DIM] = total[:, pair : pair + HEAD_DIM]
            output_ref[:, which * pair : (which + 1) * pair] = total[:, pair + HEAD_DIM :]
        for part in late:
            part.settle(1)
            part.start(2)
        gain_out[1] = gain_total(0)
        for copy in gain_copies(1):
            copy.start()
        for part in late:
            part.settle(2)
            part.start(3)
        gains_ref[...] = gain_total(1)
        for which, ref in enumerate((query_ref, value_ref)):
            total = late[which].last(3)
            ref[:, pair:] = total[:, :pair]
            key_ref[:, pair + which * HEAD_DIM : pair + (which + 1) * HEAD_DIM] = total[:, pair:]
        for block in range(4):
            stays = core == block % 2
            pl.when(stays)(row_keep(block).wait)
            pl.when(jnp.logical_not(stays))(row_copy(block).wait_send)
        for stream in range(2):
            row_copy(2 * stream).wait_recv()


def rows_back(
    dq, dk, dv, raw, attn_grad, gain, gain_ffn, wq, wk, wv, early, late
):
    keys, width = dk.shape
    rows = dq.shape[0]
    size = keys // 8
    key_block = pl.BlockSpec((size, width), lambda i: (i, 0))
    row_block = pl.BlockSpec((size, width), lambda i: (jnp.maximum(i - 4, 0), 0))
    anywhere = pl.BlockSpec(memory_space=pl.ANY)
    rows_shape = jax.ShapeDtypeStruct((2, size, width), BF16)
    early_block, late_block = early.shape[-2:], late.shape[-2:]
    lands = []
    for order in ORDERS:
        lands += landings(BITS[:2], order[2:], early_block)
        lands += landings(BITS, order, late_block)
    out = (early_block[0], 4 * HEAD_DIM)
    vector = (16, width // 8)
    return pl.pallas_call(
        rows_back_kernel,
        grid=(8,),
        out_shape=(
            rows_shape, rows_shape,
            jax.ShapeDtypeStruct(vector, F32),
        ) + (jax.ShapeDtypeStruct(out, F32),) * 4,
        in_specs=[
            row_block, key_block, key_block, key_block, row_block,
            held(gain.shape), held(gain_ffn.shape), anywhere, anywhere, anywhere,
            held(early.shape), held(late.shape),
        ],
        out_specs=(
            anywhere, anywhere, held(vector),
        ) + (held(out),) * 4,
        scratch_shapes=[
            pltpu.VMEM(wq.shape, BF16),
            pltpu.VMEM(wk.shape, BF16),
            pltpu.VMEM(wv.shape, BF16),
            pltpu.SemaphoreType.DMA((3,)),
            pltpu.VMEM((4, size, width), BF16),
            pltpu.VMEM((8, width), F32),
            pltpu.VMEM((2,) + vector, F32),
            pltpu.VMEM((10,) + vector, F32),
        ] + lands + [
            pltpu.SemaphoreType.DMA((2, 2)),
            pltpu.SemaphoreType.DMA((2,)),
            pltpu.SemaphoreType.DMA((2, 10)),
            pltpu.SemaphoreType.DMA((4, 2, 4)),
        ],
        compiler_params=pltpu.CompilerParams(
            vmem_limit_bytes=VMEM_LIMIT, dimension_semantics=("arbitrary",),
            collective_id=3, has_side_effects=True,
        ),
        cost_estimate=cost(20e9, 24e6),
        name="rows_back",
    )(
        dq, dk, dv, raw, attn_grad, gain, gain_ffn, wq, wk, wv,
        early, late,
    )


def place_kernel(
    resets_ref, offsets_ref, own_a_ref, got_a_ref, own_b_ref, got_b_ref, out_a_ref, out_b_ref
):
    core = lax.axis_index("seq")
    for out_ref, own_ref, got_ref in ((out_a_ref, own_a_ref, got_a_ref), (out_b_ref, own_b_ref, got_b_ref)):
        out_ref[core] = own_ref[...]
        out_ref[1 - core] = got_ref[...]


def place_rows(resets, offsets, outputs, outputs_got, mine_rows, their_rows):
    _, _, half, width = outputs.shape

    def slot(i, resets_ref, offsets_ref, core):
        first = first_slots(resets_ref, offsets_ref, core, 4 * half)[0]
        return jnp.where(i == jnp.where(first >= 4 * half, 1, 0), 0, 1)

    def own(i, *refs):
        return slot(i, *refs, lax.axis_index("seq"))

    def got(i, *refs):
        return slot(i, *refs, 1 - lax.axis_index("seq"))

    block = (None, half, width)
    out = jax.ShapeDtypeStruct((4, half, width), BF16)
    return pl.pallas_call(
        place_kernel,
        out_shape=(out, out),
        grid_spec=pltpu.PrefetchScalarGridSpec(
            num_scalar_prefetch=2,
            grid=(2,),
            in_specs=[
                pl.BlockSpec(
                    (None, None, half, width), lambda *a: (own(*a), lax.axis_index("seq"), 0, 0)
                ),
                pl.BlockSpec(block, lambda *a: (got(*a), 0, 0)),
                pl.BlockSpec(block, lambda *a: (own(*a), 0, 0)),
                pl.BlockSpec(block, lambda *a: (got(*a), 0, 0)),
            ],
            out_specs=(pl.BlockSpec((2, half, width), lambda i, *_: (i, 0, 0)),) * 2,
        ),
        compiler_params=params(),
        cost_estimate=cost(0, 8e6),
        name="place",
    )(resets, offsets, outputs, outputs_got, mine_rows, their_rows)


def swap_dp(block, bit):
    count = lax.axis_size("dp")
    return lax.ppermute(block, "dp", [(i, i ^ (1 << bit)) for i in range(count)])


def swap_core(block):
    return lax.ppermute(block, "seq", [(0, 1), (1, 0)])


def on_device_pair(
    inputs, memory, compressed, offsets, resets, w_query, w_key, w_value, w_output, w_hidden,
    w_return, w_compress, gain_attn, gain_ffn, out_grad, comp_grad,
):
    core = lax.axis_index("seq")
    dp_count = lax.axis_size("dp")
    streams, half, width = inputs.shape
    seg = 2 * half
    low_core = core == 0

    unused = (resets != 0) | (offsets >= 2 * seg)
    gain_a = gain_attn.astype(F32).reshape(1, width)
    gain_f = gain_ffn.astype(F32).reshape(1, width)

    x_in, x_mem, x_old, x_og, new_rows, kept_p, sent_p, kept_q, sent_q = front(
        resets, inputs, memory, compressed, out_grad, w_compress, comp_grad
    )
    got_p, got_q = swap_dp(sent_p, 0), swap_dp(sent_q, 1)
    all_rows, normed, q, k, v, og = project_rows(
        resets, offsets, x_old, x_mem, x_in, x_og, gain_a, w_query, w_key, w_value
    )
    mixed, hidden, ffn_in, lse, packed, wh_other, wr_other = attn_fwd(
        resets, offsets, q, k, v, all_rows, w_output, gain_f, kept_p, got_p, kept_q, got_q,
        w_hidden, w_return,
    )
    outputs, attn_grad, mixed_grad, gain_ffn_grad, ffn_done, ffn_part, ffn_raw, grad_compress = ffn(
        ffn_in, og, gain_f, packed, hidden, w_output, wh_other, w_hidden, wr_other, w_return
    )
    outputs = outputs.reshape(2, 2, half, width)
    dq, dk, dv, early, late, ffn_rest, outputs_got = attn_back(
        resets, offsets, q, k, v, mixed_grad, mixed, lse, normed, attn_grad, ffn_part, ffn_raw,
        outputs,
    )
    mine_rows, their_rows, gains, grad_query, grad_key, grad_value, grad_output = rows_back(
        dq, dk, dv, all_rows, attn_grad, gain_a, gain_ffn_grad, w_query, w_key, w_value, early, late
    )

    def tiles(which):
        parts = [ffn_done[which, i] for i in range(2)] + [ffn_rest[which, i] for i in range(2)]
        return jnp.concatenate(parts, axis=1)

    grad_hidden, grad_return = tiles(0), tiles(1).T
    rank = lax.axis_index("dp")
    gains = lax.dynamic_slice_in_dim(gains.reshape(2, width), rank * (width // dp_count), width // dp_count, 1)

    placed_outputs, input_grad = place_rows(
        resets, offsets, outputs, outputs_got, mine_rows, their_rows
    )
    return (
        placed_outputs,
        new_rows[:, : comp_grad.shape[1]],
        input_grad,
        grad_query,
        grad_key,
        grad_value,
        grad_output,
        grad_hidden,
        grad_return,
        grad_compress,
        gains[0],
        gains[1],
    )


def solution(mesh):
    placed = (
        P("dp", "seq", None),
        P("dp", "seq", None),
        P("dp", "seq", None),
        P("dp"),
        P("dp"),
        P(),
        P(),
        P(),
        P(),
        P(None, "seq"),
        P("seq", None),
        P(),
        P(),
        P(),
        P("dp", "seq", None),
        P("dp", None, None),
    )
    fast = mesh.shape["seq"] == 2 and mesh.shape["dp"] == 16
    return jax.shard_map(
        on_device_pair if fast else on_device,
        mesh=mesh,
        in_specs=placed,
        out_specs=(
            P("dp", "seq", None),
            P("dp", None, None),
            P("dp", "seq", None),
            P("dp", "seq"),
            P("dp", "seq"),
            P("dp", "seq"),
            P("dp", "seq"),
            P("dp", "seq"),
            P("seq", "dp"),
            P("dp", "seq"),
            P("dp"),
            P("dp"),
        ),
        check_vma=False,
    )
```

```python
import functools
import math

import jax
import jax.numpy as jnp
from jax import lax
from jax.experimental import pallas as pl
from jax.experimental.pallas import tpu as pltpu
from jax.sharding import PartitionSpec as P

HEADS = 8
HEAD_DIM = 128
RATE = 3


epsilon = 1e-05
masked_score = -1e30


def shifted(block, axis, distance):
    devices = range(lax.axis_size(axis))
    route = [(i - distance, i) for i in devices if i - distance in devices]
    return lax.ppermute(block, axis, route)


def layer_norm(values, gain):
    centred = values - jnp.mean(values, axis=-1, keepdims=True)
    spread = jnp.mean(centred * centred, axis=-1, keepdims=True)
    return centred * lax.rsqrt(spread + epsilon) * gain


def project(left, right):
    return jnp.einsum("srd,de->sre", left, right, preferred_element_type=jnp.float32)


def project_back(left, right):
    return jnp.einsum("sre,de->srd", left, right, preferred_element_type=jnp.float32)


def weight_term(left, right):
    return jnp.einsum("srd,sre->de", left, right, preferred_element_type=jnp.float32)


def key_layout(key_index, local_rows, seg_len):
    key_owner = key_index // (3 * local_rows)
    inside = key_index % (3 * local_rows)
    key_kind = inside // local_rows
    key_place = key_owner * local_rows + inside % local_rows
    mem_slot = jnp.where(key_kind == 0, key_place, seg_len + key_place)
    return (key_kind, mem_slot, key_place)


def allowed_mask(key_kind, mem_slot, key_place, query_place, offsets, keep_flag):
    memory_ok = (mem_slot[None, :] >= offsets[:, None]) & keep_flag[:, None]
    causal = key_place[None, :] <= query_place[:, None]
    return jnp.where(key_kind[None, None, :] < 2, memory_ok[:, None, :], causal[None, :, :])


def score_block(query_heads, key_heads, allowed, score_scale):
    scores = (
        jnp.einsum("sthe,skhe->shtk", query_heads, key_heads, preferred_element_type=jnp.float32)
        * score_scale
    )
    return jnp.where(allowed[:, None], scores, masked_score)


def tile_matrix(matrix, dp_count, seq_count):
    rows_total, cols_total = matrix.shape
    blocks = matrix.reshape(dp_count, rows_total // dp_count, seq_count, cols_total // seq_count)
    return blocks.transpose(0, 2, 1, 3).reshape(
        dp_count * seq_count, rows_total // dp_count, cols_total // seq_count
    )


def tile_vector(vector, dp_count, seq_count):
    piece_len = vector.shape[0] // dp_count
    pieces = vector.reshape(dp_count, 1, piece_len)
    return jnp.broadcast_to(pieces, (dp_count, seq_count, piece_len)).reshape(
        dp_count * seq_count, piece_len
    )


def on_device(
    inputs,
    memory,
    compressed,
    offsets,
    resets,
    w_query,
    w_key,
    w_value,
    w_output,
    w_hidden,
    w_return,
    w_compress,
    gain_attn,
    gain_ffn,
    out_grad,
    comp_grad,
):
    seq_count = lax.axis_size("seq")
    dp_count = lax.axis_size("dp")
    seq_rank = lax.axis_index("seq")
    streams, local_rows, feat_width = inputs.shape
    seg_len = local_rows * seq_count
    score_scale = HEAD_DIM ** (-0.5)
    keep_flag = resets == 0
    all_rows = jnp.concatenate([compressed, memory, inputs], axis=1).astype(jnp.float32)
    normed, attn_norm_back = jax.vjp(layer_norm, all_rows, gain_attn.astype(jnp.float32))
    normed_low = normed.astype(jnp.bfloat16)
    query_in = normed_low[:, 2 * local_rows :]
    query_low = project(query_in, w_query).astype(jnp.bfloat16)
    key_low = project(normed_low, w_key).astype(jnp.bfloat16)
    value_low = project(normed_low, w_value).astype(jnp.bfloat16)
    key_all, value_all = (
        lax.all_gather(key_low, "seq", axis=1, tiled=True),
        lax.all_gather(value_low, "seq", axis=1, tiled=True),
    )
    total_keys = key_all.shape[1]
    key_kind, mem_slot, key_place = key_layout(
        jnp.arange(total_keys, dtype=jnp.int32), local_rows, seg_len
    )
    query_place = seq_rank * local_rows + jnp.arange(local_rows, dtype=jnp.int32)
    allowed = allowed_mask(key_kind, mem_slot, key_place, query_place, offsets, keep_flag)
    query_heads = query_low.reshape(streams, local_rows, HEADS, HEAD_DIM)
    key_heads = key_all.reshape(streams, total_keys, HEADS, HEAD_DIM)
    value_heads = value_all.reshape(streams, total_keys, HEADS, HEAD_DIM)
    scores = score_block(query_heads, key_heads, allowed, score_scale)
    row_top = jnp.max(scores, axis=-1, keepdims=True)
    exp_scores = jnp.exp(scores - row_top)
    row_total = jnp.sum(exp_scores, axis=-1, keepdims=True)
    attn_prob = exp_scores / row_total
    log_total = row_top + jnp.log(row_total)
    mixed_low = (
        jnp.einsum(
            "shtk,skhe->sthe",
            attn_prob.astype(jnp.bfloat16),
            value_heads,
            preferred_element_type=jnp.float32,
        )
        .reshape(streams, local_rows, feat_width)
        .astype(jnp.bfloat16)
    )
    hidden = inputs.astype(jnp.float32) + project(mixed_low, w_output)
    ffn_in, ffn_norm_back = jax.vjp(layer_norm, hidden, gain_ffn.astype(jnp.float32))
    ffn_low = ffn_in.astype(jnp.bfloat16)
    ffn_all = lax.all_gather(ffn_low, "seq", axis=1, tiled=True)
    pre_act = jnp.einsum("std,df->stf", ffn_all, w_hidden, preferred_element_type=jnp.float32)
    act_float, gelu_back = jax.vjp(jax.nn.gelu, pre_act)
    act_low = act_float.astype(jnp.bfloat16)
    partial_out = jnp.einsum("stf,fd->std", act_low, w_return, preferred_element_type=jnp.float32)
    ffn_out = lax.psum_scatter(
        partial_out.astype(jnp.bfloat16), "seq", scatter_dimension=1, tiled=True
    ).astype(jnp.float32)
    cot_all = lax.all_gather(out_grad, "seq", axis=1, tiled=True)
    act_grad = jnp.einsum("std,fd->stf", cot_all, w_return, preferred_element_type=jnp.float32)
    return_part = jnp.einsum("stf,std->fd", act_low, cot_all, preferred_element_type=jnp.float32)
    pre_grad = gelu_back(act_grad)[0].astype(jnp.bfloat16)
    hidden_part = jnp.einsum("std,stf->df", ffn_all, pre_grad, preferred_element_type=jnp.float32)
    in_part = jnp.einsum("stf,df->std", pre_grad, w_hidden, preferred_element_type=jnp.float32)
    ffn_in_grad = lax.psum_scatter(in_part, "seq", scatter_dimension=1, tiled=True)
    hidden_sum, return_sum = (
        lax.psum_scatter(
            hidden_part.astype(jnp.bfloat16), "dp", scatter_dimension=0, tiled=True
        ).astype(jnp.float32),
        lax.psum_scatter(
            return_part.T.astype(jnp.bfloat16), "dp", scatter_dimension=0, tiled=True
        ).astype(jnp.float32),
    )
    grad_return = return_sum.T
    outputs = (hidden + ffn_out).astype(jnp.bfloat16)
    hidden_grad, gain_ffn_grad = ffn_norm_back(ffn_in_grad)
    hidden_grad = hidden_grad + out_grad.astype(jnp.float32)
    attn_grad_low = hidden_grad.astype(jnp.bfloat16)
    output_part = weight_term(mixed_low, attn_grad_low)
    mixed_grad = project_back(attn_grad_low, w_output).astype(jnp.bfloat16)
    mixed_heads = mixed_grad.reshape(streams, local_rows, HEADS, HEAD_DIM)
    prob_again = jnp.exp(score_block(query_heads, key_heads, allowed, score_scale) - log_total)
    prob_grad = jnp.einsum(
        "sthe,skhe->shtk", mixed_heads, value_heads, preferred_element_type=jnp.float32
    )
    prob_delta = jnp.sum(prob_again * prob_grad, axis=-1)
    score_grad = (prob_again * (prob_grad - prob_delta[..., None])).astype(jnp.bfloat16)
    query_grad = (
        (
            jnp.einsum("shtk,skhe->sthe", score_grad, key_heads, preferred_element_type=jnp.float32)
            * score_scale
        )
        .reshape(streams, local_rows, feat_width)
        .astype(jnp.bfloat16)
    )
    key_part = (
        jnp.einsum("shtk,sthe->skhe", score_grad, query_heads, preferred_element_type=jnp.float32)
        * score_scale
    ).reshape(streams, total_keys, feat_width)
    value_part = jnp.einsum(
        "shtk,sthe->skhe",
        prob_again.astype(jnp.bfloat16),
        mixed_heads,
        preferred_element_type=jnp.float32,
    ).reshape(streams, total_keys, feat_width)
    key_sum, value_sum = (
        lax.psum_scatter(
            key_part.astype(jnp.bfloat16), "seq", scatter_dimension=1, tiled=True
        ).astype(jnp.float32),
        lax.psum_scatter(
            value_part.astype(jnp.bfloat16), "seq", scatter_dimension=1, tiled=True
        ).astype(jnp.float32),
    )
    key_grad = key_sum.astype(jnp.bfloat16)
    value_grad = value_sum.astype(jnp.bfloat16)
    query_part = weight_term(query_in, query_grad)
    key_wpart = weight_term(normed_low, key_grad)
    value_wpart = weight_term(normed_low, value_grad)
    query_back = project_back(query_grad, w_query)
    normed_grad = project_back(key_grad, w_key) + project_back(value_grad, w_value)
    normed_grad = normed_grad + jnp.concatenate(
        [jnp.zeros((streams, 2 * local_rows, feat_width), jnp.float32), query_back], axis=1
    )
    rows_grad, gain_attn_grad = attn_norm_back(normed_grad)
    input_grad = (rows_grad[:, 2 * local_rows :] + hidden_grad).astype(jnp.bfloat16)
    kept_memory = memory * keep_flag[:, None, None].astype(jnp.bfloat16)
    edge_rows = shifted(kept_memory[:, : 2 * (RATE - 1)], "seq", -1)
    extended = jnp.concatenate([kept_memory, edge_rows], axis=1)
    group_count = (local_rows + RATE - 1) // RATE
    first_group = (seq_rank * local_rows + RATE - 1) // RATE
    slice_start = RATE * first_group - seq_rank * local_rows
    grouped = lax.dynamic_slice_in_dim(extended, slice_start, RATE * group_count, 1).reshape(
        streams, group_count, RATE * feat_width
    )
    piece_rows = jnp.einsum(
        "sgc,cd->sgd", grouped, w_compress, preferred_element_type=jnp.float32
    ).astype(jnp.bfloat16)
    comp_all = lax.all_gather(piece_rows, "seq", axis=1, tiled=True)
    comp_count = comp_grad.shape[1]
    out_index = jnp.arange(comp_count, dtype=jnp.int32)
    holder = RATE * out_index // local_rows
    lookup = holder * group_count + out_index - (holder * local_rows + RATE - 1) // RATE
    new_compressed = jnp.take(comp_all, lookup, axis=1)
    slot_index = first_group + jnp.arange(group_count, dtype=jnp.int32)
    slot_valid = (RATE * slot_index < (seq_rank + 1) * local_rows) & (slot_index < comp_count)
    picked = jnp.take(comp_grad, jnp.minimum(slot_index, comp_count - 1), axis=1) * slot_valid[
        None, :, None
    ].astype(jnp.bfloat16)
    compress_part = jnp.einsum("sgc,sgd->cd", grouped, picked, preferred_element_type=jnp.float32)
    reduced = (
        lax.psum_scatter(
            tile_matrix(query_part, dp_count, seq_count),
            ("dp", "seq"),
            scatter_dimension=0,
            tiled=True,
        ),
        lax.psum_scatter(
            tile_matrix(key_wpart, dp_count, seq_count),
            ("dp", "seq"),
            scatter_dimension=0,
            tiled=True,
        ),
        lax.psum_scatter(
            tile_matrix(value_wpart, dp_count, seq_count),
            ("dp", "seq"),
            scatter_dimension=0,
            tiled=True,
        ),
        lax.psum_scatter(
            tile_matrix(output_part, dp_count, seq_count),
            ("dp", "seq"),
            scatter_dimension=0,
            tiled=True,
        ),
        lax.psum_scatter(
            tile_matrix(compress_part, dp_count, seq_count),
            ("dp", "seq"),
            scatter_dimension=0,
            tiled=True,
        ),
        lax.psum_scatter(
            tile_vector(gain_attn_grad, dp_count, seq_count),
            ("dp", "seq"),
            scatter_dimension=0,
            tiled=True,
        ),
        lax.psum_scatter(
            tile_vector(gain_ffn_grad, dp_count, seq_count),
            ("dp", "seq"),
            scatter_dimension=0,
            tiled=True,
        ),
    )
    return (
        outputs,
        new_compressed,
        input_grad,
        reduced[0][0],
        reduced[1][0],
        reduced[2][0],
        reduced[3][0],
        hidden_sum,
        grad_return,
        reduced[4][0],
        reduced[5][0],
        reduced[6][0],
    )


F32 = jnp.float32
BF16 = jnp.bfloat16
NN = (((1,), (0,)), ((), ()))
NT = (((1,), (1,)), ((), ()))
TN = (((0,), (0,)), ((), ()))
VMEM_LIMIT = 60 * 1024 * 1024
SCALE = HEAD_DIM ** (-0.5)
EXP2_SCALE = SCALE * math.log2(math.e)


def dot(left, right, dims=NN):
    return lax.dot_general(left, right, dims, preferred_element_type=F32)


def params(steps=1):
    return pltpu.CompilerParams(
        vmem_limit_bytes=VMEM_LIMIT, dimension_semantics=("arbitrary",) * steps
    )


def cost(flops, bytes_accessed=0, transcendentals=0):
    return pl.CostEstimate(
        flops=int(flops), bytes_accessed=int(bytes_accessed), transcendentals=int(transcendentals)
    )


def held(shape):
    zeros = (0,) * len(shape)
    return pl.BlockSpec(shape, lambda *_: zeros, pipeline_mode=pl.Buffered(1))


def norm_parts(rows):
    centred = rows - jnp.mean(rows, axis=-1, keepdims=True)
    inverse = lax.rsqrt(jnp.mean(centred * centred, axis=-1, keepdims=True) + epsilon)
    return centred * inverse, inverse


def norm_back(grad, unit, inverse):
    return inverse * (
        grad
        - jnp.mean(grad, axis=-1, keepdims=True)
        - unit * jnp.mean(grad * unit, axis=-1, keepdims=True)
    )


def add_low(left, right):
    return (left.astype(F32) + right.astype(F32)).astype(BF16)


def mesh_place():
    rank, core = lax.axis_index("dp"), lax.axis_index("seq")

    def bit(b):
        return lax.rem(lax.div(rank, 1 << b), 2)

    def across(b):
        return rank + (1 << b) * (1 - 2 * bit(b))

    return core, bit, across


def first_slots(resets_ref, offsets_ref, core, total):
    return [
        jnp.where(resets_ref[core + 2 * j] != 0, total, offsets_ref[core + 2 * j]) for j in range(2)
    ]


def stream_a_slot(resets_ref, offsets_ref, core, total):
    first, second = first_slots(resets_ref, offsets_ref, core, total)
    return jnp.where(first >= total, second, first)


def greet(devices):
    barrier = pltpu.get_barrier_semaphore()
    for device in devices:
        pl.semaphore_signal(
            barrier, inc=1, device_id=device, device_id_type=pl.DeviceIdType.MESH
        )
    pl.semaphore_wait(barrier, len(devices))


def remote(src, dst, sems, device):
    return pltpu.make_async_remote_copy(
        src_ref=src,
        dst_ref=dst,
        send_sem=sems[0],
        recv_sem=sems[1],
        device_id=device,
        device_id_type=pl.DeviceIdType.MESH,
    )


class Chunk:
    def __init__(self, data, left, order, landing, sems, place):
        self.data, self.left, self.order = data, left, order
        self.landing, self.sems = landing, sems
        _, self.bit, self.across = place

    def at(self, swap, away):
        index = []
        for b in self.left:
            if b in self.order[:swap]:
                index.append(self.bit(b))
            elif swap < len(self.order) and b == self.order[swap]:
                index.append(1 - self.bit(b) if away else self.bit(b))
            else:
                index.append(slice(None))
        return tuple(index)

    def rest(self, swap):
        done = self.order[:swap]
        return tuple(self.bit(b) if b in done else slice(None) for b in self.left)

    def copy(self, swap):
        return remote(
            self.data.at[self.at(swap, True)],
            self.landing[swap],
            (self.sems.at[0, swap], self.sems.at[1, swap]),
            {"dp": self.across(self.order[swap])},
        )

    def start(self, swap):
        self.copy(swap).start()

    def settle(self, swap):
        self.copy(swap).wait()
        here = self.at(swap, False)
        self.data[here] = add_low(self.data[here], self.landing[swap][...])

    def last(self, swap):
        self.copy(swap).wait()
        return self.data[self.at(swap, False)].astype(F32) + self.landing[swap][...].astype(F32)


def landings(left, order, block):
    shapes, count = [], len(left)
    for _ in order:
        count -= 1
        shapes.append(pltpu.VMEM((2,) * count + block, BF16))
    return shapes


BITS = (3, 2, 1, 0)
ORDERS = ((0, 1, 2, 3), (1, 0, 2, 3))


def front_kernel(
    resets_ref, in_ref, mem_ref, old_ref, og_ref, wc_ref, cg_ref,
    x_in_ref, x_mem_ref, x_old_ref, x_og_ref, new_ref, kept_p_ref, sent_p_ref, kept_q_ref, sent_q_ref,
    mem, x_in, x_old, x_og, wc, new, core_out, core_in, row_sems, wc_sem, new_sems, core_sems, out_sems,
):
    core, bit, _ = mesh_place()
    partner = {"seq": 1 - core}
    width = in_ref.shape[2]
    groups = cg_ref.shape[1]

    weights = pltpu.make_async_copy(wc_ref, wc, wc_sem)
    weights.start()
    greet((partner,))
    moves = []
    for n, (src, dst) in enumerate(
        ((mem_ref, mem), (in_ref, x_in), (old_ref, x_old), (og_ref, x_og))
    ):
        for j in range(2):
            away = remote(
                src.at[1 - core + 2 * j], dst.at[j, core], (row_sems.at[0, n, j], row_sems.at[1, n, j]), partner
            )
            here = pltpu.make_async_copy(src.at[core + 2 * j], dst.at[j, core], row_sems.at[2, n, j])
            away.start()
            here.start()
            moves.append((away, here))
    new[...] = jnp.zeros_like(new)
    outs = []
    for j in range(2):
        moves[j][0].wait_recv()
        moves[j][1].wait()
    outs.append(pltpu.make_async_copy(mem, x_mem_ref, out_sems.at[0]))
    outs[-1].start()
    weights.wait()

    grouped = []
    for j in range(2):
        rows = mem[j].reshape(2 * mem.shape[2], width)
        group = lax.broadcasted_iota(jnp.int32, (groups, rows.shape[0]), 0)
        row = lax.broadcasted_iota(jnp.int32, (groups, rows.shape[0]), 1)
        keep = jnp.where(resets_ref[core + 2 * j] == 0, 1.0, 0.0)
        total = jnp.zeros((groups, width), F32)
        mine = []
        for r in range(RATE):
            pick = jnp.where(row == RATE * group + r, keep, 0.0).astype(BF16)
            mine.append(dot(pick, rows).astype(BF16))
            total = total + dot(mine[-1], wc[r * width : (r + 1) * width])
        grouped.append(mine)
        new[j, :groups] = total.astype(BF16)

    news = []
    for j in range(2):
        at = core + 2 * j
        news.append(remote(new.at[j], new_ref.at[at], (new_sems.at[0, j], new_sems.at[1, j]), partner))
        outs.append(pltpu.make_async_copy(new.at[j], new_ref.at[at], new_sems.at[2, j]))
        news[-1].start()
        outs[-1].start()

    half = width // 2

    def grad(r, side):
        cols = pl.ds(pl.multiple_of(side * half, half), half)
        return sum(dot(grouped[j][r], cg_ref[core + 2 * j, :, cols], TN) for j in range(2))

    crossing = []
    for r in range(RATE):
        core_out[r] = grad(r, 1 - core).astype(BF16)
        crossing.append(
            remote(core_out.at[r], core_in.at[r], (core_sems.at[0, r], core_sems.at[1, r]), partner)
        )
        crossing[-1].start()
    for n, (src, dst) in enumerate(((x_in, x_in_ref), (x_old, x_old_ref), (x_og, x_og_ref))):
        for away, here in moves[2 * n + 2 : 2 * n + 4]:
            away.wait_recv()
            here.wait()
        outs.append(pltpu.make_async_copy(src, dst, out_sems.at[1 + n]))
        outs[-1].start()
    fine = width // 16
    quarter = half // 2
    for r in range(RATE):
        total = grad(r, core)
        crossing[r].wait()
        total = (total + core_in[r].astype(F32)).astype(BF16)
        for which, (kept_ref, sent_ref) in enumerate(
            ((kept_p_ref, sent_p_ref), (kept_q_ref, sent_q_ref))
        ):
            for mine in range(2):

                @pl.when(bit(which) == mine)
                def _():
                    for t in range(16):
                        block, third = divmod(r * 16 + t, RATE)
                        place = (block >> 3, block >> 2 & 1, block >> (1 - which) & 1)
                        ref = kept_ref if block >> which & 1 == mine else sent_ref
                        ref[place + (slice(third * fine, (third + 1) * fine),)] = total[
                            t * fine : (t + 1) * fine, which * quarter : (which + 1) * quarter
                        ]
    for away, _ in moves:
        away.wait_send()
    for move in outs + news:
        move.wait()


def front(resets, inputs, memory, compressed, out_grad, w_compress, comp_grad):
    streams, half, width = inputs.shape
    anywhere = pl.BlockSpec(memory_space=pl.ANY)
    vmem = pl.BlockSpec(memory_space=pltpu.VMEM)
    pair = jax.ShapeDtypeStruct((2, 2, half, width), BF16)
    padded = -(-comp_grad.shape[1] // 16) * 16
    part = jax.ShapeDtypeStruct((2, 2, 2, RATE * width // 16, width // 4), BF16)
    return pl.pallas_call(
        front_kernel,
        out_shape=(
            pair, pair, pair, pair, jax.ShapeDtypeStruct((streams, padded, width), BF16),
            part, part, part, part,
        ),
        in_specs=[pl.BlockSpec(memory_space=pltpu.SMEM)] + [anywhere] * 5 + [vmem],
        out_specs=(anywhere,) * 5 + (vmem,) * 4,
        scratch_shapes=[
            pltpu.VMEM((2, 2, half, width), BF16),
            pltpu.VMEM((2, 2, half, width), BF16),
            pltpu.VMEM((2, 2, half, width), BF16),
            pltpu.VMEM((2, 2, half, width), BF16),
            pltpu.VMEM(w_compress.shape, BF16),
            pltpu.VMEM((2, padded, width), BF16),
            pltpu.VMEM((RATE, width, width // 2), BF16),
            pltpu.VMEM((RATE, width, width // 2), BF16),
            pltpu.SemaphoreType.DMA((3, 4, 2)),
            pltpu.SemaphoreType.DMA,
            pltpu.SemaphoreType.DMA((3, 2)),
            pltpu.SemaphoreType.DMA((2, RATE)),
            pltpu.SemaphoreType.DMA((4,)),
        ],
        compiler_params=pltpu.CompilerParams(
            vmem_limit_bytes=VMEM_LIMIT, collective_id=4, has_side_effects=True
        ),
        cost_estimate=cost(12e9, 24e6),
        name="front",
    )(resets, inputs, memory, compressed, out_grad, w_compress, comp_grad)


def project_kernel(
    resets_ref, offsets_ref, old_ref, mem_ref, in_ref, og_ref, gain_ref, wq_hbm, wk_hbm, wv_hbm,
    raw_ref, normed_ref, q_ref, k_ref, v_ref, og_out_ref,
    wq_ref, wk_ref, wv_ref, sems,
):
    step = pl.program_id(0)
    weights = [
        pltpu.make_async_copy(src, dst, sems.at[n])
        for n, (src, dst) in enumerate(((wk_hbm, wk_ref), (wv_hbm, wv_ref), (wq_hbm, wq_ref)))
    ]

    @pl.when(step == 0)
    def _():
        for copy in weights:
            copy.start()

    half, width = in_ref.shape[1:]
    size = 2 * half // 2
    for n in range(2):
        at = slice(n * size, (n + 1) * size)
        pick = lambda ref: ref[...].reshape(2 * half, width)[at]
        raw = jnp.where(step == 0, pick(old_ref), jnp.where(step == 1, pick(mem_ref), pick(in_ref)))
        raw_ref[at] = raw
        unit, _ = norm_parts(raw.astype(F32))
        normed_ref[at] = (unit * gain_ref[...]).astype(BF16)
        if n == 0:

            @pl.when(step == 0)
            def _():
                for copy in weights[:2]:
                    copy.wait()

        k_ref[at] = dot(normed_ref[at], wk_ref[...]).astype(BF16)
        v_ref[at] = dot(normed_ref[at], wv_ref[...]).astype(BF16)

    @pl.when(step == 2)
    def _():
        weights[2].wait()

    @pl.when(step >= 2)
    def _():
        q_ref[...] = dot(normed_ref[...], wq_ref[...]).astype(BF16)
        og_out_ref[...] = og_ref[...].reshape(og_out_ref.shape)


def project_rows(resets, offsets, old, mem, inputs, og, gain, wq, wk, wv):
    _, _, half, width = inputs.shape
    seg = 2 * half

    def from_pair(first):
        def index(i, resets_ref, offsets_ref):
            slots = first_slots(resets_ref, offsets_ref, lax.axis_index("seq"), 2 * seg)
            stream_a = jnp.where(slots[0] >= 2 * seg, 1, 0)
            return jnp.where(i < first + 1, stream_a, 1 - stream_a), 0, 0, 0

        return pl.BlockSpec((None, 2, half, width), index)

    keys = pl.BlockSpec((seg, width), lambda i, *_: (i, 0))
    rows = pl.BlockSpec((seg, width), lambda i, *_: (jnp.maximum(i - 2, 0), 0))
    key_shape = jax.ShapeDtypeStruct((4 * seg, width), BF16)
    row_shape = jax.ShapeDtypeStruct((2 * seg, width), BF16)
    anywhere = pl.BlockSpec(memory_space=pl.ANY)
    return pl.pallas_call(
        project_kernel,
        out_shape=(key_shape, key_shape, row_shape, key_shape, key_shape, row_shape),
        grid_spec=pltpu.PrefetchScalarGridSpec(
            num_scalar_prefetch=2,
            grid=(4,),
            in_specs=[
                from_pair(4), from_pair(4), from_pair(2), from_pair(2),
                held(gain.shape), anywhere, anywhere, anywhere,
            ],
            out_specs=(keys, keys, rows, keys, keys, rows),
            scratch_shapes=[
                pltpu.VMEM(wq.shape, BF16),
                pltpu.VMEM(wk.shape, BF16),
                pltpu.VMEM(wv.shape, BF16),
                pltpu.SemaphoreType.DMA((3,)),
            ],
        ),
        compiler_params=params(),
        cost_estimate=cost(14e9, 30e6),
        name="project",
    )(resets, offsets, old, mem, inputs, og, gain, wq, wk, wv)


def attn_fwd_kernel(
    resets_ref, offsets_ref, q_ref, k_ref, v_ref, in_ref, wo_ref, gain_ref, kept_p_ref, got_p_ref, kept_q_ref, got_q_ref,
    mixed_ref, hidden_ref, ffn_ref, lse_ref, compress_ref,
    packed, *scratch,
):
    step = pl.program_id(0)
    lands, chip_sems = scratch[:-1], scratch[-1]
    place = mesh_place()
    half = q_ref.shape[0]
    seg = 2 * half
    first_slot = stream_a_slot(resets_ref, offsets_ref, place[0], 2 * seg)
    chunks = [
        Chunk(
            packed.at[which],
            tuple(b for b in BITS if b != ORDERS[which][0]),
            ORDERS[which][1:2],
            lands[which : which + 1],
            chip_sems.at[which],
            place,
        )
        for which in range(2)
    ]

    @pl.when(step == 0)
    def _():
        greet(tuple({"dp": place[2](b)} for b in range(2)))
        packed[0] = add_low(kept_p_ref[...], got_p_ref[...])
        packed[1] = add_low(kept_q_ref[...], got_q_ref[...])
        for part in chunks:
            part.start(0)

    def run(pieces):
        def one_head(h, stats):
            cols = pl.ds(pl.multiple_of(h * HEAD_DIM, HEAD_DIM), HEAD_DIM)
            q = q_ref[:, cols]
            scores = []
            for start, size, kind in pieces:
                s = dot(q, k_ref[start : start + size, cols], NT)
                if kind == "mem":
                    slot = lax.broadcasted_iota(jnp.int32, s.shape, 1)
                    s = jnp.where(slot >= first_slot, s, masked_score)
                if kind == "diag":
                    key = lax.broadcasted_iota(jnp.int32, s.shape, 1)
                    row = lax.broadcasted_iota(jnp.int32, s.shape, 0)
                    s = jnp.where(key <= row, s, masked_score)
                scores.append(s)
            top = functools.reduce(
                jnp.maximum, [jnp.max(s, axis=-1, keepdims=True) for s in scores]
            ) * EXP2_SCALE
            mix = jnp.zeros((half, 2 * HEAD_DIM), F32)
            for s, (start, size, _) in zip(scores, pieces):
                p = jnp.exp2(s * EXP2_SCALE - top).astype(BF16)
                ones = jnp.ones((size, HEAD_DIM), BF16)
                mix = mix + dot(p, jnp.concatenate([v_ref[start : start + size, cols], ones], axis=1))
            total = mix[:, HEAD_DIM:]
            mixed_ref[:, cols] = (mix[:, :HEAD_DIM] / total).astype(BF16)
            lane = lax.broadcasted_iota(jnp.int32, stats.shape, 1)
            return jnp.where(lane == h, top + jnp.log2(total), stats)

        stats = lax.fori_loop(0, HEADS, one_head, jnp.zeros((half, 128), F32), unroll=True)
        lse_ref[...] = stats.T[:HEADS]

    cases = (
        ((0, 2 * seg, "mem"), (2 * seg, half, "diag")),
        ((0, 2 * seg, "mem"), (2 * seg, half, "full"), (2 * seg + half, half, "diag")),
        ((3 * seg, half, "diag"),),
        ((3 * seg, half, "full"), (3 * seg + half, half, "diag")),
    )
    for i, pieces in enumerate(cases[2:] + cases[:2]):
        pl.when(step == i)(functools.partial(run, pieces))
    hidden = in_ref[...].astype(F32) + dot(mixed_ref[...], wo_ref[...])
    hidden_ref[...] = hidden
    unit, _ = norm_parts(hidden)
    ffn_ref[...] = (unit * gain_ref[...]).astype(BF16)

    @pl.when(step == 3)
    def _():
        for which, part in enumerate(chunks):
            part.settle(0)
            compress_ref[which] = packed[(which,) + part.rest(1)]


def attn_fwd(resets, offsets, q, k, v, raw, wo, gain, kept_p, got_p, kept_q, got_q):
    rows, width = q.shape
    half = rows // 4
    by_block = pl.BlockSpec((half, width), lambda i: (lax.rem(i + 2, 4), 0))
    in_block = pl.BlockSpec((half, width), lambda i: (4 + lax.rem(i + 2, 4), 0))
    block = kept_p.shape[-2:]
    part = held(kept_p.shape)
    lands = []
    for which in range(2):
        lands += landings(BITS[1:], ORDERS[which][1:2], block)
    out = (2, 2, 2) + block
    return pl.pallas_call(
        attn_fwd_kernel,
        grid=(4,),
        out_shape=(
            jax.ShapeDtypeStruct((rows, width), BF16),
            jax.ShapeDtypeStruct((rows, width), F32),
            jax.ShapeDtypeStruct((rows, width), BF16),
            jax.ShapeDtypeStruct((HEADS, rows), F32),
            jax.ShapeDtypeStruct(out, BF16),
        ),
        in_specs=[
            pl.BlockSpec(memory_space=pltpu.SMEM),
            pl.BlockSpec(memory_space=pltpu.SMEM),
            by_block, held(k.shape), held(v.shape), in_block, held(wo.shape), held(gain.shape),
            part, part, part, part,
        ],
        out_specs=(
            by_block, by_block, by_block, pl.BlockSpec((HEADS, half), lambda i: (0, lax.rem(i + 2, 4))), held(out),
        ),
        scratch_shapes=[pltpu.VMEM((2,) + kept_p.shape, BF16)] + lands + [pltpu.SemaphoreType.DMA((2, 2, 1))],
        compiler_params=pltpu.CompilerParams(
            vmem_limit_bytes=VMEM_LIMIT, dimension_semantics=("arbitrary",),
            collective_id=5, has_side_effects=True,
        ),
        cost_estimate=cost(20e9, 20e6),
        name="attn_fwd",
    )(resets, offsets, q, k, v, raw, wo, gain, kept_p, got_p, kept_q, got_q)


GELU_C = math.sqrt(2.0 / math.pi)
GELU_A = 0.044715
CHUNK = 512


def gelu_pair(pre, act_grad):
    square = pre * pre
    t = jnp.tanh(pre * (GELU_C + (GELU_C * GELU_A) * square))
    cdf = 0.5 + 0.5 * t
    slope = cdf + (0.5 * pre) * (1.0 - t * t) * (GELU_C + (3.0 * GELU_C * GELU_A) * square)
    return (pre * cdf).astype(BF16), (act_grad * slope).astype(BF16)


def ffn_kernel(
    x_ref, og_ref, gain_ref, packed_ref, hidden_hbm, wo_hbm, wh0_ref, wh1_ref, wr0_ref, wr1_ref,
    out_ref, attn_grad_ref, do_ref, gain_grad_ref, done_ref, part_ref, raw_ref, compress_ref,
    hidden_ref, wo_ref, held_sems, pack0, pack1, pack_sems, wh, wr, out_acc, in_acc, act_ref, pre_ref, core_out, core_in, own_ref, land0, land1, land2, land3,
    weight_sems, core_sems, chip_sems,
):
    step = pl.program_id(0)
    last = pl.num_programs(0) - 1
    index = lax.div(step, 2)
    end = lax.div(last, 2)
    owned = lax.rem(step, 2) == 1
    rows, width = x_ref.shape
    units = wh.shape[2]
    chunks = rows // CHUNK
    place = mesh_place()
    core, _, across = place
    partner = {"seq": 1 - core}

    def fetch(at, side):
        cols = pl.ds(pl.multiple_of(at * units, units), units)
        wh_ref, wr_ref = ((wh0_ref, wr0_ref), (wh1_ref, wr1_ref))[side]
        return (
            pltpu.make_async_copy(wh_ref.at[:, cols], wh.at[side], weight_sems.at[0, side]),
            pltpu.make_async_copy(wr_ref.at[cols], wr.at[side], weight_sems.at[1, side]),
        )

    held_copies = (
        pltpu.make_async_copy(hidden_hbm, hidden_ref, held_sems.at[0]),
        pltpu.make_async_copy(wo_hbm, wo_ref, held_sems.at[1]),
    )
    packs = [
        Chunk(
            packed_ref.at[which], (3, 2), (2, 3), [pack0.at[which], pack1.at[which]],
            pack_sems.at[which], place,
        )
        for which in range(2)
    ]

    @pl.when(step == 0)
    def _():
        for copy in fetch(0, 0) + held_copies:
            copy.start()
        greet((partner,) + tuple({"dp": across(b)} for b in range(4)))
        for part in packs:
            part.start(0)
        out_acc[...] = jnp.zeros_like(out_acc)
        in_acc[...] = jnp.zeros_like(in_acc)

    @pl.when(step == 2)
    def _():
        for part in packs:
            part.settle(0)
            part.start(1)

    @pl.when(step == 4)
    def _():
        cols = compress_ref.shape[1] // 2
        for which, part in enumerate(packs):
            compress_ref[:, which * cols : (which + 1) * cols] = part.last(1)

    @pl.when(jnp.logical_not(owned))
    def _():
        for copy in fetch(index, 1):
            copy.start()
        for copy in fetch(index, 0):
            copy.wait()

    @pl.when(owned)
    def _():
        @pl.when(index < end)
        def _():
            for copy in fetch(index + 1, 0):
                copy.start()

        for copy in fetch(index, 1):
            copy.wait()

    def core_copy(which, index):
        return remote(
            core_out.at[which],
            core_in.at[which, lax.rem(index, 2)],
            (core_sems.at[0, which, index], core_sems.at[1, which, index]),
            partner,
        )

    def tile(which, index):
        return Chunk(
            own_ref.at[which, index], BITS, ORDERS[which],
            [land.at[which, index] for land in (land0, land1, land2, land3)],
            chip_sems.at[which, index], place,
        )

    def pass_on(index, swap):
        for which in range(2):
            part = tile(which, index)
            part.settle(swap)
            part.start(swap + 1)

    def finish_tile(index):
        for which in range(2):
            done_ref[which, index] = tile(which, index).last(3)

    side = lax.rem(step, 2)

    def rows_step(m, _):
        at = pl.ds(pl.multiple_of(m * CHUNK, CHUNK), CHUNK)
        pre = dot(x_ref[at, :], wh[side])
        act_grad = dot(og_ref[at, :], wr[side], NT)
        act, pre_grad = gelu_pair(pre, act_grad)
        act_ref[at, :] = act
        pre_ref[at, :] = pre_grad
        out_acc[at, :] += dot(act, wr[side])
        in_acc[at, :] += dot(pre_grad, wh[side], NT)

        return 0

    lax.fori_loop(0, chunks, rows_step, 0)

    @pl.when(owned & (index > 0))
    def _():
        pass_on(index - 1, 0)

    @pl.when(owned & (index > 1))
    def _():
        pass_on(index - 2, 2)

    @pl.when(jnp.logical_not(owned) & (index > 1))
    def _():
        pass_on(index - 2, 1)

    @pl.when(jnp.logical_not(owned) & (index > 2))
    def _():
        finish_tile(index - 3)

    for which, (left_ref, right_ref) in enumerate(((x_ref, pre_ref), (og_ref, act_ref))):
        grad = dot(left_ref[...], right_ref[...], TN)

        @pl.when(jnp.logical_not(owned))
        def _():
            @pl.when(index > 0)
            def _():
                core_copy(which, index - 1).wait_send()

            core_out[which] = grad.astype(BF16)
            core_copy(which, index).start()

        @pl.when(owned)
        def _():
            core_copy(which, index).wait_recv()
            total = grad + core_in[which, lax.rem(index, 2)].astype(F32)
            total = total.astype(BF16).reshape(own_ref.shape[2:])

            @pl.when(index < end)
            def _():
                own_ref[which, index] = total
                tile(which, index).start(0)

            @pl.when(index == end)
            def _():
                raw_ref[which] = total

    @pl.when(step == last)
    def _():
        for copy in held_copies:
            copy.wait()

        def finish(m, gain_sum):
            at = pl.ds(pl.multiple_of(m * 256, 256), 256)
            hidden = hidden_ref[at, :]
            out_ref[at, :] = (hidden + out_acc[at, :]).astype(BF16)
            unit, inverse = norm_parts(hidden)
            grad = in_acc[at, :]
            hidden_grad = og_ref[at, :].astype(F32) + norm_back(
                grad * gain_ref[...], unit, inverse
            )
            low = hidden_grad.astype(BF16)
            attn_grad_ref[at, :] = low
            do_ref[at, :] = dot(low, wo_ref[...], NT).astype(BF16)
            return gain_sum + jnp.sum(grad * unit, axis=0, keepdims=True)

        gain_grad_ref[...] = lax.fori_loop(
            0, rows // 256, finish, jnp.zeros(gain_grad_ref.shape, F32)
        )
        finish_tile(end - 2)
        for which in range(2):
            core_copy(which, end).wait_send()
            part = tile(which, end - 1)
            part.settle(1)
            part_ref[which] = part.data[part.rest(2)]


def ffn(x, og, gain, packed, hidden, wo, wh0, wh1, wr0, wr1):
    rows, width = x.shape
    units = wh0.shape[1]
    tile = 512
    steps = units // tile
    count = lax.axis_size("dp")
    block = width // count
    anywhere = pl.BlockSpec(memory_space=pl.ANY)
    whole = held((rows, width))
    low_rows = jax.ShapeDtypeStruct((rows, width), BF16)
    raw = (2, 2, 2, 2, 2, block, tile)
    part = (2, 2, 2, block, tile)
    done = (2, steps - 2, block, tile)
    tiles = (2, steps - 1)
    lands = [pltpu.VMEM(tiles + (2,) * n + (block, tile), BF16) for n in (3, 2, 1, 0)]
    pack = packed.shape[-2:]
    compress = (pack[0], 2 * pack[1])
    return pl.pallas_call(
        ffn_kernel,
        grid=(2 * steps,),
        out_shape=(
            low_rows, low_rows, low_rows, jax.ShapeDtypeStruct((1, width), F32),
            jax.ShapeDtypeStruct(done, F32),
            jax.ShapeDtypeStruct(part, BF16),
            jax.ShapeDtypeStruct(raw, BF16),
            jax.ShapeDtypeStruct(compress, F32),
        ),
        in_specs=[whole, whole, held(gain.shape), held(packed.shape)] + [anywhere] * 6,
        out_specs=(whole, whole, whole, held((1, width)), held(done), held(part), held(raw), held(compress)),
        scratch_shapes=[
            pltpu.VMEM((rows, width), F32),
            pltpu.VMEM(wo.shape, BF16),
            pltpu.SemaphoreType.DMA((2,)),
            pltpu.VMEM((2, 2) + pack, BF16),
            pltpu.VMEM((2,) + pack, BF16),
            pltpu.SemaphoreType.DMA((2, 2, 2)),
            pltpu.VMEM((2, width, tile), BF16),
            pltpu.VMEM((2, tile, width), BF16),
            pltpu.VMEM((rows, width), F32),
            pltpu.VMEM((rows, width), F32),
            pltpu.VMEM((rows, tile), BF16),
            pltpu.VMEM((rows, tile), BF16),
            pltpu.VMEM((2, width, tile), BF16),
            pltpu.VMEM((2, 2, width, tile), BF16),
            pltpu.VMEM(tiles + raw[1:], BF16),
        ] + lands + [
            pltpu.SemaphoreType.DMA((2, 2)),
            pltpu.SemaphoreType.DMA((2, 2, steps)),
            pltpu.SemaphoreType.DMA((2, steps, 2, 4)),
        ],
        compiler_params=pltpu.CompilerParams(
            vmem_limit_bytes=VMEM_LIMIT, dimension_semantics=("arbitrary",),
            collective_id=1, has_side_effects=True,
        ),
        cost_estimate=cost(75e9, 50e6),
        name="ffn",
    )(x, og, gain, packed, hidden, wo, wh0, wh1, wr0, wr1)


def attn_bwd_head(first_slot, q_ref, k_ref, v_ref, do_ref, mixed_ref, lse, dq_ref, dk_ref, dv_ref, cols):
    seg = q_ref.shape[0] // 2
    half = seg // 2
    for stream in range(2):
        base = stream * seg
        rows = slice(base, base + seg)
        lse_row = lse[:, rows]
        weight = do_ref[rows, cols].astype(F32) * mixed_ref[rows, cols].astype(F32)
        delta_row = jnp.sum(weight.T, axis=0, keepdims=True)
        key_base = 2 * seg + stream * seg
        pieces = []
        if stream == 0:
            pieces += [(start, half, 0, "mem") for start in range(0, 2 * seg, half)]
        pieces += [(key_base, half, 0, "diag"), (key_base + half, half, half, "diag")]
        dq_low = jnp.zeros((half, HEAD_DIM), F32)
        dq_high = jnp.zeros((half, HEAD_DIM), F32)
        for start, size, first, kind in pieces:
            q = q_ref[base + first : base + seg, cols]
            do = do_ref[base + first : base + seg, cols]
            k = k_ref[start : start + size, cols]
            s = dot(k, q, NT) * EXP2_SCALE - lse_row[:, first:]
            if kind == "mem":
                slot = start + lax.broadcasted_iota(jnp.int32, s.shape, 0)
                s = jnp.where(slot >= first_slot, s, masked_score)
            else:
                key = lax.broadcasted_iota(jnp.int32, s.shape, 0)
                row = lax.broadcasted_iota(jnp.int32, s.shape, 1)
                s = jnp.where(key <= row, s, masked_score)
            p = jnp.exp2(s)
            dp = dot(v_ref[start : start + size, cols], do, NT)
            ds = (p * (dp - delta_row[:, first:])).astype(BF16)
            dv_ref[start : start + size, cols] = dot(p.astype(BF16), do).astype(BF16)
            dk_ref[start : start + size, cols] = (dot(ds, q) * SCALE).astype(BF16)
            dq = dot(ds, k, TN)
            if first == 0:
                dq_low = dq_low + dq[:half]
                dq_high = dq_high + dq[half:]
            else:
                dq_high = dq_high + dq
        dq_ref[base : base + half, cols] = (dq_low * SCALE).astype(BF16)
        dq_ref[base + half : base + seg, cols] = (dq_high * SCALE).astype(BF16)


def attn_back_kernel(
    resets_ref, offsets_ref, q_ref, k_ref, v_ref, do_ref, mix_ref, lse_ref, normed_hbm, mixed_hbm, ag_ref,
    ffn_part_ref, ffn_raw_ref, outputs_hbm,
    dq_ref, dk_ref, dv_ref, early_ref, late_ref, ffn_done_ref, outputs_got, outputs_sems,
    normed_ref, mixed_ref, held_sems, grads_ref, core_out0, core_in0, core_out1, core_in1, own_ref,
    *scratch,
):
    step = pl.program_id(0)
    last = pl.num_programs(0) - 1
    place = mesh_place()
    core, _, across = place
    partner = {"seq": 1 - core}
    lands, (core_sems, chip_sems) = list(scratch[:-2]), scratch[-2:]
    chunks, ffn_parts, ffn_raws = [], [], []
    first_slot = stream_a_slot(resets_ref, offsets_ref, core, q_ref.shape[0])
    outputs_copies = [
        remote(
            outputs_hbm.at[j, 1 - core], outputs_got.at[j],
            (outputs_sems.at[0, j], outputs_sems.at[1, j]), partner,
        )
        for j in range(2)
    ]
    held_copies = (
        pltpu.make_async_copy(normed_hbm, normed_ref, held_sems.at[0]),
        pltpu.make_async_copy(mixed_hbm, mixed_ref, held_sems.at[1]),
    )

    def chunk(number, data, left, order):
        mine = [lands.pop(0) for _ in order]
        return Chunk(data, left, order, mine, chip_sems.at[number], place)

    for which in range(2):
        order = ORDERS[which]
        chunks.append(chunk(3 * which, own_ref.at[which], BITS, order[:2]))
        ffn_parts.append(chunk(3 * which + 1, ffn_part_ref.at[which], order[2:][::-1], order[2:]))
        ffn_raws.append(chunk(3 * which + 2, ffn_raw_ref.at[which], BITS, order))
    index = lax.div(step, 2)
    rows = q_ref.shape[0]
    keys = k_ref.shape[0]
    pair = q_ref.shape[1]

    @pl.when(step == 0)
    def _():
        for copy in held_copies:
            copy.start()
        greet((partner,) + tuple({"dp": across(b)} for b in range(4)))
        for part in ffn_raws + ffn_parts:
            part.start(0)
        for copy in outputs_copies:
            copy.start()

    @pl.when(step == 1)
    def _():
        for part in ffn_parts:
            part.settle(0)
            part.start(1)

    @pl.when(step == 2)
    def _():
        for which in range(2):
            ffn_done_ref[which, 0] = ffn_parts[which].last(1)

    crossing = ((core_out0, core_in0), (core_out1, core_in1))

    def core_copy(which, index):
        sent, got = crossing[index]
        return remote(
            sent.at[which],
            got.at[which],
            (core_sems.at[0, which, index], core_sems.at[1, which, index]),
            partner,
        )

    head = 4 * jnp.where(lax.rem(step, 2) == 0, 1 - core, core) + 2 * index

    def one_head(h, _):
        attn_bwd_head(
            first_slot, q_ref, k_ref, v_ref, do_ref, mix_ref, lse_ref[pl.ds(head + h, 1), :],
            dq_ref, dk_ref, dv_ref, pl.ds(pl.multiple_of(h * HEAD_DIM, HEAD_DIM), HEAD_DIM),
        )
        for n in range(1, 4):

            @pl.when((step == n) & (h == 0))
            def _():
                for part in ffn_raws + (chunks if n == 3 else []):
                    swap = 0 if part in chunks else n - 1
                    part.settle(swap)
                    part.start(swap + 1)

        return 0

    lax.fori_loop(0, 2, one_head, 0)

    @pl.when(step == 0)
    def _():
        for copy in held_copies:
            copy.wait()

    less = pair + pair // 2
    grads_ref[0, :, :pair] = dot(normed_ref[keys - rows :], dq_ref[...], TN)
    grads_ref[1, :, :pair] = dot(normed_ref[...], dv_ref[...], TN)
    key_grads = dot(normed_ref[...], dk_ref[...], TN)
    grads_ref[0, :, pair:less] = key_grads[:, : pair // 2]
    grads_ref[1, :, pair:less] = key_grads[:, pair // 2 :]

    @pl.when(step < 2)
    def _():
        output_grads = dot(mixed_ref[...], ag_ref[...], TN)
        grads_ref[0, :, less:] = output_grads[:, :pair]
        grads_ref[1, :, less:] = output_grads[:, pair:]

    for n in range(2):

        @pl.when(step == 2 * n)
        def _():
            sent = crossing[n][0]
            for which in range(2):
                sent[which] = grads_ref[which, :, : sent.shape[2]].astype(BF16)
                core_copy(which, n).start()

    def own_grads(which, index, out_ref):
        core_copy(which, index).wait()
        got = crossing[index][1]
        total = grads_ref[which, :, : got.shape[2]] + got[which].astype(F32)
        out_ref[...] = total.astype(BF16).reshape(out_ref.shape)

    @pl.when(step == 1)
    def _():
        for which in range(2):
            own_grads(which, 0, own_ref.at[which])
            chunks[which].start(0)

    @pl.when(step == last)
    def _():
        for which in range(2):
            own_grads(which, 1, late_ref.at[which])
        for which in range(2):
            chunks[which].settle(1)
            early_ref[which] = own_ref[(which,) + chunks[which].rest(2)]
            ffn_done_ref[which, 1] = ffn_raws[which].last(3)
        for copy in outputs_copies:
            copy.wait()


def attn_back(resets, offsets, q, k, v, do, mixed, lse, normed, attn_grad, ffn_part, ffn_raw, outputs):
    rows, width = q.shape
    keys = k.shape[0]
    pair = 2 * HEAD_DIM
    more, less = 2 * pair + pair // 2, pair + pair // 2
    block = (width // 16, more)

    def by_pair(count):
        def index(i):
            core = lax.axis_index("seq")
            half = jnp.where(lax.rem(i, 2) == 0, 1 - core, core)
            return 0, 2 * half + lax.div(i, 2)

        return pl.BlockSpec((count, pair), index)

    def output_half(i):
        core = lax.axis_index("seq")
        return 0, jnp.where(i == 0, 1 - core, core)

    early, late = (2, 2, 2) + block, (2, 2, 2, 2, 2, width // 16, less)
    ffn_block = ffn_raw.shape[-2:]
    done = (2, 2) + ffn_block
    lands = []
    for order in ORDERS:
        lands += landings(BITS, order[:2], block)
        lands += landings(order[2:], order[2:], ffn_block)
        lands += landings(BITS, order, ffn_block)
    return pl.pallas_call(
        attn_back_kernel,
        grid=(4,),
        out_shape=(
            jax.ShapeDtypeStruct((rows, width), BF16),
            jax.ShapeDtypeStruct((keys, width), BF16),
            jax.ShapeDtypeStruct((keys, width), BF16),
            jax.ShapeDtypeStruct(early, BF16),
            jax.ShapeDtypeStruct(late, BF16),
            jax.ShapeDtypeStruct(done, F32),
            jax.ShapeDtypeStruct((2,) + outputs.shape[2:], BF16),
        ),
        in_specs=[
            pl.BlockSpec(memory_space=pltpu.SMEM),
            pl.BlockSpec(memory_space=pltpu.SMEM),
            by_pair(rows), by_pair(keys), by_pair(keys), by_pair(rows), by_pair(rows),
            held(lse.shape), pl.BlockSpec(memory_space=pl.ANY), pl.BlockSpec(memory_space=pl.ANY),
            pl.BlockSpec((rows, 2 * pair), output_half),
            held(ffn_part.shape), held(ffn_raw.shape), pl.BlockSpec(memory_space=pl.ANY),
        ],
        out_specs=(by_pair(rows), by_pair(keys), by_pair(keys), held(early), held(late), held(done),
            pl.BlockSpec(memory_space=pl.ANY),
        ),
        scratch_shapes=[
            pltpu.SemaphoreType.DMA((2, 2)),
            pltpu.VMEM(normed.shape, BF16),
            pltpu.VMEM(mixed.shape, BF16),
            pltpu.SemaphoreType.DMA((2,)),
            pltpu.VMEM((2, width, more), F32),
            pltpu.VMEM((2, width, more), BF16),
            pltpu.VMEM((2, width, more), BF16),
            pltpu.VMEM((2, width, less), BF16),
            pltpu.VMEM((2, width, less), BF16),
            pltpu.VMEM((2, 2, 2, 2, 2) + block, BF16),
        ] + lands + [
            pltpu.SemaphoreType.DMA((2, 2, 2)),
            pltpu.SemaphoreType.DMA((6, 2, 4)),
        ],
        compiler_params=pltpu.CompilerParams(
            vmem_limit_bytes=VMEM_LIMIT, dimension_semantics=("arbitrary",),
            collective_id=2, has_side_effects=True,
        ),
        cost_estimate=cost(45e9, 24e6),
        name="attn_back",
    )(resets, offsets, q, k, v, do, mixed, lse, normed, mixed, attn_grad, ffn_part, ffn_raw, outputs)


def rows_back_kernel(
    dq_ref, dk_ref, dv_ref, raw_ref, ag_ref, gain_ref, gain_ffn_ref, wq_hbm, wk_hbm, wv_hbm,
    early_ref, late_ref,
    mine_ref, theirs_ref, gains_ref, query_ref, key_ref, value_ref, output_ref,
    wq_ref, wk_ref, wv_ref, weight_sems, rows_out, gain_acc, gain_out, gain_in, *scratch,
):
    step = pl.program_id(0)
    last = pl.num_programs(0) - 1
    place = mesh_place()
    core, _, across = place
    partner = {"seq": 1 - core}
    lands, (row_sems, local_sems, gain_sems, chip_sems) = list(scratch[:-4]), scratch[-4:]

    chunks = []

    def chunk(data, left, order):
        number = len(chunks)
        mine = [lands.pop(0) for _ in order]
        chunks.append(Chunk(data, left, order, mine, chip_sems.at[number], place))
        return chunks[-1]

    early, late = [], []
    for which in range(2):
        early.append(chunk(early_ref.at[which], BITS[:2], ORDERS[which][2:]))
        late.append(chunk(late_ref.at[which], BITS, ORDERS[which]))

    rank = lax.axis_index("dp")

    def flipped(n, bits):
        return rank + sum(across(b) - rank for i, b in enumerate(bits) if n >> i & 1)

    gain_groups = (
        [{"dp": flipped(n >> 1, (0, 1)), "seq": 1 - core if n & 1 else core} for n in range(1, 8)],
        [{"dp": flipped(n, (2, 3))} for n in range(1, 4)],
    )

    def gain_copies(stage):
        first = 7 * stage
        return [
            remote(
                gain_out.at[stage],
                gain_in.at[first + n],
                (gain_sems.at[0, first + n], gain_sems.at[1, first + n]),
                device,
            )
            for n, device in enumerate(gain_groups[stage])
        ]

    def gain_total(stage):
        for copy in gain_copies(stage):
            copy.wait()
        return gain_out[stage] + sum(gain_in[7 * stage + n] for n in range(len(gain_groups[stage])))

    def row_copy(block):
        stream = block // 2
        return remote(
            rows_out.at[block], theirs_ref.at[stream], (row_sems.at[0, stream], row_sems.at[1, stream]), partner
        )

    def row_keep(block):
        stream = block // 2
        return pltpu.make_async_copy(rows_out.at[block], mine_ref.at[stream], local_sems.at[stream])

    weights = [
        pltpu.make_async_copy(src, dst, weight_sems.at[n])
        for n, (src, dst) in enumerate(((wk_hbm, wk_ref), (wv_hbm, wv_ref), (wq_hbm, wq_ref)))
    ]

    @pl.when(step == 0)
    def _():
        for copy in weights:
            copy.start()
        greet(gain_groups[0] + gain_groups[1])
        for part in late + early:
            part.start(0)
        for copy in weights[:2]:
            copy.wait()
        gain_acc[...] = jnp.zeros_like(gain_acc)

    def normed_grad():
        return dot(dk_ref[...], wk_ref[...], NT) + dot(dv_ref[...], wv_ref[...], NT)

    unit, inverse = norm_parts(raw_ref[...].astype(F32))

    @pl.when(step < 4)
    def _():
        gain_acc[0:1] += jnp.sum(normed_grad() * unit, axis=0, keepdims=True)

    @pl.when(step == 4)
    def _():
        weights[2].wait()

    @pl.when(step >= 4)
    def _():
        grad = normed_grad() + dot(dq_ref[...], wq_ref[...], NT)
        gain_acc[0:1] += jnp.sum(grad * unit, axis=0, keepdims=True)
        rows_grad = norm_back(grad * gain_ref[...], unit, inverse)
        rows_out[step - 4] = (rows_grad + ag_ref[...].astype(F32)).astype(BF16)

    for block in range(4):
        stays = core == block % 2
        pl.when((step == block + 4) & stays)(row_keep(block).start)
        pl.when((step == block + 4) & jnp.logical_not(stays))(row_copy(block).start)

    @pl.when(step == 4)
    def _():
        for part in early:
            part.settle(0)
            part.start(1)

    @pl.when(step == 5)
    def _():
        for part in late:
            part.settle(0)
            part.start(1)

    @pl.when(step == last)
    def _():
        lanes = gain_out.shape[2]
        for n in range(8):
            cols = slice(n * lanes, (n + 1) * lanes)
            gain_out[0, n : n + 1] = gain_acc[0:1, cols]
            gain_out[0, 8 + n : 9 + n] = gain_ffn_ref[:, cols]
        for copy in gain_copies(0):
            copy.start()
        pair = 2 * HEAD_DIM
        for which, ref in enumerate((query_ref, value_ref)):
            total = early[which].last(1)
            ref[:, :pair] = total[:, :pair]
            key_ref[:, which * HEAD_DIM : (which + 1) * HEAD_DIM] = total[:, pair : pair + HEAD_DIM]
            output_ref[:, which * pair : (which + 1) * pair] = total[:, pair + HEAD_DIM :]
        for part in late:
            part.settle(1)
            part.start(2)
        gain_out[1] = gain_total(0)
        for copy in gain_copies(1):
            copy.start()
        for part in late:
            part.settle(2)
            part.start(3)
        gains_ref[...] = gain_total(1)
        for which, ref in enumerate((query_ref, value_ref)):
            total = late[which].last(3)
            ref[:, pair:] = total[:, :pair]
            key_ref[:, pair + which * HEAD_DIM : pair + (which + 1) * HEAD_DIM] = total[:, pair:]
        for block in range(4):
            stays = core == block % 2
            pl.when(stays)(row_keep(block).wait)
            pl.when(jnp.logical_not(stays))(row_copy(block).wait_send)
        for stream in range(2):
            row_copy(2 * stream).wait_recv()


def rows_back(
    dq, dk, dv, raw, attn_grad, gain, gain_ffn, wq, wk, wv, early, late
):
    keys, width = dk.shape
    rows = dq.shape[0]
    size = keys // 8
    key_block = pl.BlockSpec((size, width), lambda i: (i, 0))
    row_block = pl.BlockSpec((size, width), lambda i: (jnp.maximum(i - 4, 0), 0))
    anywhere = pl.BlockSpec(memory_space=pl.ANY)
    rows_shape = jax.ShapeDtypeStruct((2, size, width), BF16)
    early_block, late_block = early.shape[-2:], late.shape[-2:]
    lands = []
    for order in ORDERS:
        lands += landings(BITS[:2], order[2:], early_block)
        lands += landings(BITS, order, late_block)
    out = (early_block[0], 4 * HEAD_DIM)
    vector = (16, width // 8)
    return pl.pallas_call(
        rows_back_kernel,
        grid=(8,),
        out_shape=(
            rows_shape, rows_shape,
            jax.ShapeDtypeStruct(vector, F32),
        ) + (jax.ShapeDtypeStruct(out, F32),) * 4,
        in_specs=[
            row_block, key_block, key_block, key_block, row_block,
            held(gain.shape), held(gain_ffn.shape), anywhere, anywhere, anywhere,
            held(early.shape), held(late.shape),
        ],
        out_specs=(
            anywhere, anywhere, held(vector),
        ) + (held(out),) * 4,
        scratch_shapes=[
            pltpu.VMEM(wq.shape, BF16),
            pltpu.VMEM(wk.shape, BF16),
            pltpu.VMEM(wv.shape, BF16),
            pltpu.SemaphoreType.DMA((3,)),
            pltpu.VMEM((4, size, width), BF16),
            pltpu.VMEM((8, width), F32),
            pltpu.VMEM((2,) + vector, F32),
            pltpu.VMEM((10,) + vector, F32),
        ] + lands + [
            pltpu.SemaphoreType.DMA((2, 2)),
            pltpu.SemaphoreType.DMA((2,)),
            pltpu.SemaphoreType.DMA((2, 10)),
            pltpu.SemaphoreType.DMA((4, 2, 4)),
        ],
        compiler_params=pltpu.CompilerParams(
            vmem_limit_bytes=VMEM_LIMIT, dimension_semantics=("arbitrary",),
            collective_id=3, has_side_effects=True,
        ),
        cost_estimate=cost(20e9, 24e6),
        name="rows_back",
    )(
        dq, dk, dv, raw, attn_grad, gain, gain_ffn, wq, wk, wv,
        early, late,
    )


def place_kernel(
    resets_ref, offsets_ref, own_a_ref, got_a_ref, own_b_ref, got_b_ref, out_a_ref, out_b_ref
):
    core = lax.axis_index("seq")
    for out_ref, own_ref, got_ref in ((out_a_ref, own_a_ref, got_a_ref), (out_b_ref, own_b_ref, got_b_ref)):
        out_ref[core] = own_ref[...]
        out_ref[1 - core] = got_ref[...]


def place_rows(resets, offsets, outputs, outputs_got, mine_rows, their_rows):
    _, _, half, width = outputs.shape

    def slot(i, resets_ref, offsets_ref, core):
        first = first_slots(resets_ref, offsets_ref, core, 4 * half)[0]
        return jnp.where(i == jnp.where(first >= 4 * half, 1, 0), 0, 1)

    def own(i, *refs):
        return slot(i, *refs, lax.axis_index("seq"))

    def got(i, *refs):
        return slot(i, *refs, 1 - lax.axis_index("seq"))

    block = (None, half, width)
    out = jax.ShapeDtypeStruct((4, half, width), BF16)
    return pl.pallas_call(
        place_kernel,
        out_shape=(out, out),
        grid_spec=pltpu.PrefetchScalarGridSpec(
            num_scalar_prefetch=2,
            grid=(2,),
            in_specs=[
                pl.BlockSpec(
                    (None, None, half, width), lambda *a: (own(*a), lax.axis_index("seq"), 0, 0)
                ),
                pl.BlockSpec(block, lambda *a: (got(*a), 0, 0)),
                pl.BlockSpec(block, lambda *a: (own(*a), 0, 0)),
                pl.BlockSpec(block, lambda *a: (got(*a), 0, 0)),
            ],
            out_specs=(pl.BlockSpec((2, half, width), lambda i, *_: (i, 0, 0)),) * 2,
        ),
        compiler_params=params(),
        cost_estimate=cost(0, 8e6),
        name="place",
    )(resets, offsets, outputs, outputs_got, mine_rows, their_rows)


def swap_dp(block, bit):
    count = lax.axis_size("dp")
    return lax.ppermute(block, "dp", [(i, i ^ (1 << bit)) for i in range(count)])


def swap_core(block):
    return lax.ppermute(block, "seq", [(0, 1), (1, 0)])


def on_device_pair(
    inputs, memory, compressed, offsets, resets, w_query, w_key, w_value, w_output, w_hidden,
    w_return, w_compress, gain_attn, gain_ffn, out_grad, comp_grad,
):
    core = lax.axis_index("seq")
    dp_count = lax.axis_size("dp")
    streams, half, width = inputs.shape
    seg = 2 * half
    low_core = core == 0

    unused = (resets != 0) | (offsets >= 2 * seg)
    gain_a = gain_attn.astype(F32).reshape(1, width)
    gain_f = gain_ffn.astype(F32).reshape(1, width)

    x_in, x_mem, x_old, x_og, new_rows, kept_p, sent_p, kept_q, sent_q = front(
        resets, inputs, memory, compressed, out_grad, w_compress, comp_grad
    )
    got_p, got_q = swap_dp(sent_p, 0), swap_dp(sent_q, 1)
    wh_late, wr_late, x_in = lax.optimization_barrier((w_hidden, w_return, x_in))
    wh_other, wr_other = swap_core(wh_late), swap_core(wr_late)
    all_rows, normed, q, k, v, og = project_rows(
        resets, offsets, x_old, x_mem, x_in, x_og, gain_a, w_query, w_key, w_value
    )
    mixed, hidden, ffn_in, lse, packed = attn_fwd(
        resets, offsets, q, k, v, all_rows, w_output, gain_f, kept_p, got_p, kept_q, got_q
    )
    outputs, attn_grad, mixed_grad, gain_ffn_grad, ffn_done, ffn_part, ffn_raw, grad_compress = ffn(
        ffn_in, og, gain_f, packed, hidden, w_output, wh_other, w_hidden, wr_other, w_return
    )
    outputs = outputs.reshape(2, 2, half, width)
    dq, dk, dv, early, late, ffn_rest, outputs_got = attn_back(
        resets, offsets, q, k, v, mixed_grad, mixed, lse, normed, attn_grad, ffn_part, ffn_raw,
        outputs,
    )
    mine_rows, their_rows, gains, grad_query, grad_key, grad_value, grad_output = rows_back(
        dq, dk, dv, all_rows, attn_grad, gain_a, gain_ffn_grad, w_query, w_key, w_value, early, late
    )

    def tiles(which):
        parts = [ffn_done[which, i] for i in range(2)] + [ffn_rest[which, i] for i in range(2)]
        return jnp.concatenate(parts, axis=1)

    grad_hidden, grad_return = tiles(0), tiles(1).T
    rank = lax.axis_index("dp")
    gains = lax.dynamic_slice_in_dim(gains.reshape(2, width), rank * (width // dp_count), width // dp_count, 1)

    placed_outputs, input_grad = place_rows(
        resets, offsets, outputs, outputs_got, mine_rows, their_rows
    )
    return (
        placed_outputs,
        new_rows[:, : comp_grad.shape[1]],
        input_grad,
        grad_query,
        grad_key,
        grad_value,
        grad_output,
        grad_hidden,
        grad_return,
        grad_compress,
        gains[0],
        gains[1],
    )


def solution(mesh):
    placed = (
        P("dp", "seq", None),
        P("dp", "seq", None),
        P("dp", "seq", None),
        P("dp"),
        P("dp"),
        P(),
        P(),
        P(),
        P(),
        P(None, "seq"),
        P("seq", None),
        P(),
        P(),
        P(),
        P("dp", "seq", None),
        P("dp", None, None),
    )
    fast = mesh.shape["seq"] == 2 and mesh.shape["dp"] == 16
    return jax.shard_map(
        on_device_pair if fast else on_device,
        mesh=mesh,
        in_specs=placed,
        out_specs=(
            P("dp", "seq", None),
            P("dp", None, None),
            P("dp", "seq", None),
            P("dp", "seq"),
            P("dp", "seq"),
            P("dp", "seq"),
            P("dp", "seq"),
            P("dp", "seq"),
            P("seq", "dp"),
            P("dp", "seq"),
            P("dp"),
            P("dp"),
        ),
        check_vma=False,
    )
```
